32 devices in a mesh: dp: 8 (over z, x), tm: 4 (over y, core).
Axes of the slice: x: 2, y: 2, z: 4, core: 2. Of those that a mesh axis runs over, the one named last changes fastest.
Arguments:
- inputs: bfloat16 [32, 2048, 512], P('dp', 'tm'), may hold values from -6 to 6
- lengths: int32 [32], replicated, may hold values from 128 to 2048, as said below
- depth_w: bfloat16 [5, 5, 512], P(None, None, ('dp', 'tm')), may hold values from -2.5 to 2.5
- point_w: bfloat16 [5, 512, 512], P(None, ('dp', 'tm')), may hold values from -0.25 to 0.25
- gamma: bfloat16 [5, 512], P(None, ('dp', 'tm')), may hold values from 0.5 to 1.5
- beta: bfloat16 [5, 512], P(None, ('dp', 'tm')), may hold values from -3 to 3
- squeeze_w: bfloat16 [512, 64], P(('dp', 'tm')), may hold values from -0.5 to 0.5
- excite_w: bfloat16 [64, 512], P(None, ('dp', 'tm')), may hold values from -1.5 to 1.5
- resid_w: bfloat16 [512, 512], P(('dp', 'tm')), may hold values from -0.25 to 0.25
- cotangent: bfloat16 [32, 2048, 512], P('dp', 'tm'), may hold values from -6 to 6
Outputs:
- output: bfloat16 [32, 2048, 512], P('dp', 'tm')
- grad_inputs: bfloat16 [32, 2048, 512], P('dp', 'tm')
- grad_depth: float32 [5, 5, 512], P(None, None, ('dp', 'tm'))
- grad_point: float32 [5, 512, 512], P(None, ('dp', 'tm'))
- grad_gamma: float32 [5, 512], P(None, ('dp', 'tm'))
- grad_beta: float32 [5, 512], P(None, ('dp', 'tm'))
- grad_squeeze: float32 [512, 64], P(('dp', 'tm'))
- grad_excite: float32 [64, 512], P(None, ('dp', 'tm'))
- grad_resid: float32 [512, 512], P(('dp', 'tm'))
The draws below stay inside these ranges and needn't reach their ends.
Inputs may be any that keep to these rules, and one draw needn't show every extreme that they name: `lengths`: each aligned block of 4 utterances holds exactly one of length 2048; the others have at most 512 frames.
All inputs are finite; a program needn't handle non-finite values.
Results may differ from the reference program's by a relative error of at most 0.025.
Values may be sent and summed in bfloat16 or wider, within the bound.
A program may use at most 128 MiB of HBM per device.

```python
import jax
import jax.numpy as jnp
from jax import lax

C = 512
SE = 64
LAYERS = 5
KERNEL = 5
UTT_DEV = 4
BATCH = 32
LENGTH = 2048


def draw_lengths(key, part):
    key = jax.random.fold_in(key, 7)
    short_key, pick_key = jax.random.split(key)
    short_len = jax.random.randint(short_key, (BATCH,), LENGTH // 16, LENGTH // 4 + 1)
    picked = jax.random.randint(pick_key, (BATCH // UTT_DEV,), 0, UTT_DEV)
    slot_index = lax.iota(jnp.int32, BATCH) % UTT_DEV
    long_slot = jnp.repeat(picked, UTT_DEV)
    return jnp.where(slot_index == long_slot, LENGTH, short_len).astype(jnp.int32)


def level_of(own_key, dims, shards, smallest, high):
    loudness = 1.0
    for dim, parts in shards:
        heights = jax.random.uniform(jax.random.fold_in(jax.random.fold_in(own_key, 6), dim), (parts,), jnp.float32, smallest / len(shards), high / len(shards))
        loudness = loudness * jnp.repeat(jnp.exp(heights), dims[dim] // parts).reshape((-1,) + (1,) * (len(dims) - 1 - dim))
    return loudness


def bell_draw(own_key, dims, scale, reach, cuts=(), dtype=jnp.bfloat16):
    gain = level_of(own_key, dims, cuts, -0.22, 0.18) if cuts else 1.0
    values = jax.random.normal(own_key, dims, jnp.float32) * scale * gain
    return jnp.minimum(jnp.maximum(values, -reach), reach).astype(dtype)


def setup_inputs(seed: int = 0) -> dict:
    streams_of = jax.random.split(jax.random.key(seed), 11)
    inputs = bell_draw(streams_of[0], (BATCH, LENGTH, C), 1.0, 6.0, ((0, 8), (1, 4)))
    lengths = draw_lengths(jax.random.fold_in(streams_of[10], 71), 0)
    depth_w = bell_draw(streams_of[2], (LAYERS, KERNEL, C), KERNEL ** -0.5, 2.5, ((2, 32),))
    point_w = bell_draw(streams_of[3], (LAYERS, C, C), C ** -0.5, 0.25, ((1, 32),))
    gamma = jnp.clip(1.0 + 0.1 * jax.random.normal(streams_of[4], (LAYERS, C), jnp.float32), 0.5, 1.5).astype(jnp.bfloat16)
    beta = bell_draw(streams_of[5], (LAYERS, C), 0.5, 3.0, ((1, 32),))
    squeeze_w = bell_draw(streams_of[6], (C, SE), (C // 4) ** -0.5, 0.5, ((0, 32),))
    excite_w = bell_draw(streams_of[7], (SE, C), (SE // 4) ** -0.5, 1.5, ((1, 32),))
    resid_w = bell_draw(streams_of[8], (C, C), C ** -0.5, 0.25, ((0, 32),))
    cotangent = bell_draw(streams_of[9], (BATCH, LENGTH, C), 1.0, 6.0, ((0, 8), (1, 4)))
    return {"inputs": inputs, "lengths": lengths, "depth_w": depth_w, "point_w": point_w, "gamma": gamma, "beta": beta, "squeeze_w": squeeze_w, "excite_w": excite_w, "resid_w": resid_w, "cotangent": cotangent}


NORM_EPSILON = 1e-05

@jax.custom_vjp
def low(v):
    return lax.optimization_barrier(v.astype(jnp.bfloat16)).astype(jnp.float32)

@jax.custom_vjp
def low_back(v):
    return v

def low_keep(v):
    return (low(v), None)

def low_pass(kept, grad):
    return (grad,)

def back_keep(v):
    return (v, None)

def back_low(kept, grad):
    return (low(grad),)
low.defvjp(low_keep, low_pass)
low_back.defvjp(back_keep, back_low)

def swish_act(value):
    return value * jax.nn.sigmoid(value)

def forward(inputs, depth_w, point_w, gamma, beta, squeeze_w, excite_w, resid_w, frame_mask, frame_count, length_float):
    highest = lax.Precision.HIGHEST
    frames = inputs.shape[1]
    current = inputs * frame_mask
    for layer_idx in range(LAYERS):
        conv_in = low(current)
        padded = jnp.pad(conv_in, ((0, 0), (KERNEL // 2, KERNEL // 2), (0, 0)))
        conv_out = padded[:, 0:frames] * depth_w[layer_idx, 0]
        for tap_idx in range(1, KERNEL):
            conv_out = conv_out + padded[:, tap_idx:tap_idx + frames] * depth_w[layer_idx, tap_idx]
        conv_low = low_back(low(conv_out))
        pre_norm = low_back(jnp.einsum('btc,cd->btd', conv_low, point_w[layer_idx], precision=highest))
        mean_val = lax.optimization_barrier(jnp.sum(frame_mask * pre_norm, axis=(0, 1))) / frame_count
        variance = lax.optimization_barrier(jnp.sum(frame_mask * pre_norm * pre_norm, axis=(0, 1))) / frame_count - mean_val * mean_val
        inv_std = lax.rsqrt(variance + NORM_EPSILON)
        normed = (pre_norm - mean_val) * inv_std * gamma[layer_idx] + beta[layer_idx]
        current = swish_act(normed) * frame_mask
    pooled = lax.optimization_barrier(jnp.sum(current * frame_mask, axis=1)) / length_float[:, None]
    squeezed = swish_act(jnp.dot(pooled, squeeze_w, precision=highest))
    gate_val = jax.nn.sigmoid(jnp.dot(squeezed, excite_w, precision=highest))
    resid = low_back(jnp.einsum('btc,cd->btd', inputs, resid_w, precision=highest))
    total_pre = current * gate_val[:, None, :] + resid
    return swish_act(total_pre) * frame_mask

def reference(inputs, lengths, depth_w, point_w, gamma, beta, squeeze_w, excite_w, resid_w, cotangent):
    positions = lax.iota(jnp.int32, inputs.shape[1])
    frame_mask = (positions[None, :] < lengths[:, None]).astype(jnp.float32)[:, :, None]
    frame_count = jnp.sum(lengths).astype(jnp.float32)
    length_float = lengths.astype(jnp.float32)

    def forward_fn(*primals):
        return forward(*primals, frame_mask, frame_count, length_float)
    primals = tuple((a.astype(jnp.float32) for a in (inputs, depth_w, point_w, gamma, beta, squeeze_w, excite_w, resid_w)))
    result, pull_back = jax.vjp(forward_fn, *primals)
    gradients = pull_back(cotangent.astype(jnp.float32))
    return (result.astype(jnp.bfloat16), gradients[0].astype(jnp.bfloat16), gradients[1], gradients[2], gradients[3], gradients[4], gradients[5], gradients[6], gradients[7])
```

```python
import functools

import jax
import jax.numpy as jnp
from jax import lax
from jax.experimental import pallas as pl
from jax.experimental.pallas import tpu as pltpu
from jax.sharding import PartitionSpec as P

MESH = pl.DeviceIdType.MESH
NORM_EPSILON = 1e-05
LANES = 128
HIGHEST = lax.Precision.HIGHEST
F32 = jnp.float32
BF16 = jnp.bfloat16


def dot(a, b, dims=((1,), (0,)), precision=None):
    return lax.dot_general(a, b, (dims, ((), ())), precision=precision, preferred_element_type=F32)


def logistic(v):
    return 0.5 * jnp.tanh(0.5 * v) + 0.5


def block_kernel(
    cfg,
    lengths, x_any, g_any, point, taps, gamma, beta, squeeze, excite, resid,
    out_any, gin_any, gpoint_any, gres_any, gdepth, ggb, fac_p, fac_z, fac_de, fac_dq,
    xv, xs, edge, xin, gin4, halo_l, halo_r, cot, ypad, dlow, pre, hh, mask, hmask, coef, resd, act, du, drl, dn,
    dhl, ddpad, gres_in, perm_l, perm_s, back_l, back_s, outp, obuf, gbuf, gp,
    sums, send_a, send_b, recv_core, recv_chip, hsend, dhh, tsend, trecv, pool, gate, cvec,
    sem_loc, sem_cs, sem_cr, sem_ks, sem_kr, sem_hs, sem_hr, sem_ts, sem_tr, sem_xs, sem_xr, sem_os, sem_or,
):
    DP, TM, U, F, C, LAYERS, KERNEL = cfg
    NL = C // LANES
    UR = F // 4
    NU = 4 + (U - 1)
    NB = UR // 16
    R = NU * UR
    N_SRC = TM // 4
    dp, tm = lax.axis_index("dp"), lax.axis_index("tm")
    partner = tm + 1 - 2 * lax.rem(tm, 2)
    first, last = tm == 0, tm == TM - 1
    chips = [(a, 2 * b) for a in range(DP) for b in range(TM // 2) if a or b]
    chips = chips[::-1]

    def at_chip(offset):
        return (lax.rem(dp + offset[0], DP), lax.rem(tm + offset[1], TM))

    def win(u):
        return u * UR if u < 4 else F + 64 + (u - 4) * (UR + 64)

    def seg_of(u):
        return 0 if u < 4 else u - 3

    def lane(j):
        return pl.ds(pl.multiple_of(j * LANES, LANES), LANES)

    def wide(v):
        return jnp.concatenate([v] * NL, axis=1)

    def remote(src, dst, ssem, rsem, dev):
        return pltpu.make_async_remote_copy(src, dst, ssem, rsem, device_id=dev, device_id_type=MESH)

    barrier = pltpu.get_barrier_semaphore()
    load_x = pltpu.make_async_copy(x_any, xv, sem_loc.at[0])
    load_x.start()
    others = [(0, b) for b in range(1, TM, 2)]
    for offset in chips + others:
        pl.semaphore_signal(barrier, inc=1, device_id=at_chip(offset), device_id_type=MESH)

    my_len = [lengths[dp * U + b] for b in range(U)]
    long_at = jnp.int32(0)
    for b in range(1, U):
        long_at = jnp.where(my_len[b] == F * TM, jnp.int32(b), long_at)
    short_at = [jnp.where(k < long_at, k, k + 1) for k in range(U - 1)]
    short_len = [lengths[dp * U + b] for b in range(U - 1)]
    short_len = [jnp.where(k < long_at, my_len[k], my_len[k + 1]) for k in range(U - 1)]
    count = lax.fori_loop(0, DP * U, lambda i, c: c + lengths[i], jnp.int32(0)).astype(F32)
    inv_count = 1.0 / jnp.full((1, LANES), count, F32)
    rows = lax.broadcasted_iota(jnp.int32, (UR, LANES), 0)
    time_s = (rows & 15) * NB + (rows >> 4) + tm * UR
    for k in range(U - 1):
        mask[k * UR : (k + 1) * UR, :] = jnp.where(time_s < short_len[k], 1.0, 0.0)
    e16 = lax.broadcasted_iota(jnp.int32, (16, LANES), 0)
    part = (e16 & 7) >> 1
    is_left = e16 < 8
    when = jnp.where(is_left, tm * UR - 2 + (e16 & 1), tm * UR + UR + (e16 & 1))
    bound = jnp.full((16, LANES), 1 << 30, jnp.int32)
    for k in range(U - 1):
        bound = jnp.where(part == k + 1, short_len[k], bound)
    inside = jnp.where(is_left, tm, TM - 1 - tm) > 0
    hmask[...] = jnp.where(inside & (when < bound), 1.0, 0.0)

    def one_hot(ref, size, to_time):
        n = size // 16
        r0 = lax.broadcasted_iota(jnp.int32, (UR, size), 0)
        r1 = lax.broadcasted_iota(jnp.int32, (UR, size), 1)
        for c in range(size // UR):
            a, b = (r1, r0 + c * UR) if to_time else (r0 + c * UR, r1)
            hit = b == (a & 15) * n + (a >> 4)
            ref[c * UR : (c + 1) * UR, :] = jnp.where(hit, 1.0, 0.0).astype(BF16)

    one_hot(perm_l, F, False)
    one_hot(perm_s, UR, False)
    one_hot(back_l, F, True)
    one_hot(back_s, UR, True)

    @pl.when(first)
    def _():
        halo_l[...] = jnp.zeros(halo_l.shape, BF16)
        for l in range(LAYERS):
            hh[l, 0:8, :] = jnp.zeros((8, C), F32)
            dhh[l, 0:8, :] = jnp.zeros((8, C), F32)

    @pl.when(last)
    def _():
        halo_r[...] = jnp.zeros(halo_r.shape, BF16)
        for l in range(LAYERS):
            hh[l, 8:16, :] = jnp.zeros((8, C), F32)
            dhh[l, 8:16, :] = jnp.zeros((8, C), F32)

    def stage_short():
        @pl.when(tm < N_SRC)
        def _():
            for k in range(U - 1):
                def cp(c, _):
                    sl = pl.ds(pl.multiple_of(c * UR, UR), UR)
                    xs[k, sl, :] = xv[short_at[k], sl, :]
                    return 0
                lax.fori_loop(0, 4, cp, 0)

    def send_short(dst, with_halo, half):
        def act_on(d):
            if half == 0:
                d.start()
            else:
                d.wait_send()

        @pl.when(tm < N_SRC)
        def _():
            for q in range(4):
                chunk = 4 * tm + q
                main = xs.at[:, q * UR : (q + 1) * UR, :]
                head = xs.at[:, q * UR : q * UR + 16, :]
                tail = xs.at[:, (q + 1) * UR - 16 : (q + 1) * UR, :]

                def go_main():
                    act_on(remote(main, dst, sem_xs.at[q], sem_xr.at[0 if with_halo else 5], (dp, chunk)))

                def go_head():
                    act_on(remote(head, halo_r.at[1:U], sem_xs.at[4 + q], sem_xr.at[1], (dp, chunk - 1)))

                if q == 0:
                    pl.when(tm > 0)(go_main)
                    if half == 0:
                        @pl.when(tm == 0)
                        def _():
                            for k in range(U - 1):
                                dst[k] = xs[k, 0:UR, :]
                else:
                    go_main()
                if with_halo:
                    if q < 2:
                        pl.when(tm > 0)(go_head)
                    else:
                        go_head()
                    if q == 1 and half == 0:
                        @pl.when(tm == 0)
                        def _():
                            for k in range(U - 1):
                                halo_r[1 + k] = xs[k, UR : UR + 16, :]

                    @pl.when(chunk + 1 < TM)
                    def _():
                        act_on(remote(tail, halo_l.at[1:U], sem_xs.at[8 + q], sem_xr.at[2], (dp, chunk + 1)))

    def recv_short(dst, with_halo):
        @pl.when(tm > 0)
        def _():
            pltpu.make_async_copy(dst, dst, sem_xr.at[0 if with_halo else 5]).wait()
            if with_halo:
                pltpu.make_async_copy(halo_l.at[1:U], halo_l.at[1:U], sem_xr.at[2]).wait()

                @pl.when(tm < TM - 1)
                def _():
                    pltpu.make_async_copy(halo_r.at[1:U], halo_r.at[1:U], sem_xr.at[1]).wait()

    def edges(send, recv_l, recv_r, ssem, rsem, start):
        to_next = remote(send.at[1], recv_l, ssem.at[0], rsem.at[0], (dp, lax.rem(tm + 1, TM)))
        to_prev = remote(send.at[0], recv_r, ssem.at[1], rsem.at[1], (dp, lax.rem(tm + TM - 1, TM)))
        if start:
            pl.when(tm < TM - 1)(lambda: to_next.start())
            pl.when(tm > 0)(lambda: to_prev.start())
        else:
            @pl.when(tm < TM - 1)
            def _():
                to_next.wait_send()
                to_prev.wait_recv()

            @pl.when(tm > 0)
            def _():
                to_prev.wait_send()
                to_next.wait_recv()

    load_x.wait()
    edge[0] = xv[long_at, 0:16, :]
    edge[1] = xv[long_at, F - 16 : F, :]
    stage_short()
    pl.semaphore_wait(barrier, len(chips) + len(others))
    edges(edge, halo_l.at[0], halo_r.at[0], sem_xs.at[pl.ds(12, 2)], sem_xr.at[pl.ds(3, 2)], True)
    send_short(xin, True, 0)

    def to_perm_long(src, dst, base):
        for u in range(4):
            o = base(u)
            dst[o : o + UR, :] = dot(perm_l[u * UR : (u + 1) * UR, :], src).astype(BF16)

    def to_perm_short(src, dst, base, masked):
        for k in range(U - 1):
            v = dot(perm_s[...], src[k])
            if masked:
                v = v * wide(mask[k * UR : (k + 1) * UR, :])
            o = base(4 + k)
            dst[o : o + UR, :] = v.astype(BF16)

    y0 = ypad.at[0]
    to_perm_long(xv[long_at], y0, lambda u: win(u) + 32)
    edges(edge, halo_l.at[0], halo_r.at[0], sem_xs.at[pl.ds(12, 2)], sem_xr.at[pl.ds(3, 2)], False)
    recv_short(xin, True)
    to_perm_short(xin, y0, lambda u: win(u) + 32, True)
    send_short(xin, True, 1)
    load_g = pltpu.make_async_copy(g_any, xv, sem_loc.at[0])
    load_g.start()

    def fill_pads(ref, row0, n, j, b0, b1, b2, b3, halo, seg):
        e = lax.broadcasted_iota(jnp.int32, (16, LANES), 0)

        def put(at, v):
            ref[pl.ds(row0 + at * 16, 16), lane(j)] = v.astype(BF16)

        put(0, jnp.where(e == 0, halo[2 * seg : 2 * seg + 1], pltpu.roll(b2, 1, 0)))
        put(1, jnp.where(e == 0, halo[2 * seg + 1 : 2 * seg + 2], pltpu.roll(b3, 1, 0)))
        put(n + 2, jnp.where(e == 15, halo[8 + 2 * seg : 9 + 2 * seg], pltpu.roll(b0, 15, 0)))
        put(n + 3, jnp.where(e == 15, halo[9 + 2 * seg : 10 + 2 * seg], pltpu.roll(b1, 15, 0)))

    def pads_from(ref, j, halo):
        for seg in range(U):
            u0, u1 = (0, 3) if seg == 0 else (3 + seg, 3 + seg)
            n = F // 16 if seg == 0 else NB
            o0, o1 = win(u0) + 32, win(u1) + 32 + UR
            blk = [ref[o : o + 16, lane(j)].astype(F32) for o in (o0, o0 + 16, o1 - 32, o1 - 16)]
            fill_pads(ref, win(u0), n, j, *blk, halo, seg)

    def first_pads(j, _):
        left = [halo_l[s, :, lane(j)].astype(F32)[14:16] for s in range(4)]
        right = [halo_r[s, :, lane(j)].astype(F32)[0:2] for s in range(4)]
        halo = jnp.concatenate(left + right, axis=0) * hmask[...]
        pads_from(y0, j, halo)
        return 0

    lax.fori_loop(0, NL, first_pads, 0)

    def sync_core(s):
        d = remote(send_a.at[s], recv_core.at[s], sem_cs.at[s], sem_cr.at[s], (dp, partner))
        d.start()
        d.wait()
        send_b[s] = send_a[s] + recv_core[s]

    def sync_send(s):
        for i, offset in enumerate(chips):
            remote(send_b.at[s], recv_chip.at[s, i], sem_ks.at[s], sem_kr.at[s], at_chip(offset)).start()

    def sync_done(s):
        whole = recv_chip.at[s]
        pltpu.make_async_copy(whole, whole, sem_kr.at[s]).wait()
        pltpu.make_async_copy(whole, whole, sem_ks.at[s]).wait()
        total = send_b[s]
        for i in range(len(chips)):
            total = total + recv_chip[s, i]
        return total

    def conv_pass(l):
        def body(j, _):
            w = [taps[l, k : k + 1, lane(j)] for k in range(KERNEL)]
            for u in range(NU):
                o = win(u)
                v = ypad[l, o : o + UR + 64, lane(j)].astype(F32)
                t = v[0:UR] * w[0]
                for k in range(1, KERNEL):
                    t = t + v[16 * k : 16 * k + UR] * w[k]
                if u >= 4:
                    t = t * mask[(u - 4) * UR : (u - 3) * UR, :]
                dlow[l, u * UR : (u + 1) * UR, lane(j)] = t.astype(BF16)
            return 0

        lax.fori_loop(0, NL, body, 0)

    def fold8(v):
        return jnp.sum(v.reshape(v.shape[0] // 8, 8, v.shape[1]), axis=0)

    def put_edges(src, l):
        for seg in range(4):
            base = 0 if seg == 0 else F + (seg - 1) * UR
            n = F if seg == 0 else UR
            for e in range(2):
                hsend[l, 1, 2 * seg + e : 2 * seg + e + 1, :] = src(base + n - 32 + 16 * e + 15)
                hsend[l, 0, 2 * seg + e : 2 * seg + e + 1, :] = src(base + 16 * e)

    def matmul_pass(l):
        sums[...] = jnp.zeros(sums.shape, F32)

        def body(u, _):
            r = pl.ds(pl.multiple_of(u * UR, UR), UR)
            h = dot(dlow[l, r, :], point[l])
            pre[l, r, :] = h
            sums[0] += fold8(h)
            sums[1] += fold8(h * h)
            return 0

        lax.fori_loop(0, NU, body, 0)
        send_a[l, 0:1, :] = jnp.sum(sums[0], axis=0, keepdims=True)
        send_a[l, 1:2, :] = jnp.sum(sums[1], axis=0, keepdims=True)
        put_edges(lambda row: pre[l, row : row + 1, :], l)

    def layer(l, _):
        conv_pass(l)
        matmul_pass(l)
        edges(hsend.at[l], hh.at[l, 0:8], hh.at[l, 8:16], sem_hs.at[l], sem_hr.at[l], True)
        sync_core(l)
        sync_send(l)

        @pl.when(l == 0)
        def _():
            def rbody(u, _):
                o = jnp.where(u < 4, u * UR, F + 64 + (u - 4) * (UR + 64)) + 32
                src = ypad[0, pl.ds(pl.multiple_of(o, 16), UR), :]
                resd[pl.ds(pl.multiple_of(u * UR, UR), UR), :] = dot(src, resid[...])
                return 0
            lax.fori_loop(0, NU, rbody, 0)
            load_g.wait()
            stage_short()
            send_short(gin4, False, 0)
            to_perm_long(xv[long_at], cot, lambda u: u * UR)

        @pl.when(l == 1)
        def _():
            recv_short(gin4, False)
            to_perm_short(gin4, cot, lambda u: u * UR, True)
            send_short(gin4, False, 1)

        total = sync_done(l)
        edges(hsend.at[l], hh.at[l, 0:8], hh.at[l, 8:16], sem_hs.at[l], sem_hr.at[l], False)
        scale = wide(inv_count)
        mean = total[0:1] * scale
        var = total[1:2] * scale - mean * mean
        inv = lax.rsqrt(var + NORM_EPSILON)
        ga = gamma[pl.ds(l, 1), :]
        a = ga * inv
        coef[l, 0:1, :] = 0.5 * a
        coef[l, 1:2, :] = 0.5 * (beta[pl.ds(l, 1), :] - mean * a)
        coef[l, 2:3, :] = mean
        coef[l, 3:4, :] = inv
        coef[l, 4:5, :] = a

        @pl.when(l < LAYERS - 1)
        def _():
            def body(j, _):
                a, b = coef[l, 0:1, lane(j)], coef[l, 1:2, lane(j)]
                for u in range(NU):
                    v = pre[l, u * UR : (u + 1) * UR, lane(j)] * a + b
                    v = v + v * jnp.tanh(v)
                    if u >= 4:
                        v = v * mask[(u - 4) * UR : (u - 3) * UR, :]
                    o = win(u) + 32
                    ypad[l + 1, o : o + UR, lane(j)] = v.astype(BF16)
                v = hh[l, :, lane(j)] * a + b
                v = (v + v * jnp.tanh(v)) * hmask[...]
                pads_from(ypad.at[l + 1], j, v)
                return 0

            lax.fori_loop(0, NL, body, 0)
        return 0

    lax.fori_loop(0, LAYERS, layer, 0)

    top = LAYERS - 1
    pool[...] = jnp.zeros(pool.shape, F32)

    def last_act(j, _):
        a, b = coef[top, 0:1, lane(j)], coef[top, 1:2, lane(j)]
        acc = None
        for u in range(NU):
            v = pre[top, u * UR : (u + 1) * UR, lane(j)] * a + b
            v = v + v * jnp.tanh(v)
            if u >= 4:
                v = v * mask[(u - 4) * UR : (u - 3) * UR, :]
            act[u * UR : (u + 1) * UR, lane(j)] = v
            f = fold8(v)
            acc = f if u == 0 or u >= 4 else acc + f
            if u >= 3:
                pool[u - 3 : u - 2, lane(j)] = jnp.sum(acc, axis=0, keepdims=True)
        return 0

    lax.fori_loop(0, NL, last_act, 0)

    def time_sum(s, value):
        tsend[s] = value
        ds = [remote(tsend.at[s], trecv.at[s, i - 1], sem_ts.at[s], sem_tr.at[s], (dp, lax.rem(tm + i, TM))) for i in range(1, TM)]
        for d in ds:
            d.start()

    def time_done(s):
        whole = trecv.at[s]
        pltpu.make_async_copy(whole, whole, sem_tr.at[s]).wait()
        pltpu.make_async_copy(whole, whole, sem_ts.at[s]).wait()
        total = tsend[s]
        for i in range(TM - 1):
            total = total + trecv[s, i]
        return total

    e8 = lax.broadcasted_iota(jnp.int32, (8, LANES), 0)
    len8 = jnp.full((8, LANES), F * TM, jnp.int32)
    for k in range(U - 1):
        len8 = jnp.where(e8 == k + 1, short_len[k], len8)
    inv_len = 1.0 / len8.astype(F32)
    live = jnp.where(e8 < U, 1.0, 0.0)
    time_sum(0, pool[...])
    p = time_done(0) * wide(inv_len)
    sq = squeeze[...].astype(F32)
    ex = excite[...].astype(F32)
    q = dot(p, sq, precision=HIGHEST)
    sig_q = logistic(q)
    z = q * sig_q
    gate[...] = logistic(dot(z, ex, precision=HIGHEST))
    pool[...] = jnp.zeros(pool.shape, F32)

    def top_pass(j, _):
        acc = None
        for u in range(NU):
            rs = slice(u * UR, (u + 1) * UR)
            seg = seg_of(u)
            av = act[rs, lane(j)]
            half = 0.5 * (av * gate[seg : seg + 1, lane(j)] + resd[rs, lane(j)])
            t = jnp.tanh(half)
            out = half + half * t
            slope = (0.5 + 0.5 * t) * (1.0 + half * (1.0 - t))
            dv = cot[rs, lane(j)].astype(F32) * slope
            if u >= 4:
                out = out * mask[(u - 4) * UR : (u - 3) * UR, :]
            outp[rs, lane(j)] = out.astype(BF16)
            du[rs, lane(j)] = dv
            drl[rs, lane(j)] = dv.astype(BF16)
            f = fold8(dv * av)
            acc = f if u == 0 or u >= 4 else acc + f
            if u >= 3:
                pool[u - 3 : u - 2, lane(j)] = jnp.sum(acc, axis=0, keepdims=True)
        return 0

    lax.fori_loop(0, NL, top_pass, 0)
    time_sum(1, pool[...])

    def give_back(buf, src, sems, rsems, start):
        if start:
            for u in range(4):
                buf[0, u * UR : (u + 1) * UR, :] = dot(back_l[u * UR : (u + 1) * UR, :], src[0:F, :]).astype(BF16)
            for k in range(U - 1):
                xin[k] = dot(back_s[...], src[F + k * UR : F + (k + 1) * UR, :]).astype(BF16)

            @pl.when(tm >= N_SRC)
            def _():
                for k in range(U - 1):
                    buf[1 + k] = jnp.zeros((F, C), BF16)

        owner, q = tm // 4, lax.rem(tm, 4)
        d = remote(xin, buf.at[1:U, pl.ds(pl.multiple_of(q * UR, UR), UR), :], sems, rsems.at[q], (dp, owner))
        if start:
            @pl.when(first)
            def _():
                for k in range(U - 1):
                    buf[1 + k, 0:UR, :] = xin[k]

            pl.when(tm > 0)(lambda: d.start())
        else:
            pl.when(tm > 0)(lambda: d.wait_send())

            @pl.when(tm < N_SRC)
            def _():
                for i in range(4):
                    got = buf.at[1:U, i * UR : (i + 1) * UR, :]
                    arrived = pltpu.make_async_copy(got, got, rsems.at[i])
                    if i == 0:
                        pl.when(tm > 0)(lambda: arrived.wait())
                    else:
                        arrived.wait()

    give_back(obuf, outp, sem_os.at[0], sem_or.at[0], True)

    def xrows(u):
        o = win(u) + 32
        return ypad[0, o : o + UR, :]

    def resid_grads():
        acc = None
        for u in range(NU):
            rs = slice(u * UR, (u + 1) * UR)
            part = dot(xrows(u), drl[rs, :], ((0,), (0,)))
            gp[...] = part if u == 0 else gp[...] + part

        def body(u, _):
            r = pl.ds(pl.multiple_of(u * UR, UR), UR)
            gres_in[r, :] = dot(drl[r, :], resid[...], ((1,), (1,)))
            return 0

        lax.fori_loop(0, NU, body, 0)

    resid_grads()
    put_gres = pltpu.make_async_copy(gp, gres_any, sem_loc.at[1])
    put_gres.start()
    dg = time_done(1)
    gv = gate[...]
    de = dg * gv * (1.0 - gv) * wide(live)
    dz = dot(de, ex, ((1,), (1,)), precision=HIGHEST)
    dq = dz * sig_q * (1.0 + q * (1.0 - sig_q))
    cvec[...] = dot(dq, sq, ((1,), (1,)), precision=HIGHEST) * wide(inv_len)
    fac_p[...] = p
    fac_z[...] = z
    fac_de[...] = de
    fac_dq[...] = dq

    def norm_slope(l, u, j, a, b, m, s):
        h = pre[l, u * UR : (u + 1) * UR, lane(j)]
        half = h * a + b
        t = jnp.tanh(half)
        slope = (0.5 + 0.5 * t) * (1.0 + half * (1.0 - t))
        if u >= 4:
            slope = slope * mask[(u - 4) * UR : (u - 3) * UR, :]
        return slope, (h - m) * s

    def back_sums(l, s, grad_of):
        def body(j, _):
            a, b, m, i = (coef[l, r : r + 1, lane(j)] for r in range(4))
            acc0 = acc1 = None
            make = grad_of(j)
            for u in range(NU):
                slope, xc = norm_slope(l, u, j, a, b, m, i)
                v = make(u) * slope
                dn[u * UR : (u + 1) * UR, lane(j)] = v
                f0, f1 = fold8(v), fold8(v * xc)
                acc0 = f0 if u == 0 else acc0 + f0
                acc1 = f1 if u == 0 else acc1 + f1
            send_a[s, 0:1, lane(j)] = jnp.sum(acc0, axis=0, keepdims=True)
            send_a[s, 1:2, lane(j)] = jnp.sum(acc1, axis=0, keepdims=True)
            return 0

        lax.fori_loop(0, NL, body, 0)
        put_edges(lambda row: dn[row : row + 1, :], s)

    def top_grad(j):
        def make(u):
            seg = seg_of(u)
            return du[u * UR : (u + 1) * UR, lane(j)] * gate[seg : seg + 1, lane(j)] + cvec[seg : seg + 1, lane(j)]
        return make

    def conv_grad(l):
        def outer(j):
            w = [taps[l, k : k + 1, lane(j)] for k in range(KERNEL)]

            def make(u):
                o = win(u)
                v = ddpad[o : o + UR + 64, lane(j)].astype(F32)
                t = v[64 : 64 + UR] * w[0]
                for k in range(1, KERNEL):
                    t = t + v[64 - 16 * k : 64 - 16 * k + UR] * w[k]
                return t
            return make
        return outer

    back_sums(top, LAYERS, top_grad)

    def weight_grads(l):
        def body(j, _):
            acc = [None] * KERNEL
            for u in range(NU):
                o = win(u)
                v = ypad[l, o : o + UR + 64, lane(j)].astype(F32)
                g = ddpad[o + 32 : o + 32 + UR, lane(j)].astype(F32)
                for k in range(KERNEL):
                    f = fold8(v[16 * k : 16 * k + UR] * g)
                    acc[k] = f if u == 0 else acc[k] + f
            for k in range(KERNEL):
                gdepth[l, k : k + 1, lane(j)] = jnp.sum(acc[k], axis=0, keepdims=True)
            return 0

        lax.fori_loop(0, NL, body, 0)
        pltpu.make_async_copy(gp, gres_any, sem_loc.at[1]).wait()
        for u in range(NU):
            rs = slice(u * UR, (u + 1) * UR)
            part = dot(dlow[l, rs, :], dhl[rs, :], ((0,), (0,)))
            gp[...] = part if u == 0 else gp[...] + part
        pltpu.make_async_copy(gp, gpoint_any.at[l], sem_loc.at[1]).start()

    def back_layer(step, _):
        l = top - step
        s = LAYERS + step
        edges(hsend.at[s], dhh.at[l, 0:8], dhh.at[l, 8:16], sem_hs.at[s], sem_hr.at[s], True)
        sync_core(s)
        sync_send(s)

        @pl.when(step > 0)
        def _():
            weight_grads(l + 1)

        total = sync_done(s)
        edges(hsend.at[s], dhh.at[l, 0:8], dhh.at[l, 8:16], sem_hs.at[s], sem_hr.at[s], False)
        ggb[l, 0:2, :] = total
        m, i, a = coef[l, 2:3, :], coef[l, 3:4, :], coef[l, 4:5, :]
        k1 = a * i * total[1:2] * wide(inv_count)
        coef[l, 5:6, :] = k1
        coef[l, 6:7, :] = a * total[0:1] * wide(inv_count) - m * k1

        def body(j, _):
            a, k1, k0 = (coef[l, r : r + 1, lane(j)] for r in (4, 5, 6))
            for u in range(NU):
                rs = slice(u * UR, (u + 1) * UR)
                v = dn[rs, lane(j)] * a - (pre[l, rs, lane(j)] * k1 + k0)
                if u >= 4:
                    v = v * mask[(u - 4) * UR : (u - 3) * UR, :]
                dhl[rs, lane(j)] = v.astype(BF16)
            v = (dhh[l, :, lane(j)] * a - (hh[l, :, lane(j)] * k1 + k0)) * hmask[...]
            dhl[R : R + 16, lane(j)] = v.astype(BF16)
            return 0

        lax.fori_loop(0, NL, body, 0)
        hh[l] = dot(dhl[R : R + 16, :], point[l], ((1,), (1,)))

        def mm(u, _):
            o = jnp.where(u < 4, u * UR, F + 64 + (u - 4) * (UR + 64)) + 32
            v = dot(dhl[pl.ds(pl.multiple_of(u * UR, UR), UR), :], point[l], ((1,), (1,)))
            ddpad[pl.ds(pl.multiple_of(o, 16), UR), :] = v.astype(BF16)
            return 0

        lax.fori_loop(0, NU, mm, 0)

        def pad(j, _):
            pads_from(ddpad, j, hh[l, :, lane(j)].astype(BF16).astype(F32))
            return 0

        lax.fori_loop(0, NL, pad, 0)

        @pl.when(l > 0)
        def _():
            back_sums(l - 1, s + 1, conv_grad(l - 1))
        return 0

    def run_back():
        lax.fori_loop(0, LAYERS, back_layer, 0)

    conv_grad_of = conv_grad

    def conv_grad(l):
        return conv_grad_of(l + 1)

    run_back()
    give_back(obuf, outp, sem_os.at[0], sem_or.at[0], False)
    put_out = pltpu.make_async_copy(obuf, out_any, sem_loc.at[2])
    put_out.start()

    def final(j, _):
        make = conv_grad_of(0)(j)
        for u in range(NU):
            rs = slice(u * UR, (u + 1) * UR)
            v = make(u)
            if u >= 4:
                v = v * mask[(u - 4) * UR : (u - 3) * UR, :]
            outp[rs, lane(j)] = (v + gres_in[rs, lane(j)]).astype(BF16)
        return 0

    lax.fori_loop(0, NL, final, 0)
    give_back(gbuf, outp, sem_os.at[1], sem_or.at[1], True)
    weight_grads(0)
    give_back(gbuf, outp, sem_os.at[1], sem_or.at[1], False)
    put_gin = pltpu.make_async_copy(gbuf, gin_any, sem_loc.at[3])
    put_gin.start()
    pltpu.make_async_copy(gp, gres_any, sem_loc.at[1]).wait()
    put_out.wait()
    put_gin.wait()


def local(sizes, inputs, lengths, depth_w, point_w, gamma, beta, squeeze_w, excite_w, resid_w, cotangent):
    DP, TM = sizes
    U, F, C = inputs.shape
    LAYERS, KERNEL = depth_w.shape[:2]
    SE = squeeze_w.shape[1]
    UR = F // 4
    NU = 4 + U - 1
    R = NU * UR
    RP = F + 64 + (U - 1) * (UR + 64)
    S = 2 * LAYERS
    chips = DP * (TM // 2) - 1
    axes = ("dp", "tm")
    point_all, depth_all, squeeze_all, excite_all, resid_all, gamma_all, beta_all = (
        lax.all_gather(point_w, axes, axis=1, tiled=True),
        lax.all_gather(depth_w, axes, axis=2, tiled=True),
        lax.all_gather(squeeze_w, axes, axis=0, tiled=True),
        lax.all_gather(excite_w, axes, axis=1, tiled=True),
        lax.all_gather(resid_w, axes, axis=0, tiled=True),
        lax.all_gather(gamma, axes, axis=1, tiled=True),
        lax.all_gather(beta, axes, axis=1, tiled=True),
    )
    vm = pltpu.VMEM
    dma = pltpu.SemaphoreType.DMA
    any_spec = pl.BlockSpec(memory_space=pl.ANY)
    vm_spec = pl.BlockSpec(memory_space=pltpu.VMEM)
    sd = jax.ShapeDtypeStruct
    scratch = dict(
        xv=vm((U, F, C), BF16), xs=vm((U - 1, F, C), BF16), edge=vm((2, 16, C), BF16),
        xin=vm((U - 1, UR, C), BF16), gin4=vm((U - 1, UR, C), BF16),
        halo_l=vm((4, 16, C), BF16), halo_r=vm((4, 16, C), BF16),
        cot=vm((R, C), BF16), ypad=vm((LAYERS, RP, C), BF16), dlow=vm((LAYERS, R, C), BF16),
        pre=vm((LAYERS, R, C), F32), hh=vm((LAYERS, 16, C), F32),
        mask=vm(((U - 1) * UR, LANES), F32), hmask=vm((16, LANES), F32), coef=vm((LAYERS, 8, C), F32),
        resd=vm((R, C), F32), act=vm((R, C), F32), du=vm((R, C), F32), drl=vm((R, C), BF16), dn=vm((R, C), F32),
        dhl=vm((R + 16, C), BF16), ddpad=vm((RP, C), BF16), gres_in=vm((R, C), F32),
        perm_l=vm((F, F), BF16), perm_s=vm((UR, UR), BF16), back_l=vm((F, F), BF16), back_s=vm((UR, UR), BF16),
        outp=vm((R, C), BF16), obuf=vm((U, F, C), BF16), gbuf=vm((U, F, C), BF16), gp=vm((C, C), F32),
        sums=vm((2, 8, C), F32), send_a=vm((S, 2, C), F32), send_b=vm((S, 2, C), F32),
        recv_core=vm((S, 2, C), F32), recv_chip=vm((S, chips, 2, C), F32),
        hsend=vm((S, 2, 8, C), F32), dhh=vm((LAYERS, 16, C), F32),
        tsend=vm((2, 8, C), F32), trecv=vm((2, TM - 1, 8, C), F32),
        pool=vm((8, C), F32), gate=vm((8, C), F32), cvec=vm((8, C), F32),
        sem_loc=dma((4,)), sem_cs=dma((S,)), sem_cr=dma((S,)), sem_ks=dma((S,)), sem_kr=dma((S,)),
        sem_hs=dma((S, 2)), sem_hr=dma((S, 2)), sem_ts=dma((2,)), sem_tr=dma((2,)),
        sem_xs=dma((14,)), sem_xr=dma((6,)), sem_os=dma((2,)), sem_or=dma((2, 4)),
    )
    out = pl.pallas_call(
        functools.partial(block_kernel, (DP, TM, U, F, C, LAYERS, KERNEL)),
        out_shape=(
            sd((U, F, C), BF16), sd((U, F, C), BF16), sd((LAYERS, C, C), F32), sd((C, C), F32),
            sd((LAYERS, KERNEL, C), F32), sd((LAYERS, 2, C), F32),
            sd((8, C), F32), sd((8, SE), F32), sd((8, C), F32), sd((8, SE), F32),
        ),
        in_specs=[pl.BlockSpec(memory_space=pltpu.SMEM), any_spec, any_spec] + [vm_spec] * 7,
        out_specs=(any_spec,) * 4 + (vm_spec,) * 6,
        scratch_shapes=list(scratch.values()),
        compiler_params=pltpu.CompilerParams(collective_id=0, has_side_effects=True, vmem_limit_bytes=62 << 20),
    )(
        lengths, inputs, cotangent, point_all, depth_all.astype(F32), gamma_all.astype(F32), beta_all.astype(F32),
        squeeze_all, excite_all, resid_all,
    )
    out_s, gin_s, gpoint, gres, gdepth, ggb, fac_p, fac_z, fac_de, fac_dq = out
    dp_index, tm_index = lax.axis_index("dp"), lax.axis_index("tm")
    my_len = lax.dynamic_slice_in_dim(lengths, dp_index * U, U, 0)
    long_at = jnp.argmax(my_len == F * TM)
    b = lax.iota(jnp.int32, U)
    slot = jnp.where(b == long_at, 0, jnp.where(b < long_at, b + 1, b))
    result = jnp.take(out_s, slot, axis=0)
    grad_inputs = jnp.take(gin_s, slot, axis=0)
    lead = (tm_index == 0).astype(F32)
    gex = lead * jnp.dot(fac_z.T, fac_de, precision=HIGHEST)
    gsq = lead * jnp.dot(fac_p.T, fac_dq, precision=HIGHEST)
    flat = dp_index * TM + tm_index
    shard = gamma.shape[1]
    mine = lax.dynamic_slice_in_dim(ggb, flat * shard, shard, 2)
    gpoint, gdepth, gsq, gex, gres = (
        lax.psum_scatter(gpoint, axes, scatter_dimension=1, tiled=True),
        lax.psum_scatter(gdepth, axes, scatter_dimension=2, tiled=True),
        lax.psum_scatter(gsq, axes, scatter_dimension=0, tiled=True),
        lax.psum_scatter(gex, axes, scatter_dimension=1, tiled=True),
        lax.psum_scatter(gres, axes, scatter_dimension=0, tiled=True),
    )
    return result, grad_inputs, gdepth, gpoint, mine[:, 1], mine[:, 0], gsq, gex, gres


def solution(mesh):
    both = ("dp", "tm")
    rows, cols = P(both, None), P(None, both)
    frames = P("dp", "tm", None)
    taps, mats = P(None, None, both), P(None, both, None)
    sizes = (mesh.shape["dp"], mesh.shape["tm"])
    return jax.shard_map(
        functools.partial(local, sizes),
        mesh=mesh,
        in_specs=(frames, P(), taps, mats, cols, cols, rows, cols, rows, frames),
        out_specs=(frames, frames, taps, mats, cols, cols, rows, cols, rows),
        check_vma=False,
    )
```

```python
import functools

import jax
import jax.numpy as jnp
from jax import lax
from jax.experimental import pallas as pl
from jax.experimental.pallas import tpu as pltpu
from jax.sharding import PartitionSpec as P

MESH = pl.DeviceIdType.MESH
NORM_EPSILON = 1e-05
LANES = 128
HIGHEST = lax.Precision.HIGHEST
F32 = jnp.float32
BF16 = jnp.bfloat16


def dot(a, b, dims=((1,), (0,)), precision=None):
    return lax.dot_general(a, b, (dims, ((), ())), precision=precision, preferred_element_type=F32)


def logistic(v):
    return 0.5 * jnp.tanh(0.5 * v) + 0.5


def block_kernel(cfg, names, *refs):
    DP, TM, U, F, C, SE, SH, LAYERS, KERNEL, fast = cfg
    env = dict(zip(names, refs, strict=True))
    lengths, x_any, g_any = env["lengths"], env["x_any"], env["g_any"]
    out_any, gin_any = env["out_any"], env["gin_any"]
    xv, xs, edge, xin, gin4 = env["xv"], env["xs"], env["edge"], env["xin"], env["gin4"]
    halo_l, halo_r, cot, ypad, dlow = env["halo_l"], env["halo_r"], env["cot"], env["ypad"], env["dlow"]
    pre, hh, mask, hmask, coef = env["pre"], env["hh"], env["mask"], env["hmask"], env["coef"]
    resd, act, du, drl, dn = env["resd"], env["act"], env["du"], env["drl"], env["dn"]
    dhl, ddpad, gres_in = env["dhl"], env["ddpad"], env["gres_in"]
    perm_l, perm_s, back_l, back_s = env["perm_l"], env["perm_s"], env["back_l"], env["back_s"]
    outp, obuf, gbuf, gp, small = env["outp"], env["obuf"], env["gbuf"], env["gp"], env["small"]
    sums, send_a, send_b, recv_core, recv_chip = (
        env["sums"], env["send_a"], env["send_b"], env["recv_core"], env["recv_chip"]
    )
    hsend, dhh, tsend, trecv = env["hsend"], env["dhh"], env["tsend"], env["trecv"]
    pool, gate, cvec, gsmall = env["pool"], env["gate"], env["cvec"], env["gsmall"]
    ggb = env["ggb"]
    sem_loc, sem_cs, sem_cr, sem_ks, sem_kr = (
        env["sem_loc"], env["sem_cs"], env["sem_cr"], env["sem_ks"], env["sem_kr"]
    )
    sem_hs, sem_hr, sem_ts, sem_tr = env["sem_hs"], env["sem_hr"], env["sem_ts"], env["sem_tr"]
    sem_xs, sem_xr, sem_os, sem_or = env["sem_xs"], env["sem_xr"], env["sem_os"], env["sem_or"]
    MATS = LAYERS + 1
    AT_TAPS, AT_GAMMA = SE, SE + 8 * LAYERS
    AT_BETA = AT_GAMMA + 8
    NL = C // LANES
    UR = F // 4
    NU = 4 + (U - 1)
    NB = UR // 16
    R = NU * UR
    N_SRC = TM // 4
    dp, tm = lax.axis_index("dp"), lax.axis_index("tm")
    partner = tm + 1 - 2 * lax.rem(tm, 2)
    first, last = tm == 0, tm == TM - 1
    chips = [(a, 2 * b) for a in range(DP) for b in range(TM // 2) if a or b]
    chips = chips[::-1]

    def at_chip(offset):
        return (lax.rem(dp + offset[0], DP), lax.rem(tm + offset[1], TM))

    def win(u):
        return u * UR if u < 4 else F + 64 + (u - 4) * (UR + 64)

    def seg_of(u):
        return 0 if u < 4 else u - 3

    def lane(j):
        return pl.ds(pl.multiple_of(j * LANES, LANES), LANES)

    def wide(v):
        return jnp.concatenate([v] * NL, axis=1)

    def remote(src, dst, ssem, rsem, dev):
        return pltpu.make_async_remote_copy(src, dst, ssem, rsem, device_id=dev, device_id_type=MESH)

    barrier = pltpu.get_barrier_semaphore()
    load_x = pltpu.make_async_copy(x_any, xv, sem_loc.at[0])
    load_x.start()
    others = [(0, b) for b in range(1, TM, 2)]
    for offset in chips + others:
        pl.semaphore_signal(barrier, inc=1, device_id=at_chip(offset), device_id_type=MESH)

    my_len = [lengths[dp * U + b] for b in range(U)]
    long_at = jnp.int32(0)
    for b in range(1, U):
        long_at = jnp.where(my_len[b] == F * TM, jnp.int32(b), long_at)
    short_at = [jnp.where(k < long_at, k, k + 1) for k in range(U - 1)]
    short_len = [lengths[dp * U + b] for b in range(U - 1)]
    short_len = [jnp.where(k < long_at, my_len[k], my_len[k + 1]) for k in range(U - 1)]
    x, z, y, core = lax.rem(dp, 2), dp // 2, tm // 2, lax.rem(tm, 2)
    Y = TM // 2
    XY, Z = 2 * Y, DP // 2
    xy = x * Y + y
    count = lax.fori_loop(0, DP * U, lambda i, c: c + lengths[i], jnp.int32(0)).astype(F32)
    inv_count = 1.0 / jnp.full((1, LANES), count, F32)
    rows = lax.broadcasted_iota(jnp.int32, (UR, LANES), 0)
    time_s = (rows & 15) * NB + (rows >> 4) + tm * UR
    for k in range(U - 1):
        mask[k * UR : (k + 1) * UR, :] = jnp.where(time_s < short_len[k], 1.0, 0.0)
    e16 = lax.broadcasted_iota(jnp.int32, (16, LANES), 0)
    part = (e16 & 7) >> 1
    is_left = e16 < 8
    when = jnp.where(is_left, tm * UR - 2 + (e16 & 1), tm * UR + UR + (e16 & 1))
    bound = jnp.full((16, LANES), 1 << 30, jnp.int32)
    for k in range(U - 1):
        bound = jnp.where(part == k + 1, short_len[k], bound)
    inside = jnp.where(is_left, tm, TM - 1 - tm) > 0
    hmask[...] = jnp.where(inside & (when < bound), 1.0, 0.0)

    def one_hot(ref, size, to_time):
        n = size // 16
        r0 = lax.broadcasted_iota(jnp.int32, (UR, size), 0)
        r1 = lax.broadcasted_iota(jnp.int32, (UR, size), 1)
        for c in range(size // UR):
            a, b = (r1, r0 + c * UR) if to_time else (r0 + c * UR, r1)
            hit = b == (a & 15) * n + (a >> 4)
            ref[c * UR : (c + 1) * UR, :] = jnp.where(hit, 1.0, 0.0).astype(BF16)

    one_hot(perm_l, F, False)
    one_hot(perm_s, UR, False)
    one_hot(back_l, F, True)
    one_hot(back_s, UR, True)

    @pl.when(first)
    def _():
        halo_l[...] = jnp.zeros(halo_l.shape, BF16)
        for l in range(LAYERS):
            hh[l, 0:8, :] = jnp.zeros((8, C), F32)
            dhh[l, 0:8, :] = jnp.zeros((8, C), F32)

    @pl.when(last)
    def _():
        halo_r[...] = jnp.zeros(halo_r.shape, BF16)
        for l in range(LAYERS):
            hh[l, 8:16, :] = jnp.zeros((8, C), F32)
            dhh[l, 8:16, :] = jnp.zeros((8, C), F32)

    def stage_short():
        @pl.when(tm < N_SRC)
        def _():
            for k in range(U - 1):
                def cp(c, _):
                    sl = pl.ds(pl.multiple_of(c * UR, UR), UR)
                    xs[k, sl, :] = xv[short_at[k], sl, :]
                    return 0
                lax.fori_loop(0, 4, cp, 0)

    def send_short(dst, with_halo, half):
        def act_on(d):
            if half == 0:
                d.start()
            else:
                d.wait_send()

        @pl.when(tm < N_SRC)
        def _():
            for q in range(4):
                chunk = 4 * tm + q
                main = xs.at[:, q * UR : (q + 1) * UR, :]
                head = xs.at[:, q * UR : q * UR + 16, :]
                tail = xs.at[:, (q + 1) * UR - 16 : (q + 1) * UR, :]

                def go_main():
                    act_on(remote(main, dst, sem_xs.at[q], sem_xr.at[0 if with_halo else 5], (dp, chunk)))

                def go_head():
                    act_on(remote(head, halo_r.at[1:U], sem_xs.at[4 + q], sem_xr.at[1], (dp, chunk - 1)))

                if q == 0:
                    pl.when(tm > 0)(go_main)
                    if half == 0:
                        @pl.when(tm == 0)
                        def _():
                            for k in range(U - 1):
                                dst[k] = xs[k, 0:UR, :]
                else:
                    go_main()
                if with_halo:
                    if q < 2:
                        pl.when(tm > 0)(go_head)
                    else:
                        go_head()
                    if q == 1 and half == 0:
                        @pl.when(tm == 0)
                        def _():
                            for k in range(U - 1):
                                halo_r[1 + k] = xs[k, UR : UR + 16, :]

                    @pl.when(chunk + 1 < TM)
                    def _():
                        act_on(remote(tail, halo_l.at[1:U], sem_xs.at[8 + q], sem_xr.at[2], (dp, chunk + 1)))

    def recv_short(dst, with_halo):
        @pl.when(tm > 0)
        def _():
            pltpu.make_async_copy(dst, dst, sem_xr.at[0 if with_halo else 5]).wait()
            if with_halo:
                pltpu.make_async_copy(halo_l.at[1:U], halo_l.at[1:U], sem_xr.at[2]).wait()

                @pl.when(tm < TM - 1)
                def _():
                    pltpu.make_async_copy(halo_r.at[1:U], halo_r.at[1:U], sem_xr.at[1]).wait()

    def edges(send, recv_l, recv_r, ssem, rsem, start):
        to_next = remote(send.at[1], recv_l, ssem.at[0], rsem.at[0], (dp, lax.rem(tm + 1, TM)))
        to_prev = remote(send.at[0], recv_r, ssem.at[1], rsem.at[1], (dp, lax.rem(tm + TM - 1, TM)))
        if start:
            pl.when(tm < TM - 1)(lambda: to_next.start())
            pl.when(tm > 0)(lambda: to_prev.start())
        else:
            @pl.when(tm < TM - 1)
            def _():
                to_next.wait_send()
                to_prev.wait_recv()

            @pl.when(tm > 0)
            def _():
                to_prev.wait_send()
                to_next.wait_recv()

    def z_peer(r):
        return (lax.rem(dp + 2 * r, DP), tm)

    def xy_peer(r):
        other = lax.rem(xy + r, XY)
        return (z * 2 + other // Y, 2 * lax.rem(other, Y) + core)

    def total_wait(ref, sem):
        pltpu.make_async_copy(ref, ref, sem).wait()

    def gather_stage(buf, m, stage):
        ss, rs = env["sem_gs"].at[m, stage], env["sem_gr"].at[m, stage]
        if stage == 0:
            mine = buf.at[z, xy, core]
            for r in range(1, Z):
                remote(mine, mine, ss, rs, z_peer(r)).start()
        elif stage == 1:
            mine = buf.at[:, xy, core]
            for r in range(1, XY):
                remote(mine, mine, ss, rs, xy_peer(r)).start()
        else:
            mine = buf.at[:, :, core]
            remote(mine, mine, ss, rs, (dp, partner)).start()

    def gather_size(buf, stage):
        return (buf.at[0 : Z - 1, 0, 0], buf.at[:, 0 : XY - 1, 0], buf.at[:, :, 0])[stage]

    def gather_got(buf, m, stage):
        total_wait(gather_size(buf, stage), env["sem_gr"].at[m, stage])

    def gather_left(buf, m):
        for stage in range(3):
            total_wait(gather_size(buf, stage), env["sem_gs"].at[m, stage])

    if fast:
        wall, sall = env["wall"], env["sall"]

        def weights(m):
            return wall[m].reshape(C, C)

        pack = env["pack"]
        pack[...] = jnp.zeros(pack.shape, F32)
        pack[0:SE, 0:SH] = env["excite"][...].astype(F32)
        for l in range(LAYERS):
            pack[AT_TAPS + 8 * l : AT_TAPS + 8 * l + KERNEL, 0:SH] = env["taps"][l].astype(F32)
        pack[AT_GAMMA : AT_GAMMA + LAYERS, 0:SH] = env["gamma"][...].astype(F32)
        pack[AT_BETA : AT_BETA + LAYERS, 0:SH] = env["beta"][...].astype(F32)
        sall[z, xy, core, :, 0:LANES] = pack[...].T[0:SH].astype(BF16)
        pack[0:SH, 0:SE] = env["squeeze"][...].astype(F32)
        sall[z, xy, core, :, LANES : 2 * LANES] = pack[0:SH, :].astype(BF16)
        for l in range(LAYERS):
            wall[l, z, xy, core] = env["point"][l]
        wall[LAYERS, z, xy, core] = env["resid"][...]
    else:
        def weights(m):
            return env["mats"][m]

        small[...] = env["small_in"][...]

    def squeeze_all():
        if fast:
            return sall[...].reshape(C, 2 * LANES)[:, LANES : LANES + SE].astype(F32)
        return env["squeeze"][...].astype(F32)

    class Scatter:
        def __init__(self, name):
            self.send, self.core, self.xsum, self.rxy, self.zsum, self.rz, self.ss, self.rs = (
                env[name + part] for part in ("_send", "_core", "_xsum", "_rxy", "_zsum", "_rz", "_ss", "_rs")
            )
            self.dtype = self.send.dtype

        def go(self, m, stage):
            ss, rs = self.ss.at[m, stage], self.rs.at[m, stage]
            if stage == 0:
                remote(self.send.at[m, :, :, 1 - core], self.core.at[m], ss, rs, (dp, partner)).start()
            elif stage == 1:
                for r in range(1, XY):
                    other = lax.rem(xy + r, XY)
                    remote(self.xsum.at[m, other], self.rxy.at[m, r - 1], ss, rs, xy_peer(r)).start()
            else:
                for r in range(1, Z):
                    remote(self.zsum.at[m, lax.rem(z + r, Z)], self.rz.at[m, r - 1], ss, rs, z_peer(r)).start()

        def size(self, m, stage):
            return (self.core.at[m], self.rxy.at[m], self.rz.at[m])[stage]

        def left(self, m):
            for stage in range(3):
                total_wait(self.size(m, stage), self.ss.at[m, stage])

        def core_to_xy(self, m):
            total_wait(self.size(m, 0), self.rs.at[m, 0])

            def body(i, _):
                v = self.send[m, i, :, core].astype(F32) + self.core[m, i].astype(F32)
                for k in range(XY):
                    self.xsum[m, k, i] = v[k].astype(self.dtype)
                return 0

            lax.fori_loop(0, Z, body, 0)
            self.go(m, 1)

        def xy_to_z(self, m):
            total_wait(self.size(m, 1), self.rs.at[m, 1])

            def body(i, _):
                v = self.xsum[m, xy, i].astype(F32)
                for r in range(XY - 1):
                    v = v + self.rxy[m, r, i].astype(F32)
                self.zsum[m, i] = v.astype(self.dtype)
                return 0

            lax.fori_loop(0, Z, body, 0)
            self.go(m, 2)

        def result(self, m):
            total_wait(self.size(m, 2), self.rs.at[m, 2])
            v = self.zsum[m, z].astype(F32)
            for r in range(Z - 1):
                v = v + self.rz[m, r].astype(F32)
            return v

    if fast:
        big, little = Scatter("big"), Scatter("little")

    load_x.wait()
    edge[0] = xv[long_at, 0:16, :]
    edge[1] = xv[long_at, F - 16 : F, :]
    stage_short()
    pl.semaphore_wait(barrier, len(chips) + len(others))
    if fast:
        gather_stage(sall, MATS, 0)
        gather_stage(wall.at[0], 0, 0)
    edges(edge, halo_l.at[0], halo_r.at[0], sem_xs.at[pl.ds(12, 2)], sem_xr.at[pl.ds(3, 2)], True)
    send_short(xin, True, 0)
    if fast:
        for m in range(1, MATS):
            gather_stage(wall.at[m], m, 0)

    def to_perm_long(src, dst, base):
        for u in range(4):
            o = base(u)
            dst[o : o + UR, :] = dot(perm_l[u * UR : (u + 1) * UR, :], src).astype(BF16)

    def to_perm_short(src, dst, base, masked):
        for k in range(U - 1):
            v = dot(perm_s[...], src[k])
            if masked:
                v = v * wide(mask[k * UR : (k + 1) * UR, :])
            o = base(4 + k)
            dst[o : o + UR, :] = v.astype(BF16)

    y0 = ypad.at[0]
    to_perm_long(xv[long_at], y0, lambda u: win(u) + 32)
    if fast:
        gather_got(sall, MATS, 0)
        gather_stage(sall, MATS, 1)
        gather_got(wall.at[0], 0, 0)
        gather_stage(wall.at[0], 0, 1)
        gather_got(sall, MATS, 1)
        gather_stage(sall, MATS, 2)
        gather_got(wall.at[0], 0, 1)
        gather_stage(wall.at[0], 0, 2)
        gather_got(wall.at[1], 1, 0)
        gather_stage(wall.at[1], 1, 1)
        gather_got(sall, MATS, 2)
        for j in range(NL):
            part = sall[...].reshape(C, 2 * LANES)[j * LANES : (j + 1) * LANES, 0:LANES].astype(F32)
            small[:, j * LANES : (j + 1) * LANES] = part.T
    edges(edge, halo_l.at[0], halo_r.at[0], sem_xs.at[pl.ds(12, 2)], sem_xr.at[pl.ds(3, 2)], False)
    recv_short(xin, True)
    to_perm_short(xin, y0, lambda u: win(u) + 32, True)
    send_short(xin, True, 1)
    load_g = pltpu.make_async_copy(g_any, xv, sem_loc.at[0])
    load_g.start()

    def fill_pads(ref, row0, n, j, b0, b1, b2, b3, halo, seg):
        e = lax.broadcasted_iota(jnp.int32, (16, LANES), 0)

        def put(at, v):
            ref[pl.ds(row0 + at * 16, 16), lane(j)] = v.astype(BF16)

        put(0, jnp.where(e == 0, halo[2 * seg : 2 * seg + 1], pltpu.roll(b2, 1, 0)))
        put(1, jnp.where(e == 0, halo[2 * seg + 1 : 2 * seg + 2], pltpu.roll(b3, 1, 0)))
        put(n + 2, jnp.where(e == 15, halo[8 + 2 * seg : 9 + 2 * seg], pltpu.roll(b0, 15, 0)))
        put(n + 3, jnp.where(e == 15, halo[9 + 2 * seg : 10 + 2 * seg], pltpu.roll(b1, 15, 0)))

    def pads_from(ref, j, halo):
        for seg in range(U):
            u0, u1 = (0, 3) if seg == 0 else (3 + seg, 3 + seg)
            n = F // 16 if seg == 0 else NB
            o0, o1 = win(u0) + 32, win(u1) + 32 + UR
            blk = [ref[o : o + 16, lane(j)].astype(F32) for o in (o0, o0 + 16, o1 - 32, o1 - 16)]
            fill_pads(ref, win(u0), n, j, *blk, halo, seg)

    def first_pads(j, _):
        left = [halo_l[s, :, lane(j)].astype(F32)[14:16] for s in range(4)]
        right = [halo_r[s, :, lane(j)].astype(F32)[0:2] for s in range(4)]
        halo = jnp.concatenate(left + right, axis=0) * hmask[...]
        pads_from(y0, j, halo)
        return 0

    lax.fori_loop(0, NL, first_pads, 0)

    def sync_core(s):
        d = remote(send_a.at[s], recv_core.at[s], sem_cs.at[s], sem_cr.at[s], (dp, partner))
        d.start()
        d.wait()
        send_b[s] = send_a[s] + recv_core[s]

    def sync_send(s):
        for i, offset in enumerate(chips):
            remote(send_b.at[s], recv_chip.at[s, i], sem_ks.at[s], sem_kr.at[s], at_chip(offset)).start()

    def sync_done(s):
        whole = recv_chip.at[s]
        pltpu.make_async_copy(whole, whole, sem_kr.at[s]).wait()
        pltpu.make_async_copy(whole, whole, sem_ks.at[s]).wait()
        total = send_b[s]
        for i in range(len(chips)):
            total = total + recv_chip[s, i]
        return total

    def tap_rows(l, j):
        group = small[pl.ds(pl.multiple_of(AT_TAPS + 8 * l, 8), 8), lane(j)]
        return [group[k : k + 1] for k in range(KERNEL)]

    def conv_pass(l):
        def body(j, _):
            w = tap_rows(l, j)
            for u in range(NU):
                o = win(u)
                v = ypad[l, o : o + UR + 64, lane(j)].astype(F32)
                t = v[0:UR] * w[0]
                for k in range(1, KERNEL):
                    t = t + v[16 * k : 16 * k + UR] * w[k]
                if u >= 4:
                    t = t * mask[(u - 4) * UR : (u - 3) * UR, :]
                dlow[l, u * UR : (u + 1) * UR, lane(j)] = t.astype(BF16)
            return 0

        lax.fori_loop(0, NL, body, 0)

    def fold8(v):
        return jnp.sum(v.reshape(v.shape[0] // 8, 8, v.shape[1]), axis=0)

    def put_edges(src, l):
        for seg in range(4):
            base = 0 if seg == 0 else F + (seg - 1) * UR
            n = F if seg == 0 else UR
            for e in range(2):
                hsend[l, 1, 2 * seg + e : 2 * seg + e + 1, :] = src(base + n - 32 + 16 * e + 15)
                hsend[l, 0, 2 * seg + e : 2 * seg + e + 1, :] = src(base + 16 * e)

    def matmul_pass(l):
        if fast:
            gather_got(wall.at[l], l, 2)
        sums[...] = jnp.zeros(sums.shape, F32)

        def body(u, _):
            r = pl.ds(pl.multiple_of(u * UR, UR), UR)
            h = dot(dlow[l, r, :], weights(l))
            pre[l, r, :] = h
            sums[0] += fold8(h)
            sums[1] += fold8(h * h)
            return 0

        lax.fori_loop(0, NU, body, 0)
        send_a[l, 0:1, :] = jnp.sum(sums[0], axis=0, keepdims=True)
        send_a[l, 1:2, :] = jnp.sum(sums[1], axis=0, keepdims=True)
        put_edges(lambda row: pre[l, row : row + 1, :], l)

    def layer(l, _):
        conv_pass(l)
        matmul_pass(l)
        edges(hsend.at[l], hh.at[l, 0:8], hh.at[l, 8:16], sem_hs.at[l], sem_hr.at[l], True)
        sync_core(l)
        sync_send(l)

        if fast:
            @pl.when(l < LAYERS)
            def _():
                gather_got(wall.at[l + 1], l + 1, 1)
                gather_stage(wall.at[l + 1], l + 1, 2)

            @pl.when(l < LAYERS - 1)
            def _():
                gather_got(wall.at[l + 2], l + 2, 0)
                gather_stage(wall.at[l + 2], l + 2, 1)

        @pl.when(l == LAYERS - 1)
        def _():
            if fast:
                gather_got(wall.at[LAYERS], LAYERS, 2)

            def rbody(u, _):
                o = jnp.where(u < 4, u * UR, F + 64 + (u - 4) * (UR + 64)) + 32
                src = ypad[0, pl.ds(pl.multiple_of(o, 16), UR), :]
                resd[pl.ds(pl.multiple_of(u * UR, UR), UR), :] = dot(src, weights(LAYERS))
                return 0

            lax.fori_loop(0, NU, rbody, 0)

        @pl.when(l == 0)
        def _():
            load_g.wait()
            stage_short()
            send_short(gin4, False, 0)
            to_perm_long(xv[long_at], cot, lambda u: u * UR)

        @pl.when(l == 1)
        def _():
            recv_short(gin4, False)
            to_perm_short(gin4, cot, lambda u: u * UR, True)
            send_short(gin4, False, 1)

        total = sync_done(l)
        edges(hsend.at[l], hh.at[l, 0:8], hh.at[l, 8:16], sem_hs.at[l], sem_hr.at[l], False)
        scale = wide(inv_count)
        mean = total[0:1] * scale
        var = total[1:2] * scale - mean * mean
        inv = lax.rsqrt(var + NORM_EPSILON)
        ga = small[pl.ds(AT_GAMMA + l, 1), :]
        a = ga * inv
        coef[l, 0:1, :] = 0.5 * a
        coef[l, 1:2, :] = 0.5 * (small[pl.ds(AT_BETA + l, 1), :] - mean * a)
        coef[l, 2:3, :] = mean
        coef[l, 3:4, :] = inv
        coef[l, 4:5, :] = a

        @pl.when(l < LAYERS - 1)
        def _():
            def body(j, _):
                a, b = coef[l, 0:1, lane(j)], coef[l, 1:2, lane(j)]
                for u in range(NU):
                    v = pre[l, u * UR : (u + 1) * UR, lane(j)] * a + b
                    v = v + v * jnp.tanh(v)
                    if u >= 4:
                        v = v * mask[(u - 4) * UR : (u - 3) * UR, :]
                    o = win(u) + 32
                    ypad[l + 1, o : o + UR, lane(j)] = v.astype(BF16)
                v = hh[l, :, lane(j)] * a + b
                v = (v + v * jnp.tanh(v)) * hmask[...]
                pads_from(ypad.at[l + 1], j, v)
                return 0

            lax.fori_loop(0, NL, body, 0)
        return 0

    lax.fori_loop(0, LAYERS, layer, 0)

    top = LAYERS - 1
    pool[...] = jnp.zeros(pool.shape, F32)

    def last_act(j, _):
        a, b = coef[top, 0:1, lane(j)], coef[top, 1:2, lane(j)]
        acc = None
        for u in range(NU):
            v = pre[top, u * UR : (u + 1) * UR, lane(j)] * a + b
            v = v + v * jnp.tanh(v)
            if u >= 4:
                v = v * mask[(u - 4) * UR : (u - 3) * UR, :]
            act[u * UR : (u + 1) * UR, lane(j)] = v
            f = fold8(v)
            acc = f if u == 0 or u >= 4 else acc + f
            if u >= 3:
                pool[u - 3 : u - 2, lane(j)] = jnp.sum(acc, axis=0, keepdims=True)
        return 0

    lax.fori_loop(0, NL, last_act, 0)

    def time_sum(s, value):
        tsend[s] = value
        ds = [remote(tsend.at[s], trecv.at[s, i - 1], sem_ts.at[s], sem_tr.at[s], (dp, lax.rem(tm + i, TM))) for i in range(1, TM)]
        for d in ds:
            d.start()

    def time_done(s):
        whole = trecv.at[s]
        pltpu.make_async_copy(whole, whole, sem_tr.at[s]).wait()
        pltpu.make_async_copy(whole, whole, sem_ts.at[s]).wait()
        total = tsend[s]
        for i in range(TM - 1):
            total = total + trecv[s, i]
        return total

    e8 = lax.broadcasted_iota(jnp.int32, (8, LANES), 0)
    len8 = jnp.full((8, LANES), F * TM, jnp.int32)
    for k in range(U - 1):
        len8 = jnp.where(e8 == k + 1, short_len[k], len8)
    inv_len = 1.0 / len8.astype(F32)
    live = jnp.where(e8 < U, 1.0, 0.0)
    time_sum(0, pool[...])
    p = time_done(0) * wide(inv_len)
    sq = squeeze_all()
    ex = small[0:SE, :]
    q = dot(p, sq, precision=HIGHEST)
    sig_q = logistic(q)
    z_act = q * sig_q
    gate[...] = logistic(dot(z_act, ex, precision=HIGHEST))
    pool[...] = jnp.zeros(pool.shape, F32)

    def top_pass(j, _):
        acc = None
        for u in range(NU):
            rs = slice(u * UR, (u + 1) * UR)
            seg = seg_of(u)
            av = act[rs, lane(j)]
            half = 0.5 * (av * gate[seg : seg + 1, lane(j)] + resd[rs, lane(j)])
            t = jnp.tanh(half)
            out = half + half * t
            slope = (0.5 + 0.5 * t) * (1.0 + half * (1.0 - t))
            dv = cot[rs, lane(j)].astype(F32) * slope
            if u >= 4:
                out = out * mask[(u - 4) * UR : (u - 3) * UR, :]
            outp[rs, lane(j)] = out.astype(BF16)
            du[rs, lane(j)] = dv
            drl[rs, lane(j)] = dv.astype(BF16)
            f = fold8(dv * av)
            acc = f if u == 0 or u >= 4 else acc + f
            if u >= 3:
                pool[u - 3 : u - 2, lane(j)] = jnp.sum(acc, axis=0, keepdims=True)
        return 0

    lax.fori_loop(0, NL, top_pass, 0)
    time_sum(1, pool[...])

    def give_back(buf, src, sems, rsems, start):
        if start:
            for u in range(4):
                buf[0, u * UR : (u + 1) * UR, :] = dot(back_l[u * UR : (u + 1) * UR, :], src[0:F, :]).astype(BF16)
            for k in range(U - 1):
                xin[k] = dot(back_s[...], src[F + k * UR : F + (k + 1) * UR, :]).astype(BF16)

            @pl.when(tm >= N_SRC)
            def _():
                for k in range(U - 1):
                    buf[1 + k] = jnp.zeros((F, C), BF16)

        owner, q = tm // 4, lax.rem(tm, 4)
        d = remote(xin, buf.at[1:U, pl.ds(pl.multiple_of(q * UR, UR), UR), :], sems, rsems.at[q], (dp, owner))
        if start:
            @pl.when(first)
            def _():
                for k in range(U - 1):
                    buf[1 + k, 0:UR, :] = xin[k]

            pl.when(tm > 0)(lambda: d.start())
        else:
            pl.when(tm > 0)(lambda: d.wait_send())

            @pl.when(tm < N_SRC)
            def _():
                for i in range(4):
                    got = buf.at[1:U, i * UR : (i + 1) * UR, :]
                    arrived = pltpu.make_async_copy(got, got, rsems.at[i])
                    if i == 0:
                        pl.when(tm > 0)(lambda: arrived.wait())
                    else:
                        arrived.wait()

    give_back(obuf, outp, sem_os.at[0], sem_or.at[0], True)

    def put_grad(m):
        if fast:
            big.send[m] = gp[...].astype(BF16).reshape(Z, XY, 2, SH, C)
            big.go(m, 0)
        else:
            pltpu.make_async_copy(gp, env["gmats"].at[m], sem_loc.at[1]).start()

    def grad_gone():
        if not fast:
            pltpu.make_async_copy(gp, env["gmats"].at[0], sem_loc.at[1]).wait()

    def xrows(u):
        o = win(u) + 32
        return ypad[0, o : o + UR, :]

    def resid_grads():
        acc = None
        for u in range(NU):
            rs = slice(u * UR, (u + 1) * UR)
            part = dot(xrows(u), drl[rs, :], ((0,), (0,)))
            gp[...] = part if u == 0 else gp[...] + part
        put_grad(LAYERS)

        def body(u, _):
            r = pl.ds(pl.multiple_of(u * UR, UR), UR)
            gres_in[r, :] = dot(drl[r, :], weights(LAYERS), ((1,), (1,)))
            return 0

        lax.fori_loop(0, NU, body, 0)

    resid_grads()
    dg = time_done(1)
    gv = gate[...]
    de = dg * gv * (1.0 - gv) * wide(live)
    dz = dot(de, ex, ((1,), (1,)), precision=HIGHEST)
    dq = dz * sig_q * (1.0 + q * (1.0 - sig_q))
    cvec[...] = dot(dq, sq, ((1,), (1,)), precision=HIGHEST) * wide(inv_len)
    lead = jnp.where(first, 1.0, 0.0)
    zero = jnp.zeros((C, LANES - 2 * SE), F32)
    pair = [dot(de, z_act, ((0,), (0,)), precision=HIGHEST), dot(p, dq, ((0,), (0,)), precision=HIGHEST)]
    pair = jnp.concatenate(pair + [zero] * (LANES > 2 * SE), axis=1) * lead
    if fast:
        little.send[0] = pair.reshape(Z, XY, 2, SH, LANES)
        little.go(0, 0)
    else:
        env["gpair"][...] = pair

    def norm_slope(l, u, j, a, b, m, s):
        h = pre[l, u * UR : (u + 1) * UR, lane(j)]
        half = h * a + b
        t = jnp.tanh(half)
        slope = (0.5 + 0.5 * t) * (1.0 + half * (1.0 - t))
        if u >= 4:
            slope = slope * mask[(u - 4) * UR : (u - 3) * UR, :]
        return slope, (h - m) * s

    def back_sums(l, s, grad_of):
        def body(j, _):
            a, b, m, i = (coef[l, r : r + 1, lane(j)] for r in range(4))
            acc0 = acc1 = None
            make = grad_of(j)
            for u in range(NU):
                slope, xc = norm_slope(l, u, j, a, b, m, i)
                v = make(u) * slope
                dn[u * UR : (u + 1) * UR, lane(j)] = v
                f0, f1 = fold8(v), fold8(v * xc)
                acc0 = f0 if u == 0 else acc0 + f0
                acc1 = f1 if u == 0 else acc1 + f1
            send_a[s, 0:1, lane(j)] = jnp.sum(acc0, axis=0, keepdims=True)
            send_a[s, 1:2, lane(j)] = jnp.sum(acc1, axis=0, keepdims=True)
            return 0

        lax.fori_loop(0, NL, body, 0)
        put_edges(lambda row: dn[row : row + 1, :], s)

    def top_grad(j):
        def make(u):
            seg = seg_of(u)
            return du[u * UR : (u + 1) * UR, lane(j)] * gate[seg : seg + 1, lane(j)] + cvec[seg : seg + 1, lane(j)]
        return make

    def conv_grad(l):
        def outer(j):
            w = tap_rows(l, j)

            def make(u):
                o = win(u)
                v = ddpad[o : o + UR + 64, lane(j)].astype(F32)
                t = v[64 : 64 + UR] * w[0]
                for k in range(1, KERNEL):
                    t = t + v[64 - 16 * k : 64 - 16 * k + UR] * w[k]
                return t
            return make
        return outer

    back_sums(top, LAYERS, top_grad)

    def point_grad(l):
        grad_gone()
        for u in range(NU):
            rs = slice(u * UR, (u + 1) * UR)
            part = dot(dlow[l, rs, :], dhl[rs, :], ((0,), (0,)))
            gp[...] = part if u == 0 else gp[...] + part
        put_grad(l)

    def depth_grad(l):
        def body(j, _):
            acc = [None] * KERNEL
            for u in range(NU):
                o = win(u)
                v = ypad[l, o : o + UR + 64, lane(j)].astype(F32)
                g = ddpad[o + 32 : o + 32 + UR, lane(j)].astype(F32)
                for k in range(KERNEL):
                    f = fold8(v[16 * k : 16 * k + UR] * g)
                    acc[k] = f if u == 0 else acc[k] + f
            rows = [jnp.sum(acc[k], axis=0, keepdims=True) for k in range(KERNEL)]
            rows.append(jnp.zeros((8 - KERNEL, LANES), F32))
            at = pl.ds(pl.multiple_of(AT_TAPS + 8 * l, 8), 8)
            gsmall[at, lane(j)] = jnp.concatenate(rows, axis=0)
            return 0

        lax.fori_loop(0, NL, body, 0)
    def back_layer(step, _):
        l = top - step
        s = LAYERS + step
        edges(hsend.at[s], dhh.at[l, 0:8], dhh.at[l, 8:16], sem_hs.at[s], sem_hr.at[s], True)
        sync_core(s)
        sync_send(s)

        @pl.when(step > 0)
        def _():
            point_grad(l + 1)
            depth_grad(l + 1)

        if fast:
            @pl.when(step == 0)
            def _():
                little.core_to_xy(0)

            @pl.when(step == 1)
            def _():
                little.xy_to_z(0)

            @pl.when(step > 0)
            def _():
                big.xy_to_z(l + 2)

            @pl.when(step > 1)
            def _():
                env["gmats"][l + 3] = big.result(l + 3)

            big.core_to_xy(l + 1)

        total = sync_done(s)
        edges(hsend.at[s], dhh.at[l, 0:8], dhh.at[l, 8:16], sem_hs.at[s], sem_hr.at[s], False)
        ggb[l, 0:2, :] = total
        m, i, a = coef[l, 2:3, :], coef[l, 3:4, :], coef[l, 4:5, :]
        k1 = a * i * total[1:2] * wide(inv_count)
        coef[l, 5:6, :] = k1
        coef[l, 6:7, :] = a * total[0:1] * wide(inv_count) - m * k1

        def body(j, _):
            a, k1, k0 = (coef[l, r : r + 1, lane(j)] for r in (4, 5, 6))
            for u in range(NU):
                rs = slice(u * UR, (u + 1) * UR)
                v = dn[rs, lane(j)] * a - (pre[l, rs, lane(j)] * k1 + k0)
                if u >= 4:
                    v = v * mask[(u - 4) * UR : (u - 3) * UR, :]
                dhl[rs, lane(j)] = v.astype(BF16)
            v = (dhh[l, :, lane(j)] * a - (hh[l, :, lane(j)] * k1 + k0)) * hmask[...]
            dhl[R : R + 16, lane(j)] = v.astype(BF16)
            return 0

        lax.fori_loop(0, NL, body, 0)
        hh[l] = dot(dhl[R : R + 16, :], weights(l), ((1,), (1,)))

        def mm(u, _):
            o = jnp.where(u < 4, u * UR, F + 64 + (u - 4) * (UR + 64)) + 32
            v = dot(dhl[pl.ds(pl.multiple_of(u * UR, UR), UR), :], weights(l), ((1,), (1,)))
            ddpad[pl.ds(pl.multiple_of(o, 16), UR), :] = v.astype(BF16)
            return 0

        lax.fori_loop(0, NU, mm, 0)

        def pad(j, _):
            pads_from(ddpad, j, hh[l, :, lane(j)].astype(BF16).astype(F32))
            return 0

        lax.fori_loop(0, NL, pad, 0)

        @pl.when(l > 0)
        def _():
            back_sums(l - 1, s + 1, conv_grad(l - 1))
        return 0

    def run_back():
        lax.fori_loop(0, LAYERS, back_layer, 0)

    conv_grad_of = conv_grad

    def conv_grad(l):
        return conv_grad_of(l + 1)

    gsmall[...] = jnp.zeros(gsmall.shape, F32)
    run_back()
    lead_all = jnp.where(first & (dp == 0), 1.0, 0.0)
    for l in range(LAYERS):
        gsmall[AT_BETA + l : AT_BETA + l + 1, :] = ggb[l, 0:1, :] * lead_all
        gsmall[AT_GAMMA + l : AT_GAMMA + l + 1, :] = ggb[l, 1:2, :] * lead_all
    point_grad(0)
    give_back(obuf, outp, sem_os.at[0], sem_or.at[0], False)
    put_out = pltpu.make_async_copy(obuf, out_any, sem_loc.at[2])
    put_out.start()

    def final(j, _):
        make = conv_grad_of(0)(j)
        for u in range(NU):
            rs = slice(u * UR, (u + 1) * UR)
            v = make(u)
            if u >= 4:
                v = v * mask[(u - 4) * UR : (u - 3) * UR, :]
            outp[rs, lane(j)] = (v + gres_in[rs, lane(j)]).astype(BF16)
        return 0

    lax.fori_loop(0, NL, final, 0)
    give_back(gbuf, outp, sem_os.at[1], sem_or.at[1], True)
    depth_grad(0)
    if fast:
        for j in range(NL):
            rows = gsmall[:, j * LANES : (j + 1) * LANES].T
            part = rows.reshape(LANES // (2 * SH), 2, SH, LANES)
            per = LANES // (2 * SH)
            for i in range(per):
                n = j * per + i
                little.send[1, n // XY, n % XY] = part[i]
        little.go(1, 0)
        big.xy_to_z(1)
        env["gmats"][2] = big.result(2)
        big.core_to_xy(0)
        little.core_to_xy(1)
        env["gmats"][1] = big.result(1)
        env["gpair"][...] = little.result(0)
        big.xy_to_z(0)
        little.xy_to_z(1)
        env["gmats"][0] = big.result(0)
        env["grows"][...] = little.result(1)
        for m in range(MATS):
            big.left(m)
            gather_left(wall.at[m], m)
        little.left(0)
        little.left(1)
        gather_left(sall, MATS)
    else:
        env["grows"][...] = gsmall[...]
    give_back(gbuf, outp, sem_os.at[1], sem_or.at[1], False)
    put_gin = pltpu.make_async_copy(gbuf, gin_any, sem_loc.at[3])
    put_gin.start()
    grad_gone()
    put_out.wait()
    put_gin.wait()


def finish_kernel(cfg, lengths, out_s, gin_s, gmats, gpair, grows, *rest):
    DP, TM, U, F, C, SE, SH, LAYERS, KERNEL, fast = cfg
    out, gin, gdepth, gpoint, ggamma, gbeta, gsq, gex, gres, turn, sems = rest
    dp = lax.axis_index("dp")
    long_at = jnp.int32(0)
    for b in range(1, U):
        long_at = jnp.where(lengths[dp * U + b] == F * TM, jnp.int32(b), long_at)
    copies = []
    for b in range(U):
        slot = jnp.where(b == long_at, 0, jnp.where(b < long_at, b + 1, b))
        copies.append(pltpu.make_async_copy(out_s.at[slot], out.at[b], sems.at[0, b]))
        copies.append(pltpu.make_async_copy(gin_s.at[slot], gin.at[b], sems.at[1, b]))
    for c in copies:
        c.start()
    at_taps = SE
    at_gamma = SE + 8 * LAYERS
    at_beta = at_gamma + 8
    gpoint[...] = gmats[0:LAYERS]
    gres[...] = gmats[LAYERS]
    gsq[...] = gpair[:, SE : 2 * SE]
    turn[...] = jnp.zeros(turn.shape, F32)
    turn[0:SH] = gpair[...]
    gex[...] = turn[...].T[0:SE, 0:SH]
    turn[0:SH] = grows[...]
    turn[...] = turn[...].T
    for l in range(LAYERS):
        gdepth[l] = turn[at_taps + 8 * l : at_taps + 8 * l + KERNEL, 0:SH]
    ggamma[...] = turn[at_gamma : at_gamma + LAYERS, 0:SH]
    gbeta[...] = turn[at_beta : at_beta + LAYERS, 0:SH]
    for c in copies:
        c.wait()


def local(sizes, inputs, lengths, depth_w, point_w, gamma, beta, squeeze_w, excite_w, resid_w, cotangent):
    DP, TM = sizes
    U, F, C = inputs.shape
    LAYERS, KERNEL, SH = depth_w.shape
    SE = squeeze_w.shape[1]
    UR = F // 4
    NU = 4 + U - 1
    R = NU * UR
    RP = F + 64 + (U - 1) * (UR + 64)
    S = 2 * LAYERS
    chips = DP * (TM // 2) - 1
    axes = ("dp", "tm")
    fast = SH % 16 == 0 and DP % 2 == 0 and DP > 2
    Z, XY = DP // 2, TM
    MATS = LAYERS + 1
    vm = pltpu.VMEM
    dma = pltpu.SemaphoreType.DMA
    any_spec = pl.BlockSpec(memory_space=pl.ANY)
    vm_spec = pl.BlockSpec(memory_space=pltpu.VMEM)
    sm_spec = pl.BlockSpec(memory_space=pltpu.SMEM)
    sd = jax.ShapeDtypeStruct
    cfg = (DP, TM, U, F, C, SE, SH, LAYERS, KERNEL, fast)
    at_gamma = SE + 8 * LAYERS
    operands = dict(lengths=lengths, x_any=inputs, g_any=cotangent)
    specs = [sm_spec, any_spec, any_spec]
    outs = dict(out_any=sd((U, F, C), BF16), gin_any=sd((U, F, C), BF16))
    out_specs = [any_spec, any_spec]
    if fast:
        operands.update(
            point=point_w, taps=depth_w, gamma=gamma, beta=beta, squeeze=squeeze_w, excite=excite_w, resid=resid_w
        )
        specs += [vm_spec] * 7
        outs.update(gmats=sd((MATS, SH, C), F32), gpair=sd((SH, LANES), F32), grows=sd((SH, LANES), F32))
        out_specs += [vm_spec] * 3
    else:
        mats = jnp.concatenate([point_w, resid_w[None]], axis=0)
        depth_rows = jnp.pad(depth_w, ((0, 0), (0, 8 - KERNEL), (0, 0))).reshape(8 * LAYERS, SH)
        fill = ((0, 8 - LAYERS), (0, 0))
        rows = jnp.concatenate([excite_w, depth_rows, jnp.pad(gamma, fill), jnp.pad(beta, fill)], axis=0)
        rows = jnp.pad(rows, ((0, LANES - rows.shape[0]), (0, 0)))
        operands.update(
            mats=lax.all_gather(mats, axes, axis=1, tiled=True),
            small_in=lax.all_gather(rows, axes, axis=1, tiled=True).astype(F32),
            squeeze=lax.all_gather(squeeze_w, axes, axis=0, tiled=True),
        )
        specs += [vm_spec] * 3
        outs.update(gmats=sd((MATS, C, C), F32), gpair=sd((C, LANES), F32), grows=sd((LANES, C), F32))
        out_specs += [any_spec, vm_spec, vm_spec]
    scratch = dict(
        xv=vm((U, F, C), BF16), xs=vm((U - 1, F, C), BF16), edge=vm((2, 16, C), BF16),
        xin=vm((U - 1, UR, C), BF16), gin4=vm((U - 1, UR, C), BF16),
        halo_l=vm((4, 16, C), BF16), halo_r=vm((4, 16, C), BF16),
        cot=vm((R, C), BF16), ypad=vm((LAYERS, RP, C), BF16), dlow=vm((LAYERS, R, C), BF16),
        pre=vm((LAYERS, R, C), F32), hh=vm((LAYERS, 16, C), F32),
        mask=vm(((U - 1) * UR, LANES), F32), hmask=vm((16, LANES), F32), coef=vm((LAYERS, 8, C), F32),
        resd=vm((R, C), F32), act=vm((R, C), F32), du=vm((R, C), F32), drl=vm((R, C), BF16), dn=vm((R, C), F32),
        dhl=vm((R + 16, C), BF16), ddpad=vm((RP, C), BF16), gres_in=vm((R, C), F32),
        perm_l=vm((F, F), BF16), perm_s=vm((UR, UR), BF16), back_l=vm((F, F), BF16), back_s=vm((UR, UR), BF16),
        outp=vm((R, C), BF16), obuf=vm((U, F, C), BF16), gbuf=vm((U, F, C), BF16), gp=vm((C, C), F32),
        small=vm((LANES, C), F32), gsmall=vm((LANES, C), F32), ggb=vm((LAYERS, 8, C), F32),
        sums=vm((2, 8, C), F32), send_a=vm((S, 2, C), F32), send_b=vm((S, 2, C), F32),
        recv_core=vm((S, 2, C), F32), recv_chip=vm((S, chips, 2, C), F32),
        hsend=vm((S, 2, 8, C), F32), dhh=vm((LAYERS, 16, C), F32),
        tsend=vm((2, 8, C), F32), trecv=vm((2, TM - 1, 8, C), F32),
        pool=vm((8, C), F32), gate=vm((8, C), F32), cvec=vm((8, C), F32),
        sem_loc=dma((4,)), sem_cs=dma((S,)), sem_cr=dma((S,)), sem_ks=dma((S,)), sem_kr=dma((S,)),
        sem_hs=dma((S, 2)), sem_hr=dma((S, 2)), sem_ts=dma((2,)), sem_tr=dma((2,)),
        sem_xs=dma((14,)), sem_xr=dma((6,)), sem_os=dma((2,)), sem_or=dma((2, 4)),
    )
    if fast:
        scratch.update(
            wall=vm((MATS, Z, XY, 2, SH, C), BF16), sall=vm((Z, XY, 2, SH, 2 * LANES), BF16),
            pack=vm((LANES, LANES), F32), sem_gs=dma((MATS + 1, 3)), sem_gr=dma((MATS + 1, 3)),
        )
        for name, n, cols, kind in (("big", MATS, C, BF16), ("little", 2, LANES, F32)):
            scratch.update(
                {
                    name + "_send": vm((n, Z, XY, 2, SH, cols), kind),
                    name + "_core": vm((n, Z, XY, SH, cols), kind),
                    name + "_xsum": vm((n, XY, Z, SH, cols), kind),
                    name + "_rxy": vm((n, XY - 1, Z, SH, cols), kind),
                    name + "_zsum": vm((n, Z, SH, cols), kind),
                    name + "_rz": vm((n, Z - 1, SH, cols), kind),
                    name + "_ss": dma((n, 3)),
                    name + "_rs": dma((n, 3)),
                }
            )
    names = list(operands) + list(outs) + list(scratch)
    out_s, gin_s, gmats, gpair, grows = pl.pallas_call(
        functools.partial(block_kernel, cfg, names),
        out_shape=tuple(outs.values()),
        in_specs=specs,
        out_specs=tuple(out_specs),
        scratch_shapes=list(scratch.values()),
        compiler_params=pltpu.CompilerParams(collective_id=0, has_side_effects=True, vmem_limit_bytes=63 << 20),
    )(*operands.values())
    if not fast:
        gmats = lax.psum_scatter(gmats, axes, scatter_dimension=1, tiled=True)
        gpair = lax.psum_scatter(gpair, axes, scatter_dimension=0, tiled=True)
        grows = lax.psum_scatter(grows, axes, scatter_dimension=1, tiled=True).T
    sizes_out = (
        ((U, F, C), BF16), ((U, F, C), BF16), ((LAYERS, KERNEL, SH), F32), ((LAYERS, SH, C), F32), ((LAYERS, SH), F32),
        ((LAYERS, SH), F32), ((SH, SE), F32), ((SE, SH), F32), ((SH, C), F32),
    )
    return pl.pallas_call(
        functools.partial(finish_kernel, cfg),
        out_shape=tuple(sd(*size) for size in sizes_out),
        in_specs=[sm_spec, any_spec, any_spec] + [vm_spec] * 3,
        out_specs=(any_spec,) * 2 + (vm_spec,) * 7,
        scratch_shapes=[vm((LANES, LANES), F32), dma((2, U))],
    )(lengths, out_s, gin_s, gmats, gpair, grows)


def solution(mesh):
    both = ("dp", "tm")
    rows, cols = P(both, None), P(None, both)
    frames = P("dp", "tm", None)
    taps, mats = P(None, None, both), P(None, both, None)
    sizes = (mesh.shape["dp"], mesh.shape["tm"])
    return jax.shard_map(
        functools.partial(local, sizes),
        mesh=mesh,
        in_specs=(frames, P(), taps, mats, cols, cols, rows, cols, rows, frames),
        out_specs=(frames, frames, taps, mats, cols, cols, rows, cols, rows),
        check_vma=False,
    )
```

```python
import functools

import jax
import jax.numpy as jnp
from jax import lax
from jax.experimental import pallas as pl
from jax.experimental.pallas import tpu as pltpu
from jax.sharding import PartitionSpec as P

MESH = pl.DeviceIdType.MESH
NORM_EPSILON = 1e-05
LANES = 128
HIGHEST = lax.Precision.HIGHEST
F32 = jnp.float32
BF16 = jnp.bfloat16


def dot(a, b, dims=((1,), (0,)), precision=None):
    return lax.dot_general(a, b, (dims, ((), ())), precision=precision, preferred_element_type=F32)


def logistic(v):
    return 0.5 * jnp.tanh(0.5 * v) + 0.5


def block_kernel(cfg, names, *refs):
    DP, TM, U, F, C, SE, SH, LAYERS, KERNEL, fast = cfg
    env = dict(zip(names, refs, strict=True))
    lengths, x_any, g_any = env["lengths"], env["x_any"], env["g_any"]
    out_any, gin_any = env["out_any"], env["gin_any"]
    xv, xs, edge, xin, gin4 = env["xv"], env["xs"], env["edge"], env["xin"], env["gin4"]
    halo_l, halo_r, cot, ypad, dlow = env["halo_l"], env["halo_r"], env["cot"], env["ypad"], env["dlow"]
    pre, hh, mask, hmask, coef = env["pre"], env["hh"], env["mask"], env["hmask"], env["coef"]
    resd, act, du, drl, dn = env["resd"], env["act"], env["du"], env["drl"], env["dn"]
    dhl, ddpad, gres_in = env["dhl"], env["ddpad"], env["gres_in"]
    perm_l, perm_s, back_l, back_s = env["perm_l"], env["perm_s"], env["back_l"], env["back_s"]
    outp, obuf, gbuf, gp, small = env["outp"], env["obuf"], env["gbuf"], env["gp"], env["small"]
    sums, send_a, send_b, recv_core, recv_chip = (
        env["sums"], env["send_a"], env["send_b"], env["recv_core"], env["recv_chip"]
    )
    hsend, dhh, tsend, trecv = env["hsend"], env["dhh"], env["tsend"], env["trecv"]
    pool, gate, cvec, gsmall = env["pool"], env["gate"], env["cvec"], env["gsmall"]
    ggb = env["ggb"]
    sem_loc, sem_cs, sem_cr, sem_ks, sem_kr = (
        env["sem_loc"], env["sem_cs"], env["sem_cr"], env["sem_ks"], env["sem_kr"]
    )
    sem_hs, sem_hr, sem_ts, sem_tr = env["sem_hs"], env["sem_hr"], env["sem_ts"], env["sem_tr"]
    sem_xs, sem_xr, sem_os, sem_or = env["sem_xs"], env["sem_xr"], env["sem_os"], env["sem_or"]
    MATS = LAYERS + 1
    AT_TAPS, AT_GAMMA = SE, SE + 8 * LAYERS
    AT_BETA = AT_GAMMA + 8
    NL = C // LANES
    UR = F // 4
    NU = 4 + (U - 1)
    NB = UR // 16
    R = NU * UR
    N_SRC = TM // 4
    dp, tm = lax.axis_index("dp"), lax.axis_index("tm")
    partner = tm + 1 - 2 * lax.rem(tm, 2)
    first, last = tm == 0, tm == TM - 1
    chips = [(a, 2 * b) for a in range(DP) for b in range(TM // 2) if a or b]
    chips = chips[::-1]

    def at_chip(offset):
        return (lax.rem(dp + offset[0], DP), lax.rem(tm + offset[1], TM))

    def win(u):
        return u * UR if u < 4 else F + 64 + (u - 4) * (UR + 64)

    def seg_of(u):
        return 0 if u < 4 else u - 3

    def lane(j):
        return pl.ds(pl.multiple_of(j * LANES, LANES), LANES)

    def wide(v):
        return jnp.concatenate([v] * NL, axis=1)

    def remote(src, dst, ssem, rsem, dev):
        return pltpu.make_async_remote_copy(src, dst, ssem, rsem, device_id=dev, device_id_type=MESH)

    barrier = pltpu.get_barrier_semaphore()
    load_x = pltpu.make_async_copy(x_any, xv, sem_loc.at[0])
    load_x.start()
    others = [(0, b) for b in range(1, TM, 2)]
    for offset in chips + others:
        pl.semaphore_signal(barrier, inc=1, device_id=at_chip(offset), device_id_type=MESH)

    my_len = [lengths[dp * U + b] for b in range(U)]
    long_at = jnp.int32(0)
    for b in range(1, U):
        long_at = jnp.where(my_len[b] == F * TM, jnp.int32(b), long_at)
    short_at = [jnp.where(k < long_at, k, k + 1) for k in range(U - 1)]
    short_len = [lengths[dp * U + b] for b in range(U - 1)]
    short_len = [jnp.where(k < long_at, my_len[k], my_len[k + 1]) for k in range(U - 1)]
    x, z, y, core = lax.rem(dp, 2), dp // 2, tm // 2, lax.rem(tm, 2)
    Y = TM // 2
    XY, Z = 2 * Y, DP // 2
    xy = x * Y + y
    count = lax.fori_loop(0, DP * U, lambda i, c: c + lengths[i], jnp.int32(0)).astype(F32)
    inv_count = 1.0 / jnp.full((1, LANES), count, F32)
    rows = lax.broadcasted_iota(jnp.int32, (UR, LANES), 0)
    time_s = (rows & 15) * NB + (rows >> 4) + tm * UR
    for k in range(U - 1):
        mask[k * UR : (k + 1) * UR, :] = jnp.where(time_s < short_len[k], 1.0, 0.0)
    e16 = lax.broadcasted_iota(jnp.int32, (16, LANES), 0)
    part = (e16 & 7) >> 1
    is_left = e16 < 8
    when = jnp.where(is_left, tm * UR - 2 + (e16 & 1), tm * UR + UR + (e16 & 1))
    bound = jnp.full((16, LANES), 1 << 30, jnp.int32)
    for k in range(U - 1):
        bound = jnp.where(part == k + 1, short_len[k], bound)
    inside = jnp.where(is_left, tm, TM - 1 - tm) > 0
    hmask[...] = jnp.where(inside & (when < bound), 1.0, 0.0)

    def one_hot(ref, size, to_time):
        n = size // 16
        r0 = lax.broadcasted_iota(jnp.int32, (UR, size), 0)
        r1 = lax.broadcasted_iota(jnp.int32, (UR, size), 1)
        for c in range(size // UR):
            a, b = (r1, r0 + c * UR) if to_time else (r0 + c * UR, r1)
            hit = b == (a & 15) * n + (a >> 4)
            ref[c * UR : (c + 1) * UR, :] = jnp.where(hit, 1.0, 0.0).astype(BF16)

    one_hot(perm_l, F, False)
    one_hot(perm_s, UR, False)
    one_hot(back_l, F, True)
    one_hot(back_s, UR, True)

    @pl.when(first)
    def _():
        halo_l[...] = jnp.zeros(halo_l.shape, BF16)
        for l in range(LAYERS):
            hh[l, 0:8, :] = jnp.zeros((8, C), F32)
            dhh[l, 0:8, :] = jnp.zeros((8, C), F32)

    @pl.when(last)
    def _():
        halo_r[...] = jnp.zeros(halo_r.shape, BF16)
        for l in range(LAYERS):
            hh[l, 8:16, :] = jnp.zeros((8, C), F32)
            dhh[l, 8:16, :] = jnp.zeros((8, C), F32)

    def stage_short():
        @pl.when(tm < N_SRC)
        def _():
            for k in range(U - 1):
                def cp(c, _):
                    sl = pl.ds(pl.multiple_of(c * UR, UR), UR)
                    xs[k, sl, :] = xv[short_at[k], sl, :]
                    return 0
                lax.fori_loop(0, 4, cp, 0)

    def send_short(dst, with_halo, half):
        def act_on(d):
            if half == 0:
                d.start()
            else:
                d.wait_send()

        @pl.when(tm < N_SRC)
        def _():
            for q in range(4):
                chunk = 4 * tm + q
                main = xs.at[:, q * UR : (q + 1) * UR, :]
                head = xs.at[:, q * UR : q * UR + 16, :]
                tail = xs.at[:, (q + 1) * UR - 16 : (q + 1) * UR, :]

                def go_main():
                    act_on(remote(main, dst, sem_xs.at[q], sem_xr.at[0 if with_halo else 5], (dp, chunk)))

                def go_head():
                    act_on(remote(head, halo_r.at[1:U], sem_xs.at[4 + q], sem_xr.at[1], (dp, chunk - 1)))

                if q == 0:
                    pl.when(tm > 0)(go_main)
                    if half == 0:
                        @pl.when(tm == 0)
                        def _():
                            for k in range(U - 1):
                                dst[k] = xs[k, 0:UR, :]
                else:
                    go_main()
                if with_halo:
                    if q < 2:
                        pl.when(tm > 0)(go_head)
                    else:
                        go_head()
                    if q == 1 and half == 0:
                        @pl.when(tm == 0)
                        def _():
                            for k in range(U - 1):
                                halo_r[1 + k] = xs[k, UR : UR + 16, :]

                    @pl.when(chunk + 1 < TM)
                    def _():
                        act_on(remote(tail, halo_l.at[1:U], sem_xs.at[8 + q], sem_xr.at[2], (dp, chunk + 1)))

    def recv_short(dst, with_halo):
        @pl.when(tm > 0)
        def _():
            pltpu.make_async_copy(dst, dst, sem_xr.at[0 if with_halo else 5]).wait()
            if with_halo:
                pltpu.make_async_copy(halo_l.at[1:U], halo_l.at[1:U], sem_xr.at[2]).wait()

                @pl.when(tm < TM - 1)
                def _():
                    pltpu.make_async_copy(halo_r.at[1:U], halo_r.at[1:U], sem_xr.at[1]).wait()

    def edges(send, recv_l, recv_r, ssem, rsem, start):
        to_next = remote(send.at[1], recv_l, ssem.at[0], rsem.at[0], (dp, lax.rem(tm + 1, TM)))
        to_prev = remote(send.at[0], recv_r, ssem.at[1], rsem.at[1], (dp, lax.rem(tm + TM - 1, TM)))
        if start:
            pl.when(tm < TM - 1)(lambda: to_next.start())
            pl.when(tm > 0)(lambda: to_prev.start())
        else:
            @pl.when(tm < TM - 1)
            def _():
                to_next.wait_send()
                to_prev.wait_recv()

            @pl.when(tm > 0)
            def _():
                to_prev.wait_send()
                to_next.wait_recv()

    def z_peer(r):
        return (lax.rem(dp + 2 * r, DP), tm)

    def xy_peer(r):
        other = lax.rem(xy + r, XY)
        return (z * 2 + other // Y, 2 * lax.rem(other, Y) + core)

    def total_wait(ref, sem):
        pltpu.make_async_copy(ref, ref, sem).wait()

    def gather_stage(buf, m, stage):
        ss, rs = env["sem_gs"].at[m, stage], env["sem_gr"].at[m, stage]
        if stage == 0:
            mine = buf.at[z, xy, core]
            for r in range(1, Z):
                remote(mine, mine, ss, rs, z_peer(r)).start()
        elif stage == 1:
            mine = buf.at[:, xy, core]
            for r in range(1, XY):
                remote(mine, mine, ss, rs, xy_peer(r)).start()
        else:
            mine = buf.at[:, :, core]
            remote(mine, mine, ss, rs, (dp, partner)).start()

    def gather_size(buf, stage):
        return (buf.at[0 : Z - 1, 0, 0], buf.at[:, 0 : XY - 1, 0], buf.at[:, :, 0])[stage]

    def gather_got(buf, m, stage):
        total_wait(gather_size(buf, stage), env["sem_gr"].at[m, stage])

    def gather_left(buf, m):
        for stage in range(3):
            total_wait(gather_size(buf, stage), env["sem_gs"].at[m, stage])

    if fast:
        wall, sall = env["wall"], env["sall"]

        def weights(m):
            return wall[m].reshape(C, C)

        pack = env["pack"]
        pack[...] = jnp.zeros(pack.shape, F32)
        for l in range(LAYERS):
            pack[AT_TAPS + 8 * l : AT_TAPS + 8 * l + KERNEL, 0:SH] = env["taps"][l].astype(F32)
        pack[AT_GAMMA : AT_GAMMA + LAYERS, 0:SH] = env["gamma"][...].astype(F32)
        pack[AT_BETA : AT_BETA + LAYERS, 0:SH] = env["beta"][...].astype(F32)
        turned = pack[...].T[0:SH]
        pack[0:SH, :] = turned
        pack[0:SH, 0:SE] = env["excite"][...].astype(F32)
        sall[z, xy, core, :, 0:LANES] = pack[0:SH, :].astype(BF16)
        pack[0:SH, 0:SE] = env["squeeze"][...].astype(F32)
        sall[z, xy, core, :, LANES : 2 * LANES] = pack[0:SH, :].astype(BF16)
        for l in range(LAYERS):
            wall[l, z, xy, core] = env["point"][l]
        wall[LAYERS, z, xy, core] = env["resid"][...]
    else:
        def weights(m):
            return env["mats"][m]

        small[...] = env["small_in"][...]

    def squeeze_all():
        if fast:
            return sall[...].reshape(C, 2 * LANES)[:, LANES : LANES + SE].astype(F32)
        return env["squeeze"][...].astype(F32)

    class Scatter:
        def __init__(self, name):
            self.send, self.core, self.xsum, self.rxy, self.zsum, self.rz, self.ss, self.rs = (
                env[name + part] for part in ("_send", "_core", "_xsum", "_rxy", "_zsum", "_rz", "_ss", "_rs")
            )
            self.dtype = self.send.dtype

        def go(self, m, stage):
            ss, rs = self.ss.at[m, stage], self.rs.at[m, stage]
            if stage == 0:
                remote(self.send.at[m, :, :, 1 - core], self.core.at[m], ss, rs, (dp, partner)).start()
            elif stage == 1:
                for r in range(1, XY):
                    other = lax.rem(xy + r, XY)
                    remote(self.xsum.at[m, other], self.rxy.at[m, r - 1], ss, rs, xy_peer(r)).start()
            else:
                for r in range(1, Z):
                    remote(self.zsum.at[m, lax.rem(z + r, Z)], self.rz.at[m, r - 1], ss, rs, z_peer(r)).start()

        def size(self, m, stage):
            return (self.core.at[m], self.rxy.at[m], self.rz.at[m])[stage]

        def left(self, m):
            for stage in range(3):
                total_wait(self.size(m, stage), self.ss.at[m, stage])

        def core_to_xy(self, m):
            total_wait(self.size(m, 0), self.rs.at[m, 0])

            def body(i, _):
                v = self.send[m, i, :, core].astype(F32) + self.core[m, i].astype(F32)
                for k in range(XY):
                    self.xsum[m, k, i] = v[k].astype(self.dtype)
                return 0

            lax.fori_loop(0, Z, body, 0)
            self.go(m, 1)

        def xy_to_z(self, m):
            total_wait(self.size(m, 1), self.rs.at[m, 1])

            def body(i, _):
                v = self.xsum[m, xy, i].astype(F32)
                for r in range(XY - 1):
                    v = v + self.rxy[m, r, i].astype(F32)
                self.zsum[m, i] = v.astype(self.dtype)
                return 0

            lax.fori_loop(0, Z, body, 0)
            self.go(m, 2)

        def result(self, m):
            total_wait(self.size(m, 2), self.rs.at[m, 2])
            v = self.zsum[m, z].astype(F32)
            for r in range(Z - 1):
                v = v + self.rz[m, r].astype(F32)
            return v

    if fast:
        big, little = Scatter("big"), Scatter("little")

    load_x.wait()
    edge[0] = xv[long_at, 0:16, :]
    edge[1] = xv[long_at, F - 16 : F, :]
    stage_short()
    pl.semaphore_wait(barrier, len(chips) + len(others))
    if fast:
        gather_stage(sall, MATS, 0)
        gather_stage(wall.at[0], 0, 0)
    edges(edge, halo_l.at[0], halo_r.at[0], sem_xs.at[pl.ds(12, 2)], sem_xr.at[pl.ds(3, 2)], True)
    send_short(xin, True, 0)
    if fast:
        for m in range(1, MATS):
            gather_stage(wall.at[m], m, 0)

    def to_perm_long(src, dst, base):
        for u in range(4):
            o = base(u)
            dst[o : o + UR, :] = dot(perm_l[u * UR : (u + 1) * UR, :], src).astype(BF16)

    def to_perm_short(src, dst, base, masked):
        for k in range(U - 1):
            v = dot(perm_s[...], src[k])
            if masked:
                v = v * wide(mask[k * UR : (k + 1) * UR, :])
            o = base(4 + k)
            dst[o : o + UR, :] = v.astype(BF16)

    y0 = ypad.at[0]
    to_perm_long(xv[long_at], y0, lambda u: win(u) + 32)
    if fast:
        gather_got(sall, MATS, 0)
        gather_stage(sall, MATS, 1)
        gather_got(wall.at[0], 0, 0)
        gather_stage(wall.at[0], 0, 1)
        gather_got(sall, MATS, 1)
        gather_stage(sall, MATS, 2)
        gather_got(wall.at[0], 0, 1)
        gather_stage(wall.at[0], 0, 2)
        gather_got(wall.at[1], 1, 0)
        gather_stage(wall.at[1], 1, 1)
        gather_got(sall, MATS, 2)
        for j in range(NL):
            part = sall[...].reshape(C, 2 * LANES)[j * LANES : (j + 1) * LANES, 0:LANES].astype(F32)
            small[:, j * LANES : (j + 1) * LANES] = part.T
    edges(edge, halo_l.at[0], halo_r.at[0], sem_xs.at[pl.ds(12, 2)], sem_xr.at[pl.ds(3, 2)], False)
    recv_short(xin, True)
    to_perm_short(xin, y0, lambda u: win(u) + 32, True)
    send_short(xin, True, 1)
    load_g = pltpu.make_async_copy(g_any, xv, sem_loc.at[0])
    load_g.start()

    def fill_pads(ref, row0, n, j, b0, b1, b2, b3, halo, seg):
        e = lax.broadcasted_iota(jnp.int32, (16, LANES), 0)

        def put(at, v):
            ref[pl.ds(row0 + at * 16, 16), lane(j)] = v.astype(BF16)

        put(0, jnp.where(e == 0, halo[2 * seg : 2 * seg + 1], pltpu.roll(b2, 1, 0)))
        put(1, jnp.where(e == 0, halo[2 * seg + 1 : 2 * seg + 2], pltpu.roll(b3, 1, 0)))
        put(n + 2, jnp.where(e == 15, halo[8 + 2 * seg : 9 + 2 * seg], pltpu.roll(b0, 15, 0)))
        put(n + 3, jnp.where(e == 15, halo[9 + 2 * seg : 10 + 2 * seg], pltpu.roll(b1, 15, 0)))

    def pads_from(ref, j, halo):
        for seg in range(U):
            u0, u1 = (0, 3) if seg == 0 else (3 + seg, 3 + seg)
            n = F // 16 if seg == 0 else NB
            o0, o1 = win(u0) + 32, win(u1) + 32 + UR
            blk = [ref[o : o + 16, lane(j)].astype(F32) for o in (o0, o0 + 16, o1 - 32, o1 - 16)]
            fill_pads(ref, win(u0), n, j, *blk, halo, seg)

    def first_pads(j, _):
        left = [halo_l[s, :, lane(j)].astype(F32)[14:16] for s in range(4)]
        right = [halo_r[s, :, lane(j)].astype(F32)[0:2] for s in range(4)]
        halo = jnp.concatenate(left + right, axis=0) * hmask[...]
        pads_from(y0, j, halo)
        return 0

    lax.fori_loop(0, NL, first_pads, 0)

    def sync_core(s):
        d = remote(send_a.at[s], recv_core.at[s], sem_cs.at[s], sem_cr.at[s], (dp, partner))
        d.start()
        d.wait()
        send_b[s] = send_a[s] + recv_core[s]

    def sync_send(s):
        for i, offset in enumerate(chips):
            remote(send_b.at[s], recv_chip.at[s, i], sem_ks.at[s], sem_kr.at[s], at_chip(offset)).start()

    def sync_done(s):
        whole = recv_chip.at[s]
        pltpu.make_async_copy(whole, whole, sem_kr.at[s]).wait()
        pltpu.make_async_copy(whole, whole, sem_ks.at[s]).wait()
        total = send_b[s]
        for i in range(len(chips)):
            total = total + recv_chip[s, i]
        return total

    def tap_rows(l, j):
        group = small[pl.ds(pl.multiple_of(AT_TAPS + 8 * l, 8), 8), lane(j)]
        return [group[k : k + 1] for k in range(KERNEL)]

    def conv_pass(l):
        def body(j, _):
            w = tap_rows(l, j)
            for u in range(NU):
                o = win(u)
                v = ypad[l, o : o + UR + 64, lane(j)].astype(F32)
                t = v[0:UR] * w[0]
                for k in range(1, KERNEL):
                    t = t + v[16 * k : 16 * k + UR] * w[k]
                if u >= 4:
                    t = t * mask[(u - 4) * UR : (u - 3) * UR, :]
                dlow[l, u * UR : (u + 1) * UR, lane(j)] = t.astype(BF16)
            return 0

        lax.fori_loop(0, NL, body, 0)

    def fold8(v):
        return jnp.sum(v.reshape(v.shape[0] // 8, 8, v.shape[1]), axis=0)

    def put_edges(src, l):
        for seg in range(4):
            base = 0 if seg == 0 else F + (seg - 1) * UR
            n = F if seg == 0 else UR
            for e in range(2):
                hsend[l, 1, 2 * seg + e : 2 * seg + e + 1, :] = src(base + n - 32 + 16 * e + 15)
                hsend[l, 0, 2 * seg + e : 2 * seg + e + 1, :] = src(base + 16 * e)

    def matmul_pass(l):
        if fast:
            gather_got(wall.at[l], l, 2)
        sums[...] = jnp.zeros(sums.shape, F32)

        def body(u, _):
            r = pl.ds(pl.multiple_of(u * UR, UR), UR)
            h = dot(dlow[l, r, :], weights(l))
            pre[l, r, :] = h
            sums[0] += fold8(h)
            sums[1] += fold8(h * h)
            return 0

        lax.fori_loop(0, NU, body, 0)
        send_a[l, 0:1, :] = jnp.sum(sums[0], axis=0, keepdims=True)
        send_a[l, 1:2, :] = jnp.sum(sums[1], axis=0, keepdims=True)
        put_edges(lambda row: pre[l, row : row + 1, :], l)

    def layer(l, _):
        conv_pass(l)
        matmul_pass(l)
        edges(hsend.at[l], hh.at[l, 0:8], hh.at[l, 8:16], sem_hs.at[l], sem_hr.at[l], True)
        sync_core(l)
        sync_send(l)

        if fast:
            @pl.when(l < LAYERS)
            def _():
                gather_got(wall.at[l + 1], l + 1, 1)
                gather_stage(wall.at[l + 1], l + 1, 2)

            @pl.when(l < LAYERS - 1)
            def _():
                gather_got(wall.at[l + 2], l + 2, 0)
                gather_stage(wall.at[l + 2], l + 2, 1)

        @pl.when(l == LAYERS - 1)
        def _():
            if fast:
                gather_got(wall.at[LAYERS], LAYERS, 2)

            def rbody(u, _):
                o = jnp.where(u < 4, u * UR, F + 64 + (u - 4) * (UR + 64)) + 32
                src = ypad[0, pl.ds(pl.multiple_of(o, 16), UR), :]
                resd[pl.ds(pl.multiple_of(u * UR, UR), UR), :] = dot(src, weights(LAYERS))
                return 0

            lax.fori_loop(0, NU, rbody, 0)

        @pl.when(l == 0)
        def _():
            load_g.wait()
            stage_short()
            send_short(gin4, False, 0)
            to_perm_long(xv[long_at], cot, lambda u: u * UR)

        @pl.when(l == 1)
        def _():
            recv_short(gin4, False)
            to_perm_short(gin4, cot, lambda u: u * UR, True)
            send_short(gin4, False, 1)

        total = sync_done(l)
        edges(hsend.at[l], hh.at[l, 0:8], hh.at[l, 8:16], sem_hs.at[l], sem_hr.at[l], False)
        scale = wide(inv_count)
        mean = total[0:1] * scale
        var = total[1:2] * scale - mean * mean
        inv = lax.rsqrt(var + NORM_EPSILON)
        ga = small[pl.ds(AT_GAMMA + l, 1), :]
        a = ga * inv
        coef[l, 0:1, :] = 0.5 * a
        coef[l, 1:2, :] = 0.5 * (small[pl.ds(AT_BETA + l, 1), :] - mean * a)
        coef[l, 2:3, :] = mean
        coef[l, 3:4, :] = inv
        coef[l, 4:5, :] = a

        @pl.when(l < LAYERS - 1)
        def _():
            def body(j, _):
                a, b = coef[l, 0:1, lane(j)], coef[l, 1:2, lane(j)]
                for u in range(NU):
                    v = pre[l, u * UR : (u + 1) * UR, lane(j)] * a + b
                    v = v + v * jnp.tanh(v)
                    if u >= 4:
                        v = v * mask[(u - 4) * UR : (u - 3) * UR, :]
                    o = win(u) + 32
                    ypad[l + 1, o : o + UR, lane(j)] = v.astype(BF16)
                v = hh[l, :, lane(j)] * a + b
                v = (v + v * jnp.tanh(v)) * hmask[...]
                pads_from(ypad.at[l + 1], j, v)
                return 0

            lax.fori_loop(0, NL, body, 0)
        return 0

    lax.fori_loop(0, LAYERS, layer, 0)

    top = LAYERS - 1
    pool[...] = jnp.zeros(pool.shape, F32)

    def last_act(j, _):
        a, b = coef[top, 0:1, lane(j)], coef[top, 1:2, lane(j)]
        acc = None
        for u in range(NU):
            v = pre[top, u * UR : (u + 1) * UR, lane(j)] * a + b
            v = v + v * jnp.tanh(v)
            if u >= 4:
                v = v * mask[(u - 4) * UR : (u - 3) * UR, :]
            act[u * UR : (u + 1) * UR, lane(j)] = v
            f = fold8(v)
            acc = f if u == 0 or u >= 4 else acc + f
            if u >= 3:
                pool[u - 3 : u - 2, lane(j)] = jnp.sum(acc, axis=0, keepdims=True)
        return 0

    lax.fori_loop(0, NL, last_act, 0)

    def time_sum(s, value):
        tsend[s] = value
        ds = [remote(tsend.at[s], trecv.at[s, i - 1], sem_ts.at[s], sem_tr.at[s], (dp, lax.rem(tm + i, TM))) for i in range(1, TM)]
        for d in ds:
            d.start()

    def time_done(s):
        whole = trecv.at[s]
        pltpu.make_async_copy(whole, whole, sem_tr.at[s]).wait()
        pltpu.make_async_copy(whole, whole, sem_ts.at[s]).wait()
        total = tsend[s]
        for i in range(TM - 1):
            total = total + trecv[s, i]
        return total

    e8 = lax.broadcasted_iota(jnp.int32, (8, LANES), 0)
    len8 = jnp.full((8, LANES), F * TM, jnp.int32)
    for k in range(U - 1):
        len8 = jnp.where(e8 == k + 1, short_len[k], len8)
    inv_len = 1.0 / len8.astype(F32)
    live = jnp.where(e8 < U, 1.0, 0.0)
    time_sum(0, pool[...])
    p = time_done(0) * wide(inv_len)
    sq = squeeze_all()
    ex = small[0:SE, :]
    q = dot(p, sq, precision=HIGHEST)
    sig_q = logistic(q)
    z_act = q * sig_q
    gate[...] = logistic(dot(z_act, ex, precision=HIGHEST))
    pool[...] = jnp.zeros(pool.shape, F32)

    def top_pass(j, _):
        acc = None
        for u in range(NU):
            rs = slice(u * UR, (u + 1) * UR)
            seg = seg_of(u)
            av = act[rs, lane(j)]
            half = 0.5 * (av * gate[seg : seg + 1, lane(j)] + resd[rs, lane(j)])
            t = jnp.tanh(half)
            out = half + half * t
            slope = (0.5 + 0.5 * t) * (1.0 + half * (1.0 - t))
            dv = cot[rs, lane(j)].astype(F32) * slope
            if u >= 4:
                out = out * mask[(u - 4) * UR : (u - 3) * UR, :]
            outp[rs, lane(j)] = out.astype(BF16)
            du[rs, lane(j)] = dv
            drl[rs, lane(j)] = dv.astype(BF16)
            f = fold8(dv * av)
            acc = f if u == 0 or u >= 4 else acc + f
            if u >= 3:
                pool[u - 3 : u - 2, lane(j)] = jnp.sum(acc, axis=0, keepdims=True)
        return 0

    lax.fori_loop(0, NL, top_pass, 0)
    time_sum(1, pool[...])

    def give_back(buf, src, sems, rsems, start):
        if start:
            for u in range(4):
                buf[0, u * UR : (u + 1) * UR, :] = dot(back_l[u * UR : (u + 1) * UR, :], src[0:F, :]).astype(BF16)
            for k in range(U - 1):
                xin[k] = dot(back_s[...], src[F + k * UR : F + (k + 1) * UR, :]).astype(BF16)

            @pl.when(tm >= N_SRC)
            def _():
                for k in range(U - 1):
                    buf[1 + k] = jnp.zeros((F, C), BF16)

        owner, q = tm // 4, lax.rem(tm, 4)
        d = remote(xin, buf.at[1:U, pl.ds(pl.multiple_of(q * UR, UR), UR), :], sems, rsems.at[q], (dp, owner))
        if start:
            @pl.when(first)
            def _():
                for k in range(U - 1):
                    buf[1 + k, 0:UR, :] = xin[k]

            pl.when(tm > 0)(lambda: d.start())
        else:
            pl.when(tm > 0)(lambda: d.wait_send())

            @pl.when(tm < N_SRC)
            def _():
                for i in range(4):
                    got = buf.at[1:U, i * UR : (i + 1) * UR, :]
                    arrived = pltpu.make_async_copy(got, got, rsems.at[i])
                    if i == 0:
                        pl.when(tm > 0)(lambda: arrived.wait())
                    else:
                        arrived.wait()

    give_back(obuf, outp, sem_os.at[0], sem_or.at[0], True)

    def put_grad(m):
        if fast:
            big.send[m] = gp[...].astype(BF16).reshape(Z, XY, 2, SH, C)
            big.go(m, 0)
        else:
            pltpu.make_async_copy(gp, env["gmats"].at[m], sem_loc.at[1]).start()

    def grad_gone():
        if not fast:
            pltpu.make_async_copy(gp, env["gmats"].at[0], sem_loc.at[1]).wait()

    def xrows(u):
        o = win(u) + 32
        return ypad[0, o : o + UR, :]

    def resid_grads():
        acc = None
        for u in range(NU):
            rs = slice(u * UR, (u + 1) * UR)
            part = dot(xrows(u), drl[rs, :], ((0,), (0,)))
            gp[...] = part if u == 0 else gp[...] + part
        put_grad(LAYERS)

        def body(u, _):
            r = pl.ds(pl.multiple_of(u * UR, UR), UR)
            gres_in[r, :] = dot(drl[r, :], weights(LAYERS), ((1,), (1,)))
            return 0

        lax.fori_loop(0, NU, body, 0)

    resid_grads()
    dg = time_done(1)
    gv = gate[...]
    de = dg * gv * (1.0 - gv) * wide(live)
    dz = dot(de, ex, ((1,), (1,)), precision=HIGHEST)
    dq = dz * sig_q * (1.0 + q * (1.0 - sig_q))
    cvec[...] = dot(dq, sq, ((1,), (1,)), precision=HIGHEST) * wide(inv_len)
    lead = jnp.where(first, 1.0, 0.0)
    zero = jnp.zeros((C, LANES - 2 * SE), F32)
    pair = [dot(de, z_act, ((0,), (0,)), precision=HIGHEST), dot(p, dq, ((0,), (0,)), precision=HIGHEST)]
    pair = jnp.concatenate(pair + [zero] * (LANES > 2 * SE), axis=1) * lead
    if fast:
        little.send[0] = pair.reshape(Z, XY, 2, SH, LANES)
        little.go(0, 0)
    else:
        env["gpair"][...] = pair

    def norm_slope(l, u, j, a, b, m, s):
        h = pre[l, u * UR : (u + 1) * UR, lane(j)]
        half = h * a + b
        t = jnp.tanh(half)
        slope = (0.5 + 0.5 * t) * (1.0 + half * (1.0 - t))
        if u >= 4:
            slope = slope * mask[(u - 4) * UR : (u - 3) * UR, :]
        return slope, (h - m) * s

    def back_sums(l, s, grad_of):
        def body(j, _):
            a, b, m, i = (coef[l, r : r + 1, lane(j)] for r in range(4))
            acc0 = acc1 = None
            make = grad_of(j)
            for u in range(NU):
                slope, xc = norm_slope(l, u, j, a, b, m, i)
                v = make(u) * slope
                dn[u * UR : (u + 1) * UR, lane(j)] = v
                f0, f1 = fold8(v), fold8(v * xc)
                acc0 = f0 if u == 0 else acc0 + f0
                acc1 = f1 if u == 0 else acc1 + f1
            send_a[s, 0:1, lane(j)] = jnp.sum(acc0, axis=0, keepdims=True)
            send_a[s, 1:2, lane(j)] = jnp.sum(acc1, axis=0, keepdims=True)
            return 0

        lax.fori_loop(0, NL, body, 0)
        put_edges(lambda row: dn[row : row + 1, :], s)

    def top_grad(j):
        def make(u):
            seg = seg_of(u)
            return du[u * UR : (u + 1) * UR, lane(j)] * gate[seg : seg + 1, lane(j)] + cvec[seg : seg + 1, lane(j)]
        return make

    def conv_grad(l):
        def outer(j):
            w = tap_rows(l, j)

            def make(u):
                o = win(u)
                v = ddpad[o : o + UR + 64, lane(j)].astype(F32)
                t = v[64 : 64 + UR] * w[0]
                for k in range(1, KERNEL):
                    t = t + v[64 - 16 * k : 64 - 16 * k + UR] * w[k]
                return t
            return make
        return outer

    back_sums(top, LAYERS, top_grad)

    def point_grad(l):
        grad_gone()
        for u in range(NU):
            rs = slice(u * UR, (u + 1) * UR)
            part = dot(dlow[l, rs, :], dhl[rs, :], ((0,), (0,)))
            gp[...] = part if u == 0 else gp[...] + part
        put_grad(l)

    def depth_grad(l):
        def body(j, _):
            acc = [None] * KERNEL
            for u in range(NU):
                o = win(u)
                v = ypad[l, o : o + UR + 64, lane(j)].astype(F32)
                g = ddpad[o + 32 : o + 32 + UR, lane(j)].astype(F32)
                for k in range(KERNEL):
                    f = fold8(v[16 * k : 16 * k + UR] * g)
                    acc[k] = f if u == 0 else acc[k] + f
            rows = [jnp.sum(acc[k], axis=0, keepdims=True) for k in range(KERNEL)]
            rows.append(jnp.zeros((8 - KERNEL, LANES), F32))
            at = pl.ds(pl.multiple_of(AT_TAPS + 8 * l, 8), 8)
            gsmall[at, lane(j)] = jnp.concatenate(rows, axis=0)
            return 0

        lax.fori_loop(0, NL, body, 0)
    def back_layer(step, _):
        l = top - step
        s = LAYERS + step
        edges(hsend.at[s], dhh.at[l, 0:8], dhh.at[l, 8:16], sem_hs.at[s], sem_hr.at[s], True)
        sync_core(s)
        sync_send(s)

        @pl.when(step > 0)
        def _():
            point_grad(l + 1)
            depth_grad(l + 1)

        if fast:
            @pl.when(step == 0)
            def _():
                little.core_to_xy(0)

            @pl.when(step == 1)
            def _():
                little.xy_to_z(0)

            @pl.when(step > 0)
            def _():
                big.xy_to_z(l + 2)

            @pl.when(step > 1)
            def _():
                env["gmats"][l + 3] = big.result(l + 3)

            big.core_to_xy(l + 1)

        total = sync_done(s)
        edges(hsend.at[s], dhh.at[l, 0:8], dhh.at[l, 8:16], sem_hs.at[s], sem_hr.at[s], False)
        ggb[l, 0:2, :] = total
        m, i, a = coef[l, 2:3, :], coef[l, 3:4, :], coef[l, 4:5, :]
        k1 = a * i * total[1:2] * wide(inv_count)
        coef[l, 5:6, :] = k1
        coef[l, 6:7, :] = a * total[0:1] * wide(inv_count) - m * k1

        def body(j, _):
            a, k1, k0 = (coef[l, r : r + 1, lane(j)] for r in (4, 5, 6))
            for u in range(NU):
                rs = slice(u * UR, (u + 1) * UR)
                v = dn[rs, lane(j)] * a - (pre[l, rs, lane(j)] * k1 + k0)
                if u >= 4:
                    v = v * mask[(u - 4) * UR : (u - 3) * UR, :]
                dhl[rs, lane(j)] = v.astype(BF16)
            v = (dhh[l, :, lane(j)] * a - (hh[l, :, lane(j)] * k1 + k0)) * hmask[...]
            dhl[R : R + 16, lane(j)] = v.astype(BF16)
            return 0

        lax.fori_loop(0, NL, body, 0)
        hh[l] = dot(dhl[R : R + 16, :], weights(l), ((1,), (1,)))

        def mm(u, _):
            o = jnp.where(u < 4, u * UR, F + 64 + (u - 4) * (UR + 64)) + 32
            v = dot(dhl[pl.ds(pl.multiple_of(u * UR, UR), UR), :], weights(l), ((1,), (1,)))
            ddpad[pl.ds(pl.multiple_of(o, 16), UR), :] = v.astype(BF16)
            return 0

        lax.fori_loop(0, NU, mm, 0)

        def pad(j, _):
            pads_from(ddpad, j, hh[l, :, lane(j)].astype(BF16).astype(F32))
            return 0

        lax.fori_loop(0, NL, pad, 0)

        @pl.when(l > 0)
        def _():
            back_sums(l - 1, s + 1, conv_grad(l - 1))
        return 0

    def run_back():
        lax.fori_loop(0, LAYERS, back_layer, 0)

    conv_grad_of = conv_grad

    def conv_grad(l):
        return conv_grad_of(l + 1)

    gsmall[...] = jnp.zeros(gsmall.shape, F32)
    run_back()
    lead_all = jnp.where(first & (dp == 0), 1.0, 0.0)
    for l in range(LAYERS):
        gsmall[AT_BETA + l : AT_BETA + l + 1, :] = ggb[l, 0:1, :] * lead_all
        gsmall[AT_GAMMA + l : AT_GAMMA + l + 1, :] = ggb[l, 1:2, :] * lead_all
    point_grad(0)
    give_back(obuf, outp, sem_os.at[0], sem_or.at[0], False)
    put_out = pltpu.make_async_copy(obuf, out_any, sem_loc.at[2])
    put_out.start()

    def final(j, _):
        make = conv_grad_of(0)(j)
        for u in range(NU):
            rs = slice(u * UR, (u + 1) * UR)
            v = make(u)
            if u >= 4:
                v = v * mask[(u - 4) * UR : (u - 3) * UR, :]
            outp[rs, lane(j)] = (v + gres_in[rs, lane(j)]).astype(BF16)
        return 0

    lax.fori_loop(0, NL, final, 0)
    give_back(gbuf, outp, sem_os.at[1], sem_or.at[1], True)
    depth_grad(0)
    if fast:
        for j in range(NL):
            rows = gsmall[:, j * LANES : (j + 1) * LANES].T
            part = rows.reshape(LANES // (2 * SH), 2, SH, LANES)
            per = LANES // (2 * SH)
            for i in range(per):
                n = j * per + i
                little.send[1, n // XY, n % XY] = part[i]
        little.go(1, 0)
        big.xy_to_z(1)
        env["gmats"][2] = big.result(2)
        big.core_to_xy(0)
        little.core_to_xy(1)
        env["gmats"][1] = big.result(1)
        env["gpair"][...] = little.result(0)
        big.xy_to_z(0)
        little.xy_to_z(1)
        env["gmats"][0] = big.result(0)
        env["grows"][...] = little.result(1)
        for m in range(MATS):
            big.left(m)
            gather_left(wall.at[m], m)
        little.left(0)
        little.left(1)
        gather_left(sall, MATS)
    else:
        env["grows"][...] = gsmall[...]
    give_back(gbuf, outp, sem_os.at[1], sem_or.at[1], False)
    put_gin = pltpu.make_async_copy(gbuf, gin_any, sem_loc.at[3])
    put_gin.start()
    grad_gone()
    put_out.wait()
    put_gin.wait()


def finish_kernel(cfg, lengths, out_s, gin_s, gmats, gpair, grows, *rest):
    DP, TM, U, F, C, SE, SH, LAYERS, KERNEL, fast = cfg
    out, gin, gdepth, gpoint, ggamma, gbeta, gsq, gex, gres, hold, turn, sems = rest
    dp = lax.axis_index("dp")
    long_at = jnp.int32(0)
    for b in range(1, U):
        long_at = jnp.where(lengths[dp * U + b] == F * TM, jnp.int32(b), long_at)
    copies = []
    for b in range(U):
        slot = jnp.where(b == long_at, 0, jnp.where(b < long_at, b + 1, b))
        for i, (src, dst) in enumerate(((out_s, out), (gin_s, gin))):
            get = pltpu.make_async_copy(src.at[slot], hold.at[i, b], sems.at[0, i, b])
            put = pltpu.make_async_copy(hold.at[i, b], dst.at[b], sems.at[1, i, b])
            copies.append((get, put))
            get.start()
    for get, put in copies:
        get.wait()
        put.start()
    at_taps = SE
    at_gamma = SE + 8 * LAYERS
    at_beta = at_gamma + 8
    gpoint[...] = gmats[0:LAYERS]
    gres[...] = gmats[LAYERS]
    gsq[...] = gpair[:, SE : 2 * SE]
    gex[...] = gpair[:, 0:SE]
    turn[...] = jnp.zeros(turn.shape, F32)
    turn[0:SH] = grows[...]
    turn[...] = turn[...].T
    for l in range(LAYERS):
        gdepth[l] = turn[at_taps + 8 * l : at_taps + 8 * l + KERNEL, 0:SH]
    ggamma[...] = turn[at_gamma : at_gamma + LAYERS, 0:SH]
    gbeta[...] = turn[at_beta : at_beta + LAYERS, 0:SH]
    for _, put in copies:
        put.wait()


def local(sizes, inputs, lengths, depth_w, point_w, gamma, beta, squeeze_w, excite_w, resid_w, cotangent):
    DP, TM = sizes
    U, F, C = inputs.shape
    LAYERS, KERNEL, SH = depth_w.shape
    SE = squeeze_w.shape[1]
    UR = F // 4
    NU = 4 + U - 1
    R = NU * UR
    RP = F + 64 + (U - 1) * (UR + 64)
    S = 2 * LAYERS
    chips = DP * (TM // 2) - 1
    axes = ("dp", "tm")
    fast = SH % 16 == 0 and DP % 2 == 0 and DP > 2
    Z, XY = DP // 2, TM
    MATS = LAYERS + 1
    vm = pltpu.VMEM
    dma = pltpu.SemaphoreType.DMA
    any_spec = pl.BlockSpec(memory_space=pl.ANY)
    vm_spec = pl.BlockSpec(memory_space=pltpu.VMEM)
    sm_spec = pl.BlockSpec(memory_space=pltpu.SMEM)
    sd = jax.ShapeDtypeStruct
    cfg = (DP, TM, U, F, C, SE, SH, LAYERS, KERNEL, fast)
    at_gamma = SE + 8 * LAYERS
    operands = dict(lengths=lengths, x_any=inputs, g_any=cotangent)
    specs = [sm_spec, any_spec, any_spec]
    outs = dict(out_any=sd((U, F, C), BF16), gin_any=sd((U, F, C), BF16))
    out_specs = [any_spec, any_spec]
    if fast:
        operands.update(
            point=point_w, taps=depth_w, gamma=gamma, beta=beta, squeeze=squeeze_w, excite=excite_w.T, resid=resid_w
        )
        specs += [vm_spec] * 7
        outs.update(gmats=sd((MATS, SH, C), F32), gpair=sd((SH, LANES), F32), grows=sd((SH, LANES), F32))
        out_specs += [vm_spec] * 3
    else:
        mats = jnp.concatenate([point_w, resid_w[None]], axis=0)
        depth_rows = jnp.pad(depth_w, ((0, 0), (0, 8 - KERNEL), (0, 0))).reshape(8 * LAYERS, SH)
        fill = ((0, 8 - LAYERS), (0, 0))
        rows = jnp.concatenate([excite_w, depth_rows, jnp.pad(gamma, fill), jnp.pad(beta, fill)], axis=0)
        rows = jnp.pad(rows, ((0, LANES - rows.shape[0]), (0, 0)))
        operands.update(
            mats=lax.all_gather(mats, axes, axis=1, tiled=True),
            small_in=lax.all_gather(rows, axes, axis=1, tiled=True).astype(F32),
            squeeze=lax.all_gather(squeeze_w, axes, axis=0, tiled=True),
        )
        specs += [vm_spec] * 3
        outs.update(gmats=sd((MATS, C, C), F32), gpair=sd((C, LANES), F32), grows=sd((LANES, C), F32))
        out_specs += [any_spec, vm_spec, vm_spec]
    scratch = dict(
        xv=vm((U, F, C), BF16), xs=vm((U - 1, F, C), BF16), edge=vm((2, 16, C), BF16),
        xin=vm((U - 1, UR, C), BF16), gin4=vm((U - 1, UR, C), BF16),
        halo_l=vm((4, 16, C), BF16), halo_r=vm((4, 16, C), BF16),
        cot=vm((R, C), BF16), ypad=vm((LAYERS, RP, C), BF16), dlow=vm((LAYERS, R, C), BF16),
        pre=vm((LAYERS, R, C), F32), hh=vm((LAYERS, 16, C), F32),
        mask=vm(((U - 1) * UR, LANES), F32), hmask=vm((16, LANES), F32), coef=vm((LAYERS, 8, C), F32),
        resd=vm((R, C), F32), act=vm((R, C), F32), du=vm((R, C), F32), drl=vm((R, C), BF16), dn=vm((R, C), F32),
        dhl=vm((R + 16, C), BF16), ddpad=vm((RP, C), BF16), gres_in=vm((R, C), F32),
        perm_l=vm((F, F), BF16), perm_s=vm((UR, UR), BF16), back_l=vm((F, F), BF16), back_s=vm((UR, UR), BF16),
        outp=vm((R, C), BF16), obuf=vm((U, F, C), BF16), gbuf=vm((U, F, C), BF16), gp=vm((C, C), F32),
        small=vm((LANES, C), F32), gsmall=vm((LANES, C), F32), ggb=vm((LAYERS, 8, C), F32),
        sums=vm((2, 8, C), F32), send_a=vm((S, 2, C), F32), send_b=vm((S, 2, C), F32),
        recv_core=vm((S, 2, C), F32), recv_chip=vm((S, chips, 2, C), F32),
        hsend=vm((S, 2, 8, C), F32), dhh=vm((LAYERS, 16, C), F32),
        tsend=vm((2, 8, C), F32), trecv=vm((2, TM - 1, 8, C), F32),
        pool=vm((8, C), F32), gate=vm((8, C), F32), cvec=vm((8, C), F32),
        sem_loc=dma((4,)), sem_cs=dma((S,)), sem_cr=dma((S,)), sem_ks=dma((S,)), sem_kr=dma((S,)),
        sem_hs=dma((S, 2)), sem_hr=dma((S, 2)), sem_ts=dma((2,)), sem_tr=dma((2,)),
        sem_xs=dma((14,)), sem_xr=dma((6,)), sem_os=dma((2,)), sem_or=dma((2, 4)),
    )
    if fast:
        scratch.update(
            wall=vm((MATS, Z, XY, 2, SH, C), BF16), sall=vm((Z, XY, 2, SH, 2 * LANES), BF16),
            pack=vm((LANES, LANES), F32), sem_gs=dma((MATS + 1, 3)), sem_gr=dma((MATS + 1, 3)),
        )
        for name, n, cols, kind in (("big", MATS, C, BF16), ("little", 2, LANES, F32)):
            scratch.update(
                {
                    name + "_send": vm((n, Z, XY, 2, SH, cols), kind),
                    name + "_core": vm((n, Z, XY, SH, cols), kind),
                    name + "_xsum": vm((n, XY, Z, SH, cols), kind),
                    name + "_rxy": vm((n, XY - 1, Z, SH, cols), kind),
                    name + "_zsum": vm((n, Z, SH, cols), kind),
                    name + "_rz": vm((n, Z - 1, SH, cols), kind),
                    name + "_ss": dma((n, 3)),
                    name + "_rs": dma((n, 3)),
                }
            )
    names = list(operands) + list(outs) + list(scratch)
    out_s, gin_s, gmats, gpair, grows = pl.pallas_call(
        functools.partial(block_kernel, cfg, names),
        out_shape=tuple(outs.values()),
        in_specs=specs,
        out_specs=tuple(out_specs),
        scratch_shapes=list(scratch.values()),
        compiler_params=pltpu.CompilerParams(collective_id=0, has_side_effects=True, vmem_limit_bytes=63 << 20),
    )(*operands.values())
    if not fast:
        gmats = lax.psum_scatter(gmats, axes, scatter_dimension=1, tiled=True)
        gpair = lax.psum_scatter(gpair, axes, scatter_dimension=0, tiled=True)
        grows = lax.psum_scatter(grows, axes, scatter_dimension=1, tiled=True).T
    sizes_out = (
        ((U, F, C), BF16), ((U, F, C), BF16), ((LAYERS, KERNEL, SH), F32), ((LAYERS, SH, C), F32), ((LAYERS, SH), F32),
        ((LAYERS, SH), F32), ((SH, SE), F32), ((SH, SE), F32), ((SH, C), F32),
    )
    done = pl.pallas_call(
        functools.partial(finish_kernel, cfg),
        out_shape=tuple(sd(*size) for size in sizes_out),
        in_specs=[sm_spec, any_spec, any_spec] + [vm_spec] * 3,
        out_specs=(any_spec,) * 2 + (vm_spec,) * 7,
        scratch_shapes=[vm((2, U, F, C), BF16), vm((LANES, LANES), F32), dma((2, 2, U))],
    )(lengths, out_s, gin_s, gmats, gpair, grows)
    return done[:7] + (done[7].T, done[8])


def solution(mesh):
    both = ("dp", "tm")
    rows, cols = P(both, None), P(None, both)
    frames = P("dp", "tm", None)
    taps, mats = P(None, None, both), P(None, both, None)
    sizes = (mesh.shape["dp"], mesh.shape["tm"])
    return jax.shard_map(
        functools.partial(local, sizes),
        mesh=mesh,
        in_specs=(frames, P(), taps, mats, cols, cols, rows, cols, rows, frames),
        out_specs=(frames, frames, taps, mats, cols, cols, rows, cols, rows),
        check_vma=False,
    )
```

```python
import functools

import jax
import jax.numpy as jnp
from jax import lax
from jax.experimental import pallas as pl
from jax.experimental.pallas import tpu as pltpu
from jax.sharding import PartitionSpec as P

MESH = pl.DeviceIdType.MESH
NORM_EPSILON = 1e-05
LANES = 128
HIGHEST = lax.Precision.HIGHEST
F32 = jnp.float32
BF16 = jnp.bfloat16


def dot(a, b, dims=((1,), (0,)), precision=None):
    return lax.dot_general(a, b, (dims, ((), ())), precision=precision, preferred_element_type=F32)


def logistic(v):
    return 0.5 * jnp.tanh(0.5 * v) + 0.5


def block_kernel(cfg, names, *refs):
    DP, TM, U, F, C, SE, SH, LAYERS, KERNEL, fast = cfg
    env = dict(zip(names, refs, strict=True))
    lengths, x_any, g_any = env["lengths"], env["x_any"], env["g_any"]
    out_any, gin_any = env["out_any"], env["gin_any"]
    xv, xs, edge, xin, gin4 = env["xv"], env["xs"], env["edge"], env["xin"], env["gin4"]
    halo_l, halo_r, cot, ypad, dlow = env["halo_l"], env["halo_r"], env["cot"], env["ypad"], env["dlow"]
    pre, hh, mask, hmask, coef = env["pre"], env["hh"], env["mask"], env["hmask"], env["coef"]
    resd, act, du, drl, dn = env["resd"], env["act"], env["du"], env["drl"], env["dn"]
    dhl, ddpad, gres_in = env["dhl"], env["ddpad"], env["gres_in"]
    perm_l, perm_s, back_l, back_s = env["perm_l"], env["perm_s"], env["back_l"], env["back_s"]
    outp, obuf, gbuf, gp, small = env["outp"], env["obuf"], env["gbuf"], env["gp"], env["small"]
    sums, send_a, send_b, recv_core, recv_chip = (
        env["sums"], env["send_a"], env["send_b"], env["recv_core"], env["recv_chip"]
    )
    hsend, dhh, tsend, trecv = env["hsend"], env["dhh"], env["tsend"], env["trecv"]
    pool, gate, cvec, gsmall = env["pool"], env["gate"], env["cvec"], env["gsmall"]
    ggb = env["ggb"]
    sem_loc, sem_cs, sem_cr, sem_ks, sem_kr = (
        env["sem_loc"], env["sem_cs"], env["sem_cr"], env["sem_ks"], env["sem_kr"]
    )
    sem_hs, sem_hr, sem_ts, sem_tr = env["sem_hs"], env["sem_hr"], env["sem_ts"], env["sem_tr"]
    sem_xs, sem_xr, sem_os, sem_or = env["sem_xs"], env["sem_xr"], env["sem_os"], env["sem_or"]
    MATS = LAYERS + 1
    AT_TAPS, AT_GAMMA = SE, SE + 8 * LAYERS
    AT_BETA = AT_GAMMA + 8
    NL = C // LANES
    UR = F // 4
    NU = 4 + (U - 1)
    NB = UR // 16
    R = NU * UR
    N_SRC = TM // 4
    dp, tm = lax.axis_index("dp"), lax.axis_index("tm")
    partner = tm + 1 - 2 * lax.rem(tm, 2)
    first, last = tm == 0, tm == TM - 1
    chips = [(a, 2 * b) for a in range(DP) for b in range(TM // 2) if a or b]
    n_chips = len(chips) + 1
    my_chip = dp * (TM // 2) + tm // 2

    def at_chip(offset):
        return (lax.rem(dp + offset[0], DP), lax.rem(tm + offset[1], TM))

    def win(u):
        return u * UR if u < 4 else F + 64 + (u - 4) * (UR + 64)

    def seg_of(u):
        return 0 if u < 4 else u - 3

    def lane(j):
        return pl.ds(pl.multiple_of(j * LANES, LANES), LANES)

    def wide(v):
        return jnp.concatenate([v] * NL, axis=1)

    def remote(src, dst, ssem, rsem, dev):
        return pltpu.make_async_remote_copy(src, dst, ssem, rsem, device_id=dev, device_id_type=MESH)

    def total_wait(ref, sem):
        pltpu.make_async_copy(ref, ref, sem).wait()

    barrier = pltpu.get_barrier_semaphore()
    load_x = pltpu.make_async_copy(x_any, xv, sem_loc.at[0])
    load_x.start()
    others = [(0, b) for b in range(1, TM, 2)]
    for offset in chips + others:
        pl.semaphore_signal(barrier, inc=1, device_id=at_chip(offset), device_id_type=MESH)

    my_len = [lengths[dp * U + b] for b in range(U)]
    long_at = jnp.int32(0)
    for b in range(1, U):
        long_at = jnp.where(my_len[b] == F * TM, jnp.int32(b), long_at)
    short_at = [jnp.where(k < long_at, k, k + 1) for k in range(U - 1)]
    short_len = [lengths[dp * U + b] for b in range(U - 1)]
    short_len = [jnp.where(k < long_at, my_len[k], my_len[k + 1]) for k in range(U - 1)]
    x, z, y, core = lax.rem(dp, 2), dp // 2, tm // 2, lax.rem(tm, 2)
    Y = TM // 2
    Z = DP // 2
    count = lax.fori_loop(0, DP * U, lambda i, c: c + lengths[i], jnp.int32(0)).astype(F32)
    inv_count = 1.0 / jnp.full((1, LANES), count, F32)
    rows = lax.broadcasted_iota(jnp.int32, (UR, LANES), 0)
    time_s = (rows & 15) * NB + (rows >> 4) + tm * UR
    for k in range(U - 1):
        mask[k * UR : (k + 1) * UR, :] = jnp.where(time_s < short_len[k], 1.0, 0.0)
    e16 = lax.broadcasted_iota(jnp.int32, (16, LANES), 0)
    part = (e16 & 7) >> 1
    is_left = e16 < 8
    when = jnp.where(is_left, tm * UR - 2 + (e16 & 1), tm * UR + UR + (e16 & 1))
    bound = jnp.full((16, LANES), 1 << 30, jnp.int32)
    for k in range(U - 1):
        bound = jnp.where(part == k + 1, short_len[k], bound)
    inside = jnp.where(is_left, tm, TM - 1 - tm) > 0
    hmask[...] = jnp.where(inside & (when < bound), 1.0, 0.0)

    def one_hot(ref, size, to_time):
        n = size // 16
        r0 = lax.broadcasted_iota(jnp.int32, (UR, size), 0)
        r1 = lax.broadcasted_iota(jnp.int32, (UR, size), 1)
        for c in range(size // UR):
            a, b = (r1, r0 + c * UR) if to_time else (r0 + c * UR, r1)
            hit = b == (a & 15) * n + (a >> 4)
            ref[c * UR : (c + 1) * UR, :] = jnp.where(hit, 1.0, 0.0).astype(BF16)

    one_hot(perm_l, F, False)
    one_hot(perm_s, UR, False)
    one_hot(back_l, F, True)
    one_hot(back_s, UR, True)

    @pl.when(first)
    def _():
        halo_l[...] = jnp.zeros(halo_l.shape, BF16)
        for l in range(LAYERS):
            hh[l, 0:8, :] = jnp.zeros((8, C), F32)
            dhh[l, 0:8, :] = jnp.zeros((8, C), F32)

    @pl.when(last)
    def _():
        halo_r[...] = jnp.zeros(halo_r.shape, BF16)
        for l in range(LAYERS):
            hh[l, 8:16, :] = jnp.zeros((8, C), F32)
            dhh[l, 8:16, :] = jnp.zeros((8, C), F32)

    def stage_short():
        @pl.when(tm < N_SRC)
        def _():
            for k in range(U - 1):
                def cp(c, _):
                    sl = pl.ds(pl.multiple_of(c * UR, UR), UR)
                    xs[k, sl, :] = xv[short_at[k], sl, :]
                    return 0
                lax.fori_loop(0, 4, cp, 0)

    def send_short(dst, with_halo, half):
        def act_on(d):
            if half == 0:
                d.start()
            else:
                d.wait_send()

        @pl.when(tm < N_SRC)
        def _():
            for q in range(4):
                chunk = 4 * tm + q
                main = xs.at[:, q * UR : (q + 1) * UR, :]
                head = xs.at[:, q * UR : q * UR + 16, :]
                tail = xs.at[:, (q + 1) * UR - 16 : (q + 1) * UR, :]

                def go_main():
                    act_on(remote(main, dst, sem_xs.at[q], sem_xr.at[0 if with_halo else 5], (dp, chunk)))

                def go_head():
                    act_on(remote(head, halo_r.at[1:U], sem_xs.at[4 + q], sem_xr.at[1], (dp, chunk - 1)))

                if q == 0:
                    pl.when(tm > 0)(go_main)
                    if half == 0:
                        @pl.when(tm == 0)
                        def _():
                            for k in range(U - 1):
                                dst[k] = xs[k, 0:UR, :]
                else:
                    go_main()
                if with_halo:
                    if q < 2:
                        pl.when(tm > 0)(go_head)
                    else:
                        go_head()
                    if q == 1 and half == 0:
                        @pl.when(tm == 0)
                        def _():
                            for k in range(U - 1):
                                halo_r[1 + k] = xs[k, UR : UR + 16, :]

                    @pl.when(chunk + 1 < TM)
                    def _():
                        act_on(remote(tail, halo_l.at[1:U], sem_xs.at[8 + q], sem_xr.at[2], (dp, chunk + 1)))

    def recv_short(dst, with_halo):
        @pl.when(tm > 0)
        def _():
            total_wait(dst, sem_xr.at[0 if with_halo else 5])
            if with_halo:
                total_wait(halo_l.at[1:U], sem_xr.at[2])

                @pl.when(tm < TM - 1)
                def _():
                    total_wait(halo_r.at[1:U], sem_xr.at[1])

    def edges(send, recv_l, recv_r, ssem, rsem, start):
        to_next = remote(send.at[1], recv_l, ssem.at[0], rsem.at[0], (dp, lax.rem(tm + 1, TM)))
        to_prev = remote(send.at[0], recv_r, ssem.at[1], rsem.at[1], (dp, lax.rem(tm + TM - 1, TM)))
        if start:
            pl.when(tm < TM - 1)(lambda: to_next.start())
            pl.when(tm > 0)(lambda: to_prev.start())
        else:
            @pl.when(tm < TM - 1)
            def _():
                to_next.wait_send()
                to_prev.wait_recv()

            @pl.when(tm > 0)
            def _():
                to_prev.wait_send()
                to_next.wait_recv()

    def plane_peers():
        return [(a, b) for a in range(Z) for b in range(Y) if a or b]

    def plane_peer(offset):
        pz, py = lax.rem(z + offset[0], Z), lax.rem(y + offset[1], Y)
        return pz, py, (2 * pz + x, 2 * py + core)

    across = (2 * z + 1 - x, tm)

    def gather_stage(buf, m, stage):
        ss, rs = env["sem_gs"].at[m, stage], env["sem_gr"].at[m, stage]
        if stage == 0:
            mine = buf.at[z, x, y, core]
            for offset in plane_peers():
                remote(mine, mine, ss, rs, plane_peer(offset)[2]).start()
        elif stage == 1:
            mine = buf.at[:, x, :, core]
            remote(mine, mine, ss, rs, across).start()
        else:
            mine = buf.at[:, :, :, core]
            remote(mine, mine, ss, rs, (dp, partner)).start()

    def gather_wait(buf, m, stage, sems):
        if stage == 0:
            total_wait(env["little_rz" if buf is sall else "big_rz"].at[0], sems.at[m, stage])
        elif stage == 1:
            total_wait(buf.at[:, 0, :, 0], sems.at[m, stage])
        else:
            total_wait(buf.at[:, :, :, 0], sems.at[m, stage])

    def gather_got(buf, m, stage):
        gather_wait(buf, m, stage, env["sem_gr"])

    def gather_left(buf, m):
        for stage in range(3):
            gather_wait(buf, m, stage, env["sem_gs"])

    if fast:
        wall, sall = env["wall"], env["sall"]

        def weights(m):
            return wall[m].reshape(C, C)

        pack = env["pack"]
        pack[...] = jnp.zeros(pack.shape, F32)
        for l in range(LAYERS):
            pack[AT_TAPS + 8 * l : AT_TAPS + 8 * l + KERNEL, 0:SH] = env["taps"][l].astype(F32)
        pack[AT_GAMMA : AT_GAMMA + LAYERS, 0:SH] = env["gamma"][...].astype(F32)
        pack[AT_BETA : AT_BETA + LAYERS, 0:SH] = env["beta"][...].astype(F32)
        turned = pack[...].T[0:SH]
        pack[0:SH, :] = turned
        pack[0:SH, 0:SE] = env["excite"][...].astype(F32)
        sall[z, x, y, core, :, 0:LANES] = pack[0:SH, :].astype(BF16)
        pack[0:SH, 0:SE] = env["squeeze"][...].astype(F32)
        sall[z, x, y, core, :, LANES : 2 * LANES] = pack[0:SH, :].astype(BF16)
        for l in range(LAYERS):
            wall[l, z, x, y, core] = env["point"][l]
        wall[LAYERS, z, x, y, core] = env["resid"][...]
    else:
        def weights(m):
            return env["mats"][m]

        small[...] = env["small_in"][...]

    def squeeze_all():
        if fast:
            return sall[...].reshape(C, 2 * LANES)[:, LANES : LANES + SE].astype(F32)
        return env["squeeze"][...].astype(F32)

    class Scatter:
        def __init__(self, name):
            self.send, self.core, self.xsum, self.rx, self.zsum, self.rz, self.ss, self.rs = (
                env[name + part] for part in ("_send", "_core", "_xsum", "_rx", "_zsum", "_rz", "_ss", "_rs")
            )
            self.dtype = self.send.dtype

        def go(self, m, stage):
            ss, rs = self.ss.at[m, stage], self.rs.at[m, stage]
            if stage == 0:
                remote(self.send.at[m, :, :, :, 1 - core], self.core.at[m], ss, rs, (dp, partner)).start()
            elif stage == 1:
                remote(self.xsum.at[m, 1 - x], self.rx.at[m], ss, rs, across).start()
            else:
                for i, offset in enumerate(plane_peers()):
                    pz, py, peer = plane_peer(offset)
                    remote(self.zsum.at[m, pz, py], self.rz.at[m, i], ss, rs, peer).start()

        def size(self, m, stage):
            return (self.core.at[m], self.rx.at[m], self.rz.at[m])[stage]

        def left(self, m):
            for stage in range(3):
                total_wait(self.size(m, stage), self.ss.at[m, stage])

        def core_to_x(self, m):
            total_wait(self.size(m, 0), self.rs.at[m, 0])

            def body(i, _):
                v = self.send[m, i, :, :, core].astype(F32) + self.core[m, i].astype(F32)
                for k in range(2):
                    self.xsum[m, k, i] = v[k].astype(self.dtype)
                return 0

            lax.fori_loop(0, Z, body, 0)
            self.go(m, 1)

        def x_to_plane(self, m):
            total_wait(self.size(m, 1), self.rs.at[m, 1])

            def body(i, _):
                v = self.xsum[m, x, i].astype(F32) + self.rx[m, i].astype(F32)
                self.zsum[m, i] = v.astype(self.dtype)
                return 0

            lax.fori_loop(0, Z, body, 0)
            self.go(m, 2)

        def result(self, m):
            total_wait(self.size(m, 2), self.rs.at[m, 2])
            v = self.zsum[m, z, y].astype(F32)
            for i in range(Z * Y - 1):
                v = v + self.rz[m, i].astype(F32)
            return v

    if fast:
        big, little = Scatter("big"), Scatter("little")

    def to_perm_long(src, dst, base):
        for u in range(4):
            o = base(u)
            dst[o : o + UR, :] = dot(perm_l[u * UR : (u + 1) * UR, :], src).astype(BF16)

    def to_perm_short(src, dst, base, masked):
        for k in range(U - 1):
            v = dot(perm_s[...], src[k])
            if masked:
                v = v * wide(mask[k * UR : (k + 1) * UR, :])
            o = base(4 + k)
            dst[o : o + UR, :] = v.astype(BF16)

    y0 = ypad.at[0]
    load_x.wait()
    edge[0] = xv[long_at, 0:16, :]
    edge[1] = xv[long_at, F - 16 : F, :]
    stage_short()
    to_perm_long(xv[long_at], y0, lambda u: win(u) + 32)
    load_g = pltpu.make_async_copy(g_any, xv, sem_loc.at[0])
    load_g.start()
    edge_sems = (sem_xs.at[pl.ds(12, 2)], sem_xr.at[pl.ds(3, 2)])
    pl.semaphore_wait(barrier, len(chips) + len(others))
    if fast:
        gather_stage(sall, MATS, 0)
        gather_stage(wall.at[0], 0, 0)
    edges(edge, halo_l.at[0], halo_r.at[0], *edge_sems, True)
    send_short(xin, True, 0)
    if fast:
        gather_got(sall, MATS, 0)
        gather_stage(sall, MATS, 1)
        gather_got(wall.at[0], 0, 0)
        gather_stage(wall.at[0], 0, 1)
        gather_stage(wall.at[1], 1, 0)
        gather_got(sall, MATS, 1)
        gather_stage(sall, MATS, 2)
        gather_got(wall.at[0], 0, 1)
        gather_stage(wall.at[0], 0, 2)
        gather_got(sall, MATS, 2)
        for j in range(NL):
            part = sall[...].reshape(C, 2 * LANES)[j * LANES : (j + 1) * LANES, 0:LANES].astype(F32)
            small[:, j * LANES : (j + 1) * LANES] = part.T

    def fill_pads(ref, row0, n, j, b0, b1, b2, b3, halo, seg):
        e = lax.broadcasted_iota(jnp.int32, (16, LANES), 0)

        def put(at, v):
            ref[pl.ds(row0 + at * 16, 16), lane(j)] = v.astype(BF16)

        put(0, jnp.where(e == 0, halo[2 * seg : 2 * seg + 1], pltpu.roll(b2, 1, 0)))
        put(1, jnp.where(e == 0, halo[2 * seg + 1 : 2 * seg + 2], pltpu.roll(b3, 1, 0)))
        put(n + 2, jnp.where(e == 15, halo[8 + 2 * seg : 9 + 2 * seg], pltpu.roll(b0, 15, 0)))
        put(n + 3, jnp.where(e == 15, halo[9 + 2 * seg : 10 + 2 * seg], pltpu.roll(b1, 15, 0)))

    def pads_from(ref, j, halo, segs):
        for seg in segs:
            u0, u1 = (0, 3) if seg == 0 else (3 + seg, 3 + seg)
            n = F // 16 if seg == 0 else NB
            o0, o1 = win(u0) + 32, win(u1) + 32 + UR
            blk = [ref[o : o + 16, lane(j)].astype(F32) for o in (o0, o0 + 16, o1 - 32, o1 - 16)]
            fill_pads(ref, win(u0), n, j, *blk, halo, seg)

    def first_pads(segs):
        def body(j, _):
            none = jnp.zeros((2, LANES), F32)
            left = [halo_l[s, :, lane(j)].astype(F32)[14:16] if s in segs else none for s in range(4)]
            right = [halo_r[s, :, lane(j)].astype(F32)[0:2] if s in segs else none for s in range(4)]
            halo = jnp.where(hmask[...] > 0.0, jnp.concatenate(left + right, axis=0), 0.0)
            pads_from(y0, j, halo, segs)
            return 0

        lax.fori_loop(0, NL, body, 0)

    edges(edge, halo_l.at[0], halo_r.at[0], *edge_sems, False)
    first_pads([0])

    def shorts_arrive():
        recv_short(xin, True)
        to_perm_short(xin, y0, lambda u: win(u) + 32, True)
        send_short(xin, True, 1)
        first_pads(range(1, U))

    def sync_core(s):
        d = remote(send_a.at[s], recv_core.at[s], sem_cs.at[s], sem_cr.at[s], (dp, partner))
        d.start()
        d.wait()
        send_b[s] = send_a[s] + recv_core[s]

    def far_first(i):
        a, b = i // (TM // 2), lax.rem(i, TM // 2)
        up = dp < DP // 2
        to_dp = jnp.where(up, lax.rem(DP - 1 - a + DP, DP), a)
        return to_dp, b

    def sync_send(s):
        recv_chip[s, my_chip] = send_b[s]
        dst = recv_chip.at[s, my_chip]

        def one(i, _):
            to_dp, to_y = far_first(i)

            @pl.when((to_dp != dp) | (to_y != y))
            def _():
                remote(send_b.at[s], dst, sem_ks.at[s], sem_kr.at[s], (to_dp, 2 * to_y + core)).start()

            return 0

        for i in range(n_chips):
            one(i, 0)

    def sync_done(s):
        others = recv_chip.at[s, 0 : n_chips - 1]
        total_wait(others, sem_kr.at[s])
        total_wait(others, sem_ks.at[s])
        total = recv_chip[s, 0]
        for i in range(1, n_chips):
            total = total + recv_chip[s, i]
        return total

    def tap_rows(l, j):
        group = small[pl.ds(pl.multiple_of(AT_TAPS + 8 * l, 8), 8), lane(j)]
        return [group[k : k + 1] for k in range(KERNEL)]

    LONG, SHORT = range(4), range(4, NU)

    def conv_pass(l, units):
        def body(j, _):
            w = tap_rows(l, j)
            for u in units:
                o = win(u)
                v = ypad[l, o : o + UR + 64, lane(j)].astype(F32)
                t = v[0:UR] * w[0]
                for k in range(1, KERNEL):
                    t = t + v[16 * k : 16 * k + UR] * w[k]
                if u >= 4:
                    t = t * mask[(u - 4) * UR : (u - 3) * UR, :]
                dlow[l, u * UR : (u + 1) * UR, lane(j)] = t.astype(BF16)
            return 0

        lax.fori_loop(0, NL, body, 0)

    def fold8(v):
        return jnp.sum(v.reshape(v.shape[0] // 8, 8, v.shape[1]), axis=0)

    def put_edges(src, l):
        for seg in range(4):
            base = 0 if seg == 0 else F + (seg - 1) * UR
            n = F if seg == 0 else UR
            for e in range(2):
                hsend[l, 1, 2 * seg + e : 2 * seg + e + 1, :] = src(base + n - 32 + 16 * e + 15)
                hsend[l, 0, 2 * seg + e : 2 * seg + e + 1, :] = src(base + 16 * e)

    def matmul_pass(l, units):
        r = slice(units[0] * UR, (units[-1] + 1) * UR)
        h = dot(dlow[l, r, :], weights(l))
        pre[l, r, :] = h
        s0, s1 = fold8(h), fold8(h * h)
        if units[0] > 0:
            s0, s1 = s0 + sums[0], s1 + sums[1]
        sums[0] = s0
        sums[1] = s1

    def send_stats(l):
        send_a[l, 0:1, :] = jnp.sum(sums[0], axis=0, keepdims=True)
        send_a[l, 1:2, :] = jnp.sum(sums[1], axis=0, keepdims=True)
        put_edges(lambda row: pre[l, row : row + 1, :], l)

    def act_pass(l):
        def body(j, _):
            a, b = coef[l, 0:1, lane(j)], coef[l, 1:2, lane(j)]
            for u in range(NU):
                v = pre[l, u * UR : (u + 1) * UR, lane(j)] * a + b
                v = v + v * jnp.tanh(v)
                if u >= 4:
                    v = v * mask[(u - 4) * UR : (u - 3) * UR, :]
                o = win(u) + 32
                ypad[l + 1, o : o + UR, lane(j)] = v.astype(BF16)
            v = hh[l, :, lane(j)] * a + b
            v = (v + v * jnp.tanh(v)) * hmask[...]
            pads_from(ypad.at[l + 1], j, v, range(U))
            return 0

        lax.fori_loop(0, NL, body, 0)

    def layer(l, _):
        conv_pass(l, LONG)
        if fast:
            gather_got(wall.at[l], l, 2)
        matmul_pass(l, LONG)
        pl.when(l == 0)(shorts_arrive)
        conv_pass(l, SHORT)
        matmul_pass(l, SHORT)
        send_stats(l)
        edges(hsend.at[l], hh.at[l, 0:8], hh.at[l, 8:16], sem_hs.at[l], sem_hr.at[l], True)
        sync_core(l)
        sync_send(l)

        if fast:
            gather_got(wall.at[l + 1], l + 1, 0)
            gather_stage(wall.at[l + 1], l + 1, 1)

            @pl.when(l < LAYERS - 1)
            def _():
                gather_stage(wall.at[l + 2], l + 2, 0)

        @pl.when(l == 0)
        def _():
            load_g.wait()
            stage_short()
            send_short(gin4, False, 0)
            to_perm_long(xv[long_at], cot, lambda u: u * UR)

        @pl.when(l == 1)
        def _():
            recv_short(gin4, False)
            to_perm_short(gin4, cot, lambda u: u * UR, True)
            send_short(gin4, False, 1)

        if fast:
            gather_got(wall.at[l + 1], l + 1, 1)
            gather_stage(wall.at[l + 1], l + 1, 2)
        total = sync_done(l)
        edges(hsend.at[l], hh.at[l, 0:8], hh.at[l, 8:16], sem_hs.at[l], sem_hr.at[l], False)
        scale = wide(inv_count)
        mean = total[0:1] * scale
        var = total[1:2] * scale - mean * mean
        inv = lax.rsqrt(var + NORM_EPSILON)
        ga = small[pl.ds(AT_GAMMA + l, 1), :]
        a = ga * inv
        coef[l, 0:1, :] = 0.5 * a
        coef[l, 1:2, :] = 0.5 * (small[pl.ds(AT_BETA + l, 1), :] - mean * a)
        coef[l, 2:3, :] = mean
        coef[l, 3:4, :] = inv
        coef[l, 4:5, :] = a

        pl.when(l < LAYERS - 1)(lambda: act_pass(l))
        return 0

    lax.fori_loop(0, LAYERS, layer, 0)

    top = LAYERS - 1
    pool[...] = jnp.zeros(pool.shape, F32)

    def last_act(j, _):
        a, b = coef[top, 0:1, lane(j)], coef[top, 1:2, lane(j)]
        acc = None
        for u in range(NU):
            v = pre[top, u * UR : (u + 1) * UR, lane(j)] * a + b
            v = v + v * jnp.tanh(v)
            if u >= 4:
                v = v * mask[(u - 4) * UR : (u - 3) * UR, :]
            act[u * UR : (u + 1) * UR, lane(j)] = v
            f = fold8(v)
            acc = f if u == 0 or u >= 4 else acc + f
            if u >= 3:
                pool[u - 3 : u - 2, lane(j)] = jnp.sum(acc, axis=0, keepdims=True)
        return 0

    lax.fori_loop(0, NL, last_act, 0)

    def time_sum(s, value):
        tsend[s] = value
        ds = [remote(tsend.at[s], trecv.at[s, i - 1], sem_ts.at[s], sem_tr.at[s], (dp, lax.rem(tm + i, TM))) for i in range(1, TM)]
        for d in ds:
            d.start()

    def time_done(s):
        whole = trecv.at[s]
        total_wait(whole, sem_tr.at[s])
        total_wait(whole, sem_ts.at[s])
        total = tsend[s]
        for i in range(TM - 1):
            total = total + trecv[s, i]
        return total

    e8 = lax.broadcasted_iota(jnp.int32, (8, LANES), 0)
    len8 = jnp.full((8, LANES), F * TM, jnp.int32)
    for k in range(U - 1):
        len8 = jnp.where(e8 == k + 1, short_len[k], len8)
    inv_len = 1.0 / len8.astype(F32)
    live = jnp.where(e8 < U, 1.0, 0.0)
    time_sum(0, pool[...])
    if fast:
        gather_got(wall.at[LAYERS], LAYERS, 2)
    resd[0:F, :] = dot(ypad[0, 32 : 32 + F, :], weights(LAYERS))
    for u in SHORT:
        resd[u * UR : (u + 1) * UR, :] = dot(ypad[0, win(u) + 32 : win(u) + 32 + UR, :], weights(LAYERS))
    p = time_done(0) * wide(inv_len)
    sq = squeeze_all()
    ex = small[0:SE, :]
    q = dot(p, sq, precision=HIGHEST)
    sig_q = logistic(q)
    z_act = q * sig_q
    gate[...] = logistic(dot(z_act, ex, precision=HIGHEST))
    pool[...] = jnp.zeros(pool.shape, F32)

    def top_pass(j, _):
        acc = None
        for u in range(NU):
            rs = slice(u * UR, (u + 1) * UR)
            seg = seg_of(u)
            av = act[rs, lane(j)]
            half = 0.5 * (av * gate[seg : seg + 1, lane(j)] + resd[rs, lane(j)])
            t = jnp.tanh(half)
            out = half + half * t
            slope = (0.5 + 0.5 * t) * (1.0 + half * (1.0 - t))
            dv = cot[rs, lane(j)].astype(F32) * slope
            if u >= 4:
                out = out * mask[(u - 4) * UR : (u - 3) * UR, :]
            outp[rs, lane(j)] = out.astype(BF16)
            du[rs, lane(j)] = dv
            drl[rs, lane(j)] = dv.astype(BF16)
            f = fold8(dv * av)
            acc = f if u == 0 or u >= 4 else acc + f
            if u >= 3:
                pool[u - 3 : u - 2, lane(j)] = jnp.sum(acc, axis=0, keepdims=True)
        return 0

    lax.fori_loop(0, NL, top_pass, 0)
    time_sum(1, pool[...])

    def back_long(buf, src):
        for u in range(4):
            buf[0, u * UR : (u + 1) * UR, :] = dot(back_l[u * UR : (u + 1) * UR, :], src[0:F, :]).astype(BF16)

    def back_short(buf, stage, src):
        for k in range(U - 1):
            stage[k] = dot(back_s[...], src[F + k * UR : F + (k + 1) * UR, :]).astype(BF16)

        @pl.when(tm >= N_SRC)
        def _():
            for k in range(U - 1):
                buf[1 + k] = jnp.zeros((F, C), BF16)

        @pl.when(first)
        def _():
            for k in range(U - 1):
                buf[1 + k, 0:UR, :] = stage[k]

    def back_piece(buf, stage, sems, rsems, k):
        owner, q = tm // 4, lax.rem(tm, 4)
        dst = buf.at[1 + k, pl.ds(pl.multiple_of(q * UR, UR), UR), :]
        return remote(stage.at[k], dst, sems.at[k], rsems.at[k, q], (dp, owner))

    def back_send(buf, stage, sems, rsems, ks):
        @pl.when(tm > 0)
        def _():
            for k in ks:
                back_piece(buf, stage, sems, rsems, k).start()

    def back_done(buf, stage, sems, rsems):
        @pl.when(tm > 0)
        def _():
            for k in range(U - 1):
                back_piece(buf, stage, sems, rsems, k).wait_send()

        @pl.when(tm < N_SRC)
        def _():
            for k in range(U - 1):
                for i in range(4):
                    got = functools.partial(total_wait, buf.at[1 + k, i * UR : (i + 1) * UR, :], rsems.at[k, i])
                    if i == 0:
                        pl.when(tm > 0)(got)
                    else:
                        got()

    back_long(obuf, outp)
    back_short(obuf, xin, outp)

    def xrows(u):
        o = win(u) + 32
        return ypad[0, o : o + UR, :]

    def put_grad(m, total):
        if fast:
            big.send[m] = total.astype(BF16).reshape(Z, 2, Y, 2, SH, C)
            big.go(m, 0)
        else:
            gp[...] = total
            pltpu.make_async_copy(gp, env["gmats"].at[m], sem_loc.at[1]).start()

    def grad_gone():
        if not fast:
            pltpu.make_async_copy(gp, env["gmats"].at[0], sem_loc.at[1]).wait()

    def xrows(u):
        o = win(u) + 32
        return ypad[0, o : o + UR, :]

    def resid_grads():
        total = dot(ypad[0, 32 : 32 + F, :], drl[0:F, :], ((0,), (0,)))
        for u in SHORT:
            total = total + dot(xrows(u), drl[u * UR : (u + 1) * UR, :], ((0,), (0,)))
        put_grad(LAYERS, total)
        gres_in[...] = dot(drl[...], weights(LAYERS), ((1,), (1,)))

    resid_grads()
    dg = time_done(1)
    gv = gate[...]
    de = dg * gv * (1.0 - gv) * wide(live)
    dz = dot(de, ex, ((1,), (1,)), precision=HIGHEST)
    dq = dz * sig_q * (1.0 + q * (1.0 - sig_q))
    cvec[...] = dot(dq, sq, ((1,), (1,)), precision=HIGHEST) * wide(inv_len)
    lead = jnp.where(first, 1.0, 0.0)
    zero = jnp.zeros((C, LANES - 2 * SE), F32)
    pair = [dot(de, z_act, ((0,), (0,)), precision=HIGHEST), dot(p, dq, ((0,), (0,)), precision=HIGHEST)]
    pair = jnp.concatenate(pair + [zero] * (LANES > 2 * SE), axis=1) * lead
    if fast:
        little.send[0] = pair.reshape(Z, 2, Y, 2, SH, LANES)
        little.go(0, 0)
    else:
        env["gpair"][...] = pair

    def norm_slope(l, u, j, a, b, m, s):
        h = pre[l, u * UR : (u + 1) * UR, lane(j)]
        half = h * a + b
        t = jnp.tanh(half)
        slope = (0.5 + 0.5 * t) * (1.0 + half * (1.0 - t))
        if u >= 4:
            slope = slope * mask[(u - 4) * UR : (u - 3) * UR, :]
        return slope, (h - m) * s

    def back_sums(l, s, grad_of):
        def body(j, _):
            a, b, m, i = (coef[l, r : r + 1, lane(j)] for r in range(4))
            acc0 = acc1 = None
            make = grad_of(j)
            for u in range(NU):
                slope, xc = norm_slope(l, u, j, a, b, m, i)
                v = make(u) * slope
                dn[u * UR : (u + 1) * UR, lane(j)] = v
                f0, f1 = fold8(v), fold8(v * xc)
                acc0 = f0 if u == 0 else acc0 + f0
                acc1 = f1 if u == 0 else acc1 + f1
            send_a[s, 0:1, lane(j)] = jnp.sum(acc0, axis=0, keepdims=True)
            send_a[s, 1:2, lane(j)] = jnp.sum(acc1, axis=0, keepdims=True)
            return 0

        lax.fori_loop(0, NL, body, 0)
        put_edges(lambda row: dn[row : row + 1, :], s)

    def top_grad(j):
        def make(u):
            seg = seg_of(u)
            return du[u * UR : (u + 1) * UR, lane(j)] * gate[seg : seg + 1, lane(j)] + cvec[seg : seg + 1, lane(j)]
        return make

    def conv_grad(l):
        def outer(j):
            w = tap_rows(l, j)

            def make(u):
                o = win(u)
                v = ddpad[o : o + UR + 64, lane(j)].astype(F32)
                t = v[64 : 64 + UR] * w[0]
                for k in range(1, KERNEL):
                    t = t + v[64 - 16 * k : 64 - 16 * k + UR] * w[k]
                return t
            return make
        return outer

    back_sums(top, LAYERS, top_grad)

    def point_grad(l):
        grad_gone()
        put_grad(l, dot(dlow[l], dhl[0:R, :], ((0,), (0,))))

    def depth_grad(l):
        def body(j, _):
            acc = [None] * KERNEL
            for u in range(NU):
                o = win(u)
                v = ypad[l, o : o + UR + 64, lane(j)].astype(F32)
                g = ddpad[o + 32 : o + 32 + UR, lane(j)].astype(F32)
                for k in range(KERNEL):
                    f = fold8(v[16 * k : 16 * k + UR] * g)
                    acc[k] = f if u == 0 else acc[k] + f
            rows = [jnp.sum(acc[k], axis=0, keepdims=True) for k in range(KERNEL)]
            rows.append(jnp.zeros((8 - KERNEL, LANES), F32))
            at = pl.ds(pl.multiple_of(AT_TAPS + 8 * l, 8), 8)
            gsmall[at, lane(j)] = jnp.concatenate(rows, axis=0)
            return 0

        lax.fori_loop(0, NL, body, 0)
    def dh_pass(l):
        def body(j, _):
            a, k1, k0 = (coef[l, r : r + 1, lane(j)] for r in (4, 5, 6))
            for u in range(NU):
                rs = slice(u * UR, (u + 1) * UR)
                v = dn[rs, lane(j)] * a - (pre[l, rs, lane(j)] * k1 + k0)
                if u >= 4:
                    v = v * mask[(u - 4) * UR : (u - 3) * UR, :]
                dhl[rs, lane(j)] = v.astype(BF16)
            v = (dhh[l, :, lane(j)] * a - (hh[l, :, lane(j)] * k1 + k0)) * hmask[...]
            dhl[R : R + 16, lane(j)] = v.astype(BF16)
            return 0

        lax.fori_loop(0, NL, body, 0)

    def dd_pass(l):
        v = dot(dhl[...], weights(l), ((1,), (1,)))
        ddpad[32 : 32 + F, :] = v[0:F].astype(BF16)
        for u in SHORT:
            ddpad[win(u) + 32 : win(u) + 32 + UR, :] = v[u * UR : (u + 1) * UR].astype(BF16)
        hh[l] = v[R : R + 16].astype(BF16).astype(F32)

        def pad(j, _):
            pads_from(ddpad, j, hh[l, :, lane(j)], range(U))
            return 0

        lax.fori_loop(0, NL, pad, 0)

    def back_layer(step, _):
        l = top - step
        s = LAYERS + step
        edges(hsend.at[s], dhh.at[l, 0:8], dhh.at[l, 8:16], sem_hs.at[s], sem_hr.at[s], True)
        sync_core(s)
        sync_send(s)

        @pl.when(step > 0)
        def _():
            point_grad(l + 1)
            depth_grad(l + 1)

        @pl.when((step > 0) & (step < U))
        def _():
            back_send(obuf, xin, sem_os.at[0], sem_or.at[0], [step - 1])

        if fast:
            @pl.when(step == 0)
            def _():
                little.core_to_x(0)

            @pl.when(step == 1)
            def _():
                little.x_to_plane(0)

            @pl.when(step > 0)
            def _():
                big.x_to_plane(l + 2)

            @pl.when(step > 1)
            def _():
                env["gmats"][l + 3] = big.result(l + 3)

            big.core_to_x(l + 1)

        total = sync_done(s)
        edges(hsend.at[s], dhh.at[l, 0:8], dhh.at[l, 8:16], sem_hs.at[s], sem_hr.at[s], False)
        ggb[l, 0:2, :] = total
        m, i, a = coef[l, 2:3, :], coef[l, 3:4, :], coef[l, 4:5, :]
        k1 = a * i * total[1:2] * wide(inv_count)
        coef[l, 5:6, :] = k1
        coef[l, 6:7, :] = a * total[0:1] * wide(inv_count) - m * k1

        dh_pass(l)
        dd_pass(l)

        @pl.when(l > 0)
        def _():
            back_sums(l - 1, s + 1, conv_grad(l - 1))
        return 0

    def run_back():
        lax.fori_loop(0, LAYERS, back_layer, 0)

    conv_grad_of = conv_grad

    def conv_grad(l):
        return conv_grad_of(l + 1)

    gsmall[...] = jnp.zeros(gsmall.shape, F32)
    run_back()
    lead_all = jnp.where(first & (dp == 0), 1.0, 0.0)
    for l in range(LAYERS):
        gsmall[AT_BETA + l : AT_BETA + l + 1, :] = ggb[l, 0:1, :] * lead_all
        gsmall[AT_GAMMA + l : AT_GAMMA + l + 1, :] = ggb[l, 1:2, :] * lead_all
    def final_pass(units):
        def body(j, _):
            make = conv_grad_of(0)(j)
            for u in units:
                rs = slice(u * UR, (u + 1) * UR)
                v = make(u)
                if u >= 4:
                    v = v * mask[(u - 4) * UR : (u - 3) * UR, :]
                outp[rs, lane(j)] = (v + gres_in[rs, lane(j)]).astype(BF16)
            return 0

        lax.fori_loop(0, NL, body, 0)

    final_pass(SHORT)
    back_short(gbuf, gin4, outp)
    back_send(gbuf, gin4, sem_os.at[1], sem_or.at[1], range(U - 1))
    point_grad(0)
    if fast:
        big.x_to_plane(1)
    depth_grad(0)
    if fast:
        for j in range(NL):
            rows = gsmall[:, j * LANES : (j + 1) * LANES].T
            part = rows.reshape(LANES // (2 * SH), 2, SH, LANES)
            per = LANES // (2 * SH)
            for i in range(per):
                n = j * per + i
                little.send[1, n // (2 * Y), n // Y % 2, n % Y] = part[i]
        little.go(1, 0)
        big.core_to_x(0)
        little.core_to_x(1)
        env["gmats"][2] = big.result(2)
        env["gmats"][1] = big.result(1)
        env["gpair"][...] = little.result(0)
    final_pass(LONG)
    back_long(gbuf, outp)
    back_done(obuf, xin, sem_os.at[0], sem_or.at[0])
    put_out = pltpu.make_async_copy(obuf, out_any, sem_loc.at[2])
    put_out.start()
    if fast:
        big.x_to_plane(0)
        little.x_to_plane(1)
        env["gmats"][0] = big.result(0)
        env["grows"][...] = little.result(1)
        for m in range(MATS):
            big.left(m)
            gather_left(wall.at[m], m)
        little.left(0)
        little.left(1)
        gather_left(sall, MATS)
    else:
        env["grows"][...] = gsmall[...]
    back_done(gbuf, gin4, sem_os.at[1], sem_or.at[1])
    put_gin = pltpu.make_async_copy(gbuf, gin_any, sem_loc.at[3])
    put_gin.start()
    grad_gone()
    put_out.wait()
    put_gin.wait()


def finish_kernel(cfg, lengths, out_s, gin_s, gmats_any, gpair_any, grows_any, *rest):
    DP, TM, U, F, C, SE, SH, LAYERS, KERNEL, fast = cfg
    out, gin, gdepth, gpoint, ggamma, gbeta, gsq, gex, gres, hold, gmats, gpair, grows, turn, sems, sems_g = rest
    dp = lax.axis_index("dp")
    long_at = jnp.int32(0)
    for b in range(1, U):
        long_at = jnp.where(lengths[dp * U + b] == F * TM, jnp.int32(b), long_at)
    copies = []
    loads = [
        pltpu.make_async_copy(src, dst, sems_g.at[i])
        for i, (src, dst) in enumerate(((gmats_any, gmats), (gpair_any, gpair), (grows_any, grows)))
    ]
    for c in loads:
        c.start()
    for b in range(U):
        slot = jnp.where(b == long_at, 0, jnp.where(b < long_at, b + 1, b))
        for i, (src, dst) in enumerate(((out_s, out), (gin_s, gin))):
            get = pltpu.make_async_copy(src.at[slot], hold.at[i, b], sems.at[0, i, b])
            put = pltpu.make_async_copy(hold.at[i, b], dst.at[b], sems.at[1, i, b])
            copies.append((get, put))
            get.start()
    for get, put in copies:
        get.wait()
        put.start()
    for c in loads:
        c.wait()
    at_taps = SE
    at_gamma = SE + 8 * LAYERS
    at_beta = at_gamma + 8
    gpoint[...] = gmats[0:LAYERS]
    gres[...] = gmats[LAYERS]
    gsq[...] = gpair[:, SE : 2 * SE]
    gex[...] = gpair[:, 0:SE]
    turn[...] = jnp.zeros(turn.shape, F32)
    turn[0:SH] = grows[...]
    turn[...] = turn[...].T
    for l in range(LAYERS):
        gdepth[l] = turn[at_taps + 8 * l : at_taps + 8 * l + KERNEL, 0:SH]
    ggamma[...] = turn[at_gamma : at_gamma + LAYERS, 0:SH]
    gbeta[...] = turn[at_beta : at_beta + LAYERS, 0:SH]
    for _, put in copies:
        put.wait()


def local(sizes, inputs, lengths, depth_w, point_w, gamma, beta, squeeze_w, excite_w, resid_w, cotangent):
    DP, TM = sizes
    U, F, C = inputs.shape
    LAYERS, KERNEL, SH = depth_w.shape
    SE = squeeze_w.shape[1]
    UR = F // 4
    NU = 4 + U - 1
    R = NU * UR
    RP = F + 64 + (U - 1) * (UR + 64)
    S = 2 * LAYERS
    chips = DP * (TM // 2) - 1
    axes = ("dp", "tm")
    fast = SH % 16 == 0 and DP % 2 == 0 and DP > 2
    Z, Y = DP // 2, TM // 2
    MATS = LAYERS + 1
    vm = pltpu.VMEM
    dma = pltpu.SemaphoreType.DMA
    any_spec = pl.BlockSpec(memory_space=pl.ANY)
    vm_spec = pl.BlockSpec(memory_space=pltpu.VMEM)
    sm_spec = pl.BlockSpec(memory_space=pltpu.SMEM)
    sd = jax.ShapeDtypeStruct
    cfg = (DP, TM, U, F, C, SE, SH, LAYERS, KERNEL, fast)
    at_gamma = SE + 8 * LAYERS
    operands = dict(lengths=lengths, x_any=inputs, g_any=cotangent)
    specs = [sm_spec, any_spec, any_spec]
    outs = dict(out_any=sd((U, F, C), BF16), gin_any=sd((U, F, C), BF16))
    out_specs = [any_spec, any_spec]
    if fast:
        operands.update(
            point=point_w, taps=depth_w, gamma=gamma, beta=beta, squeeze=squeeze_w, excite=excite_w.T, resid=resid_w
        )
        specs += [vm_spec] * 7
        outs.update(gmats=sd((MATS, SH, C), F32), gpair=sd((SH, LANES), F32), grows=sd((SH, LANES), F32))
        out_specs += [vm_spec] * 3
    else:
        mats = jnp.concatenate([point_w, resid_w[None]], axis=0)
        depth_rows = jnp.pad(depth_w, ((0, 0), (0, 8 - KERNEL), (0, 0))).reshape(8 * LAYERS, SH)
        fill = ((0, 8 - LAYERS), (0, 0))
        rows = jnp.concatenate([excite_w, depth_rows, jnp.pad(gamma, fill), jnp.pad(beta, fill)], axis=0)
        rows = jnp.pad(rows, ((0, LANES - rows.shape[0]), (0, 0)))
        operands.update(
            mats=lax.all_gather(mats, axes, axis=1, tiled=True),
            small_in=lax.all_gather(rows, axes, axis=1, tiled=True).astype(F32),
            squeeze=lax.all_gather(squeeze_w, axes, axis=0, tiled=True),
        )
        specs += [vm_spec] * 3
        outs.update(gmats=sd((MATS, C, C), F32), gpair=sd((C, LANES), F32), grows=sd((LANES, C), F32))
        out_specs += [any_spec, vm_spec, vm_spec]
    scratch = dict(
        xv=vm((U, F, C), BF16), xs=vm((U - 1, F, C), BF16), edge=vm((2, 16, C), BF16),
        xin=vm((U - 1, UR, C), BF16), gin4=vm((U - 1, UR, C), BF16),
        halo_l=vm((4, 16, C), BF16), halo_r=vm((4, 16, C), BF16),
        cot=vm((R, C), BF16), ypad=vm((LAYERS, RP, C), BF16), dlow=vm((LAYERS, R, C), BF16),
        pre=vm((LAYERS, R, C), F32), hh=vm((LAYERS, 16, C), F32),
        mask=vm(((U - 1) * UR, LANES), F32), hmask=vm((16, LANES), F32), coef=vm((LAYERS, 8, C), F32),
        resd=vm((R, C), F32), act=vm((R, C), F32), du=vm((R, C), F32), drl=vm((R, C), BF16), dn=vm((R, C), F32),
        dhl=vm((R + 16, C), BF16), ddpad=vm((RP, C), BF16), gres_in=vm((R, C), F32),
        perm_l=vm((F, F), BF16), perm_s=vm((UR, UR), BF16), back_l=vm((F, F), BF16), back_s=vm((UR, UR), BF16),
        outp=vm((R, C), BF16), obuf=vm((U, F, C), BF16), gbuf=vm((U, F, C), BF16), gp=vm((C, C), F32),
        small=vm((LANES, C), F32), gsmall=vm((LANES, C), F32), ggb=vm((LAYERS, 8, C), F32),
        sums=vm((2, 8, C), F32), send_a=vm((S, 2, C), F32), send_b=vm((S, 2, C), F32),
        recv_core=vm((S, 2, C), F32), recv_chip=vm((S, chips + 1, 2, C), F32),
        hsend=vm((S, 2, 8, C), F32), dhh=vm((LAYERS, 16, C), F32),
        tsend=vm((2, 8, C), F32), trecv=vm((2, TM - 1, 8, C), F32),
        pool=vm((8, C), F32), gate=vm((8, C), F32), cvec=vm((8, C), F32),
        sem_loc=dma((4,)), sem_cs=dma((S,)), sem_cr=dma((S,)), sem_ks=dma((S,)), sem_kr=dma((S,)),
        sem_hs=dma((S, 2)), sem_hr=dma((S, 2)), sem_ts=dma((2,)), sem_tr=dma((2,)),
        sem_xs=dma((14,)), sem_xr=dma((6,)), sem_os=dma((2, U - 1)), sem_or=dma((2, U - 1, 4)),
    )
    if fast:
        scratch.update(
            wall=vm((MATS, Z, 2, Y, 2, SH, C), BF16), sall=vm((Z, 2, Y, 2, SH, 2 * LANES), BF16),
            pack=vm((LANES, LANES), F32), sem_gs=dma((MATS + 1, 3)), sem_gr=dma((MATS + 1, 3)),
        )
        for name, n, cols, kind in (("big", MATS, C, BF16), ("little", 2, LANES, F32)):
            scratch.update(
                {
                    name + "_send": vm((n, Z, 2, Y, 2, SH, cols), kind),
                    name + "_core": vm((n, Z, 2, Y, SH, cols), kind),
                    name + "_xsum": vm((n, 2, Z, Y, SH, cols), kind),
                    name + "_rx": vm((n, Z, Y, SH, cols), kind),
                    name + "_zsum": vm((n, Z, Y, SH, cols), kind),
                    name + "_rz": vm((n, Z * Y - 1, SH, cols), kind),
                    name + "_ss": dma((n, 3)),
                    name + "_rs": dma((n, 3)),
                }
            )
    names = list(operands) + list(outs) + list(scratch)
    out_s, gin_s, gmats, gpair, grows = pl.pallas_call(
        functools.partial(block_kernel, cfg, names),
        out_shape=tuple(outs.values()),
        in_specs=specs,
        out_specs=tuple(out_specs),
        scratch_shapes=list(scratch.values()),
        compiler_params=pltpu.CompilerParams(collective_id=0, has_side_effects=True, vmem_limit_bytes=63 << 20),
    )(*operands.values())
    if not fast:
        gmats = lax.psum_scatter(gmats, axes, scatter_dimension=1, tiled=True)
        gpair = lax.psum_scatter(gpair, axes, scatter_dimension=0, tiled=True)
        grows = lax.psum_scatter(grows, axes, scatter_dimension=1, tiled=True).T
    sizes_out = (
        ((U, F, C), BF16), ((U, F, C), BF16), ((LAYERS, KERNEL, SH), F32), ((LAYERS, SH, C), F32), ((LAYERS, SH), F32),
        ((LAYERS, SH), F32), ((SH, SE), F32), ((SH, SE), F32), ((SH, C), F32),
    )
    done = pl.pallas_call(
        functools.partial(finish_kernel, cfg),
        out_shape=tuple(sd(*size) for size in sizes_out),
        in_specs=[sm_spec] + [any_spec] * 5,
        out_specs=(any_spec,) * 2 + (vm_spec,) * 7,
        scratch_shapes=[
            vm((2, U, F, C), BF16), vm((MATS, SH, C), F32), vm((SH, LANES), F32), vm((SH, LANES), F32),
            vm((LANES, LANES), F32), dma((2, 2, U)), dma((3,)),
        ],
    )(lengths, out_s, gin_s, gmats, gpair, grows)
    return done[:7] + (done[7].T, done[8])


def solution(mesh):
    both = ("dp", "tm")
    rows, cols = P(both, None), P(None, both)
    frames = P("dp", "tm", None)
    taps, mats = P(None, None, both), P(None, both, None)
    sizes = (mesh.shape["dp"], mesh.shape["tm"])
    return jax.shard_map(
        functools.partial(local, sizes),
        mesh=mesh,
        in_specs=(frames, P(), taps, mats, cols, cols, rows, cols, rows, frames),
        out_specs=(frames, frames, taps, mats, cols, cols, rows, cols, rows),
        check_vma=False,
    )
```

```python
import functools

import jax
import jax.numpy as jnp
from jax import lax
from jax.experimental import pallas as pl
from jax.experimental.pallas import tpu as pltpu
from jax.sharding import PartitionSpec as P

MESH = pl.DeviceIdType.MESH
NORM_EPSILON = 1e-05
LANES = 128
HIGHEST = lax.Precision.HIGHEST
F32 = jnp.float32
BF16 = jnp.bfloat16


def dot(a, b, dims=((1,), (0,)), precision=None):
    return lax.dot_general(a, b, (dims, ((), ())), precision=precision, preferred_element_type=F32)


def logistic(v):
    return 0.5 * jnp.tanh(0.5 * v) + 0.5


def block_kernel(cfg, names, *refs):
    DP, TM, U, F, C, SE, SH, LAYERS, KERNEL, fast = cfg
    env = dict(zip(names, refs, strict=True))
    lengths, x_any, g_any = env["lengths"], env["x_any"], env["g_any"]
    out_any, gin_any = env["out_any"], env["gin_any"]
    xv, xs, edge, xin, gin4 = env["xv"], env["xs"], env["edge"], env["xin"], env["gin4"]
    halo_l, halo_r, cot, ypad, dlow = env["halo_l"], env["halo_r"], env["cot"], env["ypad"], env["dlow"]
    pre, hh, mask, hmask, coef = env["pre"], env["hh"], env["mask"], env["hmask"], env["coef"]
    resd, act, du, drl = env["resd"], env["act"], env["du"], env["drl"]
    dn, gres_in = act, resd
    dhl, ddpad = env["dhl"], env["ddpad"]
    perm_l, perm_s, back_l, back_s = env["perm_l"], env["perm_s"], env["back_l"], env["back_s"]
    outp, obuf, gbuf, gp, small = env["outp"], env["obuf"], env["gbuf"], env.get("gp"), env["small"]
    sums, send_a, send_b, recv_core, recv_chip = (
        env["sums"], env["send_a"], env["send_b"], env["recv_core"], env["recv_chip"]
    )
    hsend, dhh, tsend, trecv = env["hsend"], env["dhh"], env["tsend"], env["trecv"]
    pool, gate, cvec, gsmall = env["pool"], env["gate"], env["cvec"], env["gsmall"]
    hx = env["hx"]
    slope, fac, facs = env["slope"], env["fac"], env["facs"]
    ggb = env["ggb"]
    sem_loc, sem_cs, sem_cr, sem_ks, sem_kr = (
        env["sem_loc"], env["sem_cs"], env["sem_cr"], env["sem_ks"], env["sem_kr"]
    )
    sem_hs, sem_hr, sem_ts, sem_tr = env["sem_hs"], env["sem_hr"], env["sem_ts"], env["sem_tr"]
    sem_xs, sem_xr, sem_os, sem_or = env["sem_xs"], env["sem_xr"], env["sem_os"], env["sem_or"]
    MATS = LAYERS + 1
    AT_TAPS, AT_GAMMA = SE, SE + 8 * LAYERS
    AT_BETA = AT_GAMMA + 8
    NL = C // LANES
    UR = F // 4
    NU = 4 + (U - 1)
    NB = UR // 16
    R = NU * UR
    N_SRC = TM // 4
    dp, tm = lax.axis_index("dp"), lax.axis_index("tm")
    partner = tm + 1 - 2 * lax.rem(tm, 2)
    first, last = tm == 0, tm == TM - 1
    chips = [(a, 2 * b) for a in range(DP) for b in range(TM // 2) if a or b]
    n_chips = len(chips) + 1
    my_chip = dp * (TM // 2) + tm // 2

    def at_chip(offset):
        return (lax.rem(dp + offset[0], DP), lax.rem(tm + offset[1], TM))

    def win(u):
        return u * UR if u < 4 else F + 64 + (u - 4) * (UR + 64)

    def seg_of(u):
        return 0 if u < 4 else u - 3

    def lane(j):
        return slice(j * LANES, (j + 1) * LANES)

    def each_lane(body):
        for j in range(NL):
            body(j, 0)

    def wide(v):
        return jnp.concatenate([v] * NL, axis=1)

    def remote(src, dst, ssem, rsem, dev):
        return pltpu.make_async_remote_copy(src, dst, ssem, rsem, device_id=dev, device_id_type=MESH)

    def total_wait(ref, sem):
        pltpu.make_async_copy(ref, ref, sem).wait()

    barrier = pltpu.get_barrier_semaphore()
    load_x = pltpu.make_async_copy(x_any, xv, sem_loc.at[0])
    load_x.start()
    others = [(0, b) for b in range(1, TM, 2)]
    for offset in chips + others:
        pl.semaphore_signal(barrier, inc=1, device_id=at_chip(offset), device_id_type=MESH)

    my_len = [lengths[dp * U + b] for b in range(U)]
    long_at = jnp.int32(0)
    for b in range(1, U):
        long_at = jnp.where(my_len[b] == F * TM, jnp.int32(b), long_at)
    short_at = [jnp.where(k < long_at, k, k + 1) for k in range(U - 1)]
    short_len = [lengths[dp * U + b] for b in range(U - 1)]
    short_len = [jnp.where(k < long_at, my_len[k], my_len[k + 1]) for k in range(U - 1)]
    x, z, y, core = lax.rem(dp, 2), dp // 2, tm // 2, lax.rem(tm, 2)
    Y = TM // 2
    Z = DP // 2
    count = lax.fori_loop(0, DP * U, lambda i, c: c + lengths[i], jnp.int32(0)).astype(F32)
    inv_count = 1.0 / jnp.full((1, LANES), count, F32)
    rows = lax.broadcasted_iota(jnp.int32, (UR, LANES), 0)
    time_s = (rows & 15) * NB + (rows >> 4) + tm * UR
    for k in range(U - 1):
        mask[k * UR : (k + 1) * UR, :] = jnp.where(time_s < short_len[k], 1.0, 0.0)
    e16 = lax.broadcasted_iota(jnp.int32, (16, LANES), 0)
    part = (e16 & 7) >> 1
    is_left = e16 < 8
    when = jnp.where(is_left, tm * UR - 2 + (e16 & 1), tm * UR + UR + (e16 & 1))
    bound = jnp.full((16, LANES), 1 << 30, jnp.int32)
    for k in range(U - 1):
        bound = jnp.where(part == k + 1, short_len[k], bound)
    inside = jnp.where(is_left, tm, TM - 1 - tm) > 0
    hmask[...] = jnp.where(inside & (when < bound), 1.0, 0.0)

    def one_hot(ref, size, to_time):
        n = size // 16
        r0 = lax.broadcasted_iota(jnp.int32, (UR, size), 0)
        r1 = lax.broadcasted_iota(jnp.int32, (UR, size), 1)
        for c in range(size // UR):
            a, b = (r1, r0 + c * UR) if to_time else (r0 + c * UR, r1)
            hit = b == (a & 15) * n + (a >> 4)
            ref[c * UR : (c + 1) * UR, :] = jnp.where(hit, 1.0, 0.0).astype(BF16)

    one_hot(perm_l, F, False)
    one_hot(perm_s, UR, False)
    one_hot(back_l, F, True)
    one_hot(back_s, UR, True)

    @pl.when(first)
    def _():
        halo_l[...] = jnp.zeros(halo_l.shape, BF16)
        for l in range(LAYERS):
            hh[l, 0:8, :] = jnp.zeros((8, C), F32)
            dhh[l, 0:8, :] = jnp.zeros((8, C), F32)

    @pl.when(last)
    def _():
        halo_r[...] = jnp.zeros(halo_r.shape, BF16)
        for l in range(LAYERS):
            hh[l, 8:16, :] = jnp.zeros((8, C), F32)
            dhh[l, 8:16, :] = jnp.zeros((8, C), F32)

    def stage_short():
        @pl.when(tm < N_SRC)
        def _():
            for k in range(U - 1):
                def cp(c, _):
                    sl = pl.ds(pl.multiple_of(c * UR, UR), UR)
                    xs[k, sl, :] = xv[short_at[k], sl, :]
                    return 0
                lax.fori_loop(0, 4, cp, 0)

    def send_short(dst, with_halo, half):
        def act_on(d):
            if half == 0:
                d.start()
            else:
                d.wait_send()

        @pl.when(tm < N_SRC)
        def _():
            for q in range(4):
                chunk = 4 * tm + q
                main = xs.at[:, q * UR : (q + 1) * UR, :]
                head = xs.at[:, q * UR : q * UR + 16, :]
                tail = xs.at[:, (q + 1) * UR - 16 : (q + 1) * UR, :]

                def go_main():
                    act_on(remote(main, dst, sem_xs.at[q], sem_xr.at[0 if with_halo else 5], (dp, chunk)))

                def go_head():
                    act_on(remote(head, halo_r.at[1:U], sem_xs.at[4 + q], sem_xr.at[1], (dp, chunk - 1)))

                if q == 0:
                    pl.when(tm > 0)(go_main)
                    if half == 0:
                        @pl.when(tm == 0)
                        def _():
                            for k in range(U - 1):
                                dst[k] = xs[k, 0:UR, :]
                else:
                    go_main()
                if with_halo:
                    if q < 2:
                        pl.when(tm > 0)(go_head)
                    else:
                        go_head()
                    if q == 1 and half == 0:
                        @pl.when(tm == 0)
                        def _():
                            for k in range(U - 1):
                                halo_r[1 + k] = xs[k, UR : UR + 16, :]

                    @pl.when(chunk + 1 < TM)
                    def _():
                        act_on(remote(tail, halo_l.at[1:U], sem_xs.at[8 + q], sem_xr.at[2], (dp, chunk + 1)))

    def recv_short(dst, with_halo):
        @pl.when(tm > 0)
        def _():
            total_wait(dst, sem_xr.at[0 if with_halo else 5])
            if with_halo:
                total_wait(halo_l.at[1:U], sem_xr.at[2])

                @pl.when(tm < TM - 1)
                def _():
                    total_wait(halo_r.at[1:U], sem_xr.at[1])

    def edges(send, recv_l, recv_r, ssem, rsem, start):
        to_next = remote(send.at[1], recv_l, ssem.at[0], rsem.at[0], (dp, lax.rem(tm + 1, TM)))
        to_prev = remote(send.at[0], recv_r, ssem.at[1], rsem.at[1], (dp, lax.rem(tm + TM - 1, TM)))
        if start:
            pl.when(tm < TM - 1)(lambda: to_next.start())
            pl.when(tm > 0)(lambda: to_prev.start())
        else:
            @pl.when(tm < TM - 1)
            def _():
                to_next.wait_send()
                to_prev.wait_recv()

            @pl.when(tm > 0)
            def _():
                to_prev.wait_send()
                to_next.wait_recv()

    def plane_peers():
        return [(a, b) for a in range(Z) for b in range(Y) if a or b]

    def plane_peer(offset):
        pz, py = lax.rem(z + offset[0], Z), lax.rem(y + offset[1], Y)
        return pz, py, (2 * pz + x, 2 * py + core)

    across = (2 * z + 1 - x, tm)

    def gather_stage(buf, m, stage):
        ss, rs = env["sem_gs"].at[m, stage], env["sem_gr"].at[m, stage]
        if stage == 0:
            mine = buf.at[z, x, y, core]
            for offset in plane_peers():
                remote(mine, mine, ss, rs, plane_peer(offset)[2]).start()
        elif stage == 1:
            mine = buf.at[:, x, :, core]
            remote(mine, mine, ss, rs, across).start()
        else:
            mine = buf.at[:, :, :, core]
            remote(mine, mine, ss, rs, (dp, partner)).start()

    def gather_wait(buf, m, stage, sems):
        if stage == 0:
            size = env["little_rz"].at[0] if buf is sall else env["big_rz"].at[0]
            total_wait(size, sems.at[m, stage])
        elif stage == 1:
            total_wait(buf.at[:, 0, :, 0], sems.at[m, stage])
        else:
            total_wait(buf.at[:, :, :, 0], sems.at[m, stage])

    def gather_got(buf, m, stage):
        gather_wait(buf, m, stage, env["sem_gr"])

    def gather_left(buf, m):
        for stage in range(3):
            gather_wait(buf, m, stage, env["sem_gs"])

    if fast:
        wall, sall = env["wall"], env["sall"]
        halves = [(wall.at[0], 0)]

        def weights(m):
            return wall[m].reshape(C, C)

        pack = env["pack"]
        pack[...] = jnp.zeros(pack.shape, F32)
        for l in range(LAYERS):
            pack[AT_TAPS + 8 * l : AT_TAPS + 8 * l + KERNEL, 0:SH] = env["taps"][l].astype(F32)
        pack[AT_GAMMA : AT_GAMMA + LAYERS, 0:SH] = env["gamma"][...].astype(F32)
        pack[AT_BETA : AT_BETA + LAYERS, 0:SH] = env["beta"][...].astype(F32)
        turned = pack[...].T[0:SH]
        pack[0:SH, :] = turned
        pack[0:SH, 0:SE] = env["excite"][...].astype(F32)
        sall[z, x, y, core, :, 0:LANES] = pack[0:SH, :].astype(BF16)
        pack[0:SH, 0:SE] = env["squeeze"][...].astype(F32)
        sall[z, x, y, core, :, LANES : 2 * LANES] = pack[0:SH, :].astype(BF16)
        for l in range(LAYERS):
            wall[l, z, x, y, core] = env["point"][l]
        wall[LAYERS, z, x, y, core] = env["resid"][...]
    else:
        def weights(m):
            return env["mats"][m]

        small[...] = env["small_in"][...]

    def squeeze_all():
        if fast:
            return sall[...].reshape(C, 2 * LANES)[:, LANES : LANES + SE].astype(F32)
        return env["squeeze"][...].astype(F32)

    class Scatter:
        def __init__(self, name):
            self.send, self.core, self.xsum, self.rx, self.zsum, self.rz, self.ss, self.rs = (
                env[name + part] for part in ("_send", "_core", "_xsum", "_rx", "_zsum", "_rz", "_ss", "_rs")
            )
            self.dtype = self.send.dtype

        def go(self, m, stage):
            ss, rs = self.ss.at[m, stage], self.rs.at[m, stage]
            if stage == 0:
                remote(self.send.at[m, :, :, :, 1 - core], self.core.at[m], ss, rs, (dp, partner)).start()
            elif stage == 1:
                remote(self.xsum.at[m, 1 - x], self.rx.at[m], ss, rs, across).start()
            else:
                for i, offset in enumerate(plane_peers()):
                    pz, py, peer = plane_peer(offset)
                    remote(self.zsum.at[m, pz, py], self.rz.at[m, i], ss, rs, peer).start()

        def wait(self, m, stage, sems):
            total_wait((self.core.at[m], self.rx.at[m], self.rz.at[m])[stage], sems.at[m, stage])

        def left(self, m):
            for stage in range(3):
                self.wait(m, stage, self.ss)

        def core_to_x(self, m):
            self.wait(m, 0, self.rs)

            def body(i, _):
                v = self.send[m, i, :, :, core].astype(F32) + self.core[m, i].astype(F32)
                for k in range(2):
                    self.xsum[m, k, i] = v[k].astype(self.dtype)
                return 0

            lax.fori_loop(0, Z, body, 0)
            self.go(m, 1)

        def x_to_plane(self, m):
            self.wait(m, 1, self.rs)

            def body(i, _):
                v = self.xsum[m, x, i].astype(F32) + self.rx[m, i].astype(F32)
                self.zsum[m, i] = v.astype(self.dtype)
                return 0

            lax.fori_loop(0, Z, body, 0)
            self.go(m, 2)

        def result(self, m):
            self.wait(m, 2, self.rs)
            v = self.zsum[m, z, y].astype(F32)
            for i in range(Z * Y - 1):
                v = v + self.rz[m, i].astype(F32)
            return v

    if fast:
        big, little = Scatter("big"), Scatter("little")

    def to_perm_long(src, dst, base):
        for u in range(4):
            o = base(u)
            dst[o : o + UR, :] = dot(perm_l[u * UR : (u + 1) * UR, :], src).astype(BF16)

    def to_perm_short(src, dst, base, masked):
        for k in range(U - 1):
            v = dot(perm_s[...], src[k])
            if masked:
                v = v * wide(mask[k * UR : (k + 1) * UR, :])
            o = base(4 + k)
            dst[o : o + UR, :] = v.astype(BF16)

    y0 = ypad.at[0]
    load_x.wait()
    edge[0] = xv[long_at, 0:16, :]
    edge[1] = xv[long_at, F - 16 : F, :]
    stage_short()
    to_perm_long(xv[long_at], y0, lambda u: win(u) + 32)
    load_g = pltpu.make_async_copy(g_any, xv, sem_loc.at[0])
    load_g.start()
    edge_sems = (sem_xs.at[pl.ds(12, 2)], sem_xr.at[pl.ds(3, 2)])
    pl.semaphore_wait(barrier, len(chips) + len(others))
    if fast:
        gather_stage(sall, MATS, 0)
        for buf, m in halves:
            gather_stage(buf, m, 0)
    edges(edge, halo_l.at[0], halo_r.at[0], *edge_sems, True)
    send_short(xin, True, 0)
    if fast:
        for m in range(1, min(3, MATS)):
            gather_stage(wall.at[m], m, 0)
        gather_got(sall, MATS, 0)
        gather_stage(sall, MATS, 1)
        for buf, m in halves:
            gather_got(buf, m, 0)
            gather_stage(buf, m, 1)
        gather_got(sall, MATS, 1)
        gather_stage(sall, MATS, 2)
        for buf, m in halves:
            gather_got(buf, m, 1)
            gather_stage(buf, m, 2)
        gather_got(sall, MATS, 2)
        for j in range(NL):
            part = sall[...].reshape(C, 2 * LANES)[j * LANES : (j + 1) * LANES, 0:LANES].astype(F32)
            small[:, j * LANES : (j + 1) * LANES] = part.T

    def fill_pads(ref, row0, n, j, b0, b1, b2, b3, halo, seg):
        e = lax.broadcasted_iota(jnp.int32, (16, LANES), 0)

        def put(at, v):
            ref[pl.ds(row0 + at * 16, 16), lane(j)] = v.astype(BF16)

        put(0, jnp.where(e == 0, halo[2 * seg : 2 * seg + 1], pltpu.roll(b2, 1, 0)))
        put(1, jnp.where(e == 0, halo[2 * seg + 1 : 2 * seg + 2], pltpu.roll(b3, 1, 0)))
        put(n + 2, jnp.where(e == 15, halo[8 + 2 * seg : 9 + 2 * seg], pltpu.roll(b0, 15, 0)))
        put(n + 3, jnp.where(e == 15, halo[9 + 2 * seg : 10 + 2 * seg], pltpu.roll(b1, 15, 0)))

    def pads_from(ref, j, halo, segs):
        for seg in segs:
            u0, u1 = (0, 3) if seg == 0 else (3 + seg, 3 + seg)
            n = F // 16 if seg == 0 else NB
            o0, o1 = win(u0) + 32, win(u1) + 32 + UR
            blk = [ref[o : o + 16, lane(j)].astype(F32) for o in (o0, o0 + 16, o1 - 32, o1 - 16)]
            fill_pads(ref, win(u0), n, j, *blk, halo, seg)

    def first_pads(segs):
        def body(j, _):
            none = jnp.zeros((2, LANES), F32)
            left = [halo_l[s, :, lane(j)].astype(F32)[14:16] if s in segs else none for s in range(4)]
            right = [halo_r[s, :, lane(j)].astype(F32)[0:2] if s in segs else none for s in range(4)]
            halo = jnp.where(hmask[...] > 0.0, jnp.concatenate(left + right, axis=0), 0.0)
            pads_from(y0, j, halo, segs)
            return 0

        each_lane(body)

    edges(edge, halo_l.at[0], halo_r.at[0], *edge_sems, False)
    first_pads([0])

    def shorts_arrive():
        if fast:
            gather_got(wall.at[1], 1, 0)
            gather_stage(wall.at[1], 1, 1)
        recv_short(xin, True)
        to_perm_short(xin, y0, lambda u: win(u) + 32, True)
        send_short(xin, True, 1)
        first_pads(range(1, U))

    def sync_core(s):
        d = remote(send_a.at[s], recv_core.at[s], sem_cs.at[s], sem_cr.at[s], (dp, partner))
        d.start()
        d.wait()
        send_b[s] = send_a[s] + recv_core[s]

    def far_first(i):
        a, b = i // Y, lax.rem(i, Y)
        return jnp.where(dp < DP // 2, DP - 1 - a, a), b

    def sync_send(s):
        recv_chip[s, my_chip] = send_b[s]
        dst = recv_chip.at[s, my_chip]

        place = jnp.where(dp < DP // 2, DP - 1 - dp, dp) * Y + y
        for i in range(n_chips - 1):
            to_dp, to_y = far_first(jnp.where(place <= i, i + 1, i))
            remote(send_b.at[s], dst, sem_ks.at[s], sem_kr.at[s], (to_dp, 2 * to_y + core)).start()

    def sync_done(s):
        others = recv_chip.at[s, 0 : n_chips - 1]
        total_wait(others, sem_kr.at[s])
        total_wait(others, sem_ks.at[s])
        total = recv_chip[s, 0]
        for i in range(1, n_chips):
            total = total + recv_chip[s, i]
        return total

    def tap_rows(l, j):
        group = small[pl.ds(pl.multiple_of(AT_TAPS + 8 * l, 8), 8), lane(j)]
        return [group[k : k + 1] for k in range(KERNEL)]

    LONG, SHORT = range(4), range(4, NU)

    def conv_pass(l, units):
        def body(j, _):
            w = tap_rows(l, j)
            for u in units:
                o = win(u)
                v = ypad[l, o : o + UR + 64, lane(j)].astype(F32)
                t = v[0:UR] * w[0]
                for k in range(1, KERNEL):
                    t = t + v[16 * k : 16 * k + UR] * w[k]
                if u >= 4:
                    t = t * mask[(u - 4) * UR : (u - 3) * UR, :]
                dlow[l, u * UR : (u + 1) * UR, lane(j)] = t.astype(BF16)
            return 0

        each_lane(body)

    def fold8(v):
        return jnp.sum(v.reshape(v.shape[0] // 8, 8, v.shape[1]), axis=0)

    def put_edges(src, l):
        for seg in range(4):
            base = 0 if seg == 0 else F + (seg - 1) * UR
            n = F if seg == 0 else UR
            for e in range(2):
                hsend[l, 1, 2 * seg + e : 2 * seg + e + 1, :] = src(base + n - 32 + 16 * e + 15)
                hsend[l, 0, 2 * seg + e : 2 * seg + e + 1, :] = src(base + 16 * e)

    def matmul_pass(l, units):
        r = slice(units[0] * UR, (units[-1] + 1) * UR)
        h = dot(dlow[l, r, :], weights(l))
        pre[l, r, :] = h
        s0, s1 = fold8(h), fold8(h * h)
        if units[0] > 0:
            s0, s1 = s0 + sums[0], s1 + sums[1]
        sums[0] = s0
        sums[1] = s1

    def send_stats(l):
        send_a[l, 0:1, :] = jnp.sum(sums[0], axis=0, keepdims=True)
        send_a[l, 1:2, :] = jnp.sum(sums[1], axis=0, keepdims=True)
        put_edges(lambda row: pre[l, row : row + 1, :], l)

    def act_pass(l):
        def body(j, _):
            a, b = coef[l, 0:1, lane(j)], coef[l, 1:2, lane(j)]
            for u in range(NU):
                v = pre[l, u * UR : (u + 1) * UR, lane(j)] * a + b
                v = v + v * jnp.tanh(v)
                if u >= 4:
                    v = v * mask[(u - 4) * UR : (u - 3) * UR, :]
                o = win(u) + 32
                ypad[l + 1, o : o + UR, lane(j)] = v.astype(BF16)
            v = hh[l, :, lane(j)] * a + b
            v = (v + v * jnp.tanh(v)) * hmask[...]
            pads_from(ypad.at[l + 1], j, v, range(U))
            return 0

        each_lane(body)

    def prep_pass(l):
        def body(j, _):
            a, b, m, i = (coef[l, r : r + 1, lane(j)] for r in range(4))
            for u in range(NU):
                rs = slice(u * UR, (u + 1) * UR)
                h = pre[l, rs, lane(j)]
                half = h * a + b
                t = jnp.tanh(half)
                v = (0.5 + 0.5 * t) * (1.0 + half * (1.0 - t))
                if u >= 4:
                    v = v * mask[(u - 4) * UR : (u - 3) * UR, :]
                slope[l, rs, lane(j)] = v.astype(BF16)
                pre[l, rs, lane(j)] = (h - m) * i
            hx[l, :, lane(j)] = (hh[l, :, lane(j)] - m) * i
            return 0

        each_lane(body)

    def layer(l, _):
        conv_pass(l, LONG)
        if fast:
            gather_got(wall.at[l], l, 2)
        matmul_pass(l, LONG)
        pl.when(l == 0)(shorts_arrive)
        conv_pass(l, SHORT)
        matmul_pass(l, SHORT)
        send_stats(l)
        edges(hsend.at[l], hh.at[l, 0:8], hh.at[l, 8:16], sem_hs.at[l], sem_hr.at[l], True)
        sync_core(l)
        sync_send(l)

        if fast:
            gather_got(wall.at[l + 1], l + 1, 1)
            gather_stage(wall.at[l + 1], l + 1, 2)

            @pl.when(l + 2 < MATS)
            def _():
                gather_got(wall.at[l + 2], l + 2, 0)
                gather_stage(wall.at[l + 2], l + 2, 1)

            @pl.when(l + 3 < MATS)
            def _():
                gather_stage(wall.at[l + 3], l + 3, 0)

        pl.when(l > 0)(lambda: prep_pass(l - 1))

        @pl.when(l == 0)
        def _():
            load_g.wait()
            stage_short()
            send_short(gin4, False, 0)
            to_perm_long(xv[long_at], cot, lambda u: u * UR)

        @pl.when(l == 1)
        def _():
            recv_short(gin4, False)
            to_perm_short(gin4, cot, lambda u: u * UR, True)
            send_short(gin4, False, 1)

        total = sync_done(l)
        edges(hsend.at[l], hh.at[l, 0:8], hh.at[l, 8:16], sem_hs.at[l], sem_hr.at[l], False)
        scale = wide(inv_count)
        mean = total[0:1] * scale
        var = total[1:2] * scale - mean * mean
        inv = lax.rsqrt(var + NORM_EPSILON)
        ga = small[pl.ds(AT_GAMMA + l, 1), :]
        a = ga * inv
        coef[l, 0:1, :] = 0.5 * a
        coef[l, 1:2, :] = 0.5 * (small[pl.ds(AT_BETA + l, 1), :] - mean * a)
        coef[l, 2:3, :] = mean
        coef[l, 3:4, :] = inv
        coef[l, 4:5, :] = a

        pl.when(l < LAYERS - 1)(lambda: act_pass(l))
        return 0

    lax.fori_loop(0, LAYERS, layer, 0)

    top = LAYERS - 1
    pool[...] = jnp.zeros(pool.shape, F32)

    def last_act(j, _):
        a, b = coef[top, 0:1, lane(j)], coef[top, 1:2, lane(j)]
        acc = None
        for u in range(NU):
            v = pre[top, u * UR : (u + 1) * UR, lane(j)] * a + b
            v = v + v * jnp.tanh(v)
            if u >= 4:
                v = v * mask[(u - 4) * UR : (u - 3) * UR, :]
            act[u * UR : (u + 1) * UR, lane(j)] = v
            f = fold8(v)
            acc = f if u == 0 or u >= 4 else acc + f
            if u >= 3:
                pool[u - 3 : u - 2, lane(j)] = jnp.sum(acc, axis=0, keepdims=True)
        return 0

    each_lane(last_act)

    def time_sum(s, value):
        tsend[s] = value
        ds = [remote(tsend.at[s], trecv.at[s, i - 1], sem_ts.at[s], sem_tr.at[s], (dp, lax.rem(tm + i, TM))) for i in range(1, TM)]
        for d in ds:
            d.start()

    def time_done(s):
        whole = trecv.at[s]
        total_wait(whole, sem_tr.at[s])
        total_wait(whole, sem_ts.at[s])
        total = tsend[s]
        for i in range(TM - 1):
            total = total + trecv[s, i]
        return total

    e8 = lax.broadcasted_iota(jnp.int32, (8, LANES), 0)
    len8 = jnp.full((8, LANES), F * TM, jnp.int32)
    for k in range(U - 1):
        len8 = jnp.where(e8 == k + 1, short_len[k], len8)
    inv_len = 1.0 / len8.astype(F32)
    live = jnp.where(e8 < U, 1.0, 0.0)
    time_sum(0, pool[...])
    prep_pass(top)
    if fast:
        gather_got(wall.at[LAYERS], LAYERS, 2)
    resd[0:F, :] = dot(ypad[0, 32 : 32 + F, :], weights(LAYERS))
    for u in SHORT:
        resd[u * UR : (u + 1) * UR, :] = dot(ypad[0, win(u) + 32 : win(u) + 32 + UR, :], weights(LAYERS))
    p = time_done(0) * wide(inv_len)
    sq = squeeze_all()
    ex = small[0:SE, :]
    q = dot(p, sq, precision=HIGHEST)
    sig_q = logistic(q)
    z_act = q * sig_q
    gate[...] = logistic(dot(z_act, ex, precision=HIGHEST))
    pool[...] = jnp.zeros(pool.shape, F32)

    def top_pass(j, _):
        acc = None
        for u in range(NU):
            rs = slice(u * UR, (u + 1) * UR)
            seg = seg_of(u)
            av = act[rs, lane(j)]
            half = 0.5 * (av * gate[seg : seg + 1, lane(j)] + resd[rs, lane(j)])
            t = jnp.tanh(half)
            out = half + half * t
            slope = (0.5 + 0.5 * t) * (1.0 + half * (1.0 - t))
            dv = cot[rs, lane(j)].astype(F32) * slope
            if u >= 4:
                out = out * mask[(u - 4) * UR : (u - 3) * UR, :]
            outp[rs, lane(j)] = out.astype(BF16)
            du[rs, lane(j)] = dv
            drl[rs, lane(j)] = dv.astype(BF16)
            f = fold8(dv * av)
            acc = f if u == 0 or u >= 4 else acc + f
            if u >= 3:
                pool[u - 3 : u - 2, lane(j)] = jnp.sum(acc, axis=0, keepdims=True)
        return 0

    each_lane(top_pass)
    time_sum(1, pool[...])

    def back_long(buf, src):
        for u in range(4):
            buf[0, u * UR : (u + 1) * UR, :] = dot(back_l[u * UR : (u + 1) * UR, :], src[0:F, :]).astype(BF16)

    def back_short(buf, stage, src):
        for k in range(U - 1):
            stage[k] = dot(back_s[...], src[F + k * UR : F + (k + 1) * UR, :]).astype(BF16)

        @pl.when(tm >= N_SRC)
        def _():
            for k in range(U - 1):
                buf[1 + k] = jnp.zeros((F, C), BF16)

        @pl.when(first)
        def _():
            for k in range(U - 1):
                buf[1 + k, 0:UR, :] = stage[k]

    def back_piece(buf, stage, sems, rsems, k):
        owner, q = tm // 4, lax.rem(tm, 4)
        dst = buf.at[1 + k, pl.ds(pl.multiple_of(q * UR, UR), UR), :]
        return remote(stage.at[k], dst, sems.at[k], rsems.at[k, q], (dp, owner))

    def back_send(buf, stage, sems, rsems, ks):
        @pl.when(tm > 0)
        def _():
            for k in ks:
                back_piece(buf, stage, sems, rsems, k).start()

    def back_left(buf, stage, sems, rsems):
        @pl.when(tm > 0)
        def _():
            for k in range(U - 1):
                back_piece(buf, stage, sems, rsems, k).wait_send()

    def back_arrived(buf, rsems, k):
        @pl.when(tm < N_SRC)
        def _():
            for i in range(4):
                got = functools.partial(total_wait, buf.at[1 + k, i * UR : (i + 1) * UR, :], rsems.at[k, i])
                if i == 0:
                    pl.when(tm > 0)(got)
                else:
                    got()

    def back_done(buf, stage, sems, rsems):
        back_left(buf, stage, sems, rsems)
        for k in range(U - 1):
            back_arrived(buf, rsems, k)

    put_out = pltpu.make_async_copy(obuf, out_any, sem_loc.at[2])
    back_long(obuf, outp)
    back_short(obuf, xin, outp)

    def xrows(u):
        o = win(u) + 32
        return ypad[0, o : o + UR, :]

    def put_grad(m, total):
        if fast:
            big.send[m] = total.astype(BF16).reshape(Z, 2, Y, 2, SH, C)
            big.go(m, 0)
        else:
            gp[...] = total
            pltpu.make_async_copy(gp, env["gmats"].at[m], sem_loc.at[1]).start()

    def grad_gone():
        if not fast:
            pltpu.make_async_copy(gp, env["gmats"].at[0], sem_loc.at[1]).wait()

    def xrows(u):
        o = win(u) + 32
        return ypad[0, o : o + UR, :]

    def resid_grads():
        total = dot(ypad[0, 32 : 32 + F, :], drl[0:F, :], ((0,), (0,)))
        for u in SHORT:
            total = total + dot(xrows(u), drl[u * UR : (u + 1) * UR, :], ((0,), (0,)))
        put_grad(LAYERS, total)
        gres_in[...] = dot(drl[...], weights(LAYERS), ((1,), (1,)))

    resid_grads()
    dg = time_done(1)
    gv = gate[...]
    de = dg * gv * (1.0 - gv) * wide(live)
    dz = dot(de, ex, ((1,), (1,)), precision=HIGHEST)
    dq = dz * sig_q * (1.0 + q * (1.0 - sig_q))
    cvec[...] = dot(dq, sq, ((1,), (1,)), precision=HIGHEST) * wide(inv_len)
    fac[0], fac[1] = p, de
    facs[0], facs[1] = z_act, dq

    def pair_grads():
        lead = jnp.where(first, 1.0, 0.0)
        zero = jnp.zeros((C, LANES - 2 * SE), F32)
        pair = [dot(fac[1 - i], facs[i], ((0,), (0,)), precision=HIGHEST) for i in range(2)]
        pair = jnp.concatenate(pair + [zero] * (LANES > 2 * SE), axis=1) * lead
        if fast:
            little.send[0] = pair.reshape(Z, 2, Y, 2, SH, LANES)
            little.go(0, 0)
        else:
            env["gpair"][...] = pair

    def back_sums(l, s, grad_of):
        def body(j, _):
            acc0 = acc1 = None
            make = grad_of(j)
            for u in range(NU):
                rs = slice(u * UR, (u + 1) * UR)
                v = make(u) * slope[l, rs, lane(j)].astype(F32)
                xc = pre[l, rs, lane(j)]
                dn[u * UR : (u + 1) * UR, lane(j)] = v
                f0, f1 = fold8(v), fold8(v * xc)
                acc0 = f0 if u == 0 else acc0 + f0
                acc1 = f1 if u == 0 else acc1 + f1
            send_a[s, 0:1, lane(j)] = jnp.sum(acc0, axis=0, keepdims=True)
            send_a[s, 1:2, lane(j)] = jnp.sum(acc1, axis=0, keepdims=True)
            return 0

        each_lane(body)
        put_edges(lambda row: dn[row : row + 1, :], s)

    def top_grad(j):
        def make(u):
            seg = seg_of(u)
            return du[u * UR : (u + 1) * UR, lane(j)] * gate[seg : seg + 1, lane(j)] + cvec[seg : seg + 1, lane(j)]
        return make

    def conv_grad(l):
        def outer(j):
            w = tap_rows(l, j)

            def make(u):
                o = win(u)
                v = ddpad[o : o + UR + 64, lane(j)].astype(F32)
                t = v[64 : 64 + UR] * w[0]
                for k in range(1, KERNEL):
                    t = t + v[64 - 16 * k : 64 - 16 * k + UR] * w[k]
                return t
            return make
        return outer

    back_sums(top, LAYERS, top_grad)

    def point_grad(l):
        grad_gone()
        put_grad(l, dot(dlow[l], dhl[0:R, :], ((0,), (0,))))

    def depth_grad(l):
        def body(j, _):
            acc = [None] * KERNEL
            for u in range(NU):
                o = win(u)
                v = ypad[l, o : o + UR + 64, lane(j)].astype(F32)
                g = ddpad[o + 32 : o + 32 + UR, lane(j)].astype(F32)
                for k in range(KERNEL):
                    f = fold8(v[16 * k : 16 * k + UR] * g)
                    acc[k] = f if u == 0 else acc[k] + f
            rows = [jnp.sum(acc[k], axis=0, keepdims=True) for k in range(KERNEL)]
            rows.append(jnp.zeros((8 - KERNEL, LANES), F32))
            at = pl.ds(pl.multiple_of(AT_TAPS + 8 * l, 8), 8)
            gsmall[at, lane(j)] = jnp.concatenate(rows, axis=0)
            return 0

        each_lane(body)
    def dh_pass(l):
        def body(j, _):
            a, k1, k0 = (coef[l, r : r + 1, lane(j)] for r in (4, 5, 6))
            for u in range(NU):
                rs = slice(u * UR, (u + 1) * UR)
                v = dn[rs, lane(j)] * a - (pre[l, rs, lane(j)] * k1 + k0)
                if u >= 4:
                    v = v * mask[(u - 4) * UR : (u - 3) * UR, :]
                dhl[rs, lane(j)] = v.astype(BF16)
            v = (dhh[l, :, lane(j)] * a - (hx[l, :, lane(j)] * k1 + k0)) * hmask[...]
            dhl[R : R + 16, lane(j)] = v.astype(BF16)
            return 0

        each_lane(body)

    def dd_pass(l):
        v = dot(dhl[...], weights(l), ((1,), (1,)))
        ddpad[32 : 32 + F, :] = v[0:F].astype(BF16)
        for u in SHORT:
            ddpad[win(u) + 32 : win(u) + 32 + UR, :] = v[u * UR : (u + 1) * UR].astype(BF16)
        hx[l] = v[R : R + 16].astype(BF16).astype(F32)

        def pad(j, _):
            pads_from(ddpad, j, hx[l, :, lane(j)], range(U))
            return 0

        each_lane(pad)

    def back_layer(step, _):
        l = top - step
        s = LAYERS + step
        edges(hsend.at[s], dhh.at[l, 0:8], dhh.at[l, 8:16], sem_hs.at[s], sem_hr.at[s], True)
        sync_core(s)
        sync_send(s)

        @pl.when(step > 0)
        def _():
            point_grad(l + 1)
            depth_grad(l + 1)

        pl.when(step == 0)(pair_grads)

        @pl.when(step == LAYERS - 1)
        def _():
            back_done(obuf, xin, sem_os.at[0], sem_or.at[0])
            put_out.start()

        @pl.when((step > 0) & (step < U))
        def _():
            back_send(obuf, xin, sem_os.at[0], sem_or.at[0], [step - 1])

        if fast:
            @pl.when(step == 1)
            def _():
                little.core_to_x(0)

            @pl.when(step == 2)
            def _():
                little.x_to_plane(0)

            @pl.when(step > 0)
            def _():
                big.x_to_plane(l + 2)

            @pl.when(step > 1)
            def _():
                env["gmats"][l + 3] = big.result(l + 3)

            big.core_to_x(l + 1)

        total = sync_done(s)
        edges(hsend.at[s], dhh.at[l, 0:8], dhh.at[l, 8:16], sem_hs.at[s], sem_hr.at[s], False)
        ggb[l, 0:2, :] = total
        a = coef[l, 4:5, :]
        coef[l, 5:6, :] = a * total[1:2] * wide(inv_count)
        coef[l, 6:7, :] = a * total[0:1] * wide(inv_count)

        dh_pass(l)
        pl.when(l == 0)(lambda: point_grad(0))
        dd_pass(l)

        @pl.when(l > 0)
        def _():
            back_sums(l - 1, s + 1, conv_grad(l - 1))
        return 0

    def run_back():
        lax.fori_loop(0, LAYERS, back_layer, 0)

    conv_grad_of = conv_grad

    def conv_grad(l):
        return conv_grad_of(l + 1)

    gsmall[...] = jnp.zeros(gsmall.shape, F32)
    run_back()
    lead_all = jnp.where(first & (dp == 0), 1.0, 0.0)
    for l in range(LAYERS):
        gsmall[AT_BETA + l : AT_BETA + l + 1, :] = ggb[l, 0:1, :] * lead_all
        gsmall[AT_GAMMA + l : AT_GAMMA + l + 1, :] = ggb[l, 1:2, :] * lead_all
    def final_pass(units):
        def body(j, _):
            make = conv_grad_of(0)(j)
            for u in units:
                rs = slice(u * UR, (u + 1) * UR)
                v = make(u)
                if u >= 4:
                    v = v * mask[(u - 4) * UR : (u - 3) * UR, :]
                outp[rs, lane(j)] = (v + gres_in[rs, lane(j)]).astype(BF16)
            return 0

        each_lane(body)

    final_pass(SHORT)
    back_short(gbuf, gin4, outp)
    back_send(gbuf, gin4, sem_os.at[1], sem_or.at[1], range(U - 1))
    if fast:
        big.core_to_x(0)
    depth_grad(0)
    if fast:
        for j in range(NL):
            rows = gsmall[:, j * LANES : (j + 1) * LANES].T
            part = rows.reshape(LANES // (2 * SH), 2, SH, LANES)
            per = LANES // (2 * SH)
            for i in range(per):
                n = j * per + i
                little.send[1, n // (2 * Y), n // Y % 2, n % Y] = part[i]
        little.go(1, 0)
        big.x_to_plane(1)
    final_pass(LONG)
    back_long(gbuf, outp)
    put_gin = [pltpu.make_async_copy(gbuf.at[k], gin_any.at[k], sem_loc.at[3 + k]) for k in range(U)]
    put_gin[0].start()
    if fast:
        little.core_to_x(1)
        env["gmats"][2] = big.result(2)
        big.x_to_plane(0)
        little.x_to_plane(1)
        env["gpair"][...] = little.result(0)
        env["gmats"][1] = big.result(1)
        for m in range(1, MATS):
            big.left(m)
            gather_left(wall.at[m], m)
        for buf, m in halves:
            gather_left(buf, m)
        little.left(0)
        gather_left(sall, MATS)
    else:
        env["grows"][...] = gsmall[...]
    for k in range(U - 1):
        back_arrived(gbuf, sem_or.at[1], k)
        put_gin[1 + k].start()
    back_left(gbuf, gin4, sem_os.at[1], sem_or.at[1])
    if fast:
        env["gmats"][0] = big.result(0)
        env["grows"][...] = little.result(1)
        big.left(0)
        little.left(1)
    grad_gone()
    put_out.wait()
    for c in put_gin:
        c.wait()


def finish_kernel(cfg, lengths, out_s, gin_s, gmats_any, gpair_any, grows_any, *rest):
    DP, TM, U, F, C, SE, SH, LAYERS, KERNEL, fast = cfg
    out, gin, gdepth, gpoint, ggamma, gbeta, gsq, gex, gres, hold, gmats, gpair, grows, turn, sems, sems_g = rest
    dp = lax.axis_index("dp")
    long_at = jnp.int32(0)
    for b in range(1, U):
        long_at = jnp.where(lengths[dp * U + b] == F * TM, jnp.int32(b), long_at)
    copies = []
    loads = [
        pltpu.make_async_copy(src, dst, sems_g.at[i])
        for i, (src, dst) in enumerate(((gmats_any, gmats), (gpair_any, gpair), (grows_any, grows)))
    ]
    for c in loads:
        c.start()
    for b in range(U):
        slot = jnp.where(b == long_at, 0, jnp.where(b < long_at, b + 1, b))
        for i, (src, dst) in enumerate(((out_s, out), (gin_s, gin))):
            get = pltpu.make_async_copy(src.at[slot], hold.at[i, b], sems.at[0, i, b])
            put = pltpu.make_async_copy(hold.at[i, b], dst.at[b], sems.at[1, i, b])
            copies.append((get, put))
            get.start()
    for get, put in copies:
        get.wait()
        put.start()
    for c in loads:
        c.wait()
    at_taps = SE
    at_gamma = SE + 8 * LAYERS
    at_beta = at_gamma + 8
    gpoint[...] = gmats[0:LAYERS]
    gres[...] = gmats[LAYERS]
    gsq[...] = gpair[:, SE : 2 * SE]
    gex[...] = gpair[:, 0:SE]
    turn[...] = jnp.zeros(turn.shape, F32)
    turn[0:SH] = grows[...]
    turn[...] = turn[...].T
    for l in range(LAYERS):
        gdepth[l] = turn[at_taps + 8 * l : at_taps + 8 * l + KERNEL, 0:SH]
    ggamma[...] = turn[at_gamma : at_gamma + LAYERS, 0:SH]
    gbeta[...] = turn[at_beta : at_beta + LAYERS, 0:SH]
    for _, put in copies:
        put.wait()


def local(sizes, inputs, lengths, depth_w, point_w, gamma, beta, squeeze_w, excite_w, resid_w, cotangent):
    DP, TM = sizes
    U, F, C = inputs.shape
    LAYERS, KERNEL, SH = depth_w.shape
    SE = squeeze_w.shape[1]
    UR = F // 4
    NU = 4 + U - 1
    R = NU * UR
    RP = F + 64 + (U - 1) * (UR + 64)
    S = 2 * LAYERS
    chips = DP * (TM // 2) - 1
    axes = ("dp", "tm")
    fast = SH % 16 == 0 and DP % 2 == 0 and DP > 2
    Z, Y = DP // 2, TM // 2
    MATS = LAYERS + 1
    vm = pltpu.VMEM
    dma = pltpu.SemaphoreType.DMA
    any_spec = pl.BlockSpec(memory_space=pl.ANY)
    vm_spec = pl.BlockSpec(memory_space=pltpu.VMEM)
    sm_spec = pl.BlockSpec(memory_space=pltpu.SMEM)
    sd = jax.ShapeDtypeStruct
    cfg = (DP, TM, U, F, C, SE, SH, LAYERS, KERNEL, fast)
    at_gamma = SE + 8 * LAYERS
    operands = dict(lengths=lengths, x_any=inputs, g_any=cotangent)
    specs = [sm_spec, any_spec, any_spec]
    outs = dict(out_any=sd((U, F, C), BF16), gin_any=sd((U, F, C), BF16))
    out_specs = [any_spec, any_spec]
    if fast:
        operands.update(
            point=point_w, taps=depth_w, gamma=gamma, beta=beta, squeeze=squeeze_w, excite=excite_w.T, resid=resid_w
        )
        specs += [vm_spec] * 7
        outs.update(gmats=sd((MATS, SH, C), F32), gpair=sd((SH, LANES), F32), grows=sd((SH, LANES), F32))
        out_specs += [vm_spec] * 3
    else:
        mats = jnp.concatenate([point_w, resid_w[None]], axis=0)
        depth_rows = jnp.pad(depth_w, ((0, 0), (0, 8 - KERNEL), (0, 0))).reshape(8 * LAYERS, SH)
        fill = ((0, 8 - LAYERS), (0, 0))
        rows = jnp.concatenate([excite_w, depth_rows, jnp.pad(gamma, fill), jnp.pad(beta, fill)], axis=0)
        rows = jnp.pad(rows, ((0, LANES - rows.shape[0]), (0, 0)))
        operands.update(
            mats=lax.all_gather(mats, axes, axis=1, tiled=True),
            small_in=lax.all_gather(rows, axes, axis=1, tiled=True).astype(F32),
            squeeze=lax.all_gather(squeeze_w, axes, axis=0, tiled=True),
        )
        specs += [vm_spec] * 3
        outs.update(gmats=sd((MATS, C, C), F32), gpair=sd((C, LANES), F32), grows=sd((LANES, C), F32))
        out_specs += [any_spec, vm_spec, vm_spec]
    scratch = dict(
        xv=vm((U, F, C), BF16), xs=vm((U - 1, F, C), BF16), edge=vm((2, 16, C), BF16),
        xin=vm((U - 1, UR, C), BF16), gin4=vm((U - 1, UR, C), BF16),
        halo_l=vm((4, 16, C), BF16), halo_r=vm((4, 16, C), BF16),
        cot=vm((R, C), BF16), ypad=vm((LAYERS, RP, C), BF16), dlow=vm((LAYERS, R, C), BF16),
        pre=vm((LAYERS, R, C), F32), hh=vm((LAYERS, 16, C), F32), hx=vm((LAYERS, 16, C), F32),
        mask=vm(((U - 1) * UR, LANES), F32), hmask=vm((16, LANES), F32), coef=vm((LAYERS, 8, C), F32),
        resd=vm((R, C), F32), act=vm((R, C), F32), du=vm((R, C), F32), drl=vm((R, C), BF16),
        dhl=vm((R + 16, C), BF16), ddpad=vm((RP, C), BF16),
        perm_l=vm((F, F), BF16), perm_s=vm((UR, UR), BF16), back_l=vm((F, F), BF16), back_s=vm((UR, UR), BF16),
        outp=vm((R, C), BF16), obuf=vm((U, F, C), BF16), gbuf=vm((U, F, C), BF16),
        small=vm((LANES, C), F32), slope=vm((LAYERS, R, C), BF16),
        fac=vm((2, 8, C), F32), facs=vm((2, 8, SE), F32), gsmall=vm((LANES, C), F32), ggb=vm((LAYERS, 8, C), F32),
        sums=vm((2, 8, C), F32), send_a=vm((S, 2, C), F32), send_b=vm((S, 2, C), F32),
        recv_core=vm((S, 2, C), F32), recv_chip=vm((S, chips + 1, 2, C), F32),
        hsend=vm((S, 2, 8, C), F32), dhh=vm((LAYERS, 16, C), F32),
        tsend=vm((2, 8, C), F32), trecv=vm((2, TM - 1, 8, C), F32),
        pool=vm((8, C), F32), gate=vm((8, C), F32), cvec=vm((8, C), F32),
        sem_loc=dma((3 + U,)), sem_cs=dma((S,)), sem_cr=dma((S,)), sem_ks=dma((S,)), sem_kr=dma((S,)),
        sem_hs=dma((S, 2)), sem_hr=dma((S, 2)), sem_ts=dma((2,)), sem_tr=dma((2,)),
        sem_xs=dma((14,)), sem_xr=dma((6,)), sem_os=dma((2, U - 1)), sem_or=dma((2, U - 1, 4)),
    )
    if fast:
        scratch.update(
            wall=vm((MATS, Z, 2, Y, 2, SH, C), BF16), sall=vm((Z, 2, Y, 2, SH, 2 * LANES), BF16),
            pack=vm((LANES, LANES), F32), sem_gs=dma((MATS + 1, 3)), sem_gr=dma((MATS + 1, 3)),
        )
        for name, n, cols, kind in (("big", MATS, C, BF16), ("little", 2, LANES, F32)):
            scratch.update(
                {
                    name + "_send": vm((n, Z, 2, Y, 2, SH, cols), kind),
                    name + "_core": vm((n, Z, 2, Y, SH, cols), kind),
                    name + "_xsum": vm((n, 2, Z, Y, SH, cols), kind),
                    name + "_rx": vm((n, Z, Y, SH, cols), kind),
                    name + "_zsum": vm((n, Z, Y, SH, cols), kind),
                    name + "_rz": vm((n, Z * Y - 1, SH, cols), kind),
                    name + "_ss": dma((n, 3)),
                    name + "_rs": dma((n, 3)),
                }
            )
    if not fast:
        scratch.update(gp=vm((C, C), F32))
    names = list(operands) + list(outs) + list(scratch)
    out_s, gin_s, gmats, gpair, grows = pl.pallas_call(
        functools.partial(block_kernel, cfg, names),
        out_shape=tuple(outs.values()),
        in_specs=specs,
        out_specs=tuple(out_specs),
        scratch_shapes=list(scratch.values()),
        compiler_params=pltpu.CompilerParams(collective_id=0, has_side_effects=True, vmem_limit_bytes=63 << 20),
    )(*operands.values())
    if not fast:
        gmats = lax.psum_scatter(gmats, axes, scatter_dimension=1, tiled=True)
        gpair = lax.psum_scatter(gpair, axes, scatter_dimension=0, tiled=True)
        grows = lax.psum_scatter(grows, axes, scatter_dimension=1, tiled=True).T
    sizes_out = (
        ((U, F, C), BF16), ((U, F, C), BF16), ((LAYERS, KERNEL, SH), F32), ((LAYERS, SH, C), F32), ((LAYERS, SH), F32),
        ((LAYERS, SH), F32), ((SH, SE), F32), ((SH, SE), F32), ((SH, C), F32),
    )
    done = pl.pallas_call(
        functools.partial(finish_kernel, cfg),
        out_shape=tuple(sd(*size) for size in sizes_out),
        in_specs=[sm_spec] + [any_spec] * 5,
        out_specs=(any_spec,) * 2 + (vm_spec,) * 7,
        scratch_shapes=[
            vm((2, U, F, C), BF16), vm((MATS, SH, C), F32), vm((SH, LANES), F32), vm((SH, LANES), F32),
            vm((LANES, LANES), F32), dma((2, 2, U)), dma((3,)),
        ],
    )(lengths, out_s, gin_s, gmats, gpair, grows)
    return done[:7] + (done[7].T, done[8])


def solution(mesh):
    both = ("dp", "tm")
    rows, cols = P(both, None), P(None, both)
    frames = P("dp", "tm", None)
    taps, mats = P(None, None, both), P(None, both, None)
    sizes = (mesh.shape["dp"], mesh.shape["tm"])
    return jax.shard_map(
        functools.partial(local, sizes),
        mesh=mesh,
        in_specs=(frames, P(), taps, mats, cols, cols, rows, cols, rows, frames),
        out_specs=(frames, frames, taps, mats, cols, cols, rows, cols, rows),
        check_vma=False,
    )
```

```python
import functools

import jax
import jax.numpy as jnp
from jax import lax
from jax.experimental import pallas as pl
from jax.experimental.pallas import tpu as pltpu
from jax.sharding import PartitionSpec as P

MESH = pl.DeviceIdType.MESH
NORM_EPSILON = 1e-05
LANES = 128
HIGHEST = lax.Precision.HIGHEST
F32 = jnp.float32
BF16 = jnp.bfloat16


def dot(a, b, dims=((1,), (0,)), precision=None):
    return lax.dot_general(a, b, (dims, ((), ())), precision=precision, preferred_element_type=F32)


def logistic(v):
    return 0.5 * jnp.tanh(0.5 * v) + 0.5


def block_kernel(cfg, names, *refs):
    DP, TM, U, F, C, SE, SH, LAYERS, KERNEL, fast = cfg
    env = dict(zip(names, refs, strict=True))
    lengths, x_any, g_any = env["lengths"], env["x_any"], env["g_any"]
    out_any, gin_any = env["out_any"], env["gin_any"]
    xv, xs, edge, xin, gin4 = env["xv"], env["xs"], env["edge"], env["xin"], env["gin4"]
    halo_l, halo_r, cot, ypad, dlow = env["halo_l"], env["halo_r"], env["cot"], env["ypad"], env["dlow"]
    pre, hh, mask, hmask, coef = env["pre"], env["hh"], env["mask"], env["hmask"], env["coef"]
    resd, act, du, drl = env["resd"], env["act"], env["du"], env["drl"]
    dn, gres_in = act, resd
    dhl, ddpad = env["dhl"], env["ddpad"]
    perm_l, perm_s, back_l, back_s = env["perm_l"], env["perm_s"], env["back_l"], env["back_s"]
    outp, obuf, gbuf, gp, small = env["outp"], env["obuf"], env["gbuf"], env.get("gp"), env["small"]
    sums, send_a, send_b, recv_core, recv_chip = (
        env["sums"], env["send_a"], env["send_b"], env["recv_core"], env["recv_chip"]
    )
    hsend, dhh, tsend, trecv = env["hsend"], env["dhh"], env["tsend"], env["trecv"]
    pool, gate, cvec, gsmall = env["pool"], env["gate"], env["cvec"], env["gsmall"]
    hx = env["hx"]
    slope, fac, facs = env["slope"], env["fac"], env["facs"]
    ggb = env["ggb"]
    sem_loc, sem_cs, sem_cr, sem_ks, sem_kr = (
        env["sem_loc"], env["sem_cs"], env["sem_cr"], env["sem_ks"], env["sem_kr"]
    )
    sem_cot = env["sem_cot"]
    sem_hs, sem_hr, sem_ts, sem_tr = env["sem_hs"], env["sem_hr"], env["sem_ts"], env["sem_tr"]
    sem_xs, sem_xr, sem_os, sem_or = env["sem_xs"], env["sem_xr"], env["sem_os"], env["sem_or"]
    MATS = LAYERS + 1
    AT_TAPS, AT_GAMMA = SE, SE + 8 * LAYERS
    AT_BETA = AT_GAMMA + 8
    NL = C // LANES
    UR = F // 4
    NU = 4 + (U - 1)
    NB = UR // 16
    R = NU * UR
    N_SRC = TM // 4
    dp, tm = lax.axis_index("dp"), lax.axis_index("tm")
    partner = tm + 1 - 2 * lax.rem(tm, 2)
    first, last = tm == 0, tm == TM - 1
    chips = [(a, 2 * b) for a in range(DP) for b in range(TM // 2) if a or b]
    n_chips = len(chips) + 1
    my_chip = dp * (TM // 2) + tm // 2

    def other(v, a, n):
        if n & (n - 1):
            return lax.rem(v + a, n)
        total, bit = 0, 1
        while bit < n:
            own = lax.rem(v // bit, 2)
            total = total + bit * (1 - own if a & bit else own)
            bit *= 2
        return total

    def at_chip(offset):
        return (lax.rem(dp + offset[0], DP), lax.rem(tm + offset[1], TM))

    def win(u):
        return u * UR if u < 4 else F + 64 + (u - 4) * (UR + 64)

    def seg_of(u):
        return 0 if u < 4 else u - 3

    def lane(j):
        return slice(j * LANES, (j + 1) * LANES)

    def each_lane(body):
        for j in range(NL):
            body(j, 0)

    def wide(v):
        return jnp.concatenate([v] * NL, axis=1)

    def remote(src, dst, ssem, rsem, dev):
        return pltpu.make_async_remote_copy(src, dst, ssem, rsem, device_id=dev, device_id_type=MESH)

    def total_wait(ref, sem):
        pltpu.make_async_copy(ref, ref, sem).wait()

    barrier = pltpu.get_barrier_semaphore()
    load_x = pltpu.make_async_copy(x_any, xv, sem_loc.at[0])
    load_x.start()
    others = [(0, b) for b in range(1, TM, 2)]
    for offset in chips + others:
        pl.semaphore_signal(barrier, inc=1, device_id=at_chip(offset), device_id_type=MESH)

    x, z, y, core = lax.rem(dp, 2), dp // 2, tm // 2, lax.rem(tm, 2)
    Y = TM // 2
    Z = DP // 2

    my_len = [lengths[dp * U + b] for b in range(U)]
    long_at = jnp.int32(0)
    for b in range(1, U):
        long_at = jnp.where(my_len[b] == F * TM, jnp.int32(b), long_at)
    short_at = [jnp.where(k < long_at, k, k + 1) for k in range(U - 1)]
    short_len = [lengths[dp * U + b] for b in range(U - 1)]
    short_len = [jnp.where(k < long_at, my_len[k], my_len[k + 1]) for k in range(U - 1)]
    count = lax.fori_loop(0, DP * U, lambda i, c: c + lengths[i], jnp.int32(0)).astype(F32)
    inv_count = 1.0 / jnp.full((1, LANES), count, F32)
    def make_masks():
        rows = lax.broadcasted_iota(jnp.int32, (UR, LANES), 0)
        time_s = (rows & 15) * NB + (rows >> 4) + tm * UR
        for k in range(U - 1):
            mask[k * UR : (k + 1) * UR, :] = jnp.where(time_s < short_len[k], 1.0, 0.0)
        e16 = lax.broadcasted_iota(jnp.int32, (16, LANES), 0)
        part = (e16 & 7) >> 1
        is_left = e16 < 8
        when = jnp.where(is_left, tm * UR - 2 + (e16 & 1), tm * UR + UR + (e16 & 1))
        bound = jnp.full((16, LANES), 1 << 30, jnp.int32)
        for k in range(U - 1):
            bound = jnp.where(part == k + 1, short_len[k], bound)
        inside = jnp.where(is_left, tm, TM - 1 - tm) > 0
        hmask[...] = jnp.where(inside & (when < bound), 1.0, 0.0)

    def one_hot(ref, size, to_time):
        n = size // 16
        r0 = lax.broadcasted_iota(jnp.int32, (UR, size), 0)
        r1 = lax.broadcasted_iota(jnp.int32, (UR, size), 1)
        for c in range(size // UR):
            a, b = (r1, r0 + c * UR) if to_time else (r0 + c * UR, r1)
            hit = b == (a & 15) * n + (a >> 4)
            ref[c * UR : (c + 1) * UR, :] = jnp.where(hit, 1.0, 0.0).astype(BF16)

    def zero_ends():
        @pl.when(first)
        def _():
            halo_l[...] = jnp.zeros(halo_l.shape, BF16)
            for l in range(LAYERS):
                hh[l, 0:8, :] = jnp.zeros((8, C), F32)
                dhh[l, 0:8, :] = jnp.zeros((8, C), F32)

        @pl.when(last)
        def _():
            halo_r[...] = jnp.zeros(halo_r.shape, BF16)
            for l in range(LAYERS):
                hh[l, 8:16, :] = jnp.zeros((8, C), F32)
                dhh[l, 8:16, :] = jnp.zeros((8, C), F32)

    def stage_short():
        @pl.when(tm < N_SRC)
        def _():
            for k in range(U - 1):
                def cp(c, _):
                    sl = pl.ds(pl.multiple_of(c * UR, UR), UR)
                    xs[k, sl, :] = xv[short_at[k], sl, :]
                    return 0
                lax.fori_loop(0, 4, cp, 0)

    def send_short(dst, half):
        def act_on(d):
            if half == 0:
                d.start()
            else:
                d.wait_send()

        @pl.when(tm < N_SRC)
        def _():
            for q in range(4):
                chunk = 4 * tm + q
                main = xs.at[:, q * UR : (q + 1) * UR, :]
                head = xs.at[:, q * UR : q * UR + 16, :]
                tail = xs.at[:, (q + 1) * UR - 16 : (q + 1) * UR, :]

                def go_main():
                    act_on(remote(main, dst, sem_xs.at[q], sem_xr.at[0], (dp, chunk)))

                def go_head():
                    act_on(remote(head, halo_r.at[1:U], sem_xs.at[4 + q], sem_xr.at[1], (dp, chunk - 1)))

                if q == 0:
                    pl.when(tm > 0)(go_main)
                    if half == 0:
                        @pl.when(tm == 0)
                        def _():
                            for k in range(U - 1):
                                dst[k] = xs[k, 0:UR, :]
                else:
                    go_main()
                if q < 2:
                    pl.when(tm > 0)(go_head)
                else:
                    go_head()
                if q == 1 and half == 0:
                    @pl.when(tm == 0)
                    def _():
                        for k in range(U - 1):
                            halo_r[1 + k] = xs[k, UR : UR + 16, :]

                @pl.when(chunk + 1 < TM)
                def _():
                    act_on(remote(tail, halo_l.at[1:U], sem_xs.at[8 + q], sem_xr.at[2], (dp, chunk + 1)))

    S2 = 2 * LAYERS

    def cot_piece(k, half):
        @pl.when(tm < N_SRC)
        def _():
            for q in range(4):
                chunk = 4 * tm + q
                src = xs.at[k, q * UR : (q + 1) * UR, :]
                copy = remote(src, gin4.at[k], sem_cot.at[k, q], sem_cr.at[S2 + k], (dp, chunk))
                go = copy.start if half == 0 else copy.wait_send
                if q == 0:
                    pl.when(tm > 0)(go)
                else:
                    go()

        if half == 0:
            @pl.when(tm == 0)
            def _():
                gin4[k] = xs[k, 0:UR, :]

    def recv_short(dst):
        @pl.when(tm > 0)
        def _():
            total_wait(dst, sem_xr.at[0])
            total_wait(halo_l.at[1:U], sem_xr.at[2])

            @pl.when(tm < TM - 1)
            def _():
                total_wait(halo_r.at[1:U], sem_xr.at[1])

    def edges(send, recv_l, recv_r, ssem, rsem, start):
        to_next = remote(send.at[1], recv_l, ssem.at[0], rsem.at[0], (dp, lax.rem(tm + 1, TM)))
        to_prev = remote(send.at[0], recv_r, ssem.at[1], rsem.at[1], (dp, lax.rem(tm + TM - 1, TM)))
        if start:
            pl.when(tm < TM - 1)(lambda: to_next.start())
            pl.when(tm > 0)(lambda: to_prev.start())
        else:
            @pl.when(tm < TM - 1)
            def _():
                to_next.wait_send()
                to_prev.wait_recv()

            @pl.when(tm > 0)
            def _():
                to_prev.wait_send()
                to_next.wait_recv()

    def plane_peers():
        return [(a, b) for a in reversed(range(Z)) for b in reversed(range(Y)) if a or b]

    def plane_peer(offset):
        pz, py = other(z, offset[0], Z), other(y, offset[1], Y)
        return pz, py, (2 * pz + x, 2 * py + core)

    across = (2 * z + 1 - x, tm)

    def gather_stage(buf, m, stage):
        ss, rs = env["sem_gs"].at[m, stage], env["sem_gr"].at[m, stage]
        if stage == 0:
            mine = buf.at[z, x, y, core]
            for offset in plane_peers():
                remote(mine, mine, ss, rs, plane_peer(offset)[2]).start()
        elif stage == 1:
            mine = buf.at[:, x, :, core]
            remote(mine, mine, ss, rs, across).start()
        else:
            mine = buf.at[:, :, :, core]
            remote(mine, mine, ss, rs, (dp, partner)).start()

    def gather_wait(buf, m, stage, sems):
        if stage == 0:
            size = env["little_rz"].at[0] if buf is sall else env["big_rz"].at[0]
            total_wait(size, sems.at[m, stage])
        elif stage == 1:
            total_wait(buf.at[:, 0, :, 0], sems.at[m, stage])
        else:
            total_wait(buf.at[:, :, :, 0], sems.at[m, stage])

    def gather_got(buf, m, stage):
        gather_wait(buf, m, stage, env["sem_gr"])

    def gather_left(buf, m):
        for stage in range(3):
            gather_wait(buf, m, stage, env["sem_gs"])

    if fast:
        wall, sall = env["wall"], env["sall"]
        halves = [(wall.at[0], 0)]

        def weights(m):
            return wall[m].reshape(C, C)

        pack = env["pack"]
        pack[...] = jnp.zeros(pack.shape, F32)
        for l in range(LAYERS):
            pack[AT_TAPS + 8 * l : AT_TAPS + 8 * l + KERNEL, 0:SH] = env["taps"][l].astype(F32)
        pack[AT_GAMMA : AT_GAMMA + LAYERS, 0:SH] = env["gamma"][...].astype(F32)
        pack[AT_BETA : AT_BETA + LAYERS, 0:SH] = env["beta"][...].astype(F32)
        turned = pack[...].T[0:SH]
        pack[0:SH, :] = turned
        pack[0:SH, 0:SE] = env["excite"][...].astype(F32)
        sall[z, x, y, core, :, 0:LANES] = pack[0:SH, :].astype(BF16)
        pack[0:SH, 0:SE] = env["squeeze"][...].astype(F32)
        sall[z, x, y, core, :, LANES : 2 * LANES] = pack[0:SH, :].astype(BF16)
        for l in range(LAYERS):
            wall[l, z, x, y, core] = env["point"][l]
        wall[LAYERS, z, x, y, core] = env["resid"][...]
    else:
        def weights(m):
            return env["mats"][m]

        small[...] = env["small_in"][...]

    def squeeze_all():
        if fast:
            return sall[...].reshape(C, 2 * LANES)[:, LANES : LANES + SE].astype(F32)
        return env["squeeze"][...].astype(F32)

    class Scatter:
        def __init__(self, name):
            self.send, self.core, self.xsum, self.rx, self.zsum, self.rz, self.ss, self.rs = (
                env[name + part] for part in ("_send", "_core", "_xsum", "_rx", "_zsum", "_rz", "_ss", "_rs")
            )
            self.dtype = self.send.dtype

        def go(self, m, stage):
            ss, rs = self.ss.at[m, stage], self.rs.at[m, stage]
            if stage == 0:
                remote(self.send.at[m, :, :, :, 1 - core], self.core.at[m], ss, rs, (dp, partner)).start()
            elif stage == 1:
                remote(self.xsum.at[m, 1 - x], self.rx.at[m], ss, rs, across).start()
            else:
                for i, offset in enumerate(plane_peers()):
                    pz, py, peer = plane_peer(offset)
                    remote(self.zsum.at[m, pz, py], self.rz.at[m, i], ss, rs, peer).start()

        def wait(self, m, stage, sems):
            total_wait((self.core.at[m], self.rx.at[m], self.rz.at[m])[stage], sems.at[m, stage])

        def left(self, m):
            for stage in range(3):
                self.wait(m, stage, self.ss)

        def core_to_x(self, m):
            self.wait(m, 0, self.rs)

            def body(i, _):
                v = self.send[m, i, :, :, core].astype(F32) + self.core[m, i].astype(F32)
                for k in range(2):
                    self.xsum[m, k, i] = v[k].astype(self.dtype)
                return 0

            lax.fori_loop(0, Z, body, 0)
            self.go(m, 1)

        def x_to_plane(self, m):
            self.x_sum(m)
            self.go(m, 2)

        def x_sum(self, m):
            self.wait(m, 1, self.rs)

            def body(i, _):
                v = self.xsum[m, x, i].astype(F32) + self.rx[m, i].astype(F32)
                self.zsum[m, i] = v.astype(self.dtype)
                return 0

            lax.fori_loop(0, Z, body, 0)

        def result(self, m):
            self.wait(m, 2, self.rs)
            v = self.zsum[m, z, y].astype(F32)
            for i in range(Z * Y - 1):
                v = v + self.rz[m, i].astype(F32)
            return v

    if fast:
        big, little = Scatter("big"), Scatter("little")

    def to_perm_long(src, dst, base):
        for u in range(4):
            o = base(u)
            dst[o : o + UR, :] = dot(perm_l[u * UR : (u + 1) * UR, :], src).astype(BF16)

    def to_perm_short(src, dst, base, masked):
        for k in range(U - 1):
            v = dot(perm_s[...], src[k])
            if masked:
                v = v * wide(mask[k * UR : (k + 1) * UR, :])
            o = base(4 + k)
            dst[o : o + UR, :] = v.astype(BF16)

    y0 = ypad.at[0]
    zero_ends()
    pl.semaphore_wait(barrier, len(chips) + len(others))
    if fast:
        gather_stage(sall, MATS, 0)
        for buf, m in halves:
            gather_stage(buf, m, 0)
    load_x.wait()
    edge[0] = xv[long_at, 0:16, :]
    edge[1] = xv[long_at, F - 16 : F, :]
    stage_short()
    edge_sems = (sem_xs.at[pl.ds(12, 2)], sem_xr.at[pl.ds(3, 2)])
    edges(edge, halo_l.at[0], halo_r.at[0], *edge_sems, True)
    send_short(xin, 0)
    if fast:
        for m in range(1, min(3, MATS)):
            gather_stage(wall.at[m], m, 0)
    one_hot(perm_l, F, False)
    one_hot(perm_s, UR, False)
    to_perm_long(xv[long_at], y0, lambda u: win(u) + 32)
    load_g = pltpu.make_async_copy(g_any, xv, sem_loc.at[0])
    load_g.start()
    make_masks()
    if fast:
        gather_got(sall, MATS, 0)
        gather_stage(sall, MATS, 1)
        for buf, m in halves:
            gather_got(buf, m, 0)
            gather_stage(buf, m, 1)
        gather_got(sall, MATS, 1)
        gather_stage(sall, MATS, 2)
        for buf, m in halves:
            gather_got(buf, m, 1)
            gather_stage(buf, m, 2)
        gather_got(sall, MATS, 2)
        for j in range(NL):
            part = sall[...].reshape(C, 2 * LANES)[j * LANES : (j + 1) * LANES, 0:LANES].astype(F32)
            small[:, j * LANES : (j + 1) * LANES] = part.T

    def fill_pads(ref, row0, n, j, b0, b1, b2, b3, halo, seg):
        e = lax.broadcasted_iota(jnp.int32, (16, LANES), 0)

        def put(at, v):
            ref[pl.ds(row0 + at * 16, 16), lane(j)] = v.astype(BF16)

        put(0, jnp.where(e == 0, halo[2 * seg : 2 * seg + 1], pltpu.roll(b2, 1, 0)))
        put(1, jnp.where(e == 0, halo[2 * seg + 1 : 2 * seg + 2], pltpu.roll(b3, 1, 0)))
        put(n + 2, jnp.where(e == 15, halo[8 + 2 * seg : 9 + 2 * seg], pltpu.roll(b0, 15, 0)))
        put(n + 3, jnp.where(e == 15, halo[9 + 2 * seg : 10 + 2 * seg], pltpu.roll(b1, 15, 0)))

    def pads_from(ref, j, halo, segs):
        for seg in segs:
            u0, u1 = (0, 3) if seg == 0 else (3 + seg, 3 + seg)
            n = F // 16 if seg == 0 else NB
            o0, o1 = win(u0) + 32, win(u1) + 32 + UR
            blk = [ref[o : o + 16, lane(j)].astype(F32) for o in (o0, o0 + 16, o1 - 32, o1 - 16)]
            fill_pads(ref, win(u0), n, j, *blk, halo, seg)

    def first_pads(segs):
        def body(j, _):
            none = jnp.zeros((2, LANES), F32)
            left = [halo_l[s, :, lane(j)].astype(F32)[14:16] if s in segs else none for s in range(4)]
            right = [halo_r[s, :, lane(j)].astype(F32)[0:2] if s in segs else none for s in range(4)]
            halo = jnp.where(hmask[...] > 0.0, jnp.concatenate(left + right, axis=0), 0.0)
            pads_from(y0, j, halo, segs)
            return 0

        each_lane(body)

    edges(edge, halo_l.at[0], halo_r.at[0], *edge_sems, False)
    first_pads([0])

    def shorts_arrive():
        if fast:
            gather_got(wall.at[1], 1, 0)
            gather_stage(wall.at[1], 1, 1)
        recv_short(xin)
        to_perm_short(xin, y0, lambda u: win(u) + 32, True)
        send_short(xin, 1)
        first_pads(range(1, U))

    def sync_core(s):
        d = remote(send_a.at[s], recv_core.at[s], sem_cs.at[s], sem_cr.at[s], (dp, partner))
        d.start()
        d.wait()
        send_b[s] = send_a[s] + recv_core[s]

    def sync_send(s):
        recv_chip[s, my_chip] = send_b[s]
        dst = recv_chip.at[s, my_chip]

        for a in reversed(range(DP)):
            for b in reversed(range(Y)):
                if a or b:
                    there = (other(dp, a, DP), 2 * other(y, b, Y) + core)
                    remote(send_b.at[s], dst, sem_ks.at[s], sem_kr.at[s], there).start()

    def sync_done(s):
        others = recv_chip.at[s, 0 : n_chips - 1]
        total_wait(others, sem_kr.at[s])
        total_wait(others, sem_ks.at[s])
        total = recv_chip[s, 0]
        for i in range(1, n_chips):
            total = total + recv_chip[s, i]
        return total

    def tap_rows(l, j):
        group = small[pl.ds(pl.multiple_of(AT_TAPS + 8 * l, 8), 8), lane(j)]
        return [group[k : k + 1] for k in range(KERNEL)]

    LONG, SHORT = range(4), range(4, NU)

    def conv_pass(l, units):
        def body(j, _):
            w = tap_rows(l, j)
            for u in units:
                o = win(u)
                v = ypad[l, o : o + UR + 64, lane(j)].astype(F32)
                t = v[0:UR] * w[0]
                for k in range(1, KERNEL):
                    t = t + v[16 * k : 16 * k + UR] * w[k]
                if u >= 4:
                    t = t * mask[(u - 4) * UR : (u - 3) * UR, :]
                dlow[l, u * UR : (u + 1) * UR, lane(j)] = t.astype(BF16)
            return 0

        each_lane(body)

    def fold8(v):
        return jnp.sum(v.reshape(v.shape[0] // 8, 8, v.shape[1]), axis=0)

    def put_edges(src, l):
        for seg in range(4):
            base = 0 if seg == 0 else F + (seg - 1) * UR
            n = F if seg == 0 else UR
            for e in range(2):
                hsend[l, 1, 2 * seg + e : 2 * seg + e + 1, :] = src(base + n - 32 + 16 * e + 15)
                hsend[l, 0, 2 * seg + e : 2 * seg + e + 1, :] = src(base + 16 * e)

    def matmul_pass(l, units):
        r = slice(units[0] * UR, (units[-1] + 1) * UR)
        h = dot(dlow[l, r, :], weights(l))
        pre[l, r, :] = h
        s0, s1 = fold8(h), fold8(h * h)
        if units[0] > 0:
            s0, s1 = s0 + sums[0], s1 + sums[1]
        sums[0] = s0
        sums[1] = s1

    def send_stats(l):
        send_a[l, 0:1, :] = jnp.sum(sums[0], axis=0, keepdims=True)
        send_a[l, 1:2, :] = jnp.sum(sums[1], axis=0, keepdims=True)
        put_edges(lambda row: pre[l, row : row + 1, :], l)

    def act_pass(l):
        def body(j, _):
            a, b = coef[l, 0:1, lane(j)], coef[l, 1:2, lane(j)]
            for u in range(NU):
                v = pre[l, u * UR : (u + 1) * UR, lane(j)] * a + b
                v = v + v * jnp.tanh(v)
                if u >= 4:
                    v = v * mask[(u - 4) * UR : (u - 3) * UR, :]
                o = win(u) + 32
                ypad[l + 1, o : o + UR, lane(j)] = v.astype(BF16)
            v = hh[l, :, lane(j)] * a + b
            v = (v + v * jnp.tanh(v)) * hmask[...]
            pads_from(ypad.at[l + 1], j, v, range(U))
            return 0

        each_lane(body)

    def prep_pass(l):
        def body(j, _):
            a, b, m, i = (coef[l, r : r + 1, lane(j)] for r in range(4))
            for u in range(NU):
                rs = slice(u * UR, (u + 1) * UR)
                h = pre[l, rs, lane(j)]
                half = h * a + b
                t = jnp.tanh(half)
                v = (0.5 + 0.5 * t) * (1.0 + half * (1.0 - t))
                if u >= 4:
                    v = v * mask[(u - 4) * UR : (u - 3) * UR, :]
                slope[l, rs, lane(j)] = v.astype(BF16)
                pre[l, rs, lane(j)] = (h - m) * i
            hx[l, :, lane(j)] = (hh[l, :, lane(j)] - m) * i
            return 0

        each_lane(body)

    def layer(l, _):
        pl.when(l == 0)(shorts_arrive)
        conv_pass(l, LONG)
        if fast:
            gather_got(wall.at[l], l, 2)
        matmul_pass(l, LONG)
        conv_pass(l, SHORT)
        matmul_pass(l, SHORT)
        send_stats(l)
        edges(hsend.at[l], hh.at[l, 0:8], hh.at[l, 8:16], sem_hs.at[l], sem_hr.at[l], True)
        sync_core(l)
        sync_send(l)

        if fast:
            gather_got(wall.at[l + 1], l + 1, 1)
            gather_stage(wall.at[l + 1], l + 1, 2)

        pl.when(l > 0)(lambda: prep_pass(l - 1))

        @pl.when(l == 0)
        def _():
            load_g.wait()
            stage_short()
            to_perm_long(xv[long_at], cot, lambda u: u * UR)

        @pl.when(l == 1)
        def _():
            one_hot(back_l, F, True)
            one_hot(back_s, UR, True)

        @pl.when(l == LAYERS - 1)
        def _():
            for k in range(U - 1):
                cot_piece(k, 1)

            @pl.when(tm > 0)
            def _():
                for k in range(U - 1):
                    total_wait(gin4.at[k], sem_cr.at[S2 + k])

            to_perm_short(gin4, cot, lambda u: u * UR, True)

        total = sync_done(l)
        edges(hsend.at[l], hh.at[l, 0:8], hh.at[l, 8:16], sem_hs.at[l], sem_hr.at[l], False)
        if fast:
            @pl.when(l + 2 < MATS)
            def _():
                gather_got(wall.at[l + 2], l + 2, 0)
                gather_stage(wall.at[l + 2], l + 2, 1)

            @pl.when(l + 3 < MATS)
            def _():
                gather_stage(wall.at[l + 3], l + 3, 0)

        for k in range(U - 1):
            pl.when(l == k)(functools.partial(cot_piece, k, 0))
        scale = wide(inv_count)
        mean = total[0:1] * scale
        var = total[1:2] * scale - mean * mean
        inv = lax.rsqrt(var + NORM_EPSILON)
        ga = small[pl.ds(AT_GAMMA + l, 1), :]
        a = ga * inv
        coef[l, 0:1, :] = 0.5 * a
        coef[l, 1:2, :] = 0.5 * (small[pl.ds(AT_BETA + l, 1), :] - mean * a)
        coef[l, 2:3, :] = mean
        coef[l, 3:4, :] = inv
        coef[l, 4:5, :] = a

        pl.when(l < LAYERS - 1)(lambda: act_pass(l))
        return 0

    lax.fori_loop(0, LAYERS, layer, 0)

    top = LAYERS - 1
    pool[...] = jnp.zeros(pool.shape, F32)

    def last_act(j, _):
        a, b = coef[top, 0:1, lane(j)], coef[top, 1:2, lane(j)]
        acc = None
        for u in range(NU):
            v = pre[top, u * UR : (u + 1) * UR, lane(j)] * a + b
            v = v + v * jnp.tanh(v)
            if u >= 4:
                v = v * mask[(u - 4) * UR : (u - 3) * UR, :]
            act[u * UR : (u + 1) * UR, lane(j)] = v
            f = fold8(v)
            acc = f if u == 0 or u >= 4 else acc + f
            if u >= 3:
                pool[u - 3 : u - 2, lane(j)] = jnp.sum(acc, axis=0, keepdims=True)
        return 0

    each_lane(last_act)

    def time_sum(s, value):
        tsend[s] = value
        ds = [remote(tsend.at[s], trecv.at[s, i - 1], sem_ts.at[s], sem_tr.at[s], (dp, lax.rem(tm + i, TM))) for i in range(1, TM)]
        for d in ds:
            d.start()

    def time_done(s):
        whole = trecv.at[s]
        total_wait(whole, sem_tr.at[s])
        total_wait(whole, sem_ts.at[s])
        total = tsend[s]
        for i in range(TM - 1):
            total = total + trecv[s, i]
        return total

    e8 = lax.broadcasted_iota(jnp.int32, (8, LANES), 0)
    len8 = jnp.full((8, LANES), F * TM, jnp.int32)
    for k in range(U - 1):
        len8 = jnp.where(e8 == k + 1, short_len[k], len8)
    inv_len = 1.0 / len8.astype(F32)
    live = jnp.where(e8 < U, 1.0, 0.0)
    time_sum(0, pool[...])
    prep_pass(top)
    if fast:
        gather_got(wall.at[LAYERS], LAYERS, 2)
    resd[0:F, :] = dot(ypad[0, 32 : 32 + F, :], weights(LAYERS))
    for u in SHORT:
        resd[u * UR : (u + 1) * UR, :] = dot(ypad[0, win(u) + 32 : win(u) + 32 + UR, :], weights(LAYERS))
    p = time_done(0) * wide(inv_len)
    sq = squeeze_all()
    ex = small[0:SE, :]
    q = dot(p, sq, precision=HIGHEST)
    sig_q = logistic(q)
    z_act = q * sig_q
    gate[...] = logistic(dot(z_act, ex, precision=HIGHEST))
    pool[...] = jnp.zeros(pool.shape, F32)

    def top_pass(j, _):
        acc = None
        for u in range(NU):
            rs = slice(u * UR, (u + 1) * UR)
            seg = seg_of(u)
            av = act[rs, lane(j)]
            half = 0.5 * (av * gate[seg : seg + 1, lane(j)] + resd[rs, lane(j)])
            t = jnp.tanh(half)
            out = half + half * t
            slope = (0.5 + 0.5 * t) * (1.0 + half * (1.0 - t))
            dv = cot[rs, lane(j)].astype(F32) * slope
            if u >= 4:
                out = out * mask[(u - 4) * UR : (u - 3) * UR, :]
            outp[rs, lane(j)] = out.astype(BF16)
            du[rs, lane(j)] = dv
            drl[rs, lane(j)] = dv.astype(BF16)
            f = fold8(dv * av)
            acc = f if u == 0 or u >= 4 else acc + f
            if u >= 3:
                pool[u - 3 : u - 2, lane(j)] = jnp.sum(acc, axis=0, keepdims=True)
        return 0

    each_lane(top_pass)
    time_sum(1, pool[...])

    def back_long(buf, src):
        for u in range(4):
            buf[0, u * UR : (u + 1) * UR, :] = dot(back_l[u * UR : (u + 1) * UR, :], src[0:F, :]).astype(BF16)

    def back_short(buf, stage, src):
        for k in range(U - 1):
            stage[k] = dot(back_s[...], src[F + k * UR : F + (k + 1) * UR, :]).astype(BF16)

        @pl.when(tm >= N_SRC)
        def _():
            for k in range(U - 1):
                buf[1 + k] = jnp.zeros((F, C), BF16)

        @pl.when(first)
        def _():
            for k in range(U - 1):
                buf[1 + k, 0:UR, :] = stage[k]

    def back_piece(buf, stage, sems, rsems, k):
        owner, q = tm // 4, lax.rem(tm, 4)
        dst = buf.at[1 + k, pl.ds(pl.multiple_of(q * UR, UR), UR), :]
        return remote(stage.at[k], dst, sems.at[k], rsems.at[k, q], (dp, owner))

    def back_send(buf, stage, sems, rsems, ks):
        @pl.when(tm > 0)
        def _():
            for k in ks:
                back_piece(buf, stage, sems, rsems, k).start()

    def back_left(buf, stage, sems, rsems):
        @pl.when(tm > 0)
        def _():
            for k in range(U - 1):
                back_piece(buf, stage, sems, rsems, k).wait_send()

    def back_arrived(buf, rsems, k):
        @pl.when(tm < N_SRC)
        def _():
            for i in range(4):
                got = functools.partial(total_wait, buf.at[1 + k, i * UR : (i + 1) * UR, :], rsems.at[k, i])
                if i == 0:
                    pl.when(tm > 0)(got)
                else:
                    got()

    def back_done(buf, stage, sems, rsems):
        back_left(buf, stage, sems, rsems)
        for k in range(U - 1):
            back_arrived(buf, rsems, k)

    put_out = pltpu.make_async_copy(obuf, out_any, sem_loc.at[2])
    back_long(obuf, outp)
    back_short(obuf, xin, outp)

    def xrows(u):
        o = win(u) + 32
        return ypad[0, o : o + UR, :]

    def put_grad(m, total):
        if fast:
            big.send[m] = total.astype(BF16).reshape(Z, 2, Y, 2, SH, C)
            big.go(m, 0)
        else:
            gp[...] = total
            pltpu.make_async_copy(gp, env["gmats"].at[m], sem_loc.at[1]).start()

    def grad_gone():
        if not fast:
            pltpu.make_async_copy(gp, env["gmats"].at[0], sem_loc.at[1]).wait()

    def xrows(u):
        o = win(u) + 32
        return ypad[0, o : o + UR, :]

    def resid_grads():
        total = dot(ypad[0, 32 : 32 + F, :], drl[0:F, :], ((0,), (0,)))
        for u in SHORT:
            total = total + dot(xrows(u), drl[u * UR : (u + 1) * UR, :], ((0,), (0,)))
        put_grad(LAYERS, total)
        gres_in[...] = dot(drl[...], weights(LAYERS), ((1,), (1,)))

    resid_grads()
    dg = time_done(1)
    gv = gate[...]
    de = dg * gv * (1.0 - gv) * wide(live)
    dz = dot(de, ex, ((1,), (1,)), precision=HIGHEST)
    dq = dz * sig_q * (1.0 + q * (1.0 - sig_q))
    cvec[...] = dot(dq, sq, ((1,), (1,)), precision=HIGHEST) * wide(inv_len)
    fac[0], fac[1] = p, de
    facs[0], facs[1] = z_act, dq

    def pair_grads():
        lead = jnp.where(first, 1.0, 0.0)
        zero = jnp.zeros((C, LANES - 2 * SE), F32)
        pair = [dot(fac[1 - i], facs[i], ((0,), (0,)), precision=HIGHEST) for i in range(2)]
        pair = jnp.concatenate(pair + [zero] * (LANES > 2 * SE), axis=1) * lead
        if fast:
            little.send[0] = pair.reshape(Z, 2, Y, 2, SH, LANES)
            little.go(0, 0)
        else:
            env["gpair"][...] = pair

    def back_sums(l, s, grad_of):
        def body(j, _):
            acc0 = acc1 = None
            make = grad_of(j)
            for u in range(NU):
                rs = slice(u * UR, (u + 1) * UR)
                v = make(u) * slope[l, rs, lane(j)].astype(F32)
                xc = pre[l, rs, lane(j)]
                dn[u * UR : (u + 1) * UR, lane(j)] = v
                f0, f1 = fold8(v), fold8(v * xc)
                acc0 = f0 if u == 0 else acc0 + f0
                acc1 = f1 if u == 0 else acc1 + f1
            send_a[s, 0:1, lane(j)] = jnp.sum(acc0, axis=0, keepdims=True)
            send_a[s, 1:2, lane(j)] = jnp.sum(acc1, axis=0, keepdims=True)
            return 0

        each_lane(body)
        put_edges(lambda row: dn[row : row + 1, :], s)

    def top_grad(j):
        def make(u):
            seg = seg_of(u)
            return du[u * UR : (u + 1) * UR, lane(j)] * gate[seg : seg + 1, lane(j)] + cvec[seg : seg + 1, lane(j)]
        return make

    def conv_grad(l):
        def outer(j):
            w = tap_rows(l, j)

            def make(u):
                o = win(u)
                v = ddpad[o : o + UR + 64, lane(j)].astype(F32)
                t = v[64 : 64 + UR] * w[0]
                for k in range(1, KERNEL):
                    t = t + v[64 - 16 * k : 64 - 16 * k + UR] * w[k]
                return t
            return make
        return outer

    back_sums(top, LAYERS, top_grad)

    def point_grad(l):
        grad_gone()
        put_grad(l, dot(dlow[l], dhl[0:R, :], ((0,), (0,))))

    def depth_grad(l):
        def body(j, _):
            acc = [None] * KERNEL
            for u in range(NU):
                o = win(u)
                v = ypad[l, o : o + UR + 64, lane(j)].astype(F32)
                g = ddpad[o + 32 : o + 32 + UR, lane(j)].astype(F32)
                for k in range(KERNEL):
                    f = fold8(v[16 * k : 16 * k + UR] * g)
                    acc[k] = f if u == 0 else acc[k] + f
            rows = [jnp.sum(acc[k], axis=0, keepdims=True) for k in range(KERNEL)]
            rows.append(jnp.zeros((8 - KERNEL, LANES), F32))
            at = pl.ds(pl.multiple_of(AT_TAPS + 8 * l, 8), 8)
            gsmall[at, lane(j)] = jnp.concatenate(rows, axis=0)
            return 0

        each_lane(body)
    def dh_pass(l, units):
        def body(j, _):
            a, k1, k0 = (coef[l, r : r + 1, lane(j)] for r in (4, 5, 6))
            for u in units:
                rs = slice(u * UR, (u + 1) * UR)
                v = dn[rs, lane(j)] * a - (pre[l, rs, lane(j)] * k1 + k0)
                if u >= 4:
                    v = v * mask[(u - 4) * UR : (u - 3) * UR, :]
                dhl[rs, lane(j)] = v.astype(BF16)
            if units is SHORT:
                v = (dhh[l, :, lane(j)] * a - (hx[l, :, lane(j)] * k1 + k0)) * hmask[...]
                dhl[R : R + 16, lane(j)] = v.astype(BF16)
            return 0

        each_lane(body)

    def dd_pass(l):
        dh_pass(l, LONG)
        ddpad[32 : 32 + F, :] = dot(dhl[0:F, :], weights(l), ((1,), (1,))).astype(BF16)
        dh_pass(l, SHORT)
        v = dot(dhl[F : R + 16, :], weights(l), ((1,), (1,)))
        for u in SHORT:
            ddpad[win(u) + 32 : win(u) + 32 + UR, :] = v[(u - 4) * UR : (u - 3) * UR].astype(BF16)
        hx[l] = v[R - F : R - F + 16].astype(BF16).astype(F32)

        def pad(j, _):
            pads_from(ddpad, j, hx[l, :, lane(j)], range(U))
            return 0

        each_lane(pad)

    def back_layer(step, _):
        l = top - step
        s = LAYERS + step
        edges(hsend.at[s], dhh.at[l, 0:8], dhh.at[l, 8:16], sem_hs.at[s], sem_hr.at[s], True)
        sync_core(s)
        sync_send(s)

        @pl.when(step > 0)
        def _():
            point_grad(l + 1)
            depth_grad(l + 1)

        pl.when(step == 0)(pair_grads)

        @pl.when(step == LAYERS - 1)
        def _():
            back_done(obuf, xin, sem_os.at[0], sem_or.at[0])
            put_out.start()

        if fast:
            @pl.when(step == 1)
            def _():
                little.core_to_x(0)

            @pl.when(step == 2)
            def _():
                little.x_to_plane(0)

            @pl.when(step > 0)
            def _():
                big.x_sum(l + 2)

            @pl.when(step > 1)
            def _():
                env["gmats"][l + 3] = big.result(l + 3)

            big.core_to_x(l + 1)

        total = sync_done(s)
        if fast:
            pl.when(step > 0)(lambda: big.go(l + 2, 2))

        @pl.when(step < U - 1)
        def _():
            back_send(obuf, xin, sem_os.at[0], sem_or.at[0], [step])

        edges(hsend.at[s], dhh.at[l, 0:8], dhh.at[l, 8:16], sem_hs.at[s], sem_hr.at[s], False)
        ggb[l, 0:2, :] = total
        a = coef[l, 4:5, :]
        coef[l, 5:6, :] = a * total[1:2] * wide(inv_count)
        coef[l, 6:7, :] = a * total[0:1] * wide(inv_count)

        dd_pass(l)

        @pl.when(l > 0)
        def _():
            back_sums(l - 1, s + 1, conv_grad(l - 1))
        return 0

    def run_back():
        lax.fori_loop(0, LAYERS, back_layer, 0)

    conv_grad_of = conv_grad

    def conv_grad(l):
        return conv_grad_of(l + 1)

    gsmall[...] = jnp.zeros(gsmall.shape, F32)
    run_back()
    lead_all = jnp.where(first & (dp == 0), 1.0, 0.0)
    for l in range(LAYERS):
        gsmall[AT_BETA + l : AT_BETA + l + 1, :] = ggb[l, 0:1, :] * lead_all
        gsmall[AT_GAMMA + l : AT_GAMMA + l + 1, :] = ggb[l, 1:2, :] * lead_all
    def final_pass(units):
        def body(j, _):
            make = conv_grad_of(0)(j)
            for u in units:
                rs = slice(u * UR, (u + 1) * UR)
                v = make(u)
                if u >= 4:
                    v = v * mask[(u - 4) * UR : (u - 3) * UR, :]
                outp[rs, lane(j)] = (v + gres_in[rs, lane(j)]).astype(BF16)
            return 0

        each_lane(body)

    point_grad(0)
    final_pass(SHORT)
    back_short(gbuf, gin4, outp)
    back_send(gbuf, gin4, sem_os.at[1], sem_or.at[1], range(U - 1))
    if fast:
        big.core_to_x(0)
    depth_grad(0)
    if fast:
        for j in range(NL):
            rows = gsmall[:, j * LANES : (j + 1) * LANES].T
            part = rows.reshape(LANES // (2 * SH), 2, SH, LANES)
            per = LANES // (2 * SH)
            for i in range(per):
                n = j * per + i
                little.send[1, n // (2 * Y), n // Y % 2, n % Y] = part[i]
        little.go(1, 0)
        big.x_to_plane(1)
    final_pass(LONG)
    back_long(gbuf, outp)
    put_gin = [pltpu.make_async_copy(gbuf.at[k], gin_any.at[k], sem_loc.at[3 + k]) for k in range(U)]
    put_gin[0].start()
    if fast:
        little.core_to_x(1)
        env["gmats"][2] = big.result(2)
        big.x_to_plane(0)
        little.x_to_plane(1)
        env["gpair"][...] = little.result(0)
        env["gmats"][1] = big.result(1)
        for m in range(1, MATS):
            big.left(m)
            gather_left(wall.at[m], m)
        for buf, m in halves:
            gather_left(buf, m)
        little.left(0)
        gather_left(sall, MATS)
    else:
        env["grows"][...] = gsmall[...]
    for k in range(U - 1):
        back_arrived(gbuf, sem_or.at[1], k)
        put_gin[1 + k].start()
    back_left(gbuf, gin4, sem_os.at[1], sem_or.at[1])
    if fast:
        env["gmats"][0] = big.result(0)
        env["grows"][...] = little.result(1)
        big.left(0)
        little.left(1)
    grad_gone()
    put_out.wait()
    for c in put_gin:
        c.wait()


def finish_kernel(cfg, lengths, out_s, gin_s, gmats_any, gpair_any, grows_any, *rest):
    DP, TM, U, F, C, SE, SH, LAYERS, KERNEL, fast = cfg
    out, gin, gdepth, gpoint, ggamma, gbeta, gsq, gex, gres, hold, gmats, gpair, grows, turn, sems, sems_g = rest
    dp = lax.axis_index("dp")
    long_at = jnp.int32(0)
    for b in range(1, U):
        long_at = jnp.where(lengths[dp * U + b] == F * TM, jnp.int32(b), long_at)
    copies = []
    loads = [
        pltpu.make_async_copy(src, dst, sems_g.at[i])
        for i, (src, dst) in enumerate(((gmats_any, gmats), (gpair_any, gpair), (grows_any, grows)))
    ]
    for c in loads:
        c.start()
    for b in range(U):
        slot = jnp.where(b == long_at, 0, jnp.where(b < long_at, b + 1, b))
        for i, (src, dst) in enumerate(((out_s, out), (gin_s, gin))):
            get = pltpu.make_async_copy(src.at[slot], hold.at[i, b], sems.at[0, i, b])
            put = pltpu.make_async_copy(hold.at[i, b], dst.at[b], sems.at[1, i, b])
            copies.append((get, put))
            get.start()
    for get, put in copies:
        get.wait()
        put.start()
    for c in loads:
        c.wait()
    at_taps = SE
    at_gamma = SE + 8 * LAYERS
    at_beta = at_gamma + 8
    gpoint[...] = gmats[0:LAYERS]
    gres[...] = gmats[LAYERS]
    gsq[...] = gpair[:, SE : 2 * SE]
    gex[...] = gpair[:, 0:SE]
    turn[...] = jnp.zeros(turn.shape, F32)
    turn[0:SH] = grows[...]
    turn[...] = turn[...].T
    for l in range(LAYERS):
        gdepth[l] = turn[at_taps + 8 * l : at_taps + 8 * l + KERNEL, 0:SH]
    ggamma[...] = turn[at_gamma : at_gamma + LAYERS, 0:SH]
    gbeta[...] = turn[at_beta : at_beta + LAYERS, 0:SH]
    for _, put in copies:
        put.wait()


def local(sizes, inputs, lengths, depth_w, point_w, gamma, beta, squeeze_w, excite_w, resid_w, cotangent):
    DP, TM = sizes
    U, F, C = inputs.shape
    LAYERS, KERNEL, SH = depth_w.shape
    SE = squeeze_w.shape[1]
    UR = F // 4
    NU = 4 + U - 1
    R = NU * UR
    RP = F + 64 + (U - 1) * (UR + 64)
    S = 2 * LAYERS
    chips = DP * (TM // 2) - 1
    axes = ("dp", "tm")
    fast = SH % 16 == 0 and DP % 2 == 0 and DP > 2
    Z, Y = DP // 2, TM // 2
    MATS = LAYERS + 1
    vm = pltpu.VMEM
    dma = pltpu.SemaphoreType.DMA
    any_spec = pl.BlockSpec(memory_space=pl.ANY)
    vm_spec = pl.BlockSpec(memory_space=pltpu.VMEM)
    sm_spec = pl.BlockSpec(memory_space=pltpu.SMEM)
    sd = jax.ShapeDtypeStruct
    cfg = (DP, TM, U, F, C, SE, SH, LAYERS, KERNEL, fast)
    at_gamma = SE + 8 * LAYERS
    operands = dict(lengths=lengths, x_any=inputs, g_any=cotangent)
    specs = [sm_spec, any_spec, any_spec]
    outs = dict(out_any=sd((U, F, C), BF16), gin_any=sd((U, F, C), BF16))
    out_specs = [any_spec, any_spec]
    if fast:
        operands.update(
            point=point_w, taps=depth_w, gamma=gamma, beta=beta, squeeze=squeeze_w, excite=excite_w.T, resid=resid_w
        )
        specs += [vm_spec] * 7
        outs.update(gmats=sd((MATS, SH, C), F32), gpair=sd((SH, LANES), F32), grows=sd((SH, LANES), F32))
        out_specs += [vm_spec] * 3
    else:
        mats = jnp.concatenate([point_w, resid_w[None]], axis=0)
        depth_rows = jnp.pad(depth_w, ((0, 0), (0, 8 - KERNEL), (0, 0))).reshape(8 * LAYERS, SH)
        fill = ((0, 8 - LAYERS), (0, 0))
        rows = jnp.concatenate([excite_w, depth_rows, jnp.pad(gamma, fill), jnp.pad(beta, fill)], axis=0)
        rows = jnp.pad(rows, ((0, LANES - rows.shape[0]), (0, 0)))
        operands.update(
            mats=lax.all_gather(mats, axes, axis=1, tiled=True),
            small_in=lax.all_gather(rows, axes, axis=1, tiled=True).astype(F32),
            squeeze=lax.all_gather(squeeze_w, axes, axis=0, tiled=True),
        )
        specs += [vm_spec] * 3
        outs.update(gmats=sd((MATS, C, C), F32), gpair=sd((C, LANES), F32), grows=sd((LANES, C), F32))
        out_specs += [any_spec, vm_spec, vm_spec]
    scratch = dict(
        xv=vm((U, F, C), BF16), xs=vm((U - 1, F, C), BF16), edge=vm((2, 16, C), BF16),
        xin=vm((U - 1, UR, C), BF16), gin4=vm((U - 1, UR, C), BF16),
        halo_l=vm((4, 16, C), BF16), halo_r=vm((4, 16, C), BF16),
        cot=vm((R, C), BF16), ypad=vm((LAYERS, RP, C), BF16), dlow=vm((LAYERS, R, C), BF16),
        pre=vm((LAYERS, R, C), F32), hh=vm((LAYERS, 16, C), F32), hx=vm((LAYERS, 16, C), F32),
        mask=vm(((U - 1) * UR, LANES), F32), hmask=vm((16, LANES), F32), coef=vm((LAYERS, 8, C), F32),
        resd=vm((R, C), F32), act=vm((R, C), F32), du=vm((R, C), F32), drl=vm((R, C), BF16),
        dhl=vm((R + 16, C), BF16), ddpad=vm((RP, C), BF16),
        perm_l=vm((F, F), BF16), perm_s=vm((UR, UR), BF16), back_l=vm((F, F), BF16), back_s=vm((UR, UR), BF16),
        outp=vm((R, C), BF16), obuf=vm((U, F, C), BF16), gbuf=vm((U, F, C), BF16),
        small=vm((LANES, C), F32), slope=vm((LAYERS, R, C), BF16),
        fac=vm((2, 8, C), F32), facs=vm((2, 8, SE), F32), gsmall=vm((LANES, C), F32), ggb=vm((LAYERS, 8, C), F32),
        sums=vm((2, 8, C), F32), send_a=vm((S, 2, C), F32), send_b=vm((S, 2, C), F32),
        recv_core=vm((S, 2, C), F32), recv_chip=vm((S, chips + 1, 2, C), F32),
        hsend=vm((S, 2, 8, C), F32), dhh=vm((LAYERS, 16, C), F32),
        tsend=vm((2, 8, C), F32), trecv=vm((2, TM - 1, 8, C), F32),
        pool=vm((8, C), F32), gate=vm((8, C), F32), cvec=vm((8, C), F32),
        sem_loc=dma((3 + U,)), sem_cs=dma((S,)), sem_cr=dma((S + U - 1,)), sem_cot=dma((U - 1, 4)), sem_ks=dma((S,)), sem_kr=dma((S,)),
        sem_hs=dma((S, 2)), sem_hr=dma((S, 2)), sem_ts=dma((2,)), sem_tr=dma((2,)),
        sem_xs=dma((14,)), sem_xr=dma((5,)), sem_os=dma((2, U - 1)), sem_or=dma((2, U - 1, 4)),
    )
    if fast:
        scratch.update(
            wall=vm((MATS, Z, 2, Y, 2, SH, C), BF16), sall=vm((Z, 2, Y, 2, SH, 2 * LANES), BF16),
            pack=vm((LANES, LANES), F32), sem_gs=dma((MATS + 1, 3)), sem_gr=dma((MATS + 1, 3)),
        )
        for name, n, cols, kind in (("big", MATS, C, BF16), ("little", 2, LANES, F32)):
            scratch.update(
                {
                    name + "_send": vm((n, Z, 2, Y, 2, SH, cols), kind),
                    name + "_core": vm((n, Z, 2, Y, SH, cols), kind),
                    name + "_xsum": vm((n, 2, Z, Y, SH, cols), kind),
                    name + "_rx": vm((n, Z, Y, SH, cols), kind),
                    name + "_zsum": vm((n, Z, Y, SH, cols), kind),
                    name + "_rz": vm((n, Z * Y - 1, SH, cols), kind),
                    name + "_ss": dma((n, 3)),
                    name + "_rs": dma((n, 3)),
                }
            )
    if not fast:
        scratch.update(gp=vm((C, C), F32))
    names = list(operands) + list(outs) + list(scratch)
    out_s, gin_s, gmats, gpair, grows = pl.pallas_call(
        functools.partial(block_kernel, cfg, names),
        out_shape=tuple(outs.values()),
        in_specs=specs,
        out_specs=tuple(out_specs),
        scratch_shapes=list(scratch.values()),
        compiler_params=pltpu.CompilerParams(collective_id=0, has_side_effects=True, vmem_limit_bytes=63 << 20),
    )(*operands.values())
    if not fast:
        gmats = lax.psum_scatter(gmats, axes, scatter_dimension=1, tiled=True)
        gpair = lax.psum_scatter(gpair, axes, scatter_dimension=0, tiled=True)
        grows = lax.psum_scatter(grows, axes, scatter_dimension=1, tiled=True).T
    sizes_out = (
        ((U, F, C), BF16), ((U, F, C), BF16), ((LAYERS, KERNEL, SH), F32), ((LAYERS, SH, C), F32), ((LAYERS, SH), F32),
        ((LAYERS, SH), F32), ((SH, SE), F32), ((SH, SE), F32), ((SH, C), F32),
    )
    done = pl.pallas_call(
        functools.partial(finish_kernel, cfg),
        out_shape=tuple(sd(*size) for size in sizes_out),
        in_specs=[sm_spec] + [any_spec] * 5,
        out_specs=(any_spec,) * 2 + (vm_spec,) * 7,
        scratch_shapes=[
            vm((2, U, F, C), BF16), vm((MATS, SH, C), F32), vm((SH, LANES), F32), vm((SH, LANES), F32),
            vm((LANES, LANES), F32), dma((2, 2, U)), dma((3,)),
        ],
    )(lengths, out_s, gin_s, gmats, gpair, grows)
    return done[:7] + (done[7].T, done[8])


def solution(mesh):
    both = ("dp", "tm")
    rows, cols = P(both, None), P(None, both)
    frames = P("dp", "tm", None)
    taps, mats = P(None, None, both), P(None, both, None)
    sizes = (mesh.shape["dp"], mesh.shape["tm"])
    return jax.shard_map(
        functools.partial(local, sizes),
        mesh=mesh,
        in_specs=(frames, P(), taps, mats, cols, cols, rows, cols, rows, frames),
        out_specs=(frames, frames, taps, mats, cols, cols, rows, cols, rows),
        check_vma=False,
    )
```

```python
import functools

import jax
import jax.numpy as jnp
from jax import lax
from jax.experimental import pallas as pl
from jax.experimental.pallas import tpu as pltpu
from jax.sharding import PartitionSpec as P

MESH = pl.DeviceIdType.MESH
NORM_EPSILON = 1e-05
LANES = 128
HIGHEST = lax.Precision.HIGHEST
F32 = jnp.float32
BF16 = jnp.bfloat16


def dot(a, b, dims=((1,), (0,)), precision=None):
    return lax.dot_general(a, b, (dims, ((), ())), precision=precision, preferred_element_type=F32)


def logistic(v):
    return 0.5 * jnp.tanh(0.5 * v) + 0.5


def dot_parts(v, w, dims=((1,), (0,))):
    rows, parts = v.shape[0], []
    for _ in range(3):
        part = v.astype(BF16)
        parts.append(part.astype(F32))
        v = v - parts[-1]
    total = dot(jnp.concatenate(parts, axis=0).astype(BF16), w, dims)
    return total[0:rows] + total[rows : 2 * rows] + total[2 * rows :]


def block_kernel(cfg, names, *refs):
    DP, TM, U, F, C, SE, SH, LAYERS, KERNEL, fast = cfg
    env = dict(zip(names, refs, strict=True))
    lengths, x_any, g_any = env["lengths"], env["x_any"], env["g_any"]
    out_any, gin_any = env["out_any"], env["gin_any"]
    xv, xs, edge, xin, gin4 = env["xv"], env["xs"], env["edge"], env["xin"], env["gin4"]
    halo_l, halo_r, cot, ypad, dlow = env["halo_l"], env["halo_r"], env["cot"], env["ypad"], env["dlow"]
    pre, hh, mask, hmask, coef = env["pre"], env["hh"], env["mask"], env["hmask"], env["coef"]
    resd, act, du, drl = env["resd"], env["act"], env["du"], env["drl"]
    dn, gres_in = act, resd
    dhl, ddpad = env["dhl"], env["ddpad"]
    perm_l, perm_s, back_l, back_s = env["perm_l"], env["perm_s"], env["back_l"], env["back_s"]
    outp, obuf, gbuf, gp, small = env["outp"], env["obuf"], env["gbuf"], env.get("gp"), env["small"]
    sums, send_a, send_b, recv_core, recv_chip = (
        env["sums"], env["send_a"], env["send_b"], env["recv_core"], env["recv_chip"]
    )
    hsend, dhh, tsend, trecv = env["hsend"], env["dhh"], env["tsend"], env["trecv"]
    pool, gate, cvec, gsmall = env["pool"], env["gate"], env["cvec"], env["gsmall"]
    hx = env["hx"]
    slope, fac, facs = env["slope"], env["fac"], env["facs"]
    ggb = env["ggb"]
    sem_loc, sem_cs, sem_cr, sem_ks, sem_kr = (
        env["sem_loc"], env["sem_cs"], env["sem_cr"], env["sem_ks"], env["sem_kr"]
    )
    sem_cot = env["sem_cot"]
    sem_hs, sem_hr, sem_ts, sem_tr = env["sem_hs"], env["sem_hr"], env["sem_ts"], env["sem_tr"]
    sem_xs, sem_xr, sem_os, sem_or = env["sem_xs"], env["sem_xr"], env["sem_os"], env["sem_or"]
    MATS = LAYERS + 1
    AT_TAPS, AT_GAMMA = SE, SE + 8 * LAYERS
    AT_BETA = AT_GAMMA + 8
    NL = C // LANES
    UR = F // 4
    NU = 4 + (U - 1)
    NB = UR // 16
    R = NU * UR
    N_SRC = TM // 4
    dp, tm = lax.axis_index("dp"), lax.axis_index("tm")
    partner = tm + 1 - 2 * lax.rem(tm, 2)
    first, last = tm == 0, tm == TM - 1
    chips = [(a, 2 * b) for a in range(DP) for b in range(TM // 2) if a or b]
    n_chips = len(chips) + 1
    my_chip = dp * (TM // 2) + tm // 2

    def turns(v, n):
        bits = [1 << i for i in range(n.bit_length() - 1)] if n & (n - 1) == 0 else []
        return [(bit, bit * (1 - 2 * lax.rem(v // bit, 2))) for bit in bits]

    flips = {}

    def other(name, v, a, n):
        if name not in flips:
            flips[name] = turns(v, n)
        if not flips[name]:
            return lax.rem(v + a, n) if n > 1 else v
        for bit, step in flips[name]:
            if a & bit:
                v = v + step
        return v

    def at_chip(offset):
        return (lax.rem(dp + offset[0], DP), lax.rem(tm + offset[1], TM))

    def win(u):
        return u * UR if u < 4 else F + 64 + (u - 4) * (UR + 64)

    def seg_of(u):
        return 0 if u < 4 else u - 3

    def lane(j):
        return slice(j * LANES, (j + 1) * LANES)

    def each_lane(body):
        for j in range(NL):
            body(j, 0)

    def wide(v):
        return jnp.concatenate([v] * NL, axis=1)

    def remote(src, dst, ssem, rsem, dev):
        return pltpu.make_async_remote_copy(src, dst, ssem, rsem, device_id=dev, device_id_type=MESH)

    def total_wait(ref, sem):
        pltpu.make_async_copy(ref, ref, sem).wait()

    barrier = pltpu.get_barrier_semaphore()
    load_x = pltpu.make_async_copy(x_any, xv, sem_loc.at[0])
    load_x.start()
    others = [(0, b) for b in range(1, TM, 2)]
    for offset in chips + others:
        pl.semaphore_signal(barrier, inc=1, device_id=at_chip(offset), device_id_type=MESH)

    x, z, y, core = lax.rem(dp, 2), dp // 2, tm // 2, lax.rem(tm, 2)
    Y = TM // 2
    Z = DP // 2

    my_len = [lengths[dp * U + b] for b in range(U)]
    long_at = jnp.int32(0)
    for b in range(1, U):
        long_at = jnp.where(my_len[b] == F * TM, jnp.int32(b), long_at)
    short_at = [jnp.where(k < long_at, k, k + 1) for k in range(U - 1)]
    short_len = [lengths[dp * U + b] for b in range(U - 1)]
    short_len = [jnp.where(k < long_at, my_len[k], my_len[k + 1]) for k in range(U - 1)]
    count = lax.fori_loop(0, DP * U, lambda i, c: c + lengths[i], jnp.int32(0)).astype(F32)
    inv_count = 1.0 / jnp.full((1, LANES), count, F32)
    def make_masks():
        rows = lax.broadcasted_iota(jnp.int32, (UR, LANES), 0)
        time_s = (rows & 15) * NB + (rows >> 4) + tm * UR
        for k in range(U - 1):
            mask[k * UR : (k + 1) * UR, :] = jnp.where(time_s < short_len[k], 1.0, 0.0)
        e16 = lax.broadcasted_iota(jnp.int32, (16, LANES), 0)
        part = (e16 & 7) >> 1
        is_left = e16 < 8
        when = jnp.where(is_left, tm * UR - 2 + (e16 & 1), tm * UR + UR + (e16 & 1))
        bound = jnp.full((16, LANES), 1 << 30, jnp.int32)
        for k in range(U - 1):
            bound = jnp.where(part == k + 1, short_len[k], bound)
        inside = jnp.where(is_left, tm, TM - 1 - tm) > 0
        hmask[...] = jnp.where(inside & (when < bound), 1.0, 0.0)

    def one_hot(ref, size, to_time):
        n = size // 16
        r0 = lax.broadcasted_iota(jnp.int32, (UR, size), 0)
        r1 = lax.broadcasted_iota(jnp.int32, (UR, size), 1)
        for c in range(size // UR):
            a, b = (r1, r0 + c * UR) if to_time else (r0 + c * UR, r1)
            hit = b == (a & 15) * n + (a >> 4)
            ref[c * UR : (c + 1) * UR, :] = jnp.where(hit, 1.0, 0.0).astype(BF16)

    def zero_ends():
        @pl.when(first)
        def _():
            halo_l[...] = jnp.zeros(halo_l.shape, BF16)
            for l in range(LAYERS):
                hh[l, 0:8, :] = jnp.zeros((8, C), F32)
                dhh[l, 0:8, :] = jnp.zeros((8, C), F32)

        @pl.when(last)
        def _():
            halo_r[...] = jnp.zeros(halo_r.shape, BF16)
            for l in range(LAYERS):
                hh[l, 8:16, :] = jnp.zeros((8, C), F32)
                dhh[l, 8:16, :] = jnp.zeros((8, C), F32)

    def stage_short():
        @pl.when(tm < N_SRC)
        def _():
            for k in range(U - 1):
                def cp(c, _):
                    sl = pl.ds(pl.multiple_of(c * UR, UR), UR)
                    xs[k, sl, :] = xv[short_at[k], sl, :]
                    return 0
                lax.fori_loop(0, 4, cp, 0)

    def send_short(dst, half):
        def act_on(d):
            if half == 0:
                d.start()
            else:
                d.wait_send()

        @pl.when(tm < N_SRC)
        def _():
            for q in range(4):
                chunk = 4 * tm + q
                main = xs.at[:, q * UR : (q + 1) * UR, :]
                head = xs.at[:, q * UR : q * UR + 16, :]
                tail = xs.at[:, (q + 1) * UR - 16 : (q + 1) * UR, :]

                def go_main():
                    act_on(remote(main, dst, sem_xs.at[q], sem_xr.at[0], (dp, chunk)))

                def go_head():
                    act_on(remote(head, halo_r.at[1:U], sem_xs.at[4 + q], sem_xr.at[1], (dp, chunk - 1)))

                if q == 0:
                    pl.when(tm > 0)(go_main)
                    if half == 0:
                        @pl.when(tm == 0)
                        def _():
                            for k in range(U - 1):
                                dst[k] = xs[k, 0:UR, :]
                else:
                    go_main()
                if q < 2:
                    pl.when(tm > 0)(go_head)
                else:
                    go_head()
                if q == 1 and half == 0:
                    @pl.when(tm == 0)
                    def _():
                        for k in range(U - 1):
                            halo_r[1 + k] = xs[k, UR : UR + 16, :]

                @pl.when(chunk + 1 < TM)
                def _():
                    act_on(remote(tail, halo_l.at[1:U], sem_xs.at[8 + q], sem_xr.at[2], (dp, chunk + 1)))

    S2 = 2 * LAYERS

    def cot_piece(k, half):
        @pl.when(tm < N_SRC)
        def _():
            for q in range(4):
                chunk = 4 * tm + q
                src = xs.at[k, q * UR : (q + 1) * UR, :]
                copy = remote(src, gin4.at[k], sem_cot.at[k, q], sem_cr.at[S2 + k], (dp, chunk))
                go = copy.start if half == 0 else copy.wait_send
                if q == 0:
                    pl.when(tm > 0)(go)
                else:
                    go()

        if half == 0:
            @pl.when(tm == 0)
            def _():
                gin4[k] = xs[k, 0:UR, :]

    def recv_short(dst):
        @pl.when(tm > 0)
        def _():
            total_wait(dst, sem_xr.at[0])
            total_wait(halo_l.at[1:U], sem_xr.at[2])

            @pl.when(tm < TM - 1)
            def _():
                total_wait(halo_r.at[1:U], sem_xr.at[1])

    def edges(send, recv_l, recv_r, ssem, rsem, start):
        to_next = remote(send.at[1], recv_l, ssem.at[0], rsem.at[0], (dp, lax.rem(tm + 1, TM)))
        to_prev = remote(send.at[0], recv_r, ssem.at[1], rsem.at[1], (dp, lax.rem(tm + TM - 1, TM)))
        if start:
            pl.when(tm < TM - 1)(lambda: to_next.start())
            pl.when(tm > 0)(lambda: to_prev.start())
        else:
            @pl.when(tm < TM - 1)
            def _():
                to_next.wait_send()
                to_prev.wait_recv()

            @pl.when(tm > 0)
            def _():
                to_prev.wait_send()
                to_next.wait_recv()

    for name, v, n in (("dp", dp, DP), ("y", y, Y), ("z", z, Z)):
        other(name, v, 0, n)

    def plane_peers():
        return [(a, b) for a in reversed(range(Z)) for b in reversed(range(Y)) if a or b]

    def plane_peer(offset):
        pz, py = other("z", z, offset[0], Z), other("y", y, offset[1], Y)
        return pz, py, (2 * pz + x, 2 * py + core)

    across = (2 * z + 1 - x, tm)

    def gather_stage(buf, m, stage):
        ss, rs = env["sem_gs"].at[m, stage], env["sem_gr"].at[m, stage]
        if stage == 0:
            mine = buf.at[z, x, y, core]
            for offset in plane_peers():
                remote(mine, mine, ss, rs, plane_peer(offset)[2]).start()
        elif stage == 1:
            mine = buf.at[:, x, :, core]
            remote(mine, mine, ss, rs, across).start()
        else:
            mine = buf.at[:, :, :, core]
            remote(mine, mine, ss, rs, (dp, partner)).start()

    def gather_wait(buf, m, stage, sems):
        if stage == 0:
            size = env["little_rz"].at[0] if buf is sall else env["big_rz"].at[0]
            total_wait(size, sems.at[m, stage])
        elif stage == 1:
            total_wait(buf.at[:, 0, :, 0], sems.at[m, stage])
        else:
            total_wait(buf.at[:, :, :, 0], sems.at[m, stage])

    def gather_got(buf, m, stage):
        gather_wait(buf, m, stage, env["sem_gr"])

    def gather_left(buf, m):
        for stage in range(3):
            gather_wait(buf, m, stage, env["sem_gs"])

    if fast:
        wall, sall = env["wall"], env["sall"]
        halves = [(wall.at[0], 0)]

        def weights(m):
            return wall[m].reshape(C, C)

        pack = env["pack"]
        pack[...] = jnp.zeros(pack.shape, F32)
        for l in range(LAYERS):
            pack[AT_TAPS + 8 * l : AT_TAPS + 8 * l + KERNEL, 0:SH] = env["taps"][l].astype(F32)
        pack[AT_GAMMA : AT_GAMMA + LAYERS, 0:SH] = env["gamma"][...].astype(F32)
        pack[AT_BETA : AT_BETA + LAYERS, 0:SH] = env["beta"][...].astype(F32)
        turned = pack[...].T[0:SH]
        pack[0:SH, :] = turned
        pack[0:SH, 0:SE] = env["excite"][...].astype(F32)
        sall[z, x, y, core, :, 0:LANES] = pack[0:SH, :].astype(BF16)
        pack[0:SH, 0:SE] = env["squeeze"][...].astype(F32)
        sall[z, x, y, core, :, LANES : 2 * LANES] = pack[0:SH, :].astype(BF16)
        for l in range(LAYERS):
            wall[l, z, x, y, core] = env["point"][l]
        wall[LAYERS, z, x, y, core] = env["resid"][...]
    else:
        def weights(m):
            return env["mats"][m]

        small[...] = env["small_in"][...]

    def squeeze_all():
        if fast:
            return sall[...].reshape(C, 2 * LANES)[:, LANES : LANES + SE]
        return env["squeeze"][...]

    class Scatter:
        def __init__(self, name):
            self.send, self.core, self.xsum, self.rx, self.zsum, self.rz, self.ss, self.rs = (
                env[name + part] for part in ("_send", "_core", "_xsum", "_rx", "_zsum", "_rz", "_ss", "_rs")
            )
            self.dtype = self.send.dtype

        def go(self, m, stage):
            ss, rs = self.ss.at[m, stage], self.rs.at[m, stage]
            if stage == 0:
                remote(self.send.at[m, :, :, :, 1 - core], self.core.at[m], ss, rs, (dp, partner)).start()
            elif stage == 1:
                remote(self.xsum.at[m, 1 - x], self.rx.at[m], ss, rs, across).start()
            else:
                for i, offset in enumerate(plane_peers()):
                    pz, py, peer = plane_peer(offset)
                    remote(self.zsum.at[m, pz, py], self.rz.at[m, i], ss, rs, peer).start()

        def wait(self, m, stage, sems):
            total_wait((self.core.at[m], self.rx.at[m], self.rz.at[m])[stage], sems.at[m, stage])

        def left(self, m):
            for stage in range(3):
                self.wait(m, stage, self.ss)

        def core_to_x(self, m):
            self.wait(m, 0, self.rs)

            def body(i, _):
                v = self.send[m, i, :, :, core].astype(F32) + self.core[m, i].astype(F32)
                for k in range(2):
                    self.xsum[m, k, i] = v[k].astype(self.dtype)
                return 0

            lax.fori_loop(0, Z, body, 0)
            self.go(m, 1)

        def x_to_plane(self, m):
            self.x_sum(m)
            self.go(m, 2)

        def x_sum(self, m):
            self.wait(m, 1, self.rs)

            def body(i, _):
                v = self.xsum[m, x, i].astype(F32) + self.rx[m, i].astype(F32)
                self.zsum[m, i] = v.astype(self.dtype)
                return 0

            lax.fori_loop(0, Z, body, 0)

        def result(self, m):
            self.wait(m, 2, self.rs)
            v = self.zsum[m, z, y].astype(F32)
            for i in range(Z * Y - 1):
                v = v + self.rz[m, i].astype(F32)
            return v

    if fast:
        big, little = Scatter("big"), Scatter("little")

    def to_perm_long(src, dst, base):
        for u in range(4):
            o = base(u)
            dst[o : o + UR, :] = dot(perm_l[u * UR : (u + 1) * UR, :], src).astype(BF16)

    def to_perm_short(src, dst, base, masked):
        for k in range(U - 1):
            v = dot(perm_s[...], src[k])
            if masked:
                v = v * wide(mask[k * UR : (k + 1) * UR, :])
            o = base(4 + k)
            dst[o : o + UR, :] = v.astype(BF16)

    y0 = ypad.at[0]
    zero_ends()
    pl.semaphore_wait(barrier, len(chips) + len(others))
    if fast:
        gather_stage(sall, MATS, 0)
        for buf, m in halves:
            gather_stage(buf, m, 0)
    load_x.wait()
    edge[0] = xv[long_at, 0:16, :]
    edge[1] = xv[long_at, F - 16 : F, :]
    stage_short()
    edge_sems = (sem_xs.at[pl.ds(12, 2)], sem_xr.at[pl.ds(3, 2)])
    edges(edge, halo_l.at[0], halo_r.at[0], *edge_sems, True)
    send_short(xin, 0)
    if fast:
        for m in range(1, min(3, MATS)):
            gather_stage(wall.at[m], m, 0)
    one_hot(perm_l, F, False)
    one_hot(perm_s, UR, False)
    to_perm_long(xv[long_at], y0, lambda u: win(u) + 32)
    load_g = pltpu.make_async_copy(g_any, xv, sem_loc.at[0])
    load_g.start()
    make_masks()
    if fast:
        gather_got(sall, MATS, 0)
        gather_stage(sall, MATS, 1)
        for buf, m in halves:
            gather_got(buf, m, 0)
            gather_stage(buf, m, 1)
        gather_got(sall, MATS, 1)
        gather_stage(sall, MATS, 2)
        for buf, m in halves:
            gather_got(buf, m, 1)
            gather_stage(buf, m, 2)
        gather_got(sall, MATS, 2)
        for j in range(NL):
            part = sall[...].reshape(C, 2 * LANES)[j * LANES : (j + 1) * LANES, 0:LANES].astype(F32)
            small[:, j * LANES : (j + 1) * LANES] = part.T

    def fill_pads(ref, row0, n, j, b0, b1, b2, b3, halo, seg):
        e = lax.broadcasted_iota(jnp.int32, (16, LANES), 0)

        def put(at, v):
            ref[pl.ds(row0 + at * 16, 16), lane(j)] = v.astype(BF16)

        put(0, jnp.where(e == 0, halo[2 * seg : 2 * seg + 1], pltpu.roll(b2, 1, 0)))
        put(1, jnp.where(e == 0, halo[2 * seg + 1 : 2 * seg + 2], pltpu.roll(b3, 1, 0)))
        put(n + 2, jnp.where(e == 15, halo[8 + 2 * seg : 9 + 2 * seg], pltpu.roll(b0, 15, 0)))
        put(n + 3, jnp.where(e == 15, halo[9 + 2 * seg : 10 + 2 * seg], pltpu.roll(b1, 15, 0)))

    def pads_from(ref, j, halo, segs):
        for seg in segs:
            u0, u1 = (0, 3) if seg == 0 else (3 + seg, 3 + seg)
            n = F // 16 if seg == 0 else NB
            o0, o1 = win(u0) + 32, win(u1) + 32 + UR
            blk = [ref[o : o + 16, lane(j)].astype(F32) for o in (o0, o0 + 16, o1 - 32, o1 - 16)]
            fill_pads(ref, win(u0), n, j, *blk, halo, seg)

    def first_pads(segs):
        def body(j, _):
            none = jnp.zeros((2, LANES), F32)
            left = [halo_l[s, :, lane(j)].astype(F32)[14:16] if s in segs else none for s in range(4)]
            right = [halo_r[s, :, lane(j)].astype(F32)[0:2] if s in segs else none for s in range(4)]
            halo = jnp.where(hmask[...] > 0.0, jnp.concatenate(left + right, axis=0), 0.0)
            pads_from(y0, j, halo, segs)
            return 0

        each_lane(body)

    edges(edge, halo_l.at[0], halo_r.at[0], *edge_sems, False)
    first_pads([0])

    def shorts_arrive():
        if fast:
            gather_got(wall.at[1], 1, 0)
            gather_stage(wall.at[1], 1, 1)
        recv_short(xin)
        to_perm_short(xin, y0, lambda u: win(u) + 32, True)
        send_short(xin, 1)
        first_pads(range(1, U))

    def sync_core(s, meanwhile):
        d = remote(send_a.at[s], recv_core.at[s], sem_cs.at[s], sem_cr.at[s], (dp, partner))
        d.start()
        meanwhile()
        d.wait()
        send_b[s] = send_a[s] + recv_core[s]

    def sync_send(s):
        recv_chip[s, my_chip] = send_b[s]
        dst = recv_chip.at[s, my_chip]

        for a in reversed(range(DP)):
            for b in reversed(range(Y)):
                if a or b:
                    there = (other("dp", dp, a, DP), 2 * other("y", y, b, Y) + core)
                    remote(send_b.at[s], dst, sem_ks.at[s], sem_kr.at[s], there).start()

    def sync_done(s):
        others = recv_chip.at[s, 0 : n_chips - 1]
        total_wait(others, sem_kr.at[s])
        total_wait(others, sem_ks.at[s])
        total = recv_chip[s, 0]
        for i in range(1, n_chips):
            total = total + recv_chip[s, i]
        return total

    def tap_rows(l, j):
        group = small[pl.ds(pl.multiple_of(AT_TAPS + 8 * l, 8), 8), lane(j)]
        return [group[k : k + 1] for k in range(KERNEL)]

    LONG, SHORT = range(4), range(4, NU)

    def conv_pass(l, units):
        def body(j, _):
            w = tap_rows(l, j)
            for u in units:
                o = win(u)
                v = ypad[l, o : o + UR + 64, lane(j)].astype(F32)
                t = v[0:UR] * w[0]
                for k in range(1, KERNEL):
                    t = t + v[16 * k : 16 * k + UR] * w[k]
                if u >= 4:
                    t = t * mask[(u - 4) * UR : (u - 3) * UR, :]
                dlow[l, u * UR : (u + 1) * UR, lane(j)] = t.astype(BF16)
            return 0

        each_lane(body)

    def fold8(v):
        return jnp.sum(v.reshape(v.shape[0] // 8, 8, v.shape[1]), axis=0)

    def put_edges(src, l):
        for seg in range(4):
            base = 0 if seg == 0 else F + (seg - 1) * UR
            n = F if seg == 0 else UR
            for e in range(2):
                hsend[l, 1, 2 * seg + e : 2 * seg + e + 1, :] = src(base + n - 32 + 16 * e + 15)
                hsend[l, 0, 2 * seg + e : 2 * seg + e + 1, :] = src(base + 16 * e)

    def matmul_pass(l, units):
        r = slice(units[0] * UR, (units[-1] + 1) * UR)
        h = dot(dlow[l, r, :], weights(l))
        pre[l, r, :] = h
        s0, s1 = fold8(h), fold8(h * h)
        if units[0] > 0:
            s0, s1 = s0 + sums[0], s1 + sums[1]
        sums[0] = s0
        sums[1] = s1

    def send_stats(l):
        send_a[l, 0:1, :] = jnp.sum(sums[0], axis=0, keepdims=True)
        send_a[l, 1:2, :] = jnp.sum(sums[1], axis=0, keepdims=True)

    def act_pass(l):
        def body(j, _):
            a, b = coef[l, 0:1, lane(j)], coef[l, 1:2, lane(j)]
            for u in range(NU):
                v = pre[l, u * UR : (u + 1) * UR, lane(j)] * a + b
                v = v + v * jnp.tanh(v)
                if u >= 4:
                    v = v * mask[(u - 4) * UR : (u - 3) * UR, :]
                o = win(u) + 32
                ypad[l + 1, o : o + UR, lane(j)] = v.astype(BF16)
            v = hh[l, :, lane(j)] * a + b
            v = (v + v * jnp.tanh(v)) * hmask[...]
            pads_from(ypad.at[l + 1], j, v, range(U))
            return 0

        each_lane(body)

    def prep_pass(l):
        def body(j, _):
            a, b, m, i = (coef[l, r : r + 1, lane(j)] for r in range(4))
            for u in range(NU):
                rs = slice(u * UR, (u + 1) * UR)
                h = pre[l, rs, lane(j)]
                half = h * a + b
                t = jnp.tanh(half)
                v = (0.5 + 0.5 * t) * (1.0 + half * (1.0 - t))
                if u >= 4:
                    v = v * mask[(u - 4) * UR : (u - 3) * UR, :]
                slope[l, rs, lane(j)] = v.astype(BF16)
                pre[l, rs, lane(j)] = (h - m) * i
            hx[l, :, lane(j)] = (hh[l, :, lane(j)] - m) * i
            return 0

        each_lane(body)

    def layer(l, _):
        pl.when(l == 0)(shorts_arrive)
        conv_pass(l, LONG)
        if fast:
            gather_got(wall.at[l], l, 2)
        matmul_pass(l, LONG)
        conv_pass(l, SHORT)
        matmul_pass(l, SHORT)
        send_stats(l)

        def halo_out():
            put_edges(lambda row: pre[l, row : row + 1, :], l)
            edges(hsend.at[l], hh.at[l, 0:8], hh.at[l, 8:16], sem_hs.at[l], sem_hr.at[l], True)

        sync_core(l, halo_out)
        sync_send(l)

        if fast:
            gather_got(wall.at[l + 1], l + 1, 1)
            gather_stage(wall.at[l + 1], l + 1, 2)

        pl.when(l > 0)(lambda: prep_pass(l - 1))

        @pl.when(l == 0)
        def _():
            load_g.wait()
            stage_short()
            to_perm_long(xv[long_at], cot, lambda u: u * UR)

        @pl.when(l == 1)
        def _():
            one_hot(back_l, F, True)
            one_hot(back_s, UR, True)

        @pl.when(l == LAYERS - 1)
        def _():
            for k in range(U - 1):
                cot_piece(k, 1)

            @pl.when(tm > 0)
            def _():
                for k in range(U - 1):
                    total_wait(gin4.at[k], sem_cr.at[S2 + k])

            to_perm_short(gin4, cot, lambda u: u * UR, True)

        total = sync_done(l)
        edges(hsend.at[l], hh.at[l, 0:8], hh.at[l, 8:16], sem_hs.at[l], sem_hr.at[l], False)
        if fast:
            @pl.when(l + 2 < MATS)
            def _():
                gather_got(wall.at[l + 2], l + 2, 0)
                gather_stage(wall.at[l + 2], l + 2, 1)

            @pl.when(l + 3 < MATS)
            def _():
                gather_stage(wall.at[l + 3], l + 3, 0)

        for k in range(U - 1):
            pl.when(l == k)(functools.partial(cot_piece, k, 0))
        scale = wide(inv_count)
        mean = total[0:1] * scale
        var = total[1:2] * scale - mean * mean
        inv = lax.rsqrt(var + NORM_EPSILON)
        ga = small[pl.ds(AT_GAMMA + l, 1), :]
        a = ga * inv
        coef[l, 0:1, :] = 0.5 * a
        coef[l, 1:2, :] = 0.5 * (small[pl.ds(AT_BETA + l, 1), :] - mean * a)
        coef[l, 2:3, :] = mean
        coef[l, 3:4, :] = inv
        coef[l, 4:5, :] = a

        pl.when(l < LAYERS - 1)(lambda: act_pass(l))
        return 0

    lax.fori_loop(0, LAYERS, layer, 0)

    top = LAYERS - 1
    pool[...] = jnp.zeros(pool.shape, F32)

    def last_act(j, _):
        a, b = coef[top, 0:1, lane(j)], coef[top, 1:2, lane(j)]
        acc = None
        for u in range(NU):
            v = pre[top, u * UR : (u + 1) * UR, lane(j)] * a + b
            v = v + v * jnp.tanh(v)
            if u >= 4:
                v = v * mask[(u - 4) * UR : (u - 3) * UR, :]
            act[u * UR : (u + 1) * UR, lane(j)] = v
            f = fold8(v)
            acc = f if u == 0 or u >= 4 else acc + f
            if u >= 3:
                pool[u - 3 : u - 2, lane(j)] = jnp.sum(acc, axis=0, keepdims=True)
        return 0

    each_lane(last_act)

    def time_sum(s, value):
        tsend[s] = value
        ds = [remote(tsend.at[s], trecv.at[s, i - 1], sem_ts.at[s], sem_tr.at[s], (dp, lax.rem(tm + i, TM))) for i in range(1, TM)]
        for d in ds:
            d.start()

    def time_done(s):
        whole = trecv.at[s]
        total_wait(whole, sem_tr.at[s])
        total_wait(whole, sem_ts.at[s])
        total = tsend[s]
        for i in range(TM - 1):
            total = total + trecv[s, i]
        return total

    e8 = lax.broadcasted_iota(jnp.int32, (8, LANES), 0)
    len8 = jnp.full((8, LANES), F * TM, jnp.int32)
    for k in range(U - 1):
        len8 = jnp.where(e8 == k + 1, short_len[k], len8)
    inv_len = 1.0 / len8.astype(F32)
    live = jnp.where(e8 < U, 1.0, 0.0)
    time_sum(0, pool[...])
    prep_pass(top)
    if fast:
        gather_got(wall.at[LAYERS], LAYERS, 2)
    resd[0:F, :] = dot(ypad[0, 32 : 32 + F, :], weights(LAYERS))
    for u in SHORT:
        resd[u * UR : (u + 1) * UR, :] = dot(ypad[0, win(u) + 32 : win(u) + 32 + UR, :], weights(LAYERS))
    p = time_done(0) * wide(inv_len)
    sq = squeeze_all()
    ex = small[0:SE, :].astype(BF16)
    q = dot_parts(p, sq)
    sig_q = logistic(q)
    z_act = q * sig_q
    gate[...] = logistic(dot_parts(z_act, ex))
    pool[...] = jnp.zeros(pool.shape, F32)

    def top_pass(j, _):
        acc = None
        for u in range(NU):
            rs = slice(u * UR, (u + 1) * UR)
            seg = seg_of(u)
            av = act[rs, lane(j)]
            half = 0.5 * (av * gate[seg : seg + 1, lane(j)] + resd[rs, lane(j)])
            t = jnp.tanh(half)
            out = half + half * t
            slope = (0.5 + 0.5 * t) * (1.0 + half * (1.0 - t))
            dv = cot[rs, lane(j)].astype(F32) * slope
            if u >= 4:
                out = out * mask[(u - 4) * UR : (u - 3) * UR, :]
            outp[rs, lane(j)] = out.astype(BF16)
            du[rs, lane(j)] = dv
            drl[rs, lane(j)] = dv.astype(BF16)
            f = fold8(dv * av)
            acc = f if u == 0 or u >= 4 else acc + f
            if u >= 3:
                pool[u - 3 : u - 2, lane(j)] = jnp.sum(acc, axis=0, keepdims=True)
        return 0

    each_lane(top_pass)
    time_sum(1, pool[...])

    def back_long(buf, src):
        for u in range(4):
            buf[0, u * UR : (u + 1) * UR, :] = dot(back_l[u * UR : (u + 1) * UR, :], src[0:F, :]).astype(BF16)

    def back_short(buf, stage, src):
        for k in range(U - 1):
            stage[k] = dot(back_s[...], src[F + k * UR : F + (k + 1) * UR, :]).astype(BF16)

        @pl.when(tm >= N_SRC)
        def _():
            for k in range(U - 1):
                buf[1 + k] = jnp.zeros((F, C), BF16)

        @pl.when(first)
        def _():
            for k in range(U - 1):
                buf[1 + k, 0:UR, :] = stage[k]

    def back_piece(buf, stage, sems, rsems, k):
        owner, q = tm // 4, lax.rem(tm, 4)
        dst = buf.at[1 + k, pl.ds(pl.multiple_of(q * UR, UR), UR), :]
        return remote(stage.at[k], dst, sems.at[k], rsems.at[k, q], (dp, owner))

    def back_send(buf, stage, sems, rsems, ks):
        @pl.when(tm > 0)
        def _():
            for k in ks:
                back_piece(buf, stage, sems, rsems, k).start()

    def back_left(buf, stage, sems, rsems):
        @pl.when(tm > 0)
        def _():
            for k in range(U - 1):
                back_piece(buf, stage, sems, rsems, k).wait_send()

    def back_arrived(buf, rsems, k):
        @pl.when(tm < N_SRC)
        def _():
            for i in range(4):
                got = functools.partial(total_wait, buf.at[1 + k, i * UR : (i + 1) * UR, :], rsems.at[k, i])
                if i == 0:
                    pl.when(tm > 0)(got)
                else:
                    got()

    def back_done(buf, stage, sems, rsems):
        back_left(buf, stage, sems, rsems)
        for k in range(U - 1):
            back_arrived(buf, rsems, k)

    put_out = pltpu.make_async_copy(obuf, out_any, sem_loc.at[2])
    back_long(obuf, outp)
    back_short(obuf, xin, outp)

    def xrows(u):
        o = win(u) + 32
        return ypad[0, o : o + UR, :]

    def put_grad(m, total):
        if fast:
            big.send[m] = total.astype(BF16).reshape(Z, 2, Y, 2, SH, C)
            big.go(m, 0)
        else:
            gp[...] = total
            pltpu.make_async_copy(gp, env["gmats"].at[m], sem_loc.at[1]).start()

    def grad_gone():
        if not fast:
            pltpu.make_async_copy(gp, env["gmats"].at[0], sem_loc.at[1]).wait()

    def xrows(u):
        o = win(u) + 32
        return ypad[0, o : o + UR, :]

    def resid_grads():
        total = dot(ypad[0, 32 : 32 + F, :], drl[0:F, :], ((0,), (0,)))
        for u in SHORT:
            total = total + dot(xrows(u), drl[u * UR : (u + 1) * UR, :], ((0,), (0,)))
        put_grad(LAYERS, total)
        gres_in[...] = dot(drl[...], weights(LAYERS), ((1,), (1,)))

    resid_grads()
    dg = time_done(1)
    gv = gate[...]
    de = dg * gv * (1.0 - gv) * wide(live)
    dz = dot_parts(de, ex, ((1,), (1,)))
    dq = dz * sig_q * (1.0 + q * (1.0 - sig_q))
    cvec[...] = dot_parts(dq, sq, ((1,), (1,))) * wide(inv_len)
    fac[0], fac[1] = p, de
    facs[0], facs[1] = z_act, dq

    def pair_grads():
        lead = jnp.where(first, 1.0, 0.0)
        zero = jnp.zeros((C, LANES - 2 * SE), F32)
        pair = [dot(fac[1 - i], facs[i], ((0,), (0,)), precision=HIGHEST) for i in range(2)]
        pair = jnp.concatenate(pair + [zero] * (LANES > 2 * SE), axis=1) * lead
        if fast:
            little.send[0] = pair.reshape(Z, 2, Y, 2, SH, LANES)
            little.go(0, 0)
        else:
            env["gpair"][...] = pair

    def back_sums(l, s, grad_of):
        def body(j, _):
            acc0 = acc1 = None
            make = grad_of(j)
            for u in range(NU):
                rs = slice(u * UR, (u + 1) * UR)
                v = make(u) * slope[l, rs, lane(j)].astype(F32)
                xc = pre[l, rs, lane(j)]
                dn[u * UR : (u + 1) * UR, lane(j)] = v
                f0, f1 = fold8(v), fold8(v * xc)
                acc0 = f0 if u == 0 else acc0 + f0
                acc1 = f1 if u == 0 else acc1 + f1
            send_a[s, 0:1, lane(j)] = jnp.sum(acc0, axis=0, keepdims=True)
            send_a[s, 1:2, lane(j)] = jnp.sum(acc1, axis=0, keepdims=True)
            return 0

        each_lane(body)

    def top_grad(j):
        def make(u):
            seg = seg_of(u)
            return du[u * UR : (u + 1) * UR, lane(j)] * gate[seg : seg + 1, lane(j)] + cvec[seg : seg + 1, lane(j)]
        return make

    def conv_grad(l):
        def outer(j):
            w = tap_rows(l, j)

            def make(u):
                o = win(u)
                v = ddpad[o : o + UR + 64, lane(j)].astype(F32)
                t = v[64 : 64 + UR] * w[0]
                for k in range(1, KERNEL):
                    t = t + v[64 - 16 * k : 64 - 16 * k + UR] * w[k]
                return t
            return make
        return outer

    back_sums(top, LAYERS, top_grad)

    def point_grad(l):
        grad_gone()
        put_grad(l, dot(dlow[l], dhl[0:R, :], ((0,), (0,))))

    def depth_grad(l):
        def body(j, _):
            acc = [None] * KERNEL
            for u in range(NU):
                o = win(u)
                v = ypad[l, o : o + UR + 64, lane(j)].astype(F32)
                g = ddpad[o + 32 : o + 32 + UR, lane(j)].astype(F32)
                for k in range(KERNEL):
                    f = fold8(v[16 * k : 16 * k + UR] * g)
                    acc[k] = f if u == 0 else acc[k] + f
            rows = [jnp.sum(acc[k], axis=0, keepdims=True) for k in range(KERNEL)]
            rows.append(jnp.zeros((8 - KERNEL, LANES), F32))
            at = pl.ds(pl.multiple_of(AT_TAPS + 8 * l, 8), 8)
            gsmall[at, lane(j)] = jnp.concatenate(rows, axis=0)
            return 0

        each_lane(body)
    def dh_pass(l, units):
        def body(j, _):
            a, k1, k0 = (coef[l, r : r + 1, lane(j)] for r in (4, 5, 6))
            for u in units:
                rs = slice(u * UR, (u + 1) * UR)
                v = dn[rs, lane(j)] * a - (pre[l, rs, lane(j)] * k1 + k0)
                if u >= 4:
                    v = v * mask[(u - 4) * UR : (u - 3) * UR, :]
                dhl[rs, lane(j)] = v.astype(BF16)
            if units is SHORT:
                v = (dhh[l, :, lane(j)] * a - (hx[l, :, lane(j)] * k1 + k0)) * hmask[...]
                dhl[R : R + 16, lane(j)] = v.astype(BF16)
            return 0

        each_lane(body)

    def dd_pass(l):
        dh_pass(l, LONG)
        ddpad[32 : 32 + F, :] = dot(dhl[0:F, :], weights(l), ((1,), (1,))).astype(BF16)
        dh_pass(l, SHORT)
        v = dot(dhl[F : R + 16, :], weights(l), ((1,), (1,)))
        for u in SHORT:
            ddpad[win(u) + 32 : win(u) + 32 + UR, :] = v[(u - 4) * UR : (u - 3) * UR].astype(BF16)
        hx[l] = v[R - F : R - F + 16].astype(BF16).astype(F32)

        def pad(j, _):
            pads_from(ddpad, j, hx[l, :, lane(j)], range(U))
            return 0

        each_lane(pad)

    def back_layer(step, _):
        l = top - step
        s = LAYERS + step

        def halo_out():
            put_edges(lambda row: dn[row : row + 1, :], s)
            edges(hsend.at[s], dhh.at[l, 0:8], dhh.at[l, 8:16], sem_hs.at[s], sem_hr.at[s], True)

        sync_core(s, halo_out)
        sync_send(s)

        @pl.when(step > 0)
        def _():
            point_grad(l + 1)
            depth_grad(l + 1)

        pl.when(step == 0)(pair_grads)

        @pl.when(step == LAYERS - 1)
        def _():
            back_done(obuf, xin, sem_os.at[0], sem_or.at[0])
            put_out.start()

        if fast:
            @pl.when(step == 1)
            def _():
                little.core_to_x(0)

            @pl.when(step == 2)
            def _():
                little.x_to_plane(0)

            @pl.when(step > 0)
            def _():
                big.x_sum(l + 2)

            @pl.when(step > 1)
            def _():
                env["gmats"][l + 3] = big.result(l + 3)

            big.core_to_x(l + 1)

        total = sync_done(s)
        if fast:
            pl.when(step > 0)(lambda: big.go(l + 2, 2))

        @pl.when(step < U - 1)
        def _():
            back_send(obuf, xin, sem_os.at[0], sem_or.at[0], [step])

        edges(hsend.at[s], dhh.at[l, 0:8], dhh.at[l, 8:16], sem_hs.at[s], sem_hr.at[s], False)
        ggb[l, 0:2, :] = total
        a = coef[l, 4:5, :]
        coef[l, 5:6, :] = a * total[1:2] * wide(inv_count)
        coef[l, 6:7, :] = a * total[0:1] * wide(inv_count)

        dd_pass(l)

        @pl.when(l > 0)
        def _():
            back_sums(l - 1, s + 1, conv_grad(l - 1))
        return 0

    def run_back():
        lax.fori_loop(0, LAYERS, back_layer, 0)

    conv_grad_of = conv_grad

    def conv_grad(l):
        return conv_grad_of(l + 1)

    gsmall[...] = jnp.zeros(gsmall.shape, F32)
    run_back()
    lead_all = jnp.where(first & (dp == 0), 1.0, 0.0)
    for l in range(LAYERS):
        gsmall[AT_BETA + l : AT_BETA + l + 1, :] = ggb[l, 0:1, :] * lead_all
        gsmall[AT_GAMMA + l : AT_GAMMA + l + 1, :] = ggb[l, 1:2, :] * lead_all
    def final_pass(units):
        def body(j, _):
            make = conv_grad_of(0)(j)
            for u in units:
                rs = slice(u * UR, (u + 1) * UR)
                v = make(u)
                if u >= 4:
                    v = v * mask[(u - 4) * UR : (u - 3) * UR, :]
                outp[rs, lane(j)] = (v + gres_in[rs, lane(j)]).astype(BF16)
            return 0

        each_lane(body)

    point_grad(0)
    final_pass(SHORT)
    back_short(gbuf, gin4, outp)
    back_send(gbuf, gin4, sem_os.at[1], sem_or.at[1], range(U - 1))
    if fast:
        big.core_to_x(0)
    depth_grad(0)
    if fast:
        for j in range(NL):
            rows = gsmall[:, j * LANES : (j + 1) * LANES].T
            part = rows.reshape(LANES // (2 * SH), 2, SH, LANES)
            per = LANES // (2 * SH)
            for i in range(per):
                n = j * per + i
                little.send[1, n // (2 * Y), n // Y % 2, n % Y] = part[i]
        little.go(1, 0)
        big.x_to_plane(1)
    final_pass(LONG)
    back_long(gbuf, outp)
    put_gin = [pltpu.make_async_copy(gbuf.at[k], gin_any.at[k], sem_loc.at[3 + k]) for k in range(U)]
    put_gin[0].start()
    if fast:
        little.core_to_x(1)
        env["gmats"][2] = big.result(2)
        big.x_to_plane(0)
        little.x_to_plane(1)
        env["gpair"][...] = little.result(0)
        env["gmats"][1] = big.result(1)
        for m in range(1, MATS):
            big.left(m)
            gather_left(wall.at[m], m)
        for buf, m in halves:
            gather_left(buf, m)
        little.left(0)
        gather_left(sall, MATS)
    else:
        env["grows"][...] = gsmall[...]
    for k in range(U - 1):
        back_arrived(gbuf, sem_or.at[1], k)
        put_gin[1 + k].start()
    back_left(gbuf, gin4, sem_os.at[1], sem_or.at[1])
    if fast:
        env["gmats"][0] = big.result(0)
        env["grows"][...] = little.result(1)
        big.left(0)
        little.left(1)
    grad_gone()
    put_out.wait()
    for c in put_gin:
        c.wait()


def finish_kernel(cfg, lengths, out_s, gin_s, gmats_any, gpair_any, grows_any, *rest):
    DP, TM, U, F, C, SE, SH, LAYERS, KERNEL, fast = cfg
    out, gin, gdepth_any, gpoint, ggamma_any, gbeta_any, gsq_any, gex_any, gres = rest[:9]
    hold, gmats, gpair, grows, turn, gdepth, ggamma, gbeta, gsq, gex, sems, sems_g = rest[9:]
    dp = lax.axis_index("dp")
    long_at = jnp.int32(0)
    for b in range(1, U):
        long_at = jnp.where(lengths[dp * U + b] == F * TM, jnp.int32(b), long_at)
    copies = []
    loads = [
        pltpu.make_async_copy(src, dst, sems_g.at[i])
        for i, (src, dst) in enumerate(((gmats_any, gmats), (gpair_any, gpair), (grows_any, grows)))
    ]
    for c in loads:
        c.start()
    for b in range(U):
        slot = jnp.where(b == long_at, 0, jnp.where(b < long_at, b + 1, b))
        for i, (src, dst) in enumerate(((out_s, out), (gin_s, gin))):
            get = pltpu.make_async_copy(src.at[slot], hold.at[i, b], sems.at[0, i, b])
            put = pltpu.make_async_copy(hold.at[i, b], dst.at[b], sems.at[1, i, b])
            copies.append((get, put))
            get.start()
    loads[0].wait()
    results = [
        pltpu.make_async_copy(gmats.at[0:LAYERS], gpoint, sems_g.at[3]),
        pltpu.make_async_copy(gmats.at[LAYERS], gres, sems_g.at[4]),
    ]
    for c in results:
        c.start()
    for get, put in copies:
        get.wait()
        put.start()
    for c in loads[1:]:
        c.wait()
    at_taps = SE
    at_gamma = SE + 8 * LAYERS
    at_beta = at_gamma + 8
    gsq[...] = gpair[:, SE : 2 * SE]
    gex[...] = gpair[:, 0:SE]
    turn[...] = jnp.zeros(turn.shape, F32)
    turn[0:SH] = grows[...]
    turn[...] = turn[...].T
    for l in range(LAYERS):
        gdepth[l] = turn[at_taps + 8 * l : at_taps + 8 * l + KERNEL, 0:SH]
    ggamma[...] = turn[at_gamma : at_gamma + LAYERS, 0:SH]
    gbeta[...] = turn[at_beta : at_beta + LAYERS, 0:SH]
    pairs = ((gdepth, gdepth_any), (ggamma, ggamma_any), (gbeta, gbeta_any), (gsq, gsq_any), (gex, gex_any))
    for i, (src, dst) in enumerate(pairs):
        results.append(pltpu.make_async_copy(src, dst, sems_g.at[5 + i]))
        results[-1].start()
    for _, put in copies:
        put.wait()
    for c in results:
        c.wait()


def local(sizes, inputs, lengths, depth_w, point_w, gamma, beta, squeeze_w, excite_w, resid_w, cotangent):
    DP, TM = sizes
    U, F, C = inputs.shape
    LAYERS, KERNEL, SH = depth_w.shape
    SE = squeeze_w.shape[1]
    UR = F // 4
    NU = 4 + U - 1
    R = NU * UR
    RP = F + 64 + (U - 1) * (UR + 64)
    S = 2 * LAYERS
    chips = DP * (TM // 2) - 1
    axes = ("dp", "tm")
    fast = SH % 16 == 0 and DP % 2 == 0 and DP > 2
    Z, Y = DP // 2, TM // 2
    MATS = LAYERS + 1
    vm = pltpu.VMEM
    dma = pltpu.SemaphoreType.DMA
    any_spec = pl.BlockSpec(memory_space=pl.ANY)
    vm_spec = pl.BlockSpec(memory_space=pltpu.VMEM)
    sm_spec = pl.BlockSpec(memory_space=pltpu.SMEM)
    sd = jax.ShapeDtypeStruct
    cfg = (DP, TM, U, F, C, SE, SH, LAYERS, KERNEL, fast)
    at_gamma = SE + 8 * LAYERS
    operands = dict(lengths=lengths, x_any=inputs, g_any=cotangent)
    specs = [sm_spec, any_spec, any_spec]
    outs = dict(out_any=sd((U, F, C), BF16), gin_any=sd((U, F, C), BF16))
    out_specs = [any_spec, any_spec]
    if fast:
        operands.update(
            point=point_w, taps=depth_w, gamma=gamma, beta=beta, squeeze=squeeze_w, excite=excite_w.T, resid=resid_w
        )
        specs += [vm_spec] * 7
        outs.update(gmats=sd((MATS, SH, C), F32), gpair=sd((SH, LANES), F32), grows=sd((SH, LANES), F32))
        out_specs += [vm_spec] * 3
    else:
        mats = jnp.concatenate([point_w, resid_w[None]], axis=0)
        depth_rows = jnp.pad(depth_w, ((0, 0), (0, 8 - KERNEL), (0, 0))).reshape(8 * LAYERS, SH)
        fill = ((0, 8 - LAYERS), (0, 0))
        rows = jnp.concatenate([excite_w, depth_rows, jnp.pad(gamma, fill), jnp.pad(beta, fill)], axis=0)
        rows = jnp.pad(rows, ((0, LANES - rows.shape[0]), (0, 0)))
        operands.update(
            mats=lax.all_gather(mats, axes, axis=1, tiled=True),
            small_in=lax.all_gather(rows, axes, axis=1, tiled=True).astype(F32),
            squeeze=lax.all_gather(squeeze_w, axes, axis=0, tiled=True),
        )
        specs += [vm_spec] * 3
        outs.update(gmats=sd((MATS, C, C), F32), gpair=sd((C, LANES), F32), grows=sd((LANES, C), F32))
        out_specs += [any_spec, vm_spec, vm_spec]
    scratch = dict(
        xv=vm((U, F, C), BF16), xs=vm((U - 1, F, C), BF16), edge=vm((2, 16, C), BF16),
        xin=vm((U - 1, UR, C), BF16), gin4=vm((U - 1, UR, C), BF16),
        halo_l=vm((4, 16, C), BF16), halo_r=vm((4, 16, C), BF16),
        cot=vm((R, C), BF16), ypad=vm((LAYERS, RP, C), BF16), dlow=vm((LAYERS, R, C), BF16),
        pre=vm((LAYERS, R, C), F32), hh=vm((LAYERS, 16, C), F32), hx=vm((LAYERS, 16, C), F32),
        mask=vm(((U - 1) * UR, LANES), F32), hmask=vm((16, LANES), F32), coef=vm((LAYERS, 8, C), F32),
        resd=vm((R, C), F32), act=vm((R, C), F32), du=vm((R, C), F32), drl=vm((R, C), BF16),
        dhl=vm((R + 16, C), BF16), ddpad=vm((RP, C), BF16),
        perm_l=vm((F, F), BF16), perm_s=vm((UR, UR), BF16), back_l=vm((F, F), BF16), back_s=vm((UR, UR), BF16),
        outp=vm((R, C), BF16), obuf=vm((U, F, C), BF16), gbuf=vm((U, F, C), BF16),
        small=vm((LANES, C), F32), slope=vm((LAYERS, R, C), BF16),
        fac=vm((2, 8, C), F32), facs=vm((2, 8, SE), F32), gsmall=vm((LANES, C), F32), ggb=vm((LAYERS, 8, C), F32),
        sums=vm((2, 8, C), F32), send_a=vm((S, 2, C), F32), send_b=vm((S, 2, C), F32),
        recv_core=vm((S, 2, C), F32), recv_chip=vm((S, chips + 1, 2, C), F32),
        hsend=vm((S, 2, 8, C), F32), dhh=vm((LAYERS, 16, C), F32),
        tsend=vm((2, 8, C), F32), trecv=vm((2, TM - 1, 8, C), F32),
        pool=vm((8, C), F32), gate=vm((8, C), F32), cvec=vm((8, C), F32),
        sem_loc=dma((3 + U,)), sem_cs=dma((S,)), sem_cr=dma((S + U - 1,)), sem_cot=dma((U - 1, 4)), sem_ks=dma((S,)), sem_kr=dma((S,)),
        sem_hs=dma((S, 2)), sem_hr=dma((S, 2)), sem_ts=dma((2,)), sem_tr=dma((2,)),
        sem_xs=dma((14,)), sem_xr=dma((5,)), sem_os=dma((2, U - 1)), sem_or=dma((2, U - 1, 4)),
    )
    if fast:
        scratch.update(
            wall=vm((MATS, Z, 2, Y, 2, SH, C), BF16), sall=vm((Z, 2, Y, 2, SH, 2 * LANES), BF16),
            pack=vm((LANES, LANES), F32), sem_gs=dma((MATS + 1, 3)), sem_gr=dma((MATS + 1, 3)),
        )
        for name, n, cols, kind in (("big", MATS, C, BF16), ("little", 2, LANES, F32)):
            scratch.update(
                {
                    name + "_send": vm((n, Z, 2, Y, 2, SH, cols), kind),
                    name + "_core": vm((n, Z, 2, Y, SH, cols), kind),
                    name + "_xsum": vm((n, 2, Z, Y, SH, cols), kind),
                    name + "_rx": vm((n, Z, Y, SH, cols), kind),
                    name + "_zsum": vm((n, Z, Y, SH, cols), kind),
                    name + "_rz": vm((n, Z * Y - 1, SH, cols), kind),
                    name + "_ss": dma((n, 3)),
                    name + "_rs": dma((n, 3)),
                }
            )
    if not fast:
        scratch.update(gp=vm((C, C), F32))
    names = list(operands) + list(outs) + list(scratch)
    out_s, gin_s, gmats, gpair, grows = pl.pallas_call(
        functools.partial(block_kernel, cfg, names),
        out_shape=tuple(outs.values()),
        in_specs=specs,
        out_specs=tuple(out_specs),
        scratch_shapes=list(scratch.values()),
        compiler_params=pltpu.CompilerParams(collective_id=0, has_side_effects=True, vmem_limit_bytes=63 << 20),
    )(*operands.values())
    if not fast:
        gmats = lax.psum_scatter(gmats, axes, scatter_dimension=1, tiled=True)
        gpair = lax.psum_scatter(gpair, axes, scatter_dimension=0, tiled=True)
        grows = lax.psum_scatter(grows, axes, scatter_dimension=1, tiled=True).T
    sizes_out = (
        ((U, F, C), BF16), ((U, F, C), BF16), ((LAYERS, KERNEL, SH), F32), ((LAYERS, SH, C), F32), ((LAYERS, SH), F32),
        ((LAYERS, SH), F32), ((SH, SE), F32), ((SH, SE), F32), ((SH, C), F32),
    )
    done = pl.pallas_call(
        functools.partial(finish_kernel, cfg),
        out_shape=tuple(sd(*size) for size in sizes_out),
        in_specs=[sm_spec] + [any_spec] * 5,
        out_specs=(any_spec,) * 9,
        scratch_shapes=[
            vm((2, U, F, C), BF16), vm((MATS, SH, C), F32), vm((SH, LANES), F32), vm((SH, LANES), F32),
            vm((LANES, LANES), F32),
            vm((LAYERS, KERNEL, SH), F32), vm((LAYERS, SH), F32), vm((LAYERS, SH), F32), vm((SH, SE), F32),
            vm((SH, SE), F32), dma((2, 2, U)), dma((10,)),
        ],
    )(lengths, out_s, gin_s, gmats, gpair, grows)
    return done[:7] + (done[7].T, done[8])


def solution(mesh):
    both = ("dp", "tm")
    rows, cols = P(both, None), P(None, both)
    frames = P("dp", "tm", None)
    taps, mats = P(None, None, both), P(None, both, None)
    sizes = (mesh.shape["dp"], mesh.shape["tm"])
    return jax.shard_map(
        functools.partial(local, sizes),
        mesh=mesh,
        in_specs=(frames, P(), taps, mats, cols, cols, rows, cols, rows, frames),
        out_specs=(frames, frames, taps, mats, cols, cols, rows, cols, rows),
        check_vma=False,
    )
```

```python
import functools

import jax
import jax.numpy as jnp
from jax import lax
from jax.experimental import pallas as pl
from jax.experimental.pallas import tpu as pltpu
from jax.sharding import PartitionSpec as P

MESH = pl.DeviceIdType.MESH
NORM_EPSILON = 1e-05
LANES = 128
HIGHEST = lax.Precision.HIGHEST
F32 = jnp.float32
BF16 = jnp.bfloat16


def dot(a, b, dims=((1,), (0,)), precision=None):
    return lax.dot_general(a, b, (dims, ((), ())), precision=precision, preferred_element_type=F32)


def logistic(v):
    return 0.5 * jnp.tanh(0.5 * v) + 0.5


def dot_parts(v, w, dims=((1,), (0,))):
    rows, parts = v.shape[0], []
    for _ in range(3):
        part = v.astype(BF16)
        parts.append(part.astype(F32))
        v = v - parts[-1]
    total = dot(jnp.concatenate(parts, axis=0).astype(BF16), w, dims)
    return total[0:rows] + total[rows : 2 * rows] + total[2 * rows :]


def block_kernel(cfg, names, *refs):
    DP, TM, U, F, C, SE, SH, LAYERS, KERNEL, fast = cfg
    env = dict(zip(names, refs, strict=True))
    lengths, x_any, g_any = env["lengths"], env["x_any"], env["g_any"]
    out_any, gin_any = env["out_any"], env["gin_any"]
    xv, xs, edge, xin, gin4 = env["xv"], env["xs"], env["edge"], env["xin"], env["gin4"]
    halo_l, halo_r, cot, ypad, dlow = env["halo_l"], env["halo_r"], env["cot"], env["ypad"], env["dlow"]
    pre, hh, mask, hmask, coef = env["pre"], env["hh"], env["mask"], env["hmask"], env["coef"]
    resd, act, du, drl = env["resd"], env["act"], env["du"], env["drl"]
    dn, gres_in = act, resd
    dhl, ddpad = env["dhl"], env["ddpad"]
    perm_l, perm_s, back_l, back_s = env["perm_l"], env["perm_s"], env["back_l"], env["back_s"]
    outp, obuf, gbuf, gp, small = env["outp"], env["obuf"], env["gbuf"], env.get("gp"), env["small"]
    sums, send_a, send_b, recv_core, recv_chip = (
        env["sums"], env["send_a"], env["send_b"], env["recv_core"], env["recv_chip"]
    )
    hsend, dhh, tsend, trecv = env["hsend"], env["dhh"], env["tsend"], env["trecv"]
    pool, gate, cvec, gsmall = env["pool"], env["gate"], env["cvec"], env["gsmall"]
    hx = env["hx"]
    slope, fac, facs = env["slope"], env["fac"], env["facs"]
    ggb = env["ggb"]
    sem_loc, sem_cs, sem_cr, sem_ks, sem_kr = (
        env["sem_loc"], env["sem_cs"], env["sem_cr"], env["sem_ks"], env["sem_kr"]
    )
    sem_cot = env["sem_cot"]
    sem_hs, sem_hr, sem_ts, sem_tr = env["sem_hs"], env["sem_hr"], env["sem_ts"], env["sem_tr"]
    sem_xs, sem_xr, sem_os, sem_or = env["sem_xs"], env["sem_xr"], env["sem_os"], env["sem_or"]
    MATS = LAYERS + 1
    AT_TAPS, AT_GAMMA = SE, SE + 8 * LAYERS
    AT_BETA = AT_GAMMA + 8
    NL = C // LANES
    UR = F // 4
    NU = 4 + (U - 1)
    NB = UR // 16
    R = NU * UR
    N_SRC = TM // 4
    dp, tm = lax.axis_index("dp"), lax.axis_index("tm")
    partner = tm + 1 - 2 * lax.rem(tm, 2)
    first, last = tm == 0, tm == TM - 1
    chips = [(a, 2 * b) for a in range(DP) for b in range(TM // 2) if a or b]
    n_chips = len(chips) + 1
    my_chip = dp * (TM // 2) + tm // 2

    def turns(v, n):
        bits = [1 << i for i in range(n.bit_length() - 1)] if n & (n - 1) == 0 else []
        return [(bit, bit * (1 - 2 * lax.rem(v // bit, 2))) for bit in bits]

    flips = {}

    def other(name, v, a, n):
        if name not in flips:
            flips[name] = turns(v, n)
        if not flips[name]:
            return lax.rem(v + a, n) if n > 1 else v
        for bit, step in flips[name]:
            if a & bit:
                v = v + step
        return v

    def at_chip(offset):
        return (lax.rem(dp + offset[0], DP), lax.rem(tm + offset[1], TM))

    def win(u):
        return u * UR if u < 4 else F + 64 + (u - 4) * (UR + 64)

    def seg_of(u):
        return 0 if u < 4 else u - 3

    def lane(j):
        return slice(j * LANES, (j + 1) * LANES)

    def each_lane(body):
        for j in range(NL):
            body(j, 0)

    def wide(v):
        return jnp.concatenate([v] * NL, axis=1)

    def remote(src, dst, ssem, rsem, dev):
        return pltpu.make_async_remote_copy(src, dst, ssem, rsem, device_id=dev, device_id_type=MESH)

    def total_wait(ref, sem):
        pltpu.make_async_copy(ref, ref, sem).wait()

    barrier = pltpu.get_barrier_semaphore()
    load_x = pltpu.make_async_copy(x_any, xv, sem_loc.at[0])
    load_x.start()
    others = [(0, b) for b in range(1, TM, 2)]
    for offset in chips + others:
        pl.semaphore_signal(barrier, inc=1, device_id=at_chip(offset), device_id_type=MESH)

    x, z, y, core = lax.rem(dp, 2), dp // 2, tm // 2, lax.rem(tm, 2)
    Y = TM // 2
    Z = DP // 2

    my_len = [lengths[dp * U + b] for b in range(U)]
    long_at = jnp.int32(0)
    for b in range(1, U):
        long_at = jnp.where(my_len[b] == F * TM, jnp.int32(b), long_at)
    short_at = [jnp.where(k < long_at, k, k + 1) for k in range(U - 1)]
    short_len = [lengths[dp * U + b] for b in range(U - 1)]
    short_len = [jnp.where(k < long_at, my_len[k], my_len[k + 1]) for k in range(U - 1)]
    count = lax.fori_loop(0, DP * U, lambda i, c: c + lengths[i], jnp.int32(0)).astype(F32)
    inv_count = 1.0 / jnp.full((1, LANES), count, F32)
    def make_masks():
        rows = lax.broadcasted_iota(jnp.int32, (UR, LANES), 0)
        time_s = (rows & 15) * NB + (rows >> 4) + tm * UR
        for k in range(U - 1):
            mask[k * UR : (k + 1) * UR, :] = jnp.where(time_s < short_len[k], 1.0, 0.0)
        e16 = lax.broadcasted_iota(jnp.int32, (16, LANES), 0)
        part = (e16 & 7) >> 1
        is_left = e16 < 8
        when = jnp.where(is_left, tm * UR - 2 + (e16 & 1), tm * UR + UR + (e16 & 1))
        bound = jnp.full((16, LANES), 1 << 30, jnp.int32)
        for k in range(U - 1):
            bound = jnp.where(part == k + 1, short_len[k], bound)
        inside = jnp.where(is_left, tm, TM - 1 - tm) > 0
        hmask[...] = jnp.where(inside & (when < bound), 1.0, 0.0)

    def one_hot(ref, size, to_time):
        n = size // 16
        r0 = lax.broadcasted_iota(jnp.int32, (UR, size), 0)
        r1 = lax.broadcasted_iota(jnp.int32, (UR, size), 1)
        for c in range(size // UR):
            a, b = (r1, r0 + c * UR) if to_time else (r0 + c * UR, r1)
            hit = b == (a & 15) * n + (a >> 4)
            ref[c * UR : (c + 1) * UR, :] = jnp.where(hit, 1.0, 0.0).astype(BF16)

    def zero_ends():
        @pl.when(first)
        def _():
            halo_l[...] = jnp.zeros(halo_l.shape, BF16)
            for l in range(LAYERS):
                hh[l, 0:8, :] = jnp.zeros((8, C), F32)
                dhh[l, 0:8, :] = jnp.zeros((8, C), F32)

        @pl.when(last)
        def _():
            halo_r[...] = jnp.zeros(halo_r.shape, BF16)
            for l in range(LAYERS):
                hh[l, 8:16, :] = jnp.zeros((8, C), F32)
                dhh[l, 8:16, :] = jnp.zeros((8, C), F32)

    def stage_short():
        @pl.when(tm < N_SRC)
        def _():
            for k in range(U - 1):
                def cp(c, _):
                    sl = pl.ds(pl.multiple_of(c * UR, UR), UR)
                    xs[k, sl, :] = xv[short_at[k], sl, :]
                    return 0
                lax.fori_loop(0, 4, cp, 0)

    def send_short(dst, half):
        def act_on(d):
            if half == 0:
                d.start()
            else:
                d.wait_send()

        @pl.when(tm < N_SRC)
        def _():
            for q in range(4):
                chunk = 4 * tm + q
                main = xs.at[:, q * UR : (q + 1) * UR, :]
                head = xs.at[:, q * UR : q * UR + 16, :]
                tail = xs.at[:, (q + 1) * UR - 16 : (q + 1) * UR, :]

                def go_main():
                    act_on(remote(main, dst, sem_xs.at[q], sem_xr.at[0], (dp, chunk)))

                def go_head():
                    act_on(remote(head, halo_r.at[1:U], sem_xs.at[4 + q], sem_xr.at[1], (dp, chunk - 1)))

                if q == 0:
                    pl.when(tm > 0)(go_main)
                    if half == 0:
                        @pl.when(tm == 0)
                        def _():
                            for k in range(U - 1):
                                dst[k] = xs[k, 0:UR, :]
                else:
                    go_main()
                if q < 2:
                    pl.when(tm > 0)(go_head)
                else:
                    go_head()
                if q == 1 and half == 0:
                    @pl.when(tm == 0)
                    def _():
                        for k in range(U - 1):
                            halo_r[1 + k] = xs[k, UR : UR + 16, :]

                @pl.when(chunk + 1 < TM)
                def _():
                    act_on(remote(tail, halo_l.at[1:U], sem_xs.at[8 + q], sem_xr.at[2], (dp, chunk + 1)))

    S2 = 2 * LAYERS

    def cot_piece(k, half):
        @pl.when(tm < N_SRC)
        def _():
            for q in range(4):
                chunk = 4 * tm + q
                src = xs.at[k, q * UR : (q + 1) * UR, :]
                copy = remote(src, gin4.at[k], sem_cot.at[k, q], sem_cr.at[S2 + k], (dp, chunk))
                go = copy.start if half == 0 else copy.wait_send
                if q == 0:
                    pl.when(tm > 0)(go)
                else:
                    go()

        if half == 0:
            @pl.when(tm == 0)
            def _():
                gin4[k] = xs[k, 0:UR, :]

    def recv_short(dst):
        @pl.when(tm > 0)
        def _():
            total_wait(dst, sem_xr.at[0])
            total_wait(halo_l.at[1:U], sem_xr.at[2])

            @pl.when(tm < TM - 1)
            def _():
                total_wait(halo_r.at[1:U], sem_xr.at[1])

    def edges(send, recv_l, recv_r, ssem, rsem, start):
        to_next = remote(send.at[1], recv_l, ssem.at[0], rsem.at[0], (dp, lax.rem(tm + 1, TM)))
        to_prev = remote(send.at[0], recv_r, ssem.at[1], rsem.at[1], (dp, lax.rem(tm + TM - 1, TM)))
        if start:
            pl.when(tm < TM - 1)(lambda: to_next.start())
            pl.when(tm > 0)(lambda: to_prev.start())
        else:
            @pl.when(tm < TM - 1)
            def _():
                to_next.wait_send()
                to_prev.wait_recv()

            @pl.when(tm > 0)
            def _():
                to_prev.wait_send()
                to_next.wait_recv()

    for name, v, n in (("dp", dp, DP), ("y", y, Y), ("z", z, Z)):
        other(name, v, 0, n)

    def plane_peers():
        return [(a, b) for a in reversed(range(Z)) for b in reversed(range(Y)) if a or b]

    def plane_peer(offset):
        pz, py = other("z", z, offset[0], Z), other("y", y, offset[1], Y)
        return pz, py, (2 * pz + x, 2 * py + core)

    across = (2 * z + 1 - x, tm)

    def gather_stage(buf, m, stage):
        ss, rs = env["sem_gs"].at[m, stage], env["sem_gr"].at[m, stage]
        if stage == 0:
            mine = buf.at[z, x, y, core]
            for offset in plane_peers():
                remote(mine, mine, ss, rs, plane_peer(offset)[2]).start()
        elif stage == 1:
            mine = buf.at[:, x, :, core]
            remote(mine, mine, ss, rs, across).start()
        else:
            mine = buf.at[:, :, :, core]
            remote(mine, mine, ss, rs, (dp, partner)).start()

    def gather_wait(buf, m, stage, sems):
        if stage == 0:
            size = env["little_rz"].at[0] if buf is sall else env["big_rz"].at[0]
            total_wait(size, sems.at[m, stage])
        elif stage == 1:
            total_wait(buf.at[:, 0, :, 0], sems.at[m, stage])
        else:
            total_wait(buf.at[:, :, :, 0], sems.at[m, stage])

    def gather_got(buf, m, stage):
        gather_wait(buf, m, stage, env["sem_gr"])

    def gather_left(buf, m):
        for stage in range(3):
            gather_wait(buf, m, stage, env["sem_gs"])

    if fast:
        wall, sall = env["wall"], env["sall"]
        halves = [(wall.at[0], 0)]

        def weights(m):
            return wall[m].reshape(C, C)

        pack = env["pack"]
        pack[...] = jnp.zeros(pack.shape, F32)
        for l in range(LAYERS):
            pack[AT_TAPS + 8 * l : AT_TAPS + 8 * l + KERNEL, 0:SH] = env["taps"][l].astype(F32)
        pack[AT_GAMMA : AT_GAMMA + LAYERS, 0:SH] = env["gamma"][...].astype(F32)
        pack[AT_BETA : AT_BETA + LAYERS, 0:SH] = env["beta"][...].astype(F32)
        turned = pack[...].T[0:SH]
        pack[0:SH, :] = turned
        pack[0:SH, 0:SE] = env["excite"][...].astype(F32)
        sall[z, x, y, core, :, 0:LANES] = pack[0:SH, :].astype(BF16)
        pack[0:SH, 0:SE] = env["squeeze"][...].astype(F32)
        sall[z, x, y, core, :, LANES : 2 * LANES] = pack[0:SH, :].astype(BF16)
        for l in range(LAYERS):
            wall[l, z, x, y, core] = env["point"][l]
        wall[LAYERS, z, x, y, core] = env["resid"][...]
    else:
        def weights(m):
            return env["mats"][m]

        small[...] = env["small_in"][...]

    def squeeze_all():
        if fast:
            return sall[...].reshape(C, 2 * LANES)[:, LANES : LANES + SE]
        return env["squeeze"][...]

    class Scatter:
        def __init__(self, name):
            self.send, self.core, self.xsum, self.rx, self.zsum, self.rz, self.ss, self.rs = (
                env[name + part] for part in ("_send", "_core", "_xsum", "_rx", "_zsum", "_rz", "_ss", "_rs")
            )
            self.dtype = self.send.dtype

        def go(self, m, stage):
            ss, rs = self.ss.at[m, stage], self.rs.at[m, stage]
            if stage == 0:
                remote(self.send.at[m, :, :, :, 1 - core], self.core.at[m], ss, rs, (dp, partner)).start()
            elif stage == 1:
                remote(self.xsum.at[m, 1 - x], self.rx.at[m], ss, rs, across).start()
            else:
                for i, offset in enumerate(plane_peers()):
                    pz, py, peer = plane_peer(offset)
                    remote(self.zsum.at[m, pz, py], self.rz.at[m, i], ss, rs, peer).start()

        def wait(self, m, stage, sems):
            total_wait((self.core.at[m], self.rx.at[m], self.rz.at[m])[stage], sems.at[m, stage])

        def left(self, m):
            for stage in range(3):
                self.wait(m, stage, self.ss)

        def core_to_x(self, m):
            self.wait(m, 0, self.rs)

            def body(i, _):
                v = self.send[m, i, :, :, core].astype(F32) + self.core[m, i].astype(F32)
                for k in range(2):
                    self.xsum[m, k, i] = v[k].astype(self.dtype)
                return 0

            lax.fori_loop(0, Z, body, 0)
            self.go(m, 1)

        def x_to_plane(self, m):
            self.x_sum(m)
            self.go(m, 2)

        def x_sum(self, m):
            self.wait(m, 1, self.rs)

            def body(i, _):
                v = self.xsum[m, x, i].astype(F32) + self.rx[m, i].astype(F32)
                self.zsum[m, i] = v.astype(self.dtype)
                return 0

            lax.fori_loop(0, Z, body, 0)

        def result(self, m):
            self.wait(m, 2, self.rs)
            v = self.zsum[m, z, y].astype(F32)
            for i in range(Z * Y - 1):
                v = v + self.rz[m, i].astype(F32)
            return v

    if fast:
        big, little = Scatter("big"), Scatter("little")

    def to_perm_long(src, dst, base):
        for u in range(4):
            o = base(u)
            dst[o : o + UR, :] = dot(perm_l[u * UR : (u + 1) * UR, :], src).astype(BF16)

    def to_perm_short(src, dst, base, masked):
        for k in range(U - 1):
            v = dot(perm_s[...], src[k])
            if masked:
                v = v * wide(mask[k * UR : (k + 1) * UR, :])
            o = base(4 + k)
            dst[o : o + UR, :] = v.astype(BF16)

    y0 = ypad.at[0]
    zero_ends()
    pl.semaphore_wait(barrier, len(chips) + len(others))
    if fast:
        gather_stage(sall, MATS, 0)
        for buf, m in halves:
            gather_stage(buf, m, 0)
    load_x.wait()
    edge[0] = xv[long_at, 0:16, :]
    edge[1] = xv[long_at, F - 16 : F, :]
    stage_short()
    edge_sems = (sem_xs.at[pl.ds(12, 2)], sem_xr.at[pl.ds(3, 2)])
    edges(edge, halo_l.at[0], halo_r.at[0], *edge_sems, True)
    send_short(xin, 0)
    if fast:
        for m in range(1, min(3, MATS)):
            gather_stage(wall.at[m], m, 0)
    one_hot(perm_l, F, False)
    one_hot(perm_s, UR, False)
    to_perm_long(xv[long_at], y0, lambda u: win(u) + 32)
    load_g = pltpu.make_async_copy(g_any, xv, sem_loc.at[0])
    load_g.start()
    make_masks()
    if fast:
        gather_got(sall, MATS, 0)
        gather_stage(sall, MATS, 1)
        for buf, m in halves:
            gather_got(buf, m, 0)
            gather_stage(buf, m, 1)
        gather_got(sall, MATS, 1)
        gather_stage(sall, MATS, 2)
        for buf, m in halves:
            gather_got(buf, m, 1)
            gather_stage(buf, m, 2)
        gather_got(sall, MATS, 2)
        for j in range(NL):
            part = sall[...].reshape(C, 2 * LANES)[j * LANES : (j + 1) * LANES, 0:LANES].astype(F32)
            small[:, j * LANES : (j + 1) * LANES] = part.T

    def fill_pads(ref, row0, n, j, b0, b1, b2, b3, halo, seg):
        e = lax.broadcasted_iota(jnp.int32, (16, LANES), 0)

        def put(at, v):
            ref[pl.ds(row0 + at * 16, 16), lane(j)] = v.astype(BF16)

        put(0, jnp.where(e == 0, halo[2 * seg : 2 * seg + 1], pltpu.roll(b2, 1, 0)))
        put(1, jnp.where(e == 0, halo[2 * seg + 1 : 2 * seg + 2], pltpu.roll(b3, 1, 0)))
        put(n + 2, jnp.where(e == 15, halo[8 + 2 * seg : 9 + 2 * seg], pltpu.roll(b0, 15, 0)))
        put(n + 3, jnp.where(e == 15, halo[9 + 2 * seg : 10 + 2 * seg], pltpu.roll(b1, 15, 0)))

    def pads_from(ref, j, halo, segs):
        for seg in segs:
            u0, u1 = (0, 3) if seg == 0 else (3 + seg, 3 + seg)
            n = F // 16 if seg == 0 else NB
            o0, o1 = win(u0) + 32, win(u1) + 32 + UR
            blk = [ref[o : o + 16, lane(j)].astype(F32) for o in (o0, o0 + 16, o1 - 32, o1 - 16)]
            fill_pads(ref, win(u0), n, j, *blk, halo, seg)

    def first_pads(segs):
        def body(j, _):
            none = jnp.zeros((2, LANES), F32)
            left = [halo_l[s, :, lane(j)].astype(F32)[14:16] if s in segs else none for s in range(4)]
            right = [halo_r[s, :, lane(j)].astype(F32)[0:2] if s in segs else none for s in range(4)]
            halo = jnp.where(hmask[...] > 0.0, jnp.concatenate(left + right, axis=0), 0.0)
            pads_from(y0, j, halo, segs)
            return 0

        each_lane(body)

    edges(edge, halo_l.at[0], halo_r.at[0], *edge_sems, False)
    first_pads([0])

    def shorts_arrive():
        if fast:
            gather_got(wall.at[1], 1, 0)
            gather_stage(wall.at[1], 1, 1)
        recv_short(xin)
        to_perm_short(xin, y0, lambda u: win(u) + 32, True)
        send_short(xin, 1)
        first_pads(range(1, U))

    def sync_core(s, meanwhile):
        d = remote(send_a.at[s], recv_core.at[s], sem_cs.at[s], sem_cr.at[s], (dp, partner))
        d.start()
        meanwhile()
        d.wait()
        send_b[s] = send_a[s] + recv_core[s]

    def sync_send(s):
        recv_chip[s, my_chip] = send_b[s]
        dst = recv_chip.at[s, my_chip]

        for a in reversed(range(DP)):
            for b in reversed(range(Y)):
                if a or b:
                    there = (other("dp", dp, a, DP), 2 * other("y", y, b, Y) + core)
                    remote(send_b.at[s], dst, sem_ks.at[s], sem_kr.at[s], there).start()

    def sync_done(s):
        others = recv_chip.at[s, 0 : n_chips - 1]
        total_wait(others, sem_kr.at[s])
        total_wait(others, sem_ks.at[s])
        terms = [recv_chip[s, i] for i in range(n_chips)]
        while len(terms) > 1:
            terms = [sum(terms[i : i + 2][1:], terms[i]) for i in range(0, len(terms), 2)]
        return terms[0]

    def tap_rows(l, j):
        group = small[pl.ds(pl.multiple_of(AT_TAPS + 8 * l, 8), 8), lane(j)]
        return [group[k : k + 1] for k in range(KERNEL)]

    LONG, SHORT = range(4), range(4, NU)

    def conv_pass(l, units):
        def body(j, _):
            w = tap_rows(l, j)
            for u in units:
                o = win(u)
                v = ypad[l, o : o + UR + 64, lane(j)].astype(F32)
                t = v[0:UR] * w[0]
                for k in range(1, KERNEL):
                    t = t + v[16 * k : 16 * k + UR] * w[k]
                if u >= 4:
                    t = t * mask[(u - 4) * UR : (u - 3) * UR, :]
                dlow[l, u * UR : (u + 1) * UR, lane(j)] = t.astype(BF16)
            return 0

        each_lane(body)

    def fold8(v):
        return jnp.sum(v.reshape(v.shape[0] // 8, 8, v.shape[1]), axis=0)

    def put_edges(src, l):
        for seg in range(4):
            base = 0 if seg == 0 else F + (seg - 1) * UR
            n = F if seg == 0 else UR
            for e in range(2):
                hsend[l, 1, 2 * seg + e : 2 * seg + e + 1, :] = src(base + n - 32 + 16 * e + 15)
                hsend[l, 0, 2 * seg + e : 2 * seg + e + 1, :] = src(base + 16 * e)

    def matmul_pass(l, units):
        r = slice(units[0] * UR, (units[-1] + 1) * UR)
        h = dot(dlow[l, r, :], weights(l))
        pre[l, r, :] = h
        s0, s1 = fold8(h), fold8(h * h)
        if units[0] > 0:
            s0, s1 = s0 + sums[0], s1 + sums[1]
        sums[0] = s0
        sums[1] = s1

    def send_stats(l):
        send_a[l, 0:1, :] = jnp.sum(sums[0], axis=0, keepdims=True)
        send_a[l, 1:2, :] = jnp.sum(sums[1], axis=0, keepdims=True)

    def act_pass(l):
        def body(j, _):
            a, b = coef[l, 0:1, lane(j)], coef[l, 1:2, lane(j)]
            for u in range(NU):
                v = pre[l, u * UR : (u + 1) * UR, lane(j)] * a + b
                v = v + v * jnp.tanh(v)
                if u >= 4:
                    v = v * mask[(u - 4) * UR : (u - 3) * UR, :]
                o = win(u) + 32
                ypad[l + 1, o : o + UR, lane(j)] = v.astype(BF16)
            v = hh[l, :, lane(j)] * a + b
            v = (v + v * jnp.tanh(v)) * hmask[...]
            pads_from(ypad.at[l + 1], j, v, range(U))
            return 0

        each_lane(body)

    def prep_pass(l):
        def body(j, _):
            a, b, m, i = (coef[l, r : r + 1, lane(j)] for r in range(4))
            for u in range(NU):
                rs = slice(u * UR, (u + 1) * UR)
                h = pre[l, rs, lane(j)]
                half = h * a + b
                t = jnp.tanh(half)
                v = (0.5 + 0.5 * t) * (1.0 + half * (1.0 - t))
                if u >= 4:
                    v = v * mask[(u - 4) * UR : (u - 3) * UR, :]
                slope[l, rs, lane(j)] = v.astype(BF16)
                pre[l, rs, lane(j)] = (h - m) * i
            hx[l, :, lane(j)] = (hh[l, :, lane(j)] - m) * i
            return 0

        each_lane(body)

    def layer(l, _):
        pl.when(l == 0)(shorts_arrive)
        if fast:
            gather_got(wall.at[l], l, 2)
        conv_pass(l, LONG)
        matmul_pass(l, LONG)
        conv_pass(l, SHORT)
        matmul_pass(l, SHORT)
        send_stats(l)

        def halo_out():
            put_edges(lambda row: pre[l, row : row + 1, :], l)
            edges(hsend.at[l], hh.at[l, 0:8], hh.at[l, 8:16], sem_hs.at[l], sem_hr.at[l], True)

        sync_core(l, halo_out)
        sync_send(l)

        if fast:
            gather_got(wall.at[l + 1], l + 1, 1)
            gather_stage(wall.at[l + 1], l + 1, 2)

        pl.when(l > 0)(lambda: prep_pass(l - 1))

        @pl.when(l == 0)
        def _():
            load_g.wait()
            stage_short()
            to_perm_long(xv[long_at], cot, lambda u: u * UR)

        @pl.when(l == 1)
        def _():
            one_hot(back_l, F, True)
            one_hot(back_s, UR, True)

        @pl.when(l == LAYERS - 1)
        def _():
            for k in range(U - 1):
                cot_piece(k, 1)

            @pl.when(tm > 0)
            def _():
                for k in range(U - 1):
                    total_wait(gin4.at[k], sem_cr.at[S2 + k])

            to_perm_short(gin4, cot, lambda u: u * UR, True)

        if fast:
            @pl.when(l + 2 < MATS)
            def _():
                gather_got(wall.at[l + 2], l + 2, 0)
                gather_stage(wall.at[l + 2], l + 2, 1)

            @pl.when(l + 3 < MATS)
            def _():
                gather_stage(wall.at[l + 3], l + 3, 0)

        total = sync_done(l)
        edges(hsend.at[l], hh.at[l, 0:8], hh.at[l, 8:16], sem_hs.at[l], sem_hr.at[l], False)
        for k in range(U - 1):
            pl.when(l == k)(functools.partial(cot_piece, k, 0))
        scale = wide(inv_count)
        mean = total[0:1] * scale
        var = total[1:2] * scale - mean * mean
        inv = lax.rsqrt(var + NORM_EPSILON)
        ga = small[pl.ds(AT_GAMMA + l, 1), :]
        a = ga * inv
        coef[l, 0:1, :] = 0.5 * a
        coef[l, 1:2, :] = 0.5 * (small[pl.ds(AT_BETA + l, 1), :] - mean * a)
        coef[l, 2:3, :] = mean
        coef[l, 3:4, :] = inv
        coef[l, 4:5, :] = a

        pl.when(l < LAYERS - 1)(lambda: act_pass(l))
        return 0

    lax.fori_loop(0, LAYERS, layer, 0)

    top = LAYERS - 1
    pool[...] = jnp.zeros(pool.shape, F32)

    def last_act(j, _):
        a, b = coef[top, 0:1, lane(j)], coef[top, 1:2, lane(j)]
        acc = None
        for u in range(NU):
            v = pre[top, u * UR : (u + 1) * UR, lane(j)] * a + b
            v = v + v * jnp.tanh(v)
            if u >= 4:
                v = v * mask[(u - 4) * UR : (u - 3) * UR, :]
            act[u * UR : (u + 1) * UR, lane(j)] = v
            f = fold8(v)
            acc = f if u == 0 or u >= 4 else acc + f
            if u >= 3:
                pool[u - 3 : u - 2, lane(j)] = jnp.sum(acc, axis=0, keepdims=True)
        return 0

    each_lane(last_act)

    def time_sum(s, value):
        tsend[s] = value
        ds = [remote(tsend.at[s], trecv.at[s, i - 1], sem_ts.at[s], sem_tr.at[s], (dp, lax.rem(tm + i, TM))) for i in range(1, TM)]
        for d in ds:
            d.start()

    def time_done(s):
        whole = trecv.at[s]
        total_wait(whole, sem_tr.at[s])
        total_wait(whole, sem_ts.at[s])
        total = tsend[s]
        for i in range(TM - 1):
            total = total + trecv[s, i]
        return total

    e8 = lax.broadcasted_iota(jnp.int32, (8, LANES), 0)
    len8 = jnp.full((8, LANES), F * TM, jnp.int32)
    for k in range(U - 1):
        len8 = jnp.where(e8 == k + 1, short_len[k], len8)
    inv_len = 1.0 / len8.astype(F32)
    live = jnp.where(e8 < U, 1.0, 0.0)
    time_sum(0, pool[...])
    prep_pass(top)
    if fast:
        gather_got(wall.at[LAYERS], LAYERS, 2)
    resd[0:F, :] = dot(ypad[0, 32 : 32 + F, :], weights(LAYERS))
    for u in SHORT:
        resd[u * UR : (u + 1) * UR, :] = dot(ypad[0, win(u) + 32 : win(u) + 32 + UR, :], weights(LAYERS))
    p = time_done(0) * wide(inv_len)
    sq = squeeze_all()
    ex = small[0:SE, :].astype(BF16)
    q = dot_parts(p, sq)
    sig_q = logistic(q)
    z_act = q * sig_q
    gate[...] = logistic(dot_parts(z_act, ex))
    pool[...] = jnp.zeros(pool.shape, F32)

    def top_pass(j, _):
        acc = None
        for u in range(NU):
            rs = slice(u * UR, (u + 1) * UR)
            seg = seg_of(u)
            av = act[rs, lane(j)]
            half = 0.5 * (av * gate[seg : seg + 1, lane(j)] + resd[rs, lane(j)])
            t = jnp.tanh(half)
            out = half + half * t
            slope = (0.5 + 0.5 * t) * (1.0 + half * (1.0 - t))
            dv = cot[rs, lane(j)].astype(F32) * slope
            if u >= 4:
                out = out * mask[(u - 4) * UR : (u - 3) * UR, :]
            outp[rs, lane(j)] = out.astype(BF16)
            du[rs, lane(j)] = dv
            drl[rs, lane(j)] = dv.astype(BF16)
            f = fold8(dv * av)
            acc = f if u == 0 or u >= 4 else acc + f
            if u >= 3:
                pool[u - 3 : u - 2, lane(j)] = jnp.sum(acc, axis=0, keepdims=True)
        return 0

    each_lane(top_pass)
    time_sum(1, pool[...])

    def back_long(buf, src):
        for u in range(4):
            buf[0, u * UR : (u + 1) * UR, :] = dot(back_l[u * UR : (u + 1) * UR, :], src[0:F, :]).astype(BF16)

    def back_short(buf, stage, src):
        for k in range(U - 1):
            stage[k] = dot(back_s[...], src[F + k * UR : F + (k + 1) * UR, :]).astype(BF16)

        @pl.when(tm >= N_SRC)
        def _():
            for k in range(U - 1):
                buf[1 + k] = jnp.zeros((F, C), BF16)

        @pl.when(first)
        def _():
            for k in range(U - 1):
                buf[1 + k, 0:UR, :] = stage[k]

    def back_piece(buf, stage, sems, rsems, k):
        owner, q = tm // 4, lax.rem(tm, 4)
        dst = buf.at[1 + k, pl.ds(pl.multiple_of(q * UR, UR), UR), :]
        return remote(stage.at[k], dst, sems.at[k], rsems.at[k, q], (dp, owner))

    def back_send(buf, stage, sems, rsems, ks):
        @pl.when(tm > 0)
        def _():
            for k in ks:
                back_piece(buf, stage, sems, rsems, k).start()

    def back_left(buf, stage, sems, rsems):
        @pl.when(tm > 0)
        def _():
            for k in range(U - 1):
                back_piece(buf, stage, sems, rsems, k).wait_send()

    def back_arrived(buf, rsems, k):
        @pl.when(tm < N_SRC)
        def _():
            for i in range(4):
                got = functools.partial(total_wait, buf.at[1 + k, i * UR : (i + 1) * UR, :], rsems.at[k, i])
                if i == 0:
                    pl.when(tm > 0)(got)
                else:
                    got()

    def back_done(buf, stage, sems, rsems):
        back_left(buf, stage, sems, rsems)
        for k in range(U - 1):
            back_arrived(buf, rsems, k)

    put_out = pltpu.make_async_copy(obuf, out_any, sem_loc.at[2])
    back_long(obuf, outp)
    back_short(obuf, xin, outp)

    def xrows(u):
        o = win(u) + 32
        return ypad[0, o : o + UR, :]

    def put_grad(m, total):
        if fast:
            big.send[m] = total.astype(BF16).reshape(Z, 2, Y, 2, SH, C)
            big.go(m, 0)
        else:
            gp[...] = total
            pltpu.make_async_copy(gp, env["gmats"].at[m], sem_loc.at[1]).start()

    def grad_gone():
        if not fast:
            pltpu.make_async_copy(gp, env["gmats"].at[0], sem_loc.at[1]).wait()

    def xrows(u):
        o = win(u) + 32
        return ypad[0, o : o + UR, :]

    def resid_grads():
        total = dot(ypad[0, 32 : 32 + F, :], drl[0:F, :], ((0,), (0,)))
        for u in SHORT:
            total = total + dot(xrows(u), drl[u * UR : (u + 1) * UR, :], ((0,), (0,)))
        put_grad(LAYERS, total)
        gres_in[...] = dot(drl[...], weights(LAYERS), ((1,), (1,)))

    resid_grads()
    dg = time_done(1)
    gv = gate[...]
    de = dg * gv * (1.0 - gv) * wide(live)
    dz = dot_parts(de, ex, ((1,), (1,)))
    dq = dz * sig_q * (1.0 + q * (1.0 - sig_q))
    cvec[...] = dot_parts(dq, sq, ((1,), (1,))) * wide(inv_len)
    fac[0], fac[1] = p, de
    facs[0], facs[1] = z_act, dq

    def pair_grads():
        lead = jnp.where(first, 1.0, 0.0)
        zero = jnp.zeros((C, LANES - 2 * SE), F32)
        pair = [dot(fac[1 - i], facs[i], ((0,), (0,)), precision=HIGHEST) for i in range(2)]
        pair = jnp.concatenate(pair + [zero] * (LANES > 2 * SE), axis=1) * lead
        if fast:
            little.send[0] = pair.reshape(Z, 2, Y, 2, SH, LANES)
            little.go(0, 0)
        else:
            env["gpair"][...] = pair

    def back_sums(l, s, grad_of):
        def body(j, _):
            acc0 = acc1 = None
            make = grad_of(j)
            for u in range(NU):
                rs = slice(u * UR, (u + 1) * UR)
                v = make(u) * slope[l, rs, lane(j)].astype(F32)
                xc = pre[l, rs, lane(j)]
                dn[u * UR : (u + 1) * UR, lane(j)] = v
                f0, f1 = fold8(v), fold8(v * xc)
                acc0 = f0 if u == 0 else acc0 + f0
                acc1 = f1 if u == 0 else acc1 + f1
            send_a[s, 0:1, lane(j)] = jnp.sum(acc0, axis=0, keepdims=True)
            send_a[s, 1:2, lane(j)] = jnp.sum(acc1, axis=0, keepdims=True)
            return 0

        each_lane(body)

    def top_grad(j):
        def make(u):
            seg = seg_of(u)
            return du[u * UR : (u + 1) * UR, lane(j)] * gate[seg : seg + 1, lane(j)] + cvec[seg : seg + 1, lane(j)]
        return make

    def conv_grad(l):
        def outer(j):
            w = tap_rows(l, j)

            def make(u):
                o = win(u)
                v = ddpad[o : o + UR + 64, lane(j)].astype(F32)
                t = v[64 : 64 + UR] * w[0]
                for k in range(1, KERNEL):
                    t = t + v[64 - 16 * k : 64 - 16 * k + UR] * w[k]
                return t
            return make
        return outer

    back_sums(top, LAYERS, top_grad)

    def point_grad(l):
        grad_gone()
        put_grad(l, dot(dlow[l], dhl[0:R, :], ((0,), (0,))))

    def depth_grad(l):
        def body(j, _):
            acc = [None] * KERNEL
            for u in range(NU):
                o = win(u)
                v = ypad[l, o : o + UR + 64, lane(j)].astype(F32)
                g = ddpad[o + 32 : o + 32 + UR, lane(j)].astype(F32)
                for k in range(KERNEL):
                    f = fold8(v[16 * k : 16 * k + UR] * g)
                    acc[k] = f if u == 0 else acc[k] + f
            rows = [jnp.sum(acc[k], axis=0, keepdims=True) for k in range(KERNEL)]
            rows.append(jnp.zeros((8 - KERNEL, LANES), F32))
            at = pl.ds(pl.multiple_of(AT_TAPS + 8 * l, 8), 8)
            gsmall[at, lane(j)] = jnp.concatenate(rows, axis=0)
            return 0

        each_lane(body)
    def dh_pass(l, units):
        def body(j, _):
            a, k1, k0 = (coef[l, r : r + 1, lane(j)] for r in (4, 5, 6))
            for u in units:
                rs = slice(u * UR, (u + 1) * UR)
                v = dn[rs, lane(j)] * a - (pre[l, rs, lane(j)] * k1 + k0)
                if u >= 4:
                    v = v * mask[(u - 4) * UR : (u - 3) * UR, :]
                dhl[rs, lane(j)] = v.astype(BF16)
            if units is SHORT:
                v = (dhh[l, :, lane(j)] * a - (hx[l, :, lane(j)] * k1 + k0)) * hmask[...]
                dhl[R : R + 16, lane(j)] = v.astype(BF16)
            return 0

        each_lane(body)

    def dd_pass(l):
        dh_pass(l, LONG)
        ddpad[32 : 32 + F, :] = dot(dhl[0:F, :], weights(l), ((1,), (1,))).astype(BF16)
        dh_pass(l, SHORT)
        v = dot(dhl[F : R + 16, :], weights(l), ((1,), (1,)))
        for u in SHORT:
            ddpad[win(u) + 32 : win(u) + 32 + UR, :] = v[(u - 4) * UR : (u - 3) * UR].astype(BF16)
        hx[l] = v[R - F : R - F + 16].astype(BF16).astype(F32)

        def pad(j, _):
            pads_from(ddpad, j, hx[l, :, lane(j)], range(U))
            return 0

        each_lane(pad)

    def back_layer(step, _):
        l = top - step
        s = LAYERS + step

        def halo_out():
            put_edges(lambda row: dn[row : row + 1, :], s)
            edges(hsend.at[s], dhh.at[l, 0:8], dhh.at[l, 8:16], sem_hs.at[s], sem_hr.at[s], True)

        sync_core(s, halo_out)
        sync_send(s)

        @pl.when(step > 0)
        def _():
            point_grad(l + 1)
            depth_grad(l + 1)

        pl.when(step == 0)(pair_grads)

        @pl.when(step == LAYERS - 1)
        def _():
            back_done(obuf, xin, sem_os.at[0], sem_or.at[0])
            put_out.start()

        if fast:
            @pl.when(step == 1)
            def _():
                little.core_to_x(0)

            @pl.when(step == 2)
            def _():
                little.x_to_plane(0)

            @pl.when(step > 0)
            def _():
                big.x_sum(l + 2)

            @pl.when(step > 1)
            def _():
                env["keep"][l + 3] = big.result(l + 3)

            big.core_to_x(l + 1)

        if fast:
            pl.when(step > 0)(lambda: big.go(l + 2, 2))

        total = sync_done(s)
        @pl.when(step < U - 1)
        def _():
            back_send(obuf, xin, sem_os.at[0], sem_or.at[0], [step])

        edges(hsend.at[s], dhh.at[l, 0:8], dhh.at[l, 8:16], sem_hs.at[s], sem_hr.at[s], False)
        ggb[l, 0:2, :] = total
        a = coef[l, 4:5, :]
        coef[l, 5:6, :] = a * total[1:2] * wide(inv_count)
        coef[l, 6:7, :] = a * total[0:1] * wide(inv_count)

        dd_pass(l)

        @pl.when(l > 0)
        def _():
            back_sums(l - 1, s + 1, conv_grad(l - 1))
        return 0

    def run_back():
        lax.fori_loop(0, LAYERS, back_layer, 0)

    conv_grad_of = conv_grad

    def conv_grad(l):
        return conv_grad_of(l + 1)

    gsmall[...] = jnp.zeros(gsmall.shape, F32)
    run_back()
    lead_all = jnp.where(first & (dp == 0), 1.0, 0.0)
    for l in range(LAYERS):
        gsmall[AT_BETA + l : AT_BETA + l + 1, :] = ggb[l, 0:1, :] * lead_all
        gsmall[AT_GAMMA + l : AT_GAMMA + l + 1, :] = ggb[l, 1:2, :] * lead_all
    def final_pass(units):
        def body(j, _):
            make = conv_grad_of(0)(j)
            for u in units:
                rs = slice(u * UR, (u + 1) * UR)
                v = make(u)
                if u >= 4:
                    v = v * mask[(u - 4) * UR : (u - 3) * UR, :]
                outp[rs, lane(j)] = (v + gres_in[rs, lane(j)]).astype(BF16)
            return 0

        each_lane(body)

    final_pass(SHORT)
    back_short(gbuf, gin4, outp)
    back_send(gbuf, gin4, sem_os.at[1], sem_or.at[1], range(U - 1))
    point_grad(0)
    if fast:
        big.core_to_x(0)
    depth_grad(0)
    if fast:
        for j in range(NL):
            rows = gsmall[:, j * LANES : (j + 1) * LANES].T
            part = rows.reshape(LANES // (2 * SH), 2, SH, LANES)
            per = LANES // (2 * SH)
            for i in range(per):
                n = j * per + i
                little.send[1, n // (2 * Y), n // Y % 2, n % Y] = part[i]
        little.go(1, 0)
        big.x_to_plane(1)
    final_pass(LONG)
    back_long(gbuf, outp)
    put_gin = [pltpu.make_async_copy(gbuf.at[k], gin_any.at[k], sem_loc.at[3 + k]) for k in range(U)]
    put_gin[0].start()
    if fast:
        little.core_to_x(1)
        env["keep"][2] = big.result(2)
        big.x_to_plane(0)
        little.x_to_plane(1)
        env["keep_s"][0] = little.result(0)
        env["keep"][1] = big.result(1)
        early = pltpu.make_async_copy(env["keep"].at[1:MATS], env["gmats"].at[1:MATS], env["sem_keep"].at[0])
        early.start()
        for m in range(1, MATS):
            big.left(m)
            gather_left(wall.at[m], m)
        for buf, m in halves:
            gather_left(buf, m)
        little.left(0)
        gather_left(sall, MATS)
    else:
        env["grows"][...] = gsmall[...]
    for k in range(U - 1):
        back_arrived(gbuf, sem_or.at[1], k)
        put_gin[1 + k].start()
    back_left(gbuf, gin4, sem_os.at[1], sem_or.at[1])
    if fast:
        env["keep"][0] = big.result(0)
        late = [pltpu.make_async_copy(env["keep"].at[0], env["gmats"].at[0], env["sem_keep"].at[1])]
        late[0].start()
        env["keep_s"][1] = little.result(1)
        late.append(pltpu.make_async_copy(env["keep_s"].at[0], env["gpair"], env["sem_keep"].at[2]))
        late.append(pltpu.make_async_copy(env["keep_s"].at[1], env["grows"], env["sem_keep"].at[3]))
        late[1].start()
        late[2].start()
        big.left(0)
        little.left(1)
    grad_gone()
    put_out.wait()
    for c in put_gin:
        c.wait()
    if fast:
        for c in [early] + late:
            c.wait()


def finish_kernel(cfg, lengths, out_s, gin_s, gmats_any, gpair_any, grows_any, *rest):
    DP, TM, U, F, C, SE, SH, LAYERS, KERNEL, fast = cfg
    out, gin, gdepth_any, gpoint, ggamma_any, gbeta_any, gsq_any, gex_any, gres = rest[:9]
    hold, gmats, gpair, grows, turn, gdepth, ggamma, gbeta, gsq, gex, sems, sems_g = rest[9:]
    dp = lax.axis_index("dp")
    long_at = jnp.int32(0)
    for b in range(1, U):
        long_at = jnp.where(lengths[dp * U + b] == F * TM, jnp.int32(b), long_at)
    copies = []
    loads = [
        pltpu.make_async_copy(src, dst, sems_g.at[i])
        for i, (src, dst) in enumerate(((gmats_any, gmats), (gpair_any, gpair), (grows_any, grows)))
    ]
    for c in loads:
        c.start()
    for b in range(U):
        slot = jnp.where(b == long_at, 0, jnp.where(b < long_at, b + 1, b))
        for i, (src, dst) in enumerate(((out_s, out), (gin_s, gin))):
            get = pltpu.make_async_copy(src.at[slot], hold.at[i, b], sems.at[0, i, b])
            put = pltpu.make_async_copy(hold.at[i, b], dst.at[b], sems.at[1, i, b])
            copies.append((get, put))
            get.start()
    loads[0].wait()
    results = [
        pltpu.make_async_copy(gmats.at[0:LAYERS], gpoint, sems_g.at[3]),
        pltpu.make_async_copy(gmats.at[LAYERS], gres, sems_g.at[4]),
    ]
    for c in results:
        c.start()
    for get, put in copies:
        get.wait()
        put.start()
    for c in loads[1:]:
        c.wait()
    at_taps = SE
    at_gamma = SE + 8 * LAYERS
    at_beta = at_gamma + 8
    gsq[...] = gpair[:, SE : 2 * SE]
    gex[...] = gpair[:, 0:SE]
    turn[...] = jnp.zeros(turn.shape, F32)
    turn[0:SH] = grows[...]
    turn[...] = turn[...].T
    for l in range(LAYERS):
        gdepth[l] = turn[at_taps + 8 * l : at_taps + 8 * l + KERNEL, 0:SH]
    ggamma[...] = turn[at_gamma : at_gamma + LAYERS, 0:SH]
    gbeta[...] = turn[at_beta : at_beta + LAYERS, 0:SH]
    pairs = ((gdepth, gdepth_any), (ggamma, ggamma_any), (gbeta, gbeta_any), (gsq, gsq_any), (gex, gex_any))
    for i, (src, dst) in enumerate(pairs):
        results.append(pltpu.make_async_copy(src, dst, sems_g.at[5 + i]))
        results[-1].start()
    for _, put in copies:
        put.wait()
    for c in results:
        c.wait()


def local(sizes, inputs, lengths, depth_w, point_w, gamma, beta, squeeze_w, excite_w, resid_w, cotangent):
    DP, TM = sizes
    U, F, C = inputs.shape
    LAYERS, KERNEL, SH = depth_w.shape
    SE = squeeze_w.shape[1]
    UR = F // 4
    NU = 4 + U - 1
    R = NU * UR
    RP = F + 64 + (U - 1) * (UR + 64)
    S = 2 * LAYERS
    chips = DP * (TM // 2) - 1
    axes = ("dp", "tm")
    fast = SH % 16 == 0 and DP % 2 == 0 and DP > 2
    Z, Y = DP // 2, TM // 2
    MATS = LAYERS + 1
    vm = pltpu.VMEM
    dma = pltpu.SemaphoreType.DMA
    any_spec = pl.BlockSpec(memory_space=pl.ANY)
    vm_spec = pl.BlockSpec(memory_space=pltpu.VMEM)
    sm_spec = pl.BlockSpec(memory_space=pltpu.SMEM)
    sd = jax.ShapeDtypeStruct
    cfg = (DP, TM, U, F, C, SE, SH, LAYERS, KERNEL, fast)
    at_gamma = SE + 8 * LAYERS
    operands = dict(lengths=lengths, x_any=inputs, g_any=cotangent)
    specs = [sm_spec, any_spec, any_spec]
    outs = dict(out_any=sd((U, F, C), BF16), gin_any=sd((U, F, C), BF16))
    out_specs = [any_spec, any_spec]
    if fast:
        operands.update(
            point=point_w, taps=depth_w, gamma=gamma, beta=beta, squeeze=squeeze_w, excite=excite_w.T, resid=resid_w
        )
        specs += [vm_spec] * 7
        outs.update(gmats=sd((MATS, SH, C), F32), gpair=sd((SH, LANES), F32), grows=sd((SH, LANES), F32))
        out_specs += [any_spec] * 3
    else:
        mats = jnp.concatenate([point_w, resid_w[None]], axis=0)
        depth_rows = jnp.pad(depth_w, ((0, 0), (0, 8 - KERNEL), (0, 0))).reshape(8 * LAYERS, SH)
        fill = ((0, 8 - LAYERS), (0, 0))
        rows = jnp.concatenate([excite_w, depth_rows, jnp.pad(gamma, fill), jnp.pad(beta, fill)], axis=0)
        rows = jnp.pad(rows, ((0, LANES - rows.shape[0]), (0, 0)))
        operands.update(
            mats=lax.all_gather(mats, axes, axis=1, tiled=True),
            small_in=lax.all_gather(rows, axes, axis=1, tiled=True).astype(F32),
            squeeze=lax.all_gather(squeeze_w, axes, axis=0, tiled=True),
        )
        specs += [vm_spec] * 3
        outs.update(gmats=sd((MATS, C, C), F32), gpair=sd((C, LANES), F32), grows=sd((LANES, C), F32))
        out_specs += [any_spec, vm_spec, vm_spec]
    scratch = dict(
        xv=vm((U, F, C), BF16), xs=vm((U - 1, F, C), BF16), edge=vm((2, 16, C), BF16),
        xin=vm((U - 1, UR, C), BF16), gin4=vm((U - 1, UR, C), BF16),
        halo_l=vm((4, 16, C), BF16), halo_r=vm((4, 16, C), BF16),
        cot=vm((R, C), BF16), ypad=vm((LAYERS, RP, C), BF16), dlow=vm((LAYERS, R, C), BF16),
        pre=vm((LAYERS, R, C), F32), hh=vm((LAYERS, 16, C), F32), hx=vm((LAYERS, 16, C), F32),
        mask=vm(((U - 1) * UR, LANES), F32), hmask=vm((16, LANES), F32), coef=vm((LAYERS, 8, C), F32),
        resd=vm((R, C), F32), act=vm((R, C), F32), du=vm((R, C), F32), drl=vm((R, C), BF16),
        dhl=vm((R + 16, C), BF16), ddpad=vm((RP, C), BF16),
        perm_l=vm((F, F), BF16), perm_s=vm((UR, UR), BF16), back_l=vm((F, F), BF16), back_s=vm((UR, UR), BF16),
        outp=vm((R, C), BF16), obuf=vm((U, F, C), BF16), gbuf=vm((U, F, C), BF16),
        small=vm((LANES, C), F32), slope=vm((LAYERS, R, C), BF16),
        fac=vm((2, 8, C), F32), facs=vm((2, 8, SE), F32), gsmall=vm((LANES, C), F32), ggb=vm((LAYERS, 8, C), F32),
        sums=vm((2, 8, C), F32), send_a=vm((S, 2, C), F32), send_b=vm((S, 2, C), F32),
        recv_core=vm((S, 2, C), F32), recv_chip=vm((S, chips + 1, 2, C), F32),
        hsend=vm((S, 2, 8, C), F32), dhh=vm((LAYERS, 16, C), F32),
        tsend=vm((2, 8, C), F32), trecv=vm((2, TM - 1, 8, C), F32),
        pool=vm((8, C), F32), gate=vm((8, C), F32), cvec=vm((8, C), F32),
        sem_loc=dma((3 + U,)), sem_cs=dma((S,)), sem_cr=dma((S + U - 1,)), sem_cot=dma((U - 1, 4)), sem_ks=dma((S,)), sem_kr=dma((S,)),
        sem_hs=dma((S, 2)), sem_hr=dma((S, 2)), sem_ts=dma((2,)), sem_tr=dma((2,)),
        sem_xs=dma((14,)), sem_xr=dma((5,)), sem_os=dma((2, U - 1)), sem_or=dma((2, U - 1, 4)),
    )
    if fast:
        scratch.update(
            wall=vm((MATS, Z, 2, Y, 2, SH, C), BF16), sall=vm((Z, 2, Y, 2, SH, 2 * LANES), BF16),
            pack=vm((LANES, LANES), F32), keep=vm((MATS, SH, C), F32), keep_s=vm((2, SH, LANES), F32),
            sem_keep=dma((4,)), sem_gs=dma((MATS + 1, 3)), sem_gr=dma((MATS + 1, 3)),
        )
        for name, n, cols, kind in (("big", MATS, C, BF16), ("little", 2, LANES, F32)):
            scratch.update(
                {
                    name + "_send": vm((n, Z, 2, Y, 2, SH, cols), kind),
                    name + "_core": vm((n, Z, 2, Y, SH, cols), kind),
                    name + "_xsum": vm((n, 2, Z, Y, SH, cols), kind),
                    name + "_rx": vm((n, Z, Y, SH, cols), kind),
                    name + "_zsum": vm((n, Z, Y, SH, cols), kind),
                    name + "_rz": vm((n, Z * Y - 1, SH, cols), kind),
                    name + "_ss": dma((n, 3)),
                    name + "_rs": dma((n, 3)),
                }
            )
    if not fast:
        scratch.update(gp=vm((C, C), F32))
    names = list(operands) + list(outs) + list(scratch)
    out_s, gin_s, gmats, gpair, grows = pl.pallas_call(
        functools.partial(block_kernel, cfg, names),
        out_shape=tuple(outs.values()),
        in_specs=specs,
        out_specs=tuple(out_specs),
        scratch_shapes=list(scratch.values()),
        compiler_params=pltpu.CompilerParams(collective_id=0, has_side_effects=True, vmem_limit_bytes=63 << 20),
    )(*operands.values())
    if not fast:
        gmats = lax.psum_scatter(gmats, axes, scatter_dimension=1, tiled=True)
        gpair = lax.psum_scatter(gpair, axes, scatter_dimension=0, tiled=True)
        grows = lax.psum_scatter(grows, axes, scatter_dimension=1, tiled=True).T
    sizes_out = (
        ((U, F, C), BF16), ((U, F, C), BF16), ((LAYERS, KERNEL, SH), F32), ((LAYERS, SH, C), F32), ((LAYERS, SH), F32),
        ((LAYERS, SH), F32), ((SH, SE), F32), ((SH, SE), F32), ((SH, C), F32),
    )
    done = pl.pallas_call(
        functools.partial(finish_kernel, cfg),
        out_shape=tuple(sd(*size) for size in sizes_out),
        in_specs=[sm_spec] + [any_spec] * 5,
        out_specs=(any_spec,) * 9,
        scratch_shapes=[
            vm((2, U, F, C), BF16), vm((MATS, SH, C), F32), vm((SH, LANES), F32), vm((SH, LANES), F32),
            vm((LANES, LANES), F32),
            vm((LAYERS, KERNEL, SH), F32), vm((LAYERS, SH), F32), vm((LAYERS, SH), F32), vm((SH, SE), F32),
            vm((SH, SE), F32), dma((2, 2, U)), dma((10,)),
        ],
    )(lengths, out_s, gin_s, gmats, gpair, grows)
    return done[:7] + (done[7].T, done[8])


def solution(mesh):
    both = ("dp", "tm")
    rows, cols = P(both, None), P(None, both)
    frames = P("dp", "tm", None)
    taps, mats = P(None, None, both), P(None, both, None)
    sizes = (mesh.shape["dp"], mesh.shape["tm"])
    return jax.shard_map(
        functools.partial(local, sizes),
        mesh=mesh,
        in_specs=(frames, P(), taps, mats, cols, cols, rows, cols, rows, frames),
        out_specs=(frames, frames, taps, mats, cols, cols, rows, cols, rows),
        check_vma=False,
    )
```

```python
import functools

import jax
import jax.numpy as jnp
from jax import lax
from jax.experimental import pallas as pl
from jax.experimental.pallas import tpu as pltpu
from jax.sharding import PartitionSpec as P

MESH = pl.DeviceIdType.MESH
NORM_EPSILON = 1e-05
LANES = 128
HIGHEST = lax.Precision.HIGHEST
F32 = jnp.float32
BF16 = jnp.bfloat16


def dot(a, b, dims=((1,), (0,)), precision=None):
    return lax.dot_general(a, b, (dims, ((), ())), precision=precision, preferred_element_type=F32)


def logistic(v):
    return 0.5 * jnp.tanh(0.5 * v) + 0.5


def dot_parts(v, w, dims=((1,), (0,))):
    rows, parts = v.shape[0], []
    for _ in range(3):
        part = v.astype(BF16)
        parts.append(part.astype(F32))
        v = v - parts[-1]
    total = dot(jnp.concatenate(parts, axis=0).astype(BF16), w, dims)
    return total[0:rows] + total[rows : 2 * rows] + total[2 * rows :]


def block_kernel(cfg, names, *refs):
    DP, TM, U, F, C, SE, SH, LAYERS, KERNEL, fast = cfg
    env = dict(zip(names, refs, strict=True))
    lengths, x_any, g_any = env["lengths"], env["x_any"], env["g_any"]
    out_any, gin_any = env["out_any"], env["gin_any"]
    xv, xs, edge, xin, gin4 = env["xv"], env["xs"], env["edge"], env["xin"], env["gin4"]
    halo_l, halo_r, cot, ypad, dlow = env["halo_l"], env["halo_r"], env["cot"], env["ypad"], env["dlow"]
    pre, hh, mask, hmask, coef = env["pre"], env["hh"], env["mask"], env["hmask"], env["coef"]
    resd, act, du, drl = env["resd"], env["act"], env["du"], env["drl"]
    dn, gres_in = act, resd
    dhl, ddpad = env["dhl"], env["ddpad"]
    perm_l, perm_s, back_l, back_s = env["perm_l"], env["perm_s"], env["back_l"], env["back_s"]
    outp, obuf, gbuf, gp, small = env["outp"], env["obuf"], env["gbuf"], env.get("gp"), env["small"]
    sums, send_a, send_b, recv_core, recv_chip = (
        env["sums"], env["send_a"], env["send_b"], env["recv_core"], env["recv_chip"]
    )
    hsend, dhh, tsend, trecv = env["hsend"], env["dhh"], env["tsend"], env["trecv"]
    pool, gate, cvec, gsmall = env["pool"], env["gate"], env["cvec"], env["gsmall"]
    hx = env["hx"]
    slope, fac, facs = env["slope"], env["fac"], env["facs"]
    ggb = env["ggb"]
    sem_loc, sem_cs, sem_cr, sem_ks, sem_kr = (
        env["sem_loc"], env["sem_cs"], env["sem_cr"], env["sem_ks"], env["sem_kr"]
    )
    sem_cot = env["sem_cot"]
    sem_hs, sem_hr, sem_ts, sem_tr = env["sem_hs"], env["sem_hr"], env["sem_ts"], env["sem_tr"]
    sem_xs, sem_xr, sem_os, sem_or = env["sem_xs"], env["sem_xr"], env["sem_os"], env["sem_or"]
    MATS = LAYERS + 1
    AT_TAPS, AT_GAMMA = SE, SE + 8 * LAYERS
    AT_BETA = AT_GAMMA + 8
    NL = C // LANES
    UR = F // 4
    NU = 4 + (U - 1)
    NB = UR // 16
    R = NU * UR
    N_SRC = TM // 4
    dp, tm = lax.axis_index("dp"), lax.axis_index("tm")
    partner = tm + 1 - 2 * lax.rem(tm, 2)
    first, last = tm == 0, tm == TM - 1
    chips = [(a, 2 * b) for a in range(DP) for b in range(TM // 2) if a or b]
    n_chips = len(chips) + 1
    my_chip = dp * (TM // 2) + tm // 2

    def turns(v, n):
        bits = [1 << i for i in range(n.bit_length() - 1)] if n & (n - 1) == 0 else []
        return [(bit, bit * (1 - 2 * lax.rem(v // bit, 2))) for bit in bits]

    flips = {}

    def other(name, v, a, n):
        if name not in flips:
            flips[name] = turns(v, n)
        if not flips[name]:
            return lax.rem(v + a, n) if n > 1 else v
        for bit, step in flips[name]:
            if a & bit:
                v = v + step
        return v

    def at_chip(offset):
        return (lax.rem(dp + offset[0], DP), lax.rem(tm + offset[1], TM))

    def win(u):
        return u * UR if u < 4 else F + 64 + (u - 4) * (UR + 64)

    def seg_of(u):
        return 0 if u < 4 else u - 3

    def lane(j):
        return slice(j * LANES, (j + 1) * LANES)

    def each_lane(body):
        for j in range(NL):
            body(j, 0)

    def wide(v):
        return jnp.concatenate([v] * NL, axis=1)

    def remote(src, dst, ssem, rsem, dev):
        return pltpu.make_async_remote_copy(src, dst, ssem, rsem, device_id=dev, device_id_type=MESH)

    def total_wait(ref, sem):
        pltpu.make_async_copy(ref, ref, sem).wait()

    barrier = pltpu.get_barrier_semaphore()
    load_x = pltpu.make_async_copy(x_any, xv, sem_loc.at[0])
    load_x.start()
    others = [(0, b) for b in range(1, TM, 2)]
    for offset in chips + others:
        pl.semaphore_signal(barrier, inc=1, device_id=at_chip(offset), device_id_type=MESH)

    x, z, y, core = lax.rem(dp, 2), dp // 2, tm // 2, lax.rem(tm, 2)
    Y = TM // 2
    Z = DP // 2

    my_len = [lengths[dp * U + b] for b in range(U)]
    long_at = jnp.int32(0)
    for b in range(1, U):
        long_at = jnp.where(my_len[b] == F * TM, jnp.int32(b), long_at)
    short_at = [jnp.where(k < long_at, k, k + 1) for k in range(U - 1)]
    short_len = [lengths[dp * U + b] for b in range(U - 1)]
    short_len = [jnp.where(k < long_at, my_len[k], my_len[k + 1]) for k in range(U - 1)]
    count = lax.fori_loop(0, DP * U, lambda i, c: c + lengths[i], jnp.int32(0)).astype(F32)
    inv_count = 1.0 / jnp.full((1, LANES), count, F32)
    def make_masks():
        rows = lax.broadcasted_iota(jnp.int32, (UR, LANES), 0)
        time_s = (rows & 15) * NB + (rows >> 4) + tm * UR
        for k in range(U - 1):
            mask[k * UR : (k + 1) * UR, :] = jnp.where(time_s < short_len[k], 1.0, 0.0)
        e16 = lax.broadcasted_iota(jnp.int32, (16, LANES), 0)
        part = (e16 & 7) >> 1
        is_left = e16 < 8
        when = jnp.where(is_left, tm * UR - 2 + (e16 & 1), tm * UR + UR + (e16 & 1))
        bound = jnp.full((16, LANES), 1 << 30, jnp.int32)
        for k in range(U - 1):
            bound = jnp.where(part == k + 1, short_len[k], bound)
        inside = jnp.where(is_left, tm, TM - 1 - tm) > 0
        hmask[...] = jnp.where(inside & (when < bound), 1.0, 0.0)

    def one_hot(ref, size, to_time):
        n = size // 16
        r0 = lax.broadcasted_iota(jnp.int32, (UR, size), 0)
        r1 = lax.broadcasted_iota(jnp.int32, (UR, size), 1)
        for c in range(size // UR):
            a, b = (r1, r0 + c * UR) if to_time else (r0 + c * UR, r1)
            hit = b == (a & 15) * n + (a >> 4)
            ref[c * UR : (c + 1) * UR, :] = jnp.where(hit, 1.0, 0.0).astype(BF16)

    def zero_ends():
        @pl.when(first)
        def _():
            halo_l[...] = jnp.zeros(halo_l.shape, BF16)
            for l in range(LAYERS):
                hh[l, 0:8, :] = jnp.zeros((8, C), F32)
                dhh[l, 0:8, :] = jnp.zeros((8, C), F32)

        @pl.when(last)
        def _():
            halo_r[...] = jnp.zeros(halo_r.shape, BF16)
            for l in range(LAYERS):
                hh[l, 8:16, :] = jnp.zeros((8, C), F32)
                dhh[l, 8:16, :] = jnp.zeros((8, C), F32)

    def stage_short():
        @pl.when(tm < N_SRC)
        def _():
            for k in range(U - 1):
                def cp(c, _):
                    sl = pl.ds(pl.multiple_of(c * UR, UR), UR)
                    xs[k, sl, :] = xv[short_at[k], sl, :]
                    return 0
                lax.fori_loop(0, 4, cp, 0)

    def send_short(dst, half):
        def act_on(d):
            if half == 0:
                d.start()
            else:
                d.wait_send()

        @pl.when(tm < N_SRC)
        def _():
            for q in range(4):
                chunk = 4 * tm + q
                main = xs.at[:, q * UR : (q + 1) * UR, :]
                head = xs.at[:, q * UR : q * UR + 16, :]
                tail = xs.at[:, (q + 1) * UR - 16 : (q + 1) * UR, :]

                def go_main():
                    act_on(remote(main, dst, sem_xs.at[q], sem_xr.at[0], (dp, chunk)))

                def go_head():
                    act_on(remote(head, halo_r.at[1:U], sem_xs.at[4 + q], sem_xr.at[1], (dp, chunk - 1)))

                if q == 0:
                    pl.when(tm > 0)(go_main)
                    if half == 0:
                        @pl.when(tm == 0)
                        def _():
                            for k in range(U - 1):
                                dst[k] = xs[k, 0:UR, :]
                else:
                    go_main()
                if q < 2:
                    pl.when(tm > 0)(go_head)
                else:
                    go_head()
                if q == 1 and half == 0:
                    @pl.when(tm == 0)
                    def _():
                        for k in range(U - 1):
                            halo_r[1 + k] = xs[k, UR : UR + 16, :]

                @pl.when(chunk + 1 < TM)
                def _():
                    act_on(remote(tail, halo_l.at[1:U], sem_xs.at[8 + q], sem_xr.at[2], (dp, chunk + 1)))

    S2 = 2 * LAYERS

    def cot_piece(k, half):
        @pl.when(tm < N_SRC)
        def _():
            for q in range(4):
                chunk = 4 * tm + q
                src = xs.at[k, q * UR : (q + 1) * UR, :]
                copy = remote(src, gin4.at[k], sem_cot.at[k, q], sem_cr.at[S2 + k], (dp, chunk))
                go = copy.start if half == 0 else copy.wait_send
                if q == 0:
                    pl.when(tm > 0)(go)
                else:
                    go()

        if half == 0:
            @pl.when(tm == 0)
            def _():
                gin4[k] = xs[k, 0:UR, :]

    def recv_short(dst):
        @pl.when(tm > 0)
        def _():
            total_wait(dst, sem_xr.at[0])
            total_wait(halo_l.at[1:U], sem_xr.at[2])

            @pl.when(tm < TM - 1)
            def _():
                total_wait(halo_r.at[1:U], sem_xr.at[1])

    def edges(send, recv_l, recv_r, ssem, rsem, start):
        to_next = remote(send.at[1], recv_l, ssem.at[0], rsem.at[0], (dp, lax.rem(tm + 1, TM)))
        to_prev = remote(send.at[0], recv_r, ssem.at[1], rsem.at[1], (dp, lax.rem(tm + TM - 1, TM)))
        if start:
            pl.when(tm < TM - 1)(lambda: to_next.start())
            pl.when(tm > 0)(lambda: to_prev.start())
        else:
            @pl.when(tm < TM - 1)
            def _():
                to_next.wait_send()
                to_prev.wait_recv()

            @pl.when(tm > 0)
            def _():
                to_prev.wait_send()
                to_next.wait_recv()

    for name, v, n in (("dp", dp, DP), ("y", y, Y), ("z", z, Z)):
        other(name, v, 0, n)

    def plane_peers():
        return [(a, b) for a in reversed(range(Z)) for b in reversed(range(Y)) if a or b]

    def plane_peer(offset):
        pz, py = other("z", z, offset[0], Z), other("y", y, offset[1], Y)
        return pz, py, (2 * pz + x, 2 * py + core)

    across = (2 * z + 1 - x, tm)

    def gather_stage(buf, m, stage):
        ss, rs = env["sem_gs"].at[m, stage], env["sem_gr"].at[m, stage]
        if stage == 0:
            mine = buf.at[z, x, y, core]
            for offset in plane_peers():
                remote(mine, mine, ss, rs, plane_peer(offset)[2]).start()
        elif stage == 1:
            mine = buf.at[:, x, :, core]
            remote(mine, mine, ss, rs, across).start()
        else:
            mine = buf.at[:, :, :, core]
            remote(mine, mine, ss, rs, (dp, partner)).start()

    def gather_wait(buf, m, stage, sems):
        if stage == 0:
            size = env["little_rz"].at[0] if buf is sall else env["big_rz"].at[0]
            total_wait(size, sems.at[m, stage])
        elif stage == 1:
            total_wait(buf.at[:, 0, :, 0], sems.at[m, stage])
        else:
            total_wait(buf.at[:, :, :, 0], sems.at[m, stage])

    def gather_got(buf, m, stage):
        gather_wait(buf, m, stage, env["sem_gr"])

    def gather_left(buf, m):
        for stage in range(3):
            gather_wait(buf, m, stage, env["sem_gs"])

    if fast:
        wall, sall = env["wall"], env["sall"]
        halves = [(wall.at[0], 0)]

        def weights(m):
            return wall[m].reshape(C, C)

        pack = env["pack"]
        pack[...] = jnp.zeros(pack.shape, F32)
        for l in range(LAYERS):
            pack[AT_TAPS + 8 * l : AT_TAPS + 8 * l + KERNEL, 0:SH] = env["taps"][l].astype(F32)
        pack[AT_GAMMA : AT_GAMMA + LAYERS, 0:SH] = env["gamma"][...].astype(F32)
        pack[AT_BETA : AT_BETA + LAYERS, 0:SH] = env["beta"][...].astype(F32)
        turned = pack[...].T[0:SH]
        pack[0:SH, :] = turned
        pack[0:SH, 0:SE] = env["excite"][...].astype(F32)
        sall[z, x, y, core, :, 0:LANES] = pack[0:SH, :].astype(BF16)
        pack[0:SH, 0:SE] = env["squeeze"][...].astype(F32)
        sall[z, x, y, core, :, LANES : 2 * LANES] = pack[0:SH, :].astype(BF16)
        shares = [env["point"].at[l] for l in range(LAYERS)] + [env["resid"]]
        loads = [
            pltpu.make_async_copy(src, wall.at[m, z, x, y, core], env["sem_in"].at[m]) for m, src in enumerate(shares)
        ]
        for c in loads:
            c.start()
    else:
        def weights(m):
            return env["mats"][m]

        small[...] = env["small_in"][...]

    def squeeze_all():
        if fast:
            return sall[...].reshape(C, 2 * LANES)[:, LANES : LANES + SE]
        return env["squeeze"][...]

    class Scatter:
        def __init__(self, name):
            self.send, self.core, self.xsum, self.rx, self.zsum, self.rz, self.ss, self.rs = (
                env[name + part] for part in ("_send", "_core", "_xsum", "_rx", "_zsum", "_rz", "_ss", "_rs")
            )
            self.dtype = self.send.dtype

        def go(self, m, stage):
            ss, rs = self.ss.at[m, stage], self.rs.at[m, stage]
            if stage == 0:
                remote(self.send.at[m, :, :, :, 1 - core], self.core.at[m], ss, rs, (dp, partner)).start()
            elif stage == 1:
                remote(self.xsum.at[m, 1 - x], self.rx.at[m], ss, rs, across).start()
            else:
                for i, offset in enumerate(plane_peers()):
                    pz, py, peer = plane_peer(offset)
                    remote(self.zsum.at[m, pz, py], self.rz.at[m, i], ss, rs, peer).start()

        def wait(self, m, stage, sems):
            total_wait((self.core.at[m], self.rx.at[m], self.rz.at[m])[stage], sems.at[m, stage])

        def left(self, m):
            for stage in range(3):
                self.wait(m, stage, self.ss)

        def core_to_x(self, m):
            self.wait(m, 0, self.rs)

            def body(i, _):
                v = self.send[m, i, :, :, core].astype(F32) + self.core[m, i].astype(F32)
                for k in range(2):
                    self.xsum[m, k, i] = v[k].astype(self.dtype)
                return 0

            lax.fori_loop(0, Z, body, 0)
            self.go(m, 1)

        def x_to_plane(self, m):
            self.x_sum(m)
            self.go(m, 2)

        def x_sum(self, m):
            self.wait(m, 1, self.rs)

            def body(i, _):
                v = self.xsum[m, x, i].astype(F32) + self.rx[m, i].astype(F32)
                self.zsum[m, i] = v.astype(self.dtype)
                return 0

            lax.fori_loop(0, Z, body, 0)

        def result(self, m):
            self.wait(m, 2, self.rs)
            v = self.zsum[m, z, y].astype(F32)
            for i in range(Z * Y - 1):
                v = v + self.rz[m, i].astype(F32)
            return v

    if fast:
        big, little = Scatter("big"), Scatter("little")

    def to_perm_long(src, dst, base):
        for u in range(4):
            o = base(u)
            dst[o : o + UR, :] = dot(perm_l[u * UR : (u + 1) * UR, :], src).astype(BF16)

    def to_perm_short(src, dst, base, masked):
        for k in range(U - 1):
            v = dot(perm_s[...], src[k])
            if masked:
                v = v * wide(mask[k * UR : (k + 1) * UR, :])
            o = base(4 + k)
            dst[o : o + UR, :] = v.astype(BF16)

    y0 = ypad.at[0]
    zero_ends()
    if fast:
        for c in loads:
            c.wait()
    pl.semaphore_wait(barrier, len(chips) + len(others))
    if fast:
        gather_stage(sall, MATS, 0)
        for buf, m in halves:
            gather_stage(buf, m, 0)
    load_x.wait()
    edge[0] = xv[long_at, 0:16, :]
    edge[1] = xv[long_at, F - 16 : F, :]
    stage_short()
    edge_sems = (sem_xs.at[pl.ds(12, 2)], sem_xr.at[pl.ds(3, 2)])
    edges(edge, halo_l.at[0], halo_r.at[0], *edge_sems, True)
    send_short(xin, 0)
    if fast:
        for m in range(1, min(3, MATS)):
            gather_stage(wall.at[m], m, 0)
    one_hot(perm_l, F, False)
    one_hot(perm_s, UR, False)
    to_perm_long(xv[long_at], y0, lambda u: win(u) + 32)
    load_g = pltpu.make_async_copy(g_any, xv, sem_loc.at[0])
    load_g.start()
    make_masks()
    if fast:
        gather_got(sall, MATS, 0)
        gather_stage(sall, MATS, 1)
        for buf, m in halves:
            gather_got(buf, m, 0)
            gather_stage(buf, m, 1)
        gather_got(sall, MATS, 1)
        gather_stage(sall, MATS, 2)
        for buf, m in halves:
            gather_got(buf, m, 1)
            gather_stage(buf, m, 2)
        gather_got(sall, MATS, 2)
        for j in range(NL):
            part = sall[...].reshape(C, 2 * LANES)[j * LANES : (j + 1) * LANES, 0:LANES].astype(F32)
            small[:, j * LANES : (j + 1) * LANES] = part.T

    def fill_pads(ref, row0, n, j, b0, b1, b2, b3, halo, seg):
        e = lax.broadcasted_iota(jnp.int32, (16, LANES), 0)

        def put(at, v):
            ref[pl.ds(row0 + at * 16, 16), lane(j)] = v.astype(BF16)

        put(0, jnp.where(e == 0, halo[2 * seg : 2 * seg + 1], pltpu.roll(b2, 1, 0)))
        put(1, jnp.where(e == 0, halo[2 * seg + 1 : 2 * seg + 2], pltpu.roll(b3, 1, 0)))
        put(n + 2, jnp.where(e == 15, halo[8 + 2 * seg : 9 + 2 * seg], pltpu.roll(b0, 15, 0)))
        put(n + 3, jnp.where(e == 15, halo[9 + 2 * seg : 10 + 2 * seg], pltpu.roll(b1, 15, 0)))

    def pads_from(ref, j, halo, segs):
        for seg in segs:
            u0, u1 = (0, 3) if seg == 0 else (3 + seg, 3 + seg)
            n = F // 16 if seg == 0 else NB
            o0, o1 = win(u0) + 32, win(u1) + 32 + UR
            blk = [ref[o : o + 16, lane(j)].astype(F32) for o in (o0, o0 + 16, o1 - 32, o1 - 16)]
            fill_pads(ref, win(u0), n, j, *blk, halo, seg)

    def first_pads(segs):
        def body(j, _):
            none = jnp.zeros((2, LANES), F32)
            left = [halo_l[s, :, lane(j)].astype(F32)[14:16] if s in segs else none for s in range(4)]
            right = [halo_r[s, :, lane(j)].astype(F32)[0:2] if s in segs else none for s in range(4)]
            halo = jnp.where(hmask[...] > 0.0, jnp.concatenate(left + right, axis=0), 0.0)
            pads_from(y0, j, halo, segs)
            return 0

        each_lane(body)

    edges(edge, halo_l.at[0], halo_r.at[0], *edge_sems, False)
    first_pads([0])

    def shorts_arrive():
        if fast:
            gather_got(wall.at[1], 1, 0)
            gather_stage(wall.at[1], 1, 1)
        recv_short(xin)
        to_perm_short(xin, y0, lambda u: win(u) + 32, True)
        send_short(xin, 1)
        first_pads(range(1, U))

    def sync_core(s, meanwhile):
        d = remote(send_a.at[s], recv_core.at[s], sem_cs.at[s], sem_cr.at[s], (dp, partner))
        d.start()
        meanwhile()
        d.wait()
        send_b[s] = send_a[s] + recv_core[s]

    def sync_send(s):
        recv_chip[s, my_chip] = send_b[s]
        dst = recv_chip.at[s, my_chip]

        for a in reversed(range(DP)):
            for b in reversed(range(Y)):
                if a or b:
                    there = (other("dp", dp, a, DP), 2 * other("y", y, b, Y) + core)
                    remote(send_b.at[s], dst, sem_ks.at[s], sem_kr.at[s], there).start()

    def sync_done(s):
        others = recv_chip.at[s, 0 : n_chips - 1]
        total_wait(others, sem_kr.at[s])
        total_wait(others, sem_ks.at[s])
        terms = [recv_chip[s, i] for i in range(n_chips)]
        while len(terms) > 1:
            terms = [sum(terms[i : i + 2][1:], terms[i]) for i in range(0, len(terms), 2)]
        return terms[0]

    def tap_rows(l, j):
        group = small[pl.ds(pl.multiple_of(AT_TAPS + 8 * l, 8), 8), lane(j)]
        return [group[k : k + 1] for k in range(KERNEL)]

    LONG, SHORT = range(4), range(4, NU)

    def conv_pass(l, units):
        def body(j, _):
            w = tap_rows(l, j)
            for u in units:
                o = win(u)
                v = ypad[l, o : o + UR + 64, lane(j)].astype(F32)
                t = v[0:UR] * w[0]
                for k in range(1, KERNEL):
                    t = t + v[16 * k : 16 * k + UR] * w[k]
                if u >= 4:
                    t = t * mask[(u - 4) * UR : (u - 3) * UR, :]
                dlow[l, u * UR : (u + 1) * UR, lane(j)] = t.astype(BF16)
            return 0

        each_lane(body)

    def fold8(v):
        return jnp.sum(v.reshape(v.shape[0] // 8, 8, v.shape[1]), axis=0)

    def put_edges(src, l):
        for seg in range(4):
            base = 0 if seg == 0 else F + (seg - 1) * UR
            n = F if seg == 0 else UR
            for e in range(2):
                hsend[l, 1, 2 * seg + e : 2 * seg + e + 1, :] = src(base + n - 32 + 16 * e + 15)
                hsend[l, 0, 2 * seg + e : 2 * seg + e + 1, :] = src(base + 16 * e)

    def matmul_pass(l, units):
        r = slice(units[0] * UR, (units[-1] + 1) * UR)
        h = dot(dlow[l, r, :], weights(l))
        pre[l, r, :] = h
        s0, s1 = fold8(h), fold8(h * h)
        if units[0] > 0:
            s0, s1 = s0 + sums[0], s1 + sums[1]
        sums[0] = s0
        sums[1] = s1

    def send_stats(l):
        send_a[l, 0:1, :] = jnp.sum(sums[0], axis=0, keepdims=True)
        send_a[l, 1:2, :] = jnp.sum(sums[1], axis=0, keepdims=True)

    def act_pass(l):
        def body(j, _):
            a, b = coef[l, 0:1, lane(j)], coef[l, 1:2, lane(j)]
            for u in range(NU):
                v = pre[l, u * UR : (u + 1) * UR, lane(j)] * a + b
                v = v + v * jnp.tanh(v)
                if u >= 4:
                    v = v * mask[(u - 4) * UR : (u - 3) * UR, :]
                o = win(u) + 32
                ypad[l + 1, o : o + UR, lane(j)] = v.astype(BF16)
            v = hh[l, :, lane(j)] * a + b
            v = (v + v * jnp.tanh(v)) * hmask[...]
            pads_from(ypad.at[l + 1], j, v, range(U))
            return 0

        each_lane(body)

    def prep_pass(l):
        def body(j, _):
            a, b, m, i = (coef[l, r : r + 1, lane(j)] for r in range(4))
            for u in range(NU):
                rs = slice(u * UR, (u + 1) * UR)
                h = pre[l, rs, lane(j)]
                half = h * a + b
                t = jnp.tanh(half)
                v = (0.5 + 0.5 * t) * (1.0 + half * (1.0 - t))
                if u >= 4:
                    v = v * mask[(u - 4) * UR : (u - 3) * UR, :]
                slope[l, rs, lane(j)] = v.astype(BF16)
                pre[l, rs, lane(j)] = (h - m) * i
            hx[l, :, lane(j)] = (hh[l, :, lane(j)] - m) * i
            return 0

        each_lane(body)

    def layer(l, _):
        pl.when(l == 0)(shorts_arrive)
        if fast:
            gather_got(wall.at[l], l, 2)
        conv_pass(l, LONG)
        matmul_pass(l, LONG)
        conv_pass(l, SHORT)
        matmul_pass(l, SHORT)
        send_stats(l)

        def halo_out():
            put_edges(lambda row: pre[l, row : row + 1, :], l)
            edges(hsend.at[l], hh.at[l, 0:8], hh.at[l, 8:16], sem_hs.at[l], sem_hr.at[l], True)

        sync_core(l, halo_out)
        sync_send(l)

        if fast:
            gather_got(wall.at[l + 1], l + 1, 1)
            gather_stage(wall.at[l + 1], l + 1, 2)

        pl.when(l > 0)(lambda: prep_pass(l - 1))

        @pl.when(l == 0)
        def _():
            load_g.wait()
            stage_short()
            to_perm_long(xv[long_at], cot, lambda u: u * UR)

        @pl.when(l == 1)
        def _():
            one_hot(back_l, F, True)
            one_hot(back_s, UR, True)

        @pl.when(l == LAYERS - 1)
        def _():
            for k in range(U - 1):
                cot_piece(k, 1)

            @pl.when(tm > 0)
            def _():
                for k in range(U - 1):
                    total_wait(gin4.at[k], sem_cr.at[S2 + k])

            to_perm_short(gin4, cot, lambda u: u * UR, True)

        if fast:
            @pl.when(l + 2 < MATS)
            def _():
                gather_got(wall.at[l + 2], l + 2, 0)
                gather_stage(wall.at[l + 2], l + 2, 1)

            @pl.when(l + 3 < MATS)
            def _():
                gather_stage(wall.at[l + 3], l + 3, 0)

        total = sync_done(l)
        edges(hsend.at[l], hh.at[l, 0:8], hh.at[l, 8:16], sem_hs.at[l], sem_hr.at[l], False)
        for k in range(U - 1):
            pl.when(l == k)(functools.partial(cot_piece, k, 0))
        scale = wide(inv_count)
        mean = total[0:1] * scale
        var = total[1:2] * scale - mean * mean
        inv = lax.rsqrt(var + NORM_EPSILON)
        ga = small[pl.ds(AT_GAMMA + l, 1), :]
        a = ga * inv
        coef[l, 0:1, :] = 0.5 * a
        coef[l, 1:2, :] = 0.5 * (small[pl.ds(AT_BETA + l, 1), :] - mean * a)
        coef[l, 2:3, :] = mean
        coef[l, 3:4, :] = inv
        coef[l, 4:5, :] = a

        pl.when(l < LAYERS - 1)(lambda: act_pass(l))
        return 0

    lax.fori_loop(0, LAYERS, layer, 0)

    top = LAYERS - 1
    pool[...] = jnp.zeros(pool.shape, F32)

    def last_act(j, _):
        a, b = coef[top, 0:1, lane(j)], coef[top, 1:2, lane(j)]
        acc = None
        for u in range(NU):
            v = pre[top, u * UR : (u + 1) * UR, lane(j)] * a + b
            v = v + v * jnp.tanh(v)
            if u >= 4:
                v = v * mask[(u - 4) * UR : (u - 3) * UR, :]
            act[u * UR : (u + 1) * UR, lane(j)] = v
            f = fold8(v)
            acc = f if u == 0 or u >= 4 else acc + f
            if u >= 3:
                pool[u - 3 : u - 2, lane(j)] = jnp.sum(acc, axis=0, keepdims=True)
        return 0

    each_lane(last_act)

    def time_sum(s, value):
        tsend[s] = value
        ds = [remote(tsend.at[s], trecv.at[s, i - 1], sem_ts.at[s], sem_tr.at[s], (dp, lax.rem(tm + i, TM))) for i in range(1, TM)]
        for d in ds:
            d.start()

    def time_done(s):
        whole = trecv.at[s]
        total_wait(whole, sem_tr.at[s])
        total_wait(whole, sem_ts.at[s])
        total = tsend[s]
        for i in range(TM - 1):
            total = total + trecv[s, i]
        return total

    e8 = lax.broadcasted_iota(jnp.int32, (8, LANES), 0)
    len8 = jnp.full((8, LANES), F * TM, jnp.int32)
    for k in range(U - 1):
        len8 = jnp.where(e8 == k + 1, short_len[k], len8)
    inv_len = 1.0 / len8.astype(F32)
    live = jnp.where(e8 < U, 1.0, 0.0)
    time_sum(0, pool[...])
    prep_pass(top)
    if fast:
        gather_got(wall.at[LAYERS], LAYERS, 2)
    resd[0:F, :] = dot(ypad[0, 32 : 32 + F, :], weights(LAYERS))
    for u in SHORT:
        resd[u * UR : (u + 1) * UR, :] = dot(ypad[0, win(u) + 32 : win(u) + 32 + UR, :], weights(LAYERS))
    p = time_done(0) * wide(inv_len)
    sq = squeeze_all()
    ex = small[0:SE, :].astype(BF16)
    q = dot_parts(p, sq)
    sig_q = logistic(q)
    z_act = q * sig_q
    gate[...] = logistic(dot_parts(z_act, ex))
    pool[...] = jnp.zeros(pool.shape, F32)

    def top_pass(j, _):
        acc = None
        for u in range(NU):
            rs = slice(u * UR, (u + 1) * UR)
            seg = seg_of(u)
            av = act[rs, lane(j)]
            half = 0.5 * (av * gate[seg : seg + 1, lane(j)] + resd[rs, lane(j)])
            t = jnp.tanh(half)
            out = half + half * t
            slope = (0.5 + 0.5 * t) * (1.0 + half * (1.0 - t))
            dv = cot[rs, lane(j)].astype(F32) * slope
            if u >= 4:
                out = out * mask[(u - 4) * UR : (u - 3) * UR, :]
            outp[rs, lane(j)] = out.astype(BF16)
            du[rs, lane(j)] = dv
            drl[rs, lane(j)] = dv.astype(BF16)
            f = fold8(dv * av)
            acc = f if u == 0 or u >= 4 else acc + f
            if u >= 3:
                pool[u - 3 : u - 2, lane(j)] = jnp.sum(acc, axis=0, keepdims=True)
        return 0

    each_lane(top_pass)
    time_sum(1, pool[...])

    def back_long(buf, src):
        for u in range(4):
            buf[0, u * UR : (u + 1) * UR, :] = dot(back_l[u * UR : (u + 1) * UR, :], src[0:F, :]).astype(BF16)

    def back_short(buf, stage, src):
        for k in range(U - 1):
            stage[k] = dot(back_s[...], src[F + k * UR : F + (k + 1) * UR, :]).astype(BF16)

        @pl.when(tm >= N_SRC)
        def _():
            for k in range(U - 1):
                buf[1 + k] = jnp.zeros((F, C), BF16)

        @pl.when(first)
        def _():
            for k in range(U - 1):
                buf[1 + k, 0:UR, :] = stage[k]

    def back_piece(buf, stage, sems, rsems, k):
        owner, q = tm // 4, lax.rem(tm, 4)
        dst = buf.at[1 + k, pl.ds(pl.multiple_of(q * UR, UR), UR), :]
        return remote(stage.at[k], dst, sems.at[k], rsems.at[k, q], (dp, owner))

    def back_send(buf, stage, sems, rsems, ks):
        @pl.when(tm > 0)
        def _():
            for k in ks:
                back_piece(buf, stage, sems, rsems, k).start()

    def back_left(buf, stage, sems, rsems):
        @pl.when(tm > 0)
        def _():
            for k in range(U - 1):
                back_piece(buf, stage, sems, rsems, k).wait_send()

    def back_arrived(buf, rsems, k):
        @pl.when(tm < N_SRC)
        def _():
            for i in range(4):
                got = functools.partial(total_wait, buf.at[1 + k, i * UR : (i + 1) * UR, :], rsems.at[k, i])
                if i == 0:
                    pl.when(tm > 0)(got)
                else:
                    got()

    def back_done(buf, stage, sems, rsems):
        back_left(buf, stage, sems, rsems)
        for k in range(U - 1):
            back_arrived(buf, rsems, k)

    put_out = pltpu.make_async_copy(obuf, out_any, sem_loc.at[2])
    back_long(obuf, outp)
    back_short(obuf, xin, outp)

    def xrows(u):
        o = win(u) + 32
        return ypad[0, o : o + UR, :]

    def put_grad(m, total):
        if fast:
            big.send[m] = total.astype(BF16).reshape(Z, 2, Y, 2, SH, C)
            big.go(m, 0)
        else:
            gp[...] = total
            pltpu.make_async_copy(gp, env["gmats"].at[m], sem_loc.at[1]).start()

    def grad_gone():
        if not fast:
            pltpu.make_async_copy(gp, env["gmats"].at[0], sem_loc.at[1]).wait()

    def xrows(u):
        o = win(u) + 32
        return ypad[0, o : o + UR, :]

    def resid_grads():
        total = dot(ypad[0, 32 : 32 + F, :], drl[0:F, :], ((0,), (0,)))
        for u in SHORT:
            total = total + dot(xrows(u), drl[u * UR : (u + 1) * UR, :], ((0,), (0,)))
        put_grad(LAYERS, total)
        gres_in[...] = dot(drl[...], weights(LAYERS), ((1,), (1,)))

    resid_grads()
    dg = time_done(1)
    gv = gate[...]
    de = dg * gv * (1.0 - gv) * wide(live)
    dz = dot_parts(de, ex, ((1,), (1,)))
    dq = dz * sig_q * (1.0 + q * (1.0 - sig_q))
    cvec[...] = dot_parts(dq, sq, ((1,), (1,))) * wide(inv_len)
    fac[0], fac[1] = p, de
    facs[0], facs[1] = z_act, dq

    def pair_grads():
        lead = jnp.where(first, 1.0, 0.0)
        zero = jnp.zeros((C, LANES - 2 * SE), F32)
        pair = [dot(fac[1 - i], facs[i], ((0,), (0,)), precision=HIGHEST) for i in range(2)]
        pair = jnp.concatenate(pair + [zero] * (LANES > 2 * SE), axis=1) * lead
        if fast:
            little.send[0] = pair.reshape(Z, 2, Y, 2, SH, LANES)
            little.go(0, 0)
        else:
            env["gpair"][...] = pair

    def back_sums(l, s, grad_of):
        def body(j, _):
            acc0 = acc1 = None
            make = grad_of(j)
            for u in range(NU):
                rs = slice(u * UR, (u + 1) * UR)
                v = make(u) * slope[l, rs, lane(j)].astype(F32)
                xc = pre[l, rs, lane(j)]
                dn[u * UR : (u + 1) * UR, lane(j)] = v
                f0, f1 = fold8(v), fold8(v * xc)
                acc0 = f0 if u == 0 else acc0 + f0
                acc1 = f1 if u == 0 else acc1 + f1
            send_a[s, 0:1, lane(j)] = jnp.sum(acc0, axis=0, keepdims=True)
            send_a[s, 1:2, lane(j)] = jnp.sum(acc1, axis=0, keepdims=True)
            return 0

        each_lane(body)

    def top_grad(j):
        def make(u):
            seg = seg_of(u)
            return du[u * UR : (u + 1) * UR, lane(j)] * gate[seg : seg + 1, lane(j)] + cvec[seg : seg + 1, lane(j)]
        return make

    def conv_grad(l):
        def outer(j):
            w = tap_rows(l, j)

            def make(u):
                o = win(u)
                v = ddpad[o : o + UR + 64, lane(j)].astype(F32)
                t = v[64 : 64 + UR] * w[0]
                for k in range(1, KERNEL):
                    t = t + v[64 - 16 * k : 64 - 16 * k + UR] * w[k]
                return t
            return make
        return outer

    back_sums(top, LAYERS, top_grad)

    def point_grad(l):
        grad_gone()
        put_grad(l, dot(dlow[l], dhl[0:R, :], ((0,), (0,))))

    def depth_grad(l):
        def body(j, _):
            acc = [None] * KERNEL
            for u in range(NU):
                o = win(u)
                v = ypad[l, o : o + UR + 64, lane(j)].astype(F32)
                g = ddpad[o + 32 : o + 32 + UR, lane(j)].astype(F32)
                for k in range(KERNEL):
                    f = fold8(v[16 * k : 16 * k + UR] * g)
                    acc[k] = f if u == 0 else acc[k] + f
            rows = [jnp.sum(acc[k], axis=0, keepdims=True) for k in range(KERNEL)]
            rows.append(jnp.zeros((8 - KERNEL, LANES), F32))
            at = pl.ds(pl.multiple_of(AT_TAPS + 8 * l, 8), 8)
            gsmall[at, lane(j)] = jnp.concatenate(rows, axis=0)
            return 0

        each_lane(body)
    def dh_pass(l, units):
        def body(j, _):
            a, k1, k0 = (coef[l, r : r + 1, lane(j)] for r in (4, 5, 6))
            for u in units:
                rs = slice(u * UR, (u + 1) * UR)
                v = dn[rs, lane(j)] * a - (pre[l, rs, lane(j)] * k1 + k0)
                if u >= 4:
                    v = v * mask[(u - 4) * UR : (u - 3) * UR, :]
                dhl[rs, lane(j)] = v.astype(BF16)
            if units is SHORT:
                v = (dhh[l, :, lane(j)] * a - (hx[l, :, lane(j)] * k1 + k0)) * hmask[...]
                dhl[R : R + 16, lane(j)] = v.astype(BF16)
            return 0

        each_lane(body)

    def dd_pass(l):
        dh_pass(l, LONG)
        ddpad[32 : 32 + F, :] = dot(dhl[0:F, :], weights(l), ((1,), (1,))).astype(BF16)
        dh_pass(l, SHORT)
        v = dot(dhl[F : R + 16, :], weights(l), ((1,), (1,)))
        for u in SHORT:
            ddpad[win(u) + 32 : win(u) + 32 + UR, :] = v[(u - 4) * UR : (u - 3) * UR].astype(BF16)
        hx[l] = v[R - F : R - F + 16].astype(BF16).astype(F32)

        def pad(j, _):
            pads_from(ddpad, j, hx[l, :, lane(j)], range(U))
            return 0

        each_lane(pad)

    def back_layer(step, _):
        l = top - step
        s = LAYERS + step

        def halo_out():
            put_edges(lambda row: dn[row : row + 1, :], s)
            edges(hsend.at[s], dhh.at[l, 0:8], dhh.at[l, 8:16], sem_hs.at[s], sem_hr.at[s], True)

        sync_core(s, halo_out)
        sync_send(s)

        @pl.when(step > 0)
        def _():
            point_grad(l + 1)
            depth_grad(l + 1)

        pl.when(step == 0)(pair_grads)

        @pl.when(step == LAYERS - 1)
        def _():
            back_done(obuf, xin, sem_os.at[0], sem_or.at[0])
            put_out.start()

        if fast:
            @pl.when(step == 1)
            def _():
                little.core_to_x(0)

            @pl.when(step == 2)
            def _():
                little.x_to_plane(0)

            @pl.when(step > 0)
            def _():
                big.x_sum(l + 2)

            @pl.when(step > 1)
            def _():
                env["keep"][l + 3] = big.result(l + 3)

            big.core_to_x(l + 1)

        if fast:
            pl.when(step > 0)(lambda: big.go(l + 2, 2))

        total = sync_done(s)
        @pl.when(step < U - 1)
        def _():
            back_send(obuf, xin, sem_os.at[0], sem_or.at[0], [step])

        edges(hsend.at[s], dhh.at[l, 0:8], dhh.at[l, 8:16], sem_hs.at[s], sem_hr.at[s], False)
        ggb[l, 0:2, :] = total
        a = coef[l, 4:5, :]
        coef[l, 5:6, :] = a * total[1:2] * wide(inv_count)
        coef[l, 6:7, :] = a * total[0:1] * wide(inv_count)

        dd_pass(l)

        @pl.when(l > 0)
        def _():
            back_sums(l - 1, s + 1, conv_grad(l - 1))
        return 0

    def run_back():
        lax.fori_loop(0, LAYERS, back_layer, 0)

    conv_grad_of = conv_grad

    def conv_grad(l):
        return conv_grad_of(l + 1)

    gsmall[...] = jnp.zeros(gsmall.shape, F32)
    run_back()
    lead_all = jnp.where(first & (dp == 0), 1.0, 0.0)
    for l in range(LAYERS):
        gsmall[AT_BETA + l : AT_BETA + l + 1, :] = ggb[l, 0:1, :] * lead_all
        gsmall[AT_GAMMA + l : AT_GAMMA + l + 1, :] = ggb[l, 1:2, :] * lead_all
    def final_pass(units):
        def body(j, _):
            make = conv_grad_of(0)(j)
            for u in units:
                rs = slice(u * UR, (u + 1) * UR)
                v = make(u)
                if u >= 4:
                    v = v * mask[(u - 4) * UR : (u - 3) * UR, :]
                outp[rs, lane(j)] = (v + gres_in[rs, lane(j)]).astype(BF16)
            return 0

        each_lane(body)

    final_pass(SHORT)
    back_short(gbuf, gin4, outp)
    back_send(gbuf, gin4, sem_os.at[1], sem_or.at[1], range(U - 1))
    point_grad(0)
    if fast:
        big.core_to_x(0)
    depth_grad(0)
    if fast:
        for j in range(NL):
            rows = gsmall[:, j * LANES : (j + 1) * LANES].T
            part = rows.reshape(LANES // (2 * SH), 2, SH, LANES)
            per = LANES // (2 * SH)
            for i in range(per):
                n = j * per + i
                little.send[1, n // (2 * Y), n // Y % 2, n % Y] = part[i]
        little.go(1, 0)
        big.x_to_plane(1)
    final_pass(LONG)
    back_long(gbuf, outp)
    put_gin = [pltpu.make_async_copy(gbuf.at[k], gin_any.at[k], sem_loc.at[3 + k]) for k in range(U)]
    put_gin[0].start()
    if fast:
        little.core_to_x(1)
        env["keep"][2] = big.result(2)
        big.x_to_plane(0)
        little.x_to_plane(1)
        env["keep_s"][0] = little.result(0)
        env["keep"][1] = big.result(1)
        early = pltpu.make_async_copy(env["keep"].at[1:MATS], env["gmats"].at[1:MATS], env["sem_keep"].at[0])
        early.start()
        for m in range(1, MATS):
            big.left(m)
            gather_left(wall.at[m], m)
        for buf, m in halves:
            gather_left(buf, m)
        little.left(0)
        gather_left(sall, MATS)
    else:
        env["grows"][...] = gsmall[...]
    for k in range(U - 1):
        back_arrived(gbuf, sem_or.at[1], k)
        put_gin[1 + k].start()
    back_left(gbuf, gin4, sem_os.at[1], sem_or.at[1])
    if fast:
        env["keep"][0] = big.result(0)
        late = [pltpu.make_async_copy(env["keep"].at[0], env["gmats"].at[0], env["sem_keep"].at[1])]
        late[0].start()
        env["keep_s"][1] = little.result(1)
        late.append(pltpu.make_async_copy(env["keep_s"].at[0], env["gpair"], env["sem_keep"].at[2]))
        late.append(pltpu.make_async_copy(env["keep_s"].at[1], env["grows"], env["sem_keep"].at[3]))
        late[1].start()
        late[2].start()
        big.left(0)
        little.left(1)
    grad_gone()
    put_out.wait()
    for c in put_gin:
        c.wait()
    if fast:
        for c in [early] + late:
            c.wait()


def finish_kernel(cfg, lengths, out_s, gin_s, gmats_any, gpair_any, grows_any, *rest):
    DP, TM, U, F, C, SE, SH, LAYERS, KERNEL, fast = cfg
    out, gin, gdepth_any, gpoint, ggamma_any, gbeta_any, gsq_any, gex_any, gres = rest[:9]
    hold, gmats, gpair, grows, turn, gdepth, ggamma, gbeta, gsq, gex, sems, sems_g = rest[9:]
    dp = lax.axis_index("dp")
    long_at = jnp.int32(0)
    for b in range(1, U):
        long_at = jnp.where(lengths[dp * U + b] == F * TM, jnp.int32(b), long_at)
    copies = []
    loads = [
        pltpu.make_async_copy(src, dst, sems_g.at[i])
        for i, (src, dst) in enumerate(((gmats_any, gmats), (gpair_any, gpair), (grows_any, grows)))
    ]
    for c in loads:
        c.start()
    for b in range(U):
        slot = jnp.where(b == long_at, 0, jnp.where(b < long_at, b + 1, b))
        for i, (src, dst) in enumerate(((out_s, out), (gin_s, gin))):
            get = pltpu.make_async_copy(src.at[slot], hold.at[i, b], sems.at[0, i, b])
            put = pltpu.make_async_copy(hold.at[i, b], dst.at[b], sems.at[1, i, b])
            copies.append((get, put))
            get.start()
    loads[0].wait()
    results = [
        pltpu.make_async_copy(gmats.at[0:LAYERS], gpoint, sems_g.at[3]),
        pltpu.make_async_copy(gmats.at[LAYERS], gres, sems_g.at[4]),
    ]
    for c in results:
        c.start()
    for get, put in copies:
        get.wait()
        put.start()
    for c in loads[1:]:
        c.wait()
    at_taps = SE
    at_gamma = SE + 8 * LAYERS
    at_beta = at_gamma + 8
    gsq[...] = gpair[:, SE : 2 * SE]
    gex[...] = gpair[:, 0:SE]
    turn[...] = jnp.zeros(turn.shape, F32)
    turn[0:SH] = grows[...]
    turn[...] = turn[...].T
    for l in range(LAYERS):
        gdepth[l] = turn[at_taps + 8 * l : at_taps + 8 * l + KERNEL, 0:SH]
    ggamma[...] = turn[at_gamma : at_gamma + LAYERS, 0:SH]
    gbeta[...] = turn[at_beta : at_beta + LAYERS, 0:SH]
    pairs = ((gdepth, gdepth_any), (ggamma, ggamma_any), (gbeta, gbeta_any), (gsq, gsq_any), (gex, gex_any))
    for i, (src, dst) in enumerate(pairs):
        results.append(pltpu.make_async_copy(src, dst, sems_g.at[5 + i]))
        results[-1].start()
    for _, put in copies:
        put.wait()
    for c in results:
        c.wait()


def local(sizes, inputs, lengths, depth_w, point_w, gamma, beta, squeeze_w, excite_w, resid_w, cotangent):
    DP, TM = sizes
    U, F, C = inputs.shape
    LAYERS, KERNEL, SH = depth_w.shape
    SE = squeeze_w.shape[1]
    UR = F // 4
    NU = 4 + U - 1
    R = NU * UR
    RP = F + 64 + (U - 1) * (UR + 64)
    S = 2 * LAYERS
    chips = DP * (TM // 2) - 1
    axes = ("dp", "tm")
    fast = SH % 16 == 0 and DP % 2 == 0 and DP > 2
    Z, Y = DP // 2, TM // 2
    MATS = LAYERS + 1
    vm = pltpu.VMEM
    dma = pltpu.SemaphoreType.DMA
    any_spec = pl.BlockSpec(memory_space=pl.ANY)
    vm_spec = pl.BlockSpec(memory_space=pltpu.VMEM)
    sm_spec = pl.BlockSpec(memory_space=pltpu.SMEM)
    sd = jax.ShapeDtypeStruct
    cfg = (DP, TM, U, F, C, SE, SH, LAYERS, KERNEL, fast)
    at_gamma = SE + 8 * LAYERS
    operands = dict(lengths=lengths, x_any=inputs, g_any=cotangent)
    specs = [sm_spec, any_spec, any_spec]
    outs = dict(out_any=sd((U, F, C), BF16), gin_any=sd((U, F, C), BF16))
    out_specs = [any_spec, any_spec]
    if fast:
        operands.update(
            point=point_w, taps=depth_w, gamma=gamma, beta=beta, squeeze=squeeze_w, excite=excite_w.T, resid=resid_w
        )
        specs += [any_spec] + [vm_spec] * 5 + [any_spec]
        outs.update(gmats=sd((MATS, SH, C), F32), gpair=sd((SH, LANES), F32), grows=sd((SH, LANES), F32))
        out_specs += [any_spec] * 3
    else:
        mats = jnp.concatenate([point_w, resid_w[None]], axis=0)
        depth_rows = jnp.pad(depth_w, ((0, 0), (0, 8 - KERNEL), (0, 0))).reshape(8 * LAYERS, SH)
        fill = ((0, 8 - LAYERS), (0, 0))
        rows = jnp.concatenate([excite_w, depth_rows, jnp.pad(gamma, fill), jnp.pad(beta, fill)], axis=0)
        rows = jnp.pad(rows, ((0, LANES - rows.shape[0]), (0, 0)))
        operands.update(
            mats=lax.all_gather(mats, axes, axis=1, tiled=True),
            small_in=lax.all_gather(rows, axes, axis=1, tiled=True).astype(F32),
            squeeze=lax.all_gather(squeeze_w, axes, axis=0, tiled=True),
        )
        specs += [vm_spec] * 3
        outs.update(gmats=sd((MATS, C, C), F32), gpair=sd((C, LANES), F32), grows=sd((LANES, C), F32))
        out_specs += [any_spec, vm_spec, vm_spec]
    scratch = dict(
        xv=vm((U, F, C), BF16), xs=vm((U - 1, F, C), BF16), edge=vm((2, 16, C), BF16),
        xin=vm((U - 1, UR, C), BF16), gin4=vm((U - 1, UR, C), BF16),
        halo_l=vm((4, 16, C), BF16), halo_r=vm((4, 16, C), BF16),
        cot=vm((R, C), BF16), ypad=vm((LAYERS, RP, C), BF16), dlow=vm((LAYERS, R, C), BF16),
        pre=vm((LAYERS, R, C), F32), hh=vm((LAYERS, 16, C), F32), hx=vm((LAYERS, 16, C), F32),
        mask=vm(((U - 1) * UR, LANES), F32), hmask=vm((16, LANES), F32), coef=vm((LAYERS, 8, C), F32),
        resd=vm((R, C), F32), act=vm((R, C), F32), du=vm((R, C), F32), drl=vm((R, C), BF16),
        dhl=vm((R + 16, C), BF16), ddpad=vm((RP, C), BF16),
        perm_l=vm((F, F), BF16), perm_s=vm((UR, UR), BF16), back_l=vm((F, F), BF16), back_s=vm((UR, UR), BF16),
        outp=vm((R, C), BF16), obuf=vm((U, F, C), BF16), gbuf=vm((U, F, C), BF16),
        small=vm((LANES, C), F32), slope=vm((LAYERS, R, C), BF16),
        fac=vm((2, 8, C), F32), facs=vm((2, 8, SE), F32), gsmall=vm((LANES, C), F32), ggb=vm((LAYERS, 8, C), F32),
        sums=vm((2, 8, C), F32), send_a=vm((S, 2, C), F32), send_b=vm((S, 2, C), F32),
        recv_core=vm((S, 2, C), F32), recv_chip=vm((S, chips + 1, 2, C), F32),
        hsend=vm((S, 2, 8, C), F32), dhh=vm((LAYERS, 16, C), F32),
        tsend=vm((2, 8, C), F32), trecv=vm((2, TM - 1, 8, C), F32),
        pool=vm((8, C), F32), gate=vm((8, C), F32), cvec=vm((8, C), F32),
        sem_loc=dma((3 + U,)), sem_cs=dma((S,)), sem_cr=dma((S + U - 1,)), sem_cot=dma((U - 1, 4)), sem_ks=dma((S,)), sem_kr=dma((S,)),
        sem_hs=dma((S, 2)), sem_hr=dma((S, 2)), sem_ts=dma((2,)), sem_tr=dma((2,)),
        sem_xs=dma((14,)), sem_xr=dma((5,)), sem_os=dma((2, U - 1)), sem_or=dma((2, U - 1, 4)),
    )
    if fast:
        scratch.update(
            wall=vm((MATS, Z, 2, Y, 2, SH, C), BF16), sall=vm((Z, 2, Y, 2, SH, 2 * LANES), BF16),
            pack=vm((LANES, LANES), F32), keep=vm((MATS, SH, C), F32), keep_s=vm((2, SH, LANES), F32),
            sem_keep=dma((4,)), sem_in=dma((MATS,)), sem_gs=dma((MATS + 1, 3)), sem_gr=dma((MATS + 1, 3)),
        )
        for name, n, cols, kind in (("big", MATS, C, BF16), ("little", 2, LANES, F32)):
            scratch.update(
                {
                    name + "_send": vm((n, Z, 2, Y, 2, SH, cols), kind),
                    name + "_core": vm((n, Z, 2, Y, SH, cols), kind),
                    name + "_xsum": vm((n, 2, Z, Y, SH, cols), kind),
                    name + "_rx": vm((n, Z, Y, SH, cols), kind),
                    name + "_zsum": vm((n, Z, Y, SH, cols), kind),
                    name + "_rz": vm((n, Z * Y - 1, SH, cols), kind),
                    name + "_ss": dma((n, 3)),
                    name + "_rs": dma((n, 3)),
                }
            )
    if not fast:
        scratch.update(gp=vm((C, C), F32))
    names = list(operands) + list(outs) + list(scratch)
    out_s, gin_s, gmats, gpair, grows = pl.pallas_call(
        functools.partial(block_kernel, cfg, names),
        out_shape=tuple(outs.values()),
        in_specs=specs,
        out_specs=tuple(out_specs),
        scratch_shapes=list(scratch.values()),
        compiler_params=pltpu.CompilerParams(collective_id=0, has_side_effects=True, vmem_limit_bytes=63 << 20),
    )(*operands.values())
    if not fast:
        gmats = lax.psum_scatter(gmats, axes, scatter_dimension=1, tiled=True)
        gpair = lax.psum_scatter(gpair, axes, scatter_dimension=0, tiled=True)
        grows = lax.psum_scatter(grows, axes, scatter_dimension=1, tiled=True).T
    sizes_out = (
        ((U, F, C), BF16), ((U, F, C), BF16), ((LAYERS, KERNEL, SH), F32), ((LAYERS, SH, C), F32), ((LAYERS, SH), F32),
        ((LAYERS, SH), F32), ((SH, SE), F32), ((SH, SE), F32), ((SH, C), F32),
    )
    done = pl.pallas_call(
        functools.partial(finish_kernel, cfg),
        out_shape=tuple(sd(*size) for size in sizes_out),
        in_specs=[sm_spec] + [any_spec] * 5,
        out_specs=(any_spec,) * 9,
        scratch_shapes=[
            vm((2, U, F, C), BF16), vm((MATS, SH, C), F32), vm((SH, LANES), F32), vm((SH, LANES), F32),
            vm((LANES, LANES), F32),
            vm((LAYERS, KERNEL, SH), F32), vm((LAYERS, SH), F32), vm((LAYERS, SH), F32), vm((SH, SE), F32),
            vm((SH, SE), F32), dma((2, 2, U)), dma((10,)),
        ],
    )(lengths, out_s, gin_s, gmats, gpair, grows)
    return done[:7] + (done[7].T, done[8])


def solution(mesh):
    both = ("dp", "tm")
    rows, cols = P(both, None), P(None, both)
    frames = P("dp", "tm", None)
    taps, mats = P(None, None, both), P(None, both, None)
    sizes = (mesh.shape["dp"], mesh.shape["tm"])
    return jax.shard_map(
        functools.partial(local, sizes),
        mesh=mesh,
        in_specs=(frames, P(), taps, mats, cols, cols, rows, cols, rows, frames),
        out_specs=(frames, frames, taps, mats, cols, cols, rows, cols, rows),
        check_vma=False,
    )
```
